32 devices in a mesh: section: 2 (over y), dp: 16 (over z, x, core).
Axes of the slice: x: 2, y: 2, z: 4, core: 2. Of those that a mesh axis runs over, the one named last changes fastest.
Arguments:
- boundary: bfloat16 [2, 32, 1024, 768], P('section', 'dp'), may hold values from -6 to 6
- doc_lengths: int32 [32], P('dp'), may hold values from 256 to 1024, as said below
- horizontal: int32 [32, 1024], P('dp'), may hold values from 0 to 511
- vertical: int32 [32, 1024], P('dp'), may hold values from 0 to 511
- attention_in: bfloat16 [2, 768, 2304], P('section'), may hold values from -0.21875 to 0.21875
- attention_out: bfloat16 [2, 768, 768], P('section'), may hold values from -1.75 to 1.75
- expand_weight: bfloat16 [2, 768, 3072], P('section'), may hold values from -0.21875 to 0.21875
- contract_weight: bfloat16 [2, 768, 3072], P('section'), may hold values from -0.109375 to 0.109375
- norm_gains: bfloat16 [2, 2, 768], P('section'), may hold values from 0.5 to 1.5
- bias_rows: bfloat16 [2, 6, 768], P('section'), may hold values from -3 to 3
- expand_bias: bfloat16 [2, 3072], P('section'), may hold values from -3 to 3
- position_table: bfloat16 [2, 32, 12], P('section'), may hold values from -3 to 3
- horizontal_table: bfloat16 [2, 31, 12], P('section'), may hold values from -3 to 3
- vertical_table: bfloat16 [2, 31, 12], P('section'), may hold values from -3 to 3
Outputs:
- boundary_out: bfloat16 [2, 32, 1024, 768], P('section', 'dp')
- grad_attention_in: float32 [2, 768, 2304], P('section')
- grad_attention_out: float32 [2, 768, 768], P('section')
- grad_expand_weight: float32 [2, 768, 3072], P('section')
- grad_contract_weight: float32 [2, 768, 3072], P('section')
- grad_norm_gains: float32 [2, 2, 768], P('section')
- grad_bias_rows: float32 [2, 6, 768], P('section')
- grad_expand_bias: float32 [2, 3072], P('section')
- grad_position_table: float32 [2, 32, 12], P('section')
- grad_horizontal_table: float32 [2, 31, 12], P('section')
- grad_vertical_table: float32 [2, 31, 12], P('section')
The draws below stay inside these ranges and needn't reach their ends.
Inputs may be any that keep to these rules, and one draw needn't show every extreme that they name: A window's tokens fill its first doc_lengths slots and the rest is padding; in every draw some window has 1024 tokens and some has 256.
All inputs are finite; a program needn't handle non-finite values.
Results may differ from the reference program's by a relative error of at most 0.03.
Values may be sent and summed in bfloat16 or wider, within the bound.
No kernel may reach another device: no remote copies, remote signals or barrier semaphores. Data moves between devices by JAX's collectives and lax.ppermute only.
A program may use at most 448 MiB of HBM per device.

```python
import jax
import jax.numpy as jnp
from jax import lax

D = 768
H = 12
FF = 3072
BUCKETS = 32
GRID = 16
XB = 31
SPAN = 32
WIN = 1024
BLK = 512
DOCS = 32


def draw_doc_lengths(key, part):
    key_values, key_chosen = jax.random.split(jax.random.fold_in(key, 3))
    values = jax.random.randint(key_values, (DOCS,), WIN // 4, WIN + 1, dtype=jnp.int32)
    chosen = jax.random.randint(key_chosen, (), 0, DOCS, dtype=jnp.int32)
    doc_ids = jnp.arange(DOCS, dtype=jnp.int32)
    values = jnp.where(doc_ids == chosen, WIN, values)
    return jnp.where(doc_ids == (chosen + 1) % DOCS, WIN // 4, values)


def coordinate_draw(key, horizontal_axis):
    page_size = GRID * SPAN
    key_jitter, key_edge = jax.random.split(key)
    slot_ids = jnp.arange(WIN, dtype=jnp.int32)[None, :]
    if horizontal_axis:
        step_size = page_size // 24
        line_base = slot_ids % 24 * step_size
    else:
        step_size = page_size // (WIN // 24 + 1)
        line_base = slot_ids // 24 * step_size
    jitter = jax.random.randint(key_jitter, (DOCS, WIN), 0, step_size, dtype=jnp.int32)
    values = line_base + jitter
    flat_ids = jnp.arange(DOCS * WIN, dtype=jnp.int32).reshape(DOCS, WIN)
    chosen = jax.random.randint(key_edge, (), 0, DOCS * WIN, dtype=jnp.int32)
    return jnp.where(flat_ids == chosen, page_size - 1, values)


def draw_horizontal(key, part):
    return coordinate_draw(jax.random.fold_in(key, 7), True)


def draw_vertical(key, part):
    return coordinate_draw(jax.random.fold_in(key, 11), False)


def block_scale(stream_key, dims, pieces, low, largest):
    def one(position, shards_of):
        steps = jax.random.uniform(jax.random.fold_in(jax.random.fold_in(stream_key, 6), position), (shards_of,), jnp.float32, low / len(pieces), largest / len(pieces))
        return jnp.repeat(jnp.exp(steps), dims[position] // shards_of).reshape((-1,) + (1,) * (len(dims) - position - 1))

    gain = one(*pieces[0])
    for cut in pieces[1:]:
        gain = gain * one(*cut)
    return gain


def gaussian(rng, extent, spread, most, pieces=(), kind=jnp.bfloat16):
    result = jax.random.normal(rng, extent, jnp.float32) * spread
    if len(pieces) > 0:
        result = block_scale(rng, extent, pieces, -0.22, 0.18) * result
    return jnp.clip(result, min=-most, max=most).astype(kind)


def setup_inputs(seed: int = 0) -> dict:
    streams_of = jax.random.split(jax.random.key(seed), 15)
    boundary = gaussian(streams_of[0], (2, DOCS, WIN, D), 1.0, 6.0, ((0, 2), (1, 16)))
    doc_lengths = draw_doc_lengths(jax.random.fold_in(streams_of[14], 71), 0)
    horizontal = draw_horizontal(jax.random.fold_in(streams_of[14], 71), 0)
    vertical = draw_vertical(jax.random.fold_in(streams_of[14], 71), 0)
    attention_in = gaussian(streams_of[4], (2, D, 3 * D), D ** -0.5, 0.21875, ((0, 2),))
    attention_out = gaussian(streams_of[5], (2, D, D), (D // 64) ** -0.5, 1.75, ((0, 2),))
    expand_weight = gaussian(streams_of[6], (2, D, FF), D ** -0.5, 0.21875, ((0, 2),))
    contract_weight = gaussian(streams_of[7], (2, D, FF), FF ** -0.5, 0.109375, ((0, 2),))
    norm_gains = jnp.clip(1.0 + 0.1 * jax.random.normal(streams_of[8], (2, 2, D), jnp.float32), 0.5, 1.5).astype(jnp.bfloat16)
    bias_rows = gaussian(streams_of[9], (2, 6, D), 0.5, 3.0, ((0, 2),))
    expand_bias = gaussian(streams_of[10], (2, FF), 0.5, 3.0, ((0, 2),))
    position_table = gaussian(streams_of[11], (2, BUCKETS, H), 0.5, 3.0, ((0, 2),))
    horizontal_table = gaussian(streams_of[12], (2, XB, H), 0.5, 3.0, ((0, 2),))
    vertical_table = gaussian(streams_of[13], (2, XB, H), 0.5, 3.0, ((0, 2),))
    return dict(boundary=boundary, doc_lengths=doc_lengths, horizontal=horizontal, vertical=vertical, attention_in=attention_in, attention_out=attention_out, expand_weight=expand_weight, contract_weight=contract_weight, norm_gains=norm_gains, bias_rows=bias_rows, expand_bias=expand_bias, position_table=position_table, horizontal_table=horizontal_table, vertical_table=vertical_table)


@jax.custom_vjp
def low(v):
    return lax.optimization_barrier(v.astype(jnp.bfloat16)).astype(jnp.float32)

@jax.custom_vjp
def low_back(v):
    return v

def low_keep(v):
    return (low(v), None)

def low_pass(kept, grad):
    return (grad,)

def back_keep(v):
    return (v, None)

def back_low(kept, grad):
    return (low(grad),)
low.defvjp(low_keep, low_pass)
low_back.defvjp(back_keep, back_low)
epsilon = 1e-05
masked_score = -1e+30
score_scale = 0.125

def matmul_high(left_side, right_side):
    return jnp.dot(left_side, right_side, precision=lax.Precision.HIGHEST, preferred_element_type=jnp.float32)

def layer_norm(summed, norm_gain, offset):
    center = summed - lax.optimization_barrier(jnp.mean(summed, axis=-1, keepdims=True))
    second = lax.optimization_barrier(jnp.mean(center * center, axis=-1, keepdims=True))
    return center * lax.rsqrt(second + epsilon) * norm_gain + offset

def attention_block(block_begin, query_heads, key_heads, value_heads, tables, horizontal_row, vertical_row, key_valid):
    position_rows, horizontal_rows, vertical_rows = tables
    slot_ids = jnp.arange(WIN).astype(jnp.int32)
    query_slots = lax.dynamic_slice_in_dim(slot_ids, block_begin, BLK, 0)
    query_across = lax.dynamic_slice_in_dim(horizontal_row, block_begin, BLK, 0)
    query_down = lax.dynamic_slice_in_dim(vertical_row, block_begin, BLK, 0)
    half_span = BUCKETS // 2
    position_ids = jnp.clip(query_slots[:, None] // SPAN - slot_ids[None, :] // SPAN, -half_span, half_span - 1) + half_span
    across_ids = query_across[:, None] // SPAN - horizontal_row[None, :] // SPAN + GRID - 1
    down_ids = query_down[:, None] // SPAN - vertical_row[None, :] // SPAN + GRID - 1
    rel_bias = position_rows[position_ids] + horizontal_rows[across_ids] + vertical_rows[down_ids]
    query_block = lax.dynamic_slice_in_dim(query_heads, block_begin, BLK, 0)
    scores = jnp.einsum('qhd,khd->hqk', query_block, key_heads, precision=lax.Precision.HIGHEST) * score_scale
    scores = low_back(scores + jnp.transpose(rel_bias, (2, 0, 1)))
    scores = jnp.where(key_valid[None, None, :], scores, masked_score)
    weights = jax.nn.softmax(scores, axis=-1)
    return jnp.einsum('hqk,khd->qhd', low(weights), value_heads, precision=lax.Precision.HIGHEST)

def layer_apply(params, layer_in, length, horizontal_row, vertical_row):
    attention_in, attention_out, expand_weight, contract_weight, gain_rows, bias_rows, expand_bias, position_rows, horizontal_rows, vertical_rows = params
    model_width = layer_in.shape[1]
    head_count = position_rows.shape[1]
    head_size = model_width // head_count
    joined_bias = jnp.concatenate([bias_rows[0], jnp.zeros_like(bias_rows[0]), bias_rows[1]])
    joined = low_back(matmul_high(layer_in, attention_in) + joined_bias)
    query_heads = low(joined[:, :model_width]).reshape(WIN, head_count, head_size)
    key_heads = low(joined[:, model_width:2 * model_width]).reshape(WIN, head_count, head_size)
    value_heads = low(joined[:, 2 * model_width:]).reshape(WIN, head_count, head_size)
    key_valid = jnp.arange(WIN).astype(jnp.int32) < length
    block_starts = (jnp.arange(WIN // BLK) * BLK).astype(jnp.int32)

    def one_block(block_begin):
        return attention_block(block_begin, query_heads, key_heads, value_heads, (position_rows, horizontal_rows, vertical_rows), horizontal_row, vertical_row, key_valid)
    attended = lax.map(jax.checkpoint(one_block), block_starts).reshape(WIN, model_width)
    attended_low = low(low_back(attended))
    summed_one = low_back(matmul_high(attended_low, attention_out) + bias_rows[2]) + layer_in
    hidden_one = layer_norm(summed_one, gain_rows[0], bias_rows[3])
    pre_gelu = low_back(matmul_high(low(hidden_one), expand_weight) + expand_bias)
    gelu_low = low(jax.nn.gelu(pre_gelu, approximate=False))
    summed_two = low_back(matmul_high(gelu_low, contract_weight.T) + bias_rows[4]) + hidden_one
    return layer_norm(summed_two, gain_rows[1], bias_rows[5])

def reference(boundary, doc_lengths, horizontal, vertical, attention_in, attention_out, expand_weight, contract_weight, norm_gains, bias_rows, expand_bias, position_table, horizontal_table, vertical_table):
    params = tuple((weight_set.astype(jnp.float32) for weight_set in (attention_in, attention_out, expand_weight, contract_weight, norm_gains, bias_rows, expand_bias, position_table, horizontal_table, vertical_table)))
    inputs_all = boundary[0].astype(jnp.float32)
    cotangent = boundary[1].astype(jnp.float32)

    def forward(params_all, inputs_given):
        first_params = tuple((entry[0] for entry in params_all))
        second_params = tuple((entry[1] for entry in params_all))

        def one_window(window_items):
            window_in, length, horizontal_row, vertical_row = window_items
            first_out = layer_apply(first_params, window_in, length, horizontal_row, vertical_row)
            second_in = low_back(low(first_out))
            return layer_apply(second_params, second_in, length, horizontal_row, vertical_row)
        return lax.map(jax.checkpoint(one_window), (inputs_given, doc_lengths, horizontal, vertical))
    outputs, pull_back = jax.vjp(forward, params, inputs_all)
    grad_params, grad_inputs = pull_back(cotangent)
    boundary_out = jnp.stack([grad_inputs.astype(jnp.bfloat16), outputs.astype(jnp.bfloat16)])
    return (boundary_out, grad_params[0], grad_params[1], grad_params[2], grad_params[3], grad_params[4], grad_params[5], grad_params[6], grad_params[7], grad_params[8], grad_params[9])
```

```python
import functools
import math

import jax
import jax.numpy as jnp
from jax import lax
from jax.experimental import pallas as pl
from jax.experimental.pallas import tpu as pltpu
from jax.sharding import PartitionSpec as P

GRID = 16
SPAN = 32
KEY_BLOCK = 256
ROW_BLOCK = 256
FF_BLOCK = 768
HALF = 64
PAIR = 128

epsilon = 1e-05
masked = -1e30
score_scale = 0.125
VMEM_LIMIT = 58 * 1024 * 1024

f32 = jnp.float32
bf16 = jnp.bfloat16

dot_nn = lambda a, b: lax.dot_general(a, b, (((1,), (0,)), ((), ())), preferred_element_type=f32)
dot_nt = lambda a, b: lax.dot_general(a, b, (((1,), (1,)), ((), ())), preferred_element_type=f32)
dot_tn = lambda a, b: lax.dot_general(a, b, (((0,), (0,)), ((), ())), preferred_element_type=f32)


def params_for(axes):
    return pltpu.CompilerParams(
        dimension_semantics=("arbitrary",) * axes, vmem_limit_bytes=VMEM_LIMIT
    )


ANY = pl.BlockSpec(memory_space=pl.ANY)


def like(a):
    return jax.ShapeDtypeStruct(a.shape, a.dtype)


def fixed(shape):
    return pl.BlockSpec(shape, lambda i, sp: (0,) * len(shape), pipeline_mode=pl.Buffered(1))


def stacked(rows, cols):
    return pl.BlockSpec((1, rows, cols), lambda i, sp: (sp[0], i, 0))


def plain(rows, cols):
    return pl.BlockSpec((rows, cols), lambda i, sp: (i, 0))


def call(body, sp, grid, ins, outs, aliased, scratch=(), us=10):
    operands = [a for a, _ in ins] + [a for a, _ in aliased]
    in_specs = [s for _, s in ins] + [ANY] * len(aliased)
    out_shape = [like(a) for a, _ in aliased] + [s for s, _ in outs]
    out_specs = [s for _, s in aliased] + [s for _, s in outs]
    kept = len(aliased)
    first = len(ins)

    def run(sp_ref, *refs):
        body(sp_ref, *refs[:first], *refs[first + kept :])

    return pl.pallas_call(
        run,
        grid_spec=pltpu.PrefetchScalarGridSpec(
            num_scalar_prefetch=1,
            grid=grid,
            in_specs=in_specs,
            out_specs=out_specs,
            scratch_shapes=list(scratch),
        ),
        out_shape=out_shape,
        input_output_aliases={1 + first + j: j for j in range(kept)},
        compiler_params=params_for(len(grid)),
        cost_estimate=pl.CostEstimate(
            flops=us * 1_000_000_000, bytes_accessed=us * 1_000_000, transcendentals=0
        ),
    )(sp, *operands)


def unwritten(shapes):
    return pl.pallas_call(
        lambda *refs: None, out_shape=shapes, out_specs=[ANY] * len(shapes)
    )()


def qkv_body(sp, x_ref, w_ref, b_ref, q_ref, kv_ref, fresh_ref):
    width = x_ref.shape[2]
    x = x_ref[0]
    q = dot_nn(x, w_ref[:, :width]) + b_ref[:, :width]
    q_ref[0] = (q.astype(bf16) * score_scale).astype(bf16)
    kv = (dot_nn(x, w_ref[:, width:]) + b_ref[:, width:]).astype(bf16)
    for begin in range(0, width, PAIR):
        for part, at in ((kv[:, begin : begin + PAIR], 0), (kv[:, width + begin : width + begin + PAIR], PAIR)):
            cols = slice(2 * begin + at, 2 * begin + at + PAIR)
            kv_ref[0, :, cols] = part
            fresh_ref[:, cols] = part


def qkv_call(sp, x_all, weight, bias, q_all, kv_all):
    rows, width = x_all.shape[1], x_all.shape[2]
    return call(
        qkv_body,
        sp,
        (rows // ROW_BLOCK,),
        [
            (x_all, stacked(ROW_BLOCK, width)),
            (weight, fixed(weight.shape)),
            (bias, fixed(bias.shape)),
        ],
        [(jax.ShapeDtypeStruct((rows, 2 * width), bf16), plain(ROW_BLOCK, 2 * width))],
        [(q_all, stacked(ROW_BLOCK, width)), (kv_all, stacked(ROW_BLOCK, 2 * width))],
        us=5,
    )


def low_half(shape):
    return lax.broadcasted_iota(jnp.int32, shape, 1) < HALF


def split_three(value, lane):
    high = value.astype(bf16).astype(f32)
    rest = value - high
    mid = rest.astype(bf16).astype(f32)
    last = rest - mid
    place = lane % HALF
    out = jnp.where(place == 0, high, jnp.where(place == 1, mid, jnp.where(place == 2, last, 0.0)))
    return out.astype(bf16)


def key_side(hot_ref, m_ref, begin, rows, length):
    ks = dot_nn(hot_ref[0, pl.ds(begin, rows), :], m_ref[...])
    lane = lax.broadcasted_iota(jnp.int32, ks.shape, 1)
    slot = lax.broadcasted_iota(jnp.int32, ks.shape, 0) + begin
    position_cells = 2 * rows // SPAN
    dead = (slot >= length) & (lane % HALF < position_cells)
    return jnp.where(dead, masked, ks).astype(bf16)


def attend_body(
    sp, q_ref, own_ref, peer_ref, hot_ref, m_ref, a_ref, rest_ref, lse_ref, kept_ref, kc, vc,
):
    rows = q_ref.shape[1]
    own = pl.multiple_of(sp[2] * rows, rows)
    peer = pl.multiple_of(rows - sp[2] * rows, rows)
    low = low_half((rows, PAIR))
    one = jnp.ones((rows, PAIR), bf16)
    for begin, kv_ref in ((own, own_ref), (peer, peer_ref)):
        k = kv_ref[:, :PAIR]
        v = kv_ref[:, PAIR:]
        ks = key_side(hot_ref, m_ref, begin, rows, sp[3])
        kc[0, pl.ds(begin, rows), :] = jnp.where(low, k, ks)
        kc[1, pl.ds(begin, rows), :] = jnp.where(low, ks, k)
        vc[0, pl.ds(begin, rows), :] = jnp.where(low, v, one)
        vc[1, pl.ds(begin, rows), :] = jnp.where(low, one, v)
    kept_ref[0] = peer_ref[...]

    def variant(keys):
        block_low = low_half((ROW_BLOCK, PAIR))
        lane = lax.broadcasted_iota(jnp.int32, (ROW_BLOCK, PAIR), 1)
        for r in range(0, rows, ROW_BLOCK):
            q = q_ref[0, r : r + ROW_BLOCK, :]
            side = hot_ref[0, pl.ds(own + r, ROW_BLOCK), :]
            outs = []
            peaks = []
            for head in (0, 1):
                cat = jnp.where(block_low, q, side) if head == 0 else jnp.where(block_low, side, q)
                s = dot_nt(cat, kc[head, :keys, :])
                peak = jnp.max(s, axis=1, keepdims=True)
                e = jnp.exp(s - peak).astype(bf16)
                outs.append(dot_nn(e, vc[head, :keys, :]))
                peaks.append(peak)
            top = jnp.where(block_low, outs[0], outs[1])
            total = pltpu.roll(jnp.where(block_low, outs[1], outs[0]), HALF, 1)
            mixed = top / total
            mixed_low = mixed.astype(bf16)
            a_ref[0, r : r + ROW_BLOCK, :] = mixed_low
            rest_ref[0, r : r + ROW_BLOCK, :] = (mixed - mixed_low.astype(f32)).astype(bf16)
            lse = jnp.where(block_low, peaks[0], peaks[1]) + jnp.log(total)
            lse_ref[0, r : r + ROW_BLOCK, :] = split_three(-lse, lane)

    for blocks in range(1, 2 * rows // KEY_BLOCK + 1):
        pl.when(sp[1] == blocks)(functools.partial(variant, blocks * KEY_BLOCK))


def attend_call(sp, q_all, kv_own, kv_peer, hot2_all, matrix, bufs):
    rows, width = q_all.shape[1], q_all.shape[2]
    pairs = width // PAIR
    by_pair = pl.BlockSpec((1, rows, PAIR), lambda p, sp: (sp[0], 0, p))
    kv_spec = pl.BlockSpec((rows, 2 * PAIR), lambda p, sp: (0, p))
    kept_spec = pl.BlockSpec((1, rows, 2 * PAIR), lambda p, sp: (sp[0], 0, p))
    return call(
        attend_body,
        sp,
        (pairs,),
        [
            (q_all, by_pair),
            (kv_own, kv_spec),
            (kv_peer, kv_spec),
            (hot2_all, pl.BlockSpec((1, 2 * rows, PAIR), lambda p, sp: (sp[0], 0, 0))),
            (matrix, pl.BlockSpec((PAIR, PAIR), lambda p, sp: (0, p))),
        ],
        [],
        [(b, by_pair) for b in bufs[:-1]] + [(bufs[-1], kept_spec)],
        [pltpu.VMEM((2, 2 * rows, PAIR), bf16), pltpu.VMEM((2, 2 * rows, PAIR), bf16)],
        us=17,
    )


def gelu_both(x):
    mag = jnp.abs(x)
    t = 1.0 / (1.0 + (0.3275911 / math.sqrt(2.0)) * mag)
    bell = jnp.exp(x * x * -0.5)
    poly = t * (
        0.5 * 0.254829592
        + t * (
            0.5 * -0.284496736
            + t * (0.5 * 1.421413741 + t * (0.5 * -1.453152027 + t * (0.5 * 1.061405429)))
        )
    )
    tail = poly * bell
    cdf = jnp.where(x >= 0.0, 1.0 - tail, tail)
    return x * cdf, cdf + x * bell * (1.0 / math.sqrt(2.0 * math.pi))


def centered(u):
    c = u - jnp.mean(u, axis=1, keepdims=True)
    r = lax.rsqrt(jnp.mean(c * c, axis=1, keepdims=True) + epsilon)
    return c * r, r


def dense_body(
    sp, a_ref, x_ref, wo_ref, w1_ref, w2_ref, gain_ref, bias_ref, eb_ref,
    n1_ref, h1_ref, g_ref, d_ref, n2_ref, r_ref, y_ref, fresh_ref,
):
    u1 = dot_nn(a_ref[0], wo_ref[...]) + bias_ref[2:3, :] + x_ref[0].astype(f32)
    n1, r1 = centered(u1)
    h1 = n1 * gain_ref[0:1, :] + bias_ref[3:4, :]
    h1_low = h1.astype(bf16)
    n1_ref[0] = n1.astype(bf16)
    h1_ref[0] = h1_low
    u2 = h1 + bias_ref[4:5, :]
    for c in range(0, w1_ref.shape[1], FF_BLOCK):
        f = dot_nn(h1_low, w1_ref[:, c : c + FF_BLOCK]) + eb_ref[:, c : c + FF_BLOCK]
        g, d = gelu_both(f)
        g = g.astype(bf16)
        g_ref[0, :, c : c + FF_BLOCK] = g
        d_ref[0, :, c : c + FF_BLOCK] = d.astype(bf16)
        u2 = u2 + dot_nt(g, w2_ref[:, c : c + FF_BLOCK])
    n2, r2 = centered(u2)
    n2_ref[0] = n2.astype(bf16)
    y = (n2 * gain_ref[1:2, :] + bias_ref[5:6, :]).astype(bf16)
    y_ref[0] = y
    fresh_ref[...] = y
    r_ref[0] = jnp.where(low_half(r_ref.shape[1:]), r1, r2)


def dense_call(sp, a_all, x_all, wo, w1, w2, gains, biases, eb, bufs):
    rows, width = a_all.shape[1], a_all.shape[2]
    hidden = w1.shape[1]
    row = stacked(ROW_BLOCK, width)
    wide = stacked(ROW_BLOCK, hidden)
    n1_all, h1_all, g_all, d_all, n2_all, r_all, y_all = bufs
    return call(
        dense_body,
        sp,
        (rows // ROW_BLOCK,),
        [(a_all, row), (x_all, row)]
        + [(w, fixed(w.shape)) for w in (wo, w1, w2, gains, biases, eb)],
        [(jax.ShapeDtypeStruct((rows, width), bf16), plain(ROW_BLOCK, width))],
        [
            (n1_all, row), (h1_all, row), (g_all, wide), (d_all, wide), (n2_all, row),
            (r_all, stacked(ROW_BLOCK, PAIR)), (y_all, row),
        ],
        us=16,
    )


def column_sum(v):
    return jnp.sum(v, axis=0, keepdims=True)


def norm_back(dy, n, r, gain):
    dn = dy * gain
    return r * (dn - jnp.mean(dn, axis=1, keepdims=True) - n * jnp.mean(dn * n, axis=1, keepdims=True))


def dense_back_body(
    sp, dy_ref, n2_ref, r_ref, d_ref, n1_ref, a_ref, rest_ref, wo_ref, w1_ref, w2_ref, gain_ref, sel_ref,
    db2_ref, df_ref, db1_ref, st_ref, se_ref, do_ref, dd_ref,
):
    width = dy_ref.shape[2]
    dy = dy_ref[0].astype(f32)
    n2 = n2_ref[0].astype(f32)
    r = r_ref[0]
    r1, r2 = r[:, 0:1], r[:, HALF : HALF + 1]
    du2 = norm_back(dy, n2, r2, gain_ref[1:2, :])
    db2 = du2.astype(bf16)
    db2_ref[0] = db2
    dh1 = du2
    sums = []
    for c in range(0, w1_ref.shape[1], FF_BLOCK):
        df = dot_nn(db2, w2_ref[:, c : c + FF_BLOCK]) * d_ref[0, :, c : c + FF_BLOCK].astype(f32)
        sums.append(column_sum(df))
        df = df.astype(bf16)
        df_ref[0, :, c : c + FF_BLOCK] = df
        dh1 = dh1 + dot_nt(df, w1_ref[:, c : c + FF_BLOCK])
    n1 = n1_ref[0].astype(f32)
    du1 = norm_back(dh1, n1, r1, gain_ref[0:1, :])
    db1 = du1.astype(bf16)
    db1_ref[0] = db1
    do = dot_nt(db1, wo_ref[...]).astype(bf16)
    do_ref[...] = do
    mixed = do.astype(f32) * (a_ref[0].astype(f32) + rest_ref[0].astype(f32))
    mixed_low = mixed.astype(bf16)
    inner = dot_nn(mixed_low, sel_ref[...])
    inner = inner + dot_nn((mixed - mixed_low.astype(f32)).astype(bf16), sel_ref[...])
    lane = lax.broadcasted_iota(jnp.int32, inner.shape, 1)
    dd_ref[...] = split_three(-inner, lane)
    rows = [
        column_sum(du1), column_sum(dh1), column_sum(du2), column_sum(dy),
        column_sum(dh1 * n1), column_sum(dy * n2), jnp.zeros((2, width), f32),
    ]
    stats = jnp.concatenate(rows, axis=0)
    wide = jnp.concatenate(sums, axis=1)

    @pl.when(pl.program_id(0) == 0)
    def _():
        st_ref[0] = stats
        se_ref[0] = wide

    @pl.when(pl.program_id(0) != 0)
    def _():
        st_ref[0] += stats
        se_ref[0] += wide


def dense_back_call(sp, dy_all, n2_all, r_all, d_all, n1_all, a_all, rest_all, wo, w1, w2, gains, sel, bufs):
    rows, width = dy_all.shape[1], dy_all.shape[2]
    hidden = w1.shape[1]
    row = stacked(ROW_BLOCK, width)
    wide = stacked(ROW_BLOCK, hidden)
    db2_all, df_all, db1_all, st_all, se_all = bufs
    once = lambda a: pl.BlockSpec((1,) + a.shape[1:], lambda i, sp: (sp[0], 0, 0))
    return call(
        dense_back_body,
        sp,
        (rows // ROW_BLOCK,),
        [
            (dy_all, row), (n2_all, row), (r_all, stacked(ROW_BLOCK, PAIR)), (d_all, wide),
            (n1_all, row), (a_all, row), (rest_all, row),
        ]
        + [(w, fixed(w.shape)) for w in (wo, w1, w2, gains, sel)],
        [(jax.ShapeDtypeStruct((rows, width), bf16), plain(ROW_BLOCK, width))] * 2,
        [(db2_all, row), (df_all, wide), (db1_all, row), (st_all, once(st_all)), (se_all, once(se_all))],
        us=16,
    )


def attend_back_body(
    sp, q_ref, own_ref, peer_ref, hot2_ref, m_ref, lse_ref, do_ref, dd_ref, hot_ref,
    cell_ref, dq_ref, keep_ref, send_ref, kc, kt, vc, qc, dc, dk, dv,
):
    rows = q_ref.shape[1]
    total = 2 * rows
    own = pl.multiple_of(sp[2] * rows, rows)
    peer = pl.multiple_of(rows - sp[2] * rows, rows)
    low = low_half((rows, PAIR))
    place = lax.broadcasted_iota(jnp.int32, (rows, PAIR), 1)
    first = place < 3
    second = (place >= HALF) & (place < HALF + 3)
    ones = jnp.where((place % HALF) < 3, 1.0, 0.0).astype(bf16)
    only_low = jnp.where(first, 1.0, 0.0).astype(bf16)
    only_high = jnp.where(second, 1.0, 0.0).astype(bf16)
    for begin, kv_ref in ((own, own_ref), (peer, peer_ref)):
        k = kv_ref[0, :, :PAIR]
        v = kv_ref[0, :, PAIR:]
        ks = key_side(hot2_ref, m_ref, begin, rows, sp[3])
        kc[0, pl.ds(begin, rows), :PAIR] = jnp.where(low, k, ks)
        kc[1, pl.ds(begin, rows), :PAIR] = jnp.where(low, ks, k)
        kc[0, pl.ds(begin, rows), PAIR:] = only_low
        kc[1, pl.ds(begin, rows), PAIR:] = only_high
        vc[0, pl.ds(begin, rows), :] = jnp.where(low, v, ones)
        vc[1, pl.ds(begin, rows), :] = jnp.where(low, ones, v)
        kt[:, pl.ds(begin, rows)] = k.T
    q = q_ref[0]
    side = hot2_ref[0, pl.ds(own, rows), :]
    do = do_ref[...]
    dd = dd_ref[...]
    qc[0, :, :PAIR] = jnp.where(low, q, side)
    qc[1, :, :PAIR] = jnp.where(low, side, q)
    qc[0, :, PAIR:] = lse_ref[0]
    qc[1, :, PAIR:] = lse_ref[0]
    dc[0] = jnp.where(low, do, dd)
    dc[1] = jnp.where(low, dd, do)

    def variant(blocks):
        block_low = low_half((KEY_BLOCK, PAIR))
        dq = [None, None]
        for b in range(blocks):
            at = slice(b * KEY_BLOCK, (b + 1) * KEY_BLOCK)
            dvs = []
            dks = []
            for head in (0, 1):
                p = jnp.exp(dot_nt(kc[head, at, :], qc[head]))
                dp = dot_nt(vc[head, at, :], dc[head])
                ds = (p * dp).astype(bf16)
                dvs.append(dot_nn(p.astype(bf16), do_ref[...]))
                dks.append(dot_nn(ds, qc[head, :, :PAIR]))
                part = dot_nn(kt[head * HALF : (head + 1) * HALF, at], ds)
                dq[head] = part if dq[head] is None else dq[head] + part
            dv[at, :] = jnp.where(block_low, dvs[0], dvs[1]).astype(bf16)
            dk[0, at, :] = jnp.where(block_low, dks[0], dks[1]).astype(bf16)
            dk[1, at, :] = jnp.where(block_low, dks[1], dks[0]).astype(bf16)
        left = slice(blocks * KEY_BLOCK, total)
        if blocks * KEY_BLOCK < total:
            zero = jnp.zeros((total - blocks * KEY_BLOCK, PAIR), bf16)
            dv[left, :] = zero
            dk[0, left, :] = zero
            dk[1, left, :] = zero
        both = jnp.concatenate(dq, axis=0)
        dq_ref[...] = (both.T * score_scale).astype(bf16)

    for blocks in range(1, total // KEY_BLOCK + 1):
        pl.when(sp[1] == blocks)(functools.partial(variant, blocks))
    cell_ref[0] = dot_nn(hot_ref[0], dk[1])
    for begin, out_ref in ((own, keep_ref), (peer, send_ref)):
        out_ref[:, :PAIR] = dk[0, pl.ds(begin, rows), :]
        out_ref[:, PAIR:] = dv[pl.ds(begin, rows), :]


def attend_back_call(
    sp, q_all, kv_all, peer_all, hot2_all, matrix, lse_all, do, dd, hot_all, cell_all
):
    rows, width = q_all.shape[1], q_all.shape[2]
    pairs = width // PAIR
    by_pair = pl.BlockSpec((1, rows, PAIR), lambda p, sp: (sp[0], 0, p))
    flat = pl.BlockSpec((rows, PAIR), lambda p, sp: (0, p))
    kv_spec = pl.BlockSpec((1, rows, 2 * PAIR), lambda p, sp: (sp[0], 0, p))
    flat_kv = pl.BlockSpec((rows, 2 * PAIR), lambda p, sp: (0, p))
    total = 2 * rows
    out_kv = jax.ShapeDtypeStruct((rows, 2 * width), bf16)
    out = jax.ShapeDtypeStruct((rows, width), bf16)
    return call(
        attend_back_body,
        sp,
        (pairs,),
        [
            (q_all, by_pair),
            (kv_all, kv_spec),
            (peer_all, kv_spec),
            (hot2_all, pl.BlockSpec((1, total, PAIR), lambda p, sp: (sp[0], 0, 0))),
            (matrix, pl.BlockSpec((PAIR, PAIR), lambda p, sp: (0, p))),
            (lse_all, by_pair),
            (do, flat),
            (dd, flat),
            (hot_all, pl.BlockSpec((1, HALF, total), lambda p, sp: (sp[0], 0, 0))),
        ],
        [(out, flat), (out_kv, flat_kv), (out_kv, flat_kv)],
        [(cell_all, pl.BlockSpec((1, HALF, PAIR), lambda p, sp: (sp[0], 0, p)))],
        [
            pltpu.VMEM((2, total, 2 * PAIR), bf16),
            pltpu.VMEM((PAIR, total), bf16),
            pltpu.VMEM((2, total, PAIR), bf16),
            pltpu.VMEM((2, rows, 2 * PAIR), bf16),
            pltpu.VMEM((2, rows, PAIR), bf16),
            pltpu.VMEM((2, total, PAIR), bf16),
            pltpu.VMEM((total, PAIR), bf16),
        ],
        us=25,
    )


def input_back_body(
    sp, dq_ref, own_ref, got_ref, db1_ref, w_ref, dj_ref, sj_ref, dx_ref, fresh_ref
):
    width = dq_ref.shape[1]
    dq = dq_ref[...]
    both = own_ref[...].astype(f32) + got_ref[...].astype(f32)
    part = lambda at: jnp.concatenate(
        [both[:, p + at : p + at + PAIR] for p in range(0, 2 * width, 2 * PAIR)], axis=1
    )
    dk = part(0).astype(bf16)
    dv32 = part(PAIR)
    dv = dv32.astype(bf16)
    dj_ref[0, :, :width] = dq
    dj_ref[0, :, width : 2 * width] = dk
    dj_ref[0, :, 2 * width :] = dv
    dx = db1_ref[0].astype(f32)
    dx = dx + dot_nt(dq, w_ref[:, :width])
    dx = dx + dot_nt(dk, w_ref[:, width : 2 * width])
    dx = dx + dot_nt(dv, w_ref[:, 2 * width :])
    dx = dx.astype(bf16)
    dx_ref[0] = dx
    fresh_ref[...] = dx
    stats = jnp.concatenate(
        [column_sum(dq.astype(f32)), column_sum(dv32), jnp.zeros((6, width), f32)], axis=0
    )

    @pl.when(pl.program_id(0) == 0)
    def _():
        sj_ref[0] = stats

    @pl.when(pl.program_id(0) != 0)
    def _():
        sj_ref[0] += stats


def input_back_call(sp, dq, own, got, db1_all, weight, dj_all, sj_all, dx_all):
    rows, width = dq.shape
    row = stacked(ROW_BLOCK, width)
    flat = plain(ROW_BLOCK, width)
    flat_kv = plain(ROW_BLOCK, 2 * width)
    return call(
        input_back_body,
        sp,
        (rows // ROW_BLOCK,),
        [(dq, flat), (own, flat_kv), (got, flat_kv), (db1_all, row), (weight, fixed(weight.shape))],
        [(jax.ShapeDtypeStruct((rows, width), bf16), flat)],
        [
            (dj_all, stacked(ROW_BLOCK, 3 * width)),
            (sj_all, pl.BlockSpec((1,) + sj_all.shape[1:], lambda i, sp: (sp[0], 0, 0))),
            (dx_all, row),
        ],
        us=6,
    )


def bucket_maps(position_cells, counts):
    key = jnp.arange(HALF, dtype=jnp.int32)[:, None]
    query = jnp.arange(HALF, dtype=jnp.int32)[None, :]
    begins = (0, position_cells, position_cells + GRID, HALF)
    bucket = jnp.full((HALF, HALF), -1, jnp.int32)
    base = 0
    for j, offset in enumerate((counts[0] // 2, GRID - 1, GRID - 1)):
        inside = (key >= begins[j]) & (key < begins[j + 1]) & (query >= begins[j]) & (query < begins[j + 1])
        ids = jnp.clip(query - key, -offset, counts[j] - 1 - offset) + offset + base
        bucket = jnp.where(inside, ids, bucket)
        base += counts[j]
    return bucket[:, :, None] == jnp.arange(base, dtype=jnp.int32)


def cell_matrix(tables, maps):
    whole = jnp.concatenate(tables, axis=0)
    heads = whole.shape[1]
    whole = whole.reshape(-1, heads // 2, 2)[:, :, ::-1].reshape(-1, heads)
    m = jnp.einsum("bh,xcb->xhc", whole, maps.astype(bf16), preferred_element_type=f32)
    m = m.reshape(HALF, heads * HALF).astype(bf16)
    return jnp.concatenate([m, jnp.zeros_like(m)], axis=0)


def table_grads(cells, maps, counts):
    heads = cells.shape[1] // HALF
    whole = jnp.einsum(
        "xcb,xhc->bh", maps.astype(f32), cells.reshape(HALF, heads, HALF), precision=lax.Precision.HIGHEST
    )
    whole = whole.reshape(-1, heads // 2, 2)[:, :, ::-1].reshape(-1, heads)
    a, b = counts[0], counts[0] + counts[1]
    return [whole[:a], whole[a:b], whole[b:]]


class Ring:
    def __init__(self, count):
        self.count = count
        self.index = lax.axis_index("dp")
        bits = list(range(1, count.bit_length() - 1))
        turned = bits[:2][::-1] + bits[2:]
        self.steps = list(zip(bits, turned))

    def bit(self, step):
        even, odd = step
        return jnp.where(self.index % 2 == 0, (self.index >> even) & 1, (self.index >> odd) & 1)

    def send(self, a, step):
        even, odd = step
        pairs = [(i, i ^ (1 << (even if i % 2 == 0 else odd))) for i in range(self.count)]
        return lax.ppermute(a, "dp", pairs)

    def swap(self, a):
        return lax.ppermute(a, "dp", [(i, i ^ 1) for i in range(self.count)])

    def reduce(self, part):
        for step in self.steps:
            half = part.shape[0] // 2
            bit = self.bit(step)
            keep = lax.dynamic_slice_in_dim(part, bit * half, half, 0)
            give = lax.dynamic_slice_in_dim(part, (1 - bit) * half, half, 0)
            part = keep + self.send(give, step)
        return part

    def gather(self, part):
        for step in self.steps[::-1]:
            first = self.bit(step) == 0
            got = self.send(part, step)
            part = jnp.concatenate(
                [jnp.where(first, part, got), jnp.where(first, got, part)], axis=0
            )
        return part

    def whole(self, part):
        got = self.swap(part).astype(f32)
        part = part.astype(f32)
        first = self.index % 2 == 0
        return jnp.concatenate([jnp.where(first, part, got), jnp.where(first, got, part)], axis=0)

    def total(self, part):
        for bit in range(self.count.bit_length() - 1):
            part = part + lax.ppermute(part, "dp", [(i, i ^ (1 << bit)) for i in range(self.count)])
        return part


SLOTS = (
    (("F", 0), None),
    (("F", 1), ("F", 0)),
    (("F", 2), ("B", 0)),
    (("F", 3), ("F", 1)),
    (("B", 0), ("B", 1)),
    (None, ("F", 2)),
    (("B", 1), ("B", 2)),
    (None, ("F", 3)),
    (("B", 2), ("B", 3)),
    (("B", 3), None),
)


def on_device(
    boundary, doc_lengths, horizontal, vertical, attention_in, attention_out, expand_weight,
    contract_weight, norm_gains, bias_rows, expand_bias, position_table, horizontal_table,
    vertical_table,
):
    section = lax.axis_index("section")
    dp_count = lax.axis_size("dp")
    core = lax.axis_index("dp") % 2
    swap = [(i, i ^ 1) for i in range(dp_count)]
    exchange = lambda a: lax.ppermute(a, "dp", swap)

    own = boundary[0]
    micro, slots, width = own.shape
    rows = slots // 2
    windows = 2 * micro
    hidden = expand_weight.shape[2]
    heads = position_table.shape[2]
    pairs = heads // 2
    w_in, w_out, w1, w2 = attention_in[0], attention_out[0], expand_weight[0], contract_weight[0]
    gains = norm_gains[0].astype(f32)
    biases = bias_rows[0].astype(f32)
    eb = expand_bias.astype(f32)
    in_bias = jnp.concatenate([biases[0], jnp.zeros_like(biases[0]), biases[1]])[None]
    tables = (position_table[0], horizontal_table[0], vertical_table[0])
    counts = tuple(t.shape[0] for t in tables)
    position_cells = slots // SPAN
    maps = bucket_maps(position_cells, counts)
    ring = Ring(dp_count)

    def both(mine, theirs):
        return jnp.concatenate(
            [jnp.where(core == 0, mine, theirs), jnp.where(core == 0, theirs, mine)], axis=0
        )

    halves = own.reshape(micro, 2, rows, width)
    own_half = jnp.where(core == 0, halves[:, 0], halves[:, 1])
    other_half = jnp.where(core == 0, halves[:, 1], halves[:, 0])
    own_all = both(own_half, exchange(other_half))
    places = jnp.concatenate(
        [horizontal, vertical, jnp.broadcast_to(doc_lengths[:, None], (micro, PAIR))], axis=1
    )
    places = both(places, exchange(places))
    across_cell = places[:, :slots] // SPAN
    down_cell = places[:, slots : 2 * slots] // SPAN
    lengths = places[:, 2 * slots]
    ids = jnp.arange(slots, dtype=jnp.int32)
    cell_ids = jnp.arange(HALF, dtype=jnp.int32)
    position_cell = jnp.broadcast_to((ids // SPAN)[None], (windows, slots))

    def hot_of(cells, axis):
        p, a, d = (jnp.expand_dims(c, axis) for c in cells)
        lanes = cell_ids[None, :, None] if axis == 1 else cell_ids[None, None, :]
        return (
            (lanes == p) | (lanes == a + position_cells) | (lanes == d + position_cells + GRID)
        ).astype(bf16)

    cells = (position_cell, across_cell, down_cell)
    hot_all = hot_of(cells, 1)
    hot2_all = hot_of(cells, 2)
    hot2_all = jnp.concatenate([hot2_all, hot2_all], axis=2)
    matrix = cell_matrix(tables, maps)

    lane_ids = jnp.arange(width, dtype=jnp.int32)
    sel = (lane_ids[:, None] // HALF == (lane_ids[None, :] // HALF) ^ 1).astype(bf16)

    blocks_of = (lengths + KEY_BLOCK - 1) // KEY_BLOCK
    infos = []
    for zero, one in SLOTS:
        w = jnp.where(section == 0, zero[1] if zero else 0, one[1] if one else 0).astype(jnp.int32)
        infos.append(jnp.stack([w, blocks_of[w], core.astype(jnp.int32), lengths[w]]))

    widths = dict(
        q=width, kv=2 * width, a=width, rest=width, lse=width, peer=2 * width, n1=width, h1=width,
        g=hidden, d=hidden, n2=width, y=width, db2=width, df=hidden, db1=width, dj=3 * width, dx=width,
    )
    shapes = {n: jax.ShapeDtypeStruct((windows, rows, c), bf16) for n, c in widths.items()}
    shapes["r"] = jax.ShapeDtypeStruct((windows, rows, PAIR), f32)
    shapes["st"] = shapes["sj"] = jax.ShapeDtypeStruct((windows, 8, width), f32)
    shapes["se"] = jax.ShapeDtypeStruct((windows, 1, hidden), f32)
    shapes["cell"] = jax.ShapeDtypeStruct((windows, HALF, width), f32)
    st = dict(zip(shapes, unwritten(list(shapes.values()))))
    st.update(x=own_all, dy=own_all)

    def forward_pre(sp, s):
        q, kv, fresh = qkv_call(sp, s["x"], w_in, in_bias, s["q"], s["kv"])
        return dict(s, q=q, kv=kv), fresh

    def forward_post(sp, s, kv_own, kv_peer):
        mixed = ("a", "rest", "lse", "peer")
        s = dict(s)
        s.update(
            zip(mixed, attend_call(
                sp, s["q"], kv_own, kv_peer, hot2_all, matrix, tuple(s[n] for n in mixed)
            ))
        )
        names = ("n1", "h1", "g", "d", "n2", "r", "y")
        outs = dense_call(
            sp, s["a"], s["x"], w_out, w1, w2, gains, biases, eb, tuple(s[n] for n in names)
        )
        s.update(zip(names, outs[:-1]))
        return s, outs[-1]

    def dense_back(sp, s):
        names = ("db2", "df", "db1", "st", "se")
        outs = dense_back_call(
            sp, s["dy"], s["n2"], s["r"], s["d"], s["n1"], s["a"], s["rest"], w_out, w1, w2, gains, sel,
            tuple(s[n] for n in names),
        )
        s = dict(s)
        s.update(zip(names, outs[:5]))
        return s, tuple(outs[5:])

    def attend_back(sp, s, grads):
        cell, dq, keep, send = attend_back_call(
            sp, s["q"], s["kv"], s["peer"], hot2_all, matrix, s["lse"], *grads, hot_all, s["cell"]
        )
        return dict(s, cell=cell), (dq, keep), send

    def backward_pre(sp, s):
        s, grads = dense_back(sp, s)
        return attend_back(sp, s, grads)

    def backward_post(sp, s, own_parts, received):
        dj, sj, dx, fresh = input_back_call(
            sp, *own_parts, received, s["db1"], w_in, s["dj"], s["sj"], s["dx"]
        )
        return dict(s, dj=dj, sj=sj, dx=dx), fresh

    def put(name, s, sp, value, role):
        w = sp[0]
        old = lax.dynamic_index_in_dim(s[name], w, 0, keepdims=False)
        new = jnp.where(section == role, value, old)
        return dict(s, **{name: lax.dynamic_update_index_in_dim(s[name], new, w, 0)})

    blank_row = jnp.zeros((rows, width), bf16)
    blank_kv = jnp.zeros((rows, 2 * width), bf16)
    inbox = {}

    for number, (zero, one) in enumerate(SLOTS[:-1]):
        sp = infos[number]
        kinds = (zero[0] if zero else None, one[0] if one else None)
        if one and one[0] == "F":
            st = put("x", st, sp, inbox.pop(("F", one[1])), 1)
        if zero and zero[0] == "B":
            st = put("dy", st, sp, inbox.pop(("B", zero[1])), 0)
        if kinds == ("F", "F") or number == 0:
            st, fresh = forward_pre(sp, st)
            st, out = forward_post(sp, st, fresh, exchange(fresh))
        elif kinds == (None, "F"):
            active = section == 1
            st, fresh = lax.cond(
                active, lambda s: forward_pre(sp, s), lambda s: (s, blank_kv), st
            )
            peer = exchange(fresh)
            st, out = lax.cond(
                active, lambda s, a, b: forward_post(sp, s, a, b), lambda s, a, b: (s, blank_row),
                st, fresh, peer,
            )
        elif kinds == ("B", "B"):
            st, mine, send = backward_pre(sp, st)
            st, out = backward_post(sp, st, mine, exchange(send))
        else:

            def forward_start(s):
                s, fresh = forward_pre(sp, s)
                return s, (blank_row, blank_kv), fresh

            st, mine, send = lax.cond(
                section == 0, forward_start, lambda s: backward_pre(sp, s), st
            )
            send, inbox["F", 1] = lax.optimization_barrier((send, inbox["F", 1]))
            got = exchange(send)
            st, out = lax.cond(
                section == 0,
                lambda s, mine, send, got: forward_post(sp, s, send, got),
                lambda s, mine, send, got: backward_post(sp, s, mine, got),
                st, mine, send, got,
            )
        pairs = ([(0, 1)] if zero and zero[0] == "F" else []) + (
            [(1, 0)] if one and one[0] == "B" else []
        )
        if pairs:
            moved = lax.ppermute(out, "section", pairs)
            if (0, 1) in pairs:
                inbox[zero] = moved
            if (1, 0) in pairs:
                inbox[one] = moved

    def weight(a, b):
        left = st[a].reshape(windows * rows, st[a].shape[2])
        right = st[b].reshape(windows * rows, st[b].shape[2])
        half = left.shape[1] // 2
        part = lambda at: dot_tn(
            lax.dynamic_slice_in_dim(left, at * half, half, 1), right
        ).astype(bf16)
        return part(1 - core), part(core)

    def paired(give, keep):
        return keep + exchange(give)

    last = SLOTS[-1][0]
    sp = infos[-1]
    active = section == 0
    st = put("dy", st, sp, inbox.pop(last), 0)
    st, grads = lax.cond(
        active, lambda s: dense_back(sp, s), lambda s: (s, (blank_row,) * 2), st
    )
    sums_contract = ring.reduce(paired(*weight("db2", "g")))
    sums_expand = ring.reduce(paired(*weight("h1", "df")))
    st, mine, send = lax.cond(
        active, lambda s, g: attend_back(sp, s, g),
        lambda s, g: (s, (blank_row, blank_kv), blank_kv), st, grads,
    )
    got = exchange(send)
    st, out = lax.cond(
        active, lambda s, a, b: backward_post(sp, s, a, b), lambda s, a, b: (s, blank_row),
        st, mine, got,
    )
    (give_in, keep_in), (give_out, keep_out) = weight("x", "dj"), weight("a", "db1")
    beside = lambda a, b: jnp.concatenate([a, b], axis=1)
    sums_attend = ring.reduce(paired(beside(give_in, give_out), beside(keep_in, keep_out)))
    g_contract = ring.whole(ring.gather(sums_contract))
    g_expand = ring.whole(ring.gather(sums_expand))
    g_attend = ring.whole(ring.gather(sums_attend))
    g_in, g_out = g_attend[:, : 3 * width], g_attend[:, 3 * width :]

    sums = jnp.sum(st["st"], axis=0)
    joined_sums = jnp.sum(st["sj"], axis=0)
    wide = jnp.sum(st["se"], axis=0)
    small = [
        joined_sums[0:2], sums[0:6], wide,
    ] + table_grads(jnp.sum(st["cell"], axis=0), maps, counts)
    packed = jnp.concatenate([s.reshape(-1) for s in small])
    size = packed.shape[0]
    packed = jnp.pad(packed, (0, -size % 1024)).reshape(-1, PAIR)
    packed = ring.total(packed).reshape(-1)
    pieces = []
    begin = 0
    for s in small:
        count = math.prod(s.shape)
        pieces.append(packed[begin : begin + count].reshape(s.shape))
        begin += count
    joined_sums, sums, wide, table_p, table_h, table_v = pieces
    grad_bias = jnp.concatenate([joined_sums, sums[0:4]], axis=0)
    grad_gain = sums[4:6]

    result = jnp.where(section == 0, st["dx"], st["y"])
    mine_first, mine_second = result[:micro], result[micro:]
    keep = jnp.where(core == 0, mine_first, mine_second)
    give = exchange(jnp.where(core == 0, mine_second, mine_first))
    out_halves = jnp.stack(
        [jnp.where(core == 0, keep, give), jnp.where(core == 0, give, keep)], axis=1
    )
    boundary_out = out_halves.reshape(1, micro, slots, width)
    return (
        boundary_out, g_in[None], g_out[None], g_expand[None], g_contract[None], grad_gain[None], grad_bias[None], wide,
        table_p[None], table_h[None], table_v[None],
    )


def solution(mesh):
    section = P("section", None, None)
    placed = (
        P("section", "dp", None, None), P("dp"), P("dp", None), P("dp", None), section, section,
        section, section, section, section, P("section", None), section, section, section,
    )
    return jax.shard_map(
        on_device,
        mesh=mesh,
        in_specs=placed,
        out_specs=(
            P("section", "dp", None, None), section, section, section, section, section, section,
            P("section", None), section, section, section,
        ),
        check_vma=False,
    )
```

```python
import functools
import math

import jax
import jax.numpy as jnp
from jax import lax
from jax.experimental import pallas as pl
from jax.experimental.pallas import tpu as pltpu
from jax.sharding import PartitionSpec as P

GRID = 16
SPAN = 32
KEY_BLOCK = 256
ROW_BLOCK = 256
FF_BLOCK = 768
PAIRS = 2
HALF = 64
PAIR = 128

epsilon = 1e-05
masked = -1e30
score_scale = 0.125
VMEM_LIMIT = 40 * 1024 * 1024

f32 = jnp.float32
bf16 = jnp.bfloat16

dot_nn = lambda a, b: lax.dot_general(a, b, (((1,), (0,)), ((), ())), preferred_element_type=f32)
dot_nt = lambda a, b: lax.dot_general(a, b, (((1,), (1,)), ((), ())), preferred_element_type=f32)
dot_tn = lambda a, b: lax.dot_general(a, b, (((0,), (0,)), ((), ())), preferred_element_type=f32)


def params_for(axes):
    return pltpu.CompilerParams(
        dimension_semantics=("arbitrary",) * axes, vmem_limit_bytes=VMEM_LIMIT
    )


ANY = pl.BlockSpec(memory_space=pl.ANY)


def like(a):
    return jax.ShapeDtypeStruct(a.shape, a.dtype)


RESIDENT = pl.BlockSpec(memory_space=pltpu.VMEM)


def fixed(shape):
    return pl.BlockSpec(shape, lambda i, sp: (0,) * len(shape), pipeline_mode=pl.Buffered(1))


def this_step(count):
    return pl.ds(pl.multiple_of(pl.program_id(0) * count, count), count)


def stacked(rows, cols):
    return pl.BlockSpec((1, rows, cols), lambda i, sp: (sp[0], i, 0))


def plain(rows, cols):
    return pl.BlockSpec((rows, cols), lambda i, sp: (i, 0))


def call(body, sp, grid, ins, outs, aliased, scratch=(), us=10):
    operands = [a for a, _ in ins] + [a for a, _ in aliased]
    in_specs = [s for _, s in ins] + [ANY] * len(aliased)
    out_shape = [like(a) for a, _ in aliased] + [s for s, _ in outs]
    out_specs = [s for _, s in aliased] + [s for _, s in outs]
    kept = len(aliased)
    first = len(ins)

    def run(sp_ref, *refs):
        body(sp_ref, *refs[:first], *refs[first + kept :])

    return pl.pallas_call(
        run,
        grid_spec=pltpu.PrefetchScalarGridSpec(
            num_scalar_prefetch=1,
            grid=grid,
            in_specs=in_specs,
            out_specs=out_specs,
            scratch_shapes=list(scratch),
        ),
        out_shape=out_shape,
        input_output_aliases={1 + first + j: j for j in range(kept)},
        compiler_params=params_for(len(grid)),
        cost_estimate=pl.CostEstimate(
            flops=us * 1_000_000_000, bytes_accessed=us * 1_000_000, transcendentals=0
        ),
    )(sp, *operands)


def unwritten(shapes):
    return pl.pallas_call(
        lambda *refs: None, out_shape=shapes, out_specs=[ANY] * len(shapes),
        compiler_params=pltpu.CompilerParams(vmem_limit_bytes=2 * 1024 * 1024),
    )()


def in_vmem(arrays):
    def body(*refs):
        count = len(arrays)
        copies = [
            pltpu.make_async_copy(refs[j], refs[count + j], refs[-1].at[j]) for j in range(count)
        ]
        for copy in copies:
            copy.start()
        for copy in copies:
            copy.wait()

    return pl.pallas_call(
        body,
        out_shape=[pltpu.VMEM(a.shape, a.dtype) for a in arrays],
        in_specs=[ANY] * len(arrays),
        out_specs=[RESIDENT] * len(arrays),
        scratch_shapes=[pltpu.SemaphoreType.DMA((len(arrays),))],
        compiler_params=pltpu.CompilerParams(vmem_limit_bytes=2 * 1024 * 1024),
    )(*arrays)


def at_window(rows, cols):
    return pl.BlockSpec((1, rows, cols), lambda i, sp: (sp[0], 0, i))


def whole_window(rows, cols):
    return pl.BlockSpec((1, rows, cols), lambda i, sp: (sp[0], 0, 0))


def columns(rows, cols, begin=0):
    return pl.BlockSpec((rows, cols), lambda i, sp: (0, begin + i))


def qkv_body(sp, x_ref, got_ref, w_ref, b_ref, x_out, q_ref, kv_ref, fresh_ref):
    width = x_ref.shape[2]
    cols = q_ref.shape[2]
    x = jnp.where(sp[4] == 1, got_ref[...], x_ref[0])

    @pl.when(pl.program_id(0) == 0)
    def _():
        x_out[0] = x

    def part(j):
        at = pl.ds(pl.multiple_of(j * width + pl.program_id(0) * cols, cols), cols)
        return dot_nn(x, w_ref[:, at]) + b_ref[:, at]

    q_ref[0] = (part(0).astype(bf16) * score_scale).astype(bf16)
    k = part(1).astype(bf16)
    v = part(2).astype(bf16)
    for begin in range(0, cols, PAIR):
        for value, at in ((k, 0), (v, PAIR)):
            to = slice(2 * begin + at, 2 * begin + at + PAIR)
            kv_ref[0, :, to] = value[:, begin : begin + PAIR]
            fresh_ref[:, to] = value[:, begin : begin + PAIR]


def qkv_call(sp, own_all, got, weight, bias, x_all, q_all, kv_all):
    rows, width = x_all.shape[1], x_all.shape[2]
    cols = PAIRS * PAIR
    return call(
        qkv_body,
        sp,
        (width // cols,),
        [
            (own_all, whole_window(rows, width)), (got, fixed(got.shape)), (weight, RESIDENT),
            (bias, fixed(bias.shape)),
        ],
        [(jax.ShapeDtypeStruct((rows, 2 * width), bf16), columns(rows, 2 * cols))],
        [
            (x_all, whole_window(rows, width)), (q_all, at_window(rows, cols)),
            (kv_all, at_window(rows, 2 * cols)),
        ],
        us=4,
    )


def low_half(shape):
    return lax.broadcasted_iota(jnp.int32, shape, 1) < HALF


def split_three(value):
    place = lax.broadcasted_iota(jnp.int32, value.shape, 1) % HALF
    high = value.astype(bf16).astype(f32)
    rest = value - high
    mid = rest.astype(bf16).astype(f32)
    last = rest - mid
    out = jnp.where(place == 0, high, jnp.where(place == 1, mid, jnp.where(place == 2, last, 0.0)))
    return out.astype(bf16)


def in_order(first, own, peer):
    return jnp.concatenate([jnp.where(first, own, peer), jnp.where(first, peer, own)], axis=0)


def attend_body(
    sp, q_ref, own_ref, peer_ref, side_ref, hot_ref, m_ref, a_ref, rest_ref, lse_ref, kept_ref
):
    rows = q_ref.shape[1]
    first = sp[2] == 0
    kept_ref[0] = peer_ref[...]

    def variant(keys):
        low = low_half((rows, PAIR))
        key_low = low_half((keys, PAIR))
        one = jnp.ones((keys, PAIR), bf16)
        side = side_ref[0]
        hot = hot_ref[0, :keys, :]
        for n in range(PAIRS):
            cols = slice(n * PAIR, (n + 1) * PAIR)
            kv = slice(2 * n * PAIR, 2 * (n + 1) * PAIR)
            both = in_order(first, own_ref[:, kv], peer_ref[:, kv])[:keys]
            k, v = both[:, :PAIR], both[:, PAIR:]
            ks = dot_nn(hot, m_ref[:, cols]).astype(bf16)
            q = q_ref[0, :, cols]
            outs = []
            peaks = []
            for head in (0, 1):
                pick = (lambda m, x, y: jnp.where(m, x, y)) if head == 0 else (
                    lambda m, x, y: jnp.where(m, y, x)
                )
                s = dot_nt(pick(low, q, side), pick(key_low, k, ks))
                peak = jnp.max(s, axis=1, keepdims=True)
                e = jnp.exp(s - peak).astype(bf16)
                outs.append(dot_nn(e, pick(key_low, v, one)))
                peaks.append(peak)
            top = jnp.where(low, outs[0], outs[1])
            total = pltpu.roll(jnp.where(low, outs[1], outs[0]), HALF, 1)
            mixed = top / total
            mixed_low = mixed.astype(bf16)
            a_ref[0, :, cols] = mixed_low
            rest_ref[0, :, cols] = (mixed - mixed_low.astype(f32)).astype(bf16)
            lse = jnp.where(low, peaks[0], peaks[1]) + jnp.log(total)
            lse_ref[0, :, cols] = split_three(-lse)

    for blocks in range(1, 2 * rows // KEY_BLOCK + 1):
        pl.when(sp[1] == blocks)(functools.partial(variant, blocks * KEY_BLOCK))


def attend_call(sp, q_all, kv_own, kv_peer, side_all, hot_all, matrix, bufs):
    rows, width = q_all.shape[1], q_all.shape[2]
    cols = PAIRS * PAIR
    part = at_window(rows, cols)
    return call(
        attend_body,
        sp,
        (width // cols,),
        [
            (q_all, part),
            (kv_own, columns(rows, 2 * cols)),
            (kv_peer, columns(rows, 2 * cols)),
            (side_all, whole_window(rows, PAIR)),
            (hot_all, whole_window(2 * rows, PAIR)),
            (matrix, columns(PAIR, cols)),
        ],
        [],
        [(b, part) for b in bufs[:-1]] + [(bufs[-1], at_window(rows, 2 * cols))],
        us=14,
    )


def gelu_both(x):
    cdf = 0.5 + 0.5 * lax.erf(x * math.sqrt(0.5))
    bell = jnp.exp(x * x * -0.5)
    return x * cdf, cdf + x * bell * (1.0 / math.sqrt(2.0 * math.pi))


def centered(u):
    c = u - jnp.mean(u, axis=1, keepdims=True)
    r = lax.rsqrt(jnp.mean(c * c, axis=1, keepdims=True) + epsilon)
    return c * r, r


class Moves:
    def __init__(self, sems):
        self.sems = sems
        self.used = 0
        self.out = []

    def start(self, source, target):
        copy = pltpu.make_async_copy(source, target, self.sems.at[self.used])
        self.used += 1
        copy.start()
        return copy

    def write(self, source, target):
        self.out.append(self.start(source, target))

    def finish(self):
        for copy in self.out:
            copy.wait()


def chunks(width):
    return [slice(c, c + FF_BLOCK) for c in range(0, width, FF_BLOCK)]


def dense_body(
    sp, a_ref, x_ref, wo_ref, w1_ref, w2_ref, gain_ref, bias_ref, eb_ref,
    n1_hbm, h1_hbm, g_hbm, d_hbm, n2_hbm, r_hbm, fresh_ref,
    n1_ref, h1_ref, g_ref, d_ref, n2_ref, r_ref, sems,
):
    w = sp[0]
    moves = Moves(sems)
    parts = chunks(w1_ref.shape[1])
    u1 = dot_nn(a_ref[0], wo_ref[...]) + bias_ref[2:3, :] + x_ref[0].astype(f32)
    n1, r1 = centered(u1)
    h1 = n1 * gain_ref[0:1, :] + bias_ref[3:4, :]
    h1_low = h1.astype(bf16)
    n1_ref[...] = n1.astype(bf16)
    h1_ref[...] = h1_low
    moves.write(n1_ref, n1_hbm.at[w])
    moves.write(h1_ref, h1_hbm.at[w])
    u2 = h1 + bias_ref[4:5, :]
    for c in parts:
        g, d = gelu_both(dot_nn(h1_low, w1_ref[:, c]) + eb_ref[:, c])
        g = g.astype(bf16)
        g_ref[:, c] = g
        d_ref[:, c] = d.astype(bf16)
        moves.write(g_ref.at[:, c], g_hbm.at[w, :, c])
        moves.write(d_ref.at[:, c], d_hbm.at[w, :, c])
        u2 = u2 + dot_nt(g, w2_ref[:, c])
    n2, r2 = centered(u2)
    n2_ref[...] = n2.astype(bf16)
    moves.write(n2_ref, n2_hbm.at[w])
    r_ref[...] = jnp.where(low_half(r_ref.shape), r1, r2)
    moves.write(r_ref, r_hbm.at[w])
    fresh_ref[...] = (n2 * gain_ref[1:2, :] + bias_ref[5:6, :]).astype(bf16)
    moves.finish()


def dense_call(sp, a_all, x_all, wo, w1, w2, gains, biases, eb, bufs):
    rows, width = a_all.shape[1], a_all.shape[2]
    hidden = w1.shape[1]
    row = whole_window(rows, width)
    vmem = lambda *shape: pltpu.VMEM(shape, bf16)
    return call(
        dense_body,
        sp,
        (1,),
        [
            (a_all, row), (x_all, row), (wo, RESIDENT), (w1, RESIDENT), (w2, RESIDENT), (gains, fixed(gains.shape)),
            (biases, fixed(biases.shape)), (eb, fixed(eb.shape)),
        ],
        [(jax.ShapeDtypeStruct((rows, width), bf16), pl.BlockSpec((rows, width), lambda i, sp: (0, 0)))],
        [(b, ANY) for b in bufs],
        [
            vmem(rows, width), vmem(rows, width), vmem(rows, hidden), vmem(rows, hidden), vmem(rows, width),
            pltpu.VMEM((rows, PAIR), f32), pltpu.SemaphoreType.DMA((4 + 2 * (hidden // FF_BLOCK),)),
        ],
        us=10,
    )


def column_sum(v):
    return jnp.sum(v, axis=0, keepdims=True)


def norm_back(dy, n, r, gain):
    dn = dy * gain
    return r * (dn - jnp.mean(dn, axis=1, keepdims=True) - n * jnp.mean(dn * n, axis=1, keepdims=True))


def dense_back_body(
    sp, dy_ref, got_ref, n2_ref, r_ref, gain_ref, sel_ref, wo_ref, w1_ref, w2_ref, d_hbm, n1_hbm, a_hbm,
    rest_hbm, db2_hbm, df_hbm, db1_hbm, st_ref, se_ref, do_ref, dd_ref,
    d_ref, n1_ref, a_ref, rest_ref, db2_ref, df_ref, db1_ref, sems,
):
    w = sp[0]
    width = dy_ref.shape[2]
    moves = Moves(sems)
    parts = chunks(w1_ref.shape[1])
    loads = [moves.start(d_hbm.at[w, :, c], d_ref.at[:, c]) for c in parts]
    last = [
        moves.start(n1_hbm.at[w], n1_ref), moves.start(a_hbm.at[w], a_ref),
        moves.start(rest_hbm.at[w], rest_ref),
    ]
    r = r_ref[0]
    dy = jnp.where(sp[4] == 1, dy_ref[0], got_ref[...]).astype(f32)
    n2 = n2_ref[0].astype(f32)
    du2 = norm_back(dy, n2, r[:, HALF : HALF + 1], gain_ref[1:2, :])
    db2 = du2.astype(bf16)
    db2_ref[...] = db2
    moves.write(db2_ref, db2_hbm.at[w])
    st_ref[0, 2:3, :] = column_sum(du2)
    st_ref[0, 3:4, :] = column_sum(dy)
    st_ref[0, 5:6, :] = column_sum(dy * n2)
    st_ref[0, 6:8, :] = jnp.zeros((2, width), f32)
    dh1 = du2
    for c, load in zip(parts, loads):
        load.wait()
        df = dot_nn(db2, w2_ref[:, c]) * d_ref[:, c].astype(f32)
        se_ref[0, :, c] = column_sum(df)
        df = df.astype(bf16)
        df_ref[:, c] = df
        moves.write(df_ref.at[:, c], df_hbm.at[w, :, c])
        dh1 = dh1 + dot_nt(df, w1_ref[:, c])
    for load in last:
        load.wait()
    n1 = n1_ref[...].astype(f32)
    du1 = norm_back(dh1, n1, r[:, 0:1], gain_ref[0:1, :])
    db1 = du1.astype(bf16)
    db1_ref[...] = db1
    moves.write(db1_ref, db1_hbm.at[w])
    st_ref[0, 0:1, :] = column_sum(du1)
    st_ref[0, 1:2, :] = column_sum(dh1)
    st_ref[0, 4:5, :] = column_sum(dh1 * n1)
    do = dot_nt(db1, wo_ref[...]).astype(bf16)
    do_ref[...] = do
    mixed = do.astype(f32) * (a_ref[...].astype(f32) + rest_ref[...].astype(f32))
    high = mixed.astype(bf16)
    low = (mixed - high.astype(f32)).astype(bf16)
    for begin in range(0, width, PAIR):
        cols = slice(begin, begin + PAIR)
        inner = dot_nn(high[:, cols], sel_ref[...]) + dot_nn(low[:, cols], sel_ref[...])
        dd_ref[:, cols] = split_three(-inner)
    moves.finish()


def dense_back_call(
    sp, dy_all, got, n2_all, r_all, d_all, n1_all, a_all, rest_all, wo, w1, w2, gains, sel, bufs
):
    rows, width = got.shape
    hidden = w1.shape[1]
    row = whole_window(rows, width)
    db2_all, df_all, db1_all, st_all, se_all = bufs
    flat = (jax.ShapeDtypeStruct((rows, width), bf16), pl.BlockSpec((rows, width), lambda i, sp: (0, 0)))
    vmem = lambda *shape: pltpu.VMEM(shape, bf16)
    return call(
        dense_back_body,
        sp,
        (1,),
        [
            (dy_all, row), (got, fixed(got.shape)), (n2_all, row), (r_all, whole_window(rows, PAIR)),
            (gains, fixed(gains.shape)), (sel, fixed(sel.shape)), (wo, RESIDENT), (w1, RESIDENT),
            (w2, RESIDENT),
        ]
        + [(b, ANY) for b in (d_all, n1_all, a_all, rest_all)],
        [flat, flat],
        [
            (db2_all, ANY), (df_all, ANY), (db1_all, ANY), (st_all, whole_window(8, width)),
            (se_all, whole_window(1, hidden)),
        ],
        [
            vmem(rows, hidden), vmem(rows, width), vmem(rows, width), vmem(rows, width), vmem(rows, width),
            vmem(rows, hidden), vmem(rows, width), pltpu.SemaphoreType.DMA((5 + 2 * (hidden // FF_BLOCK),)),
        ],
        us=10,
    )


def attend_back_body(
    sp, q_ref, own_ref, peer_ref, side_ref, hot_ref, m_ref, lse_ref, do_ref, dd_ref, turned_ref,
    cell_ref, dq_ref, keep_ref, send_ref,
):
    rows = q_ref.shape[1]
    total = 2 * rows
    first = sp[2] == 0

    def variant(blocks):
        keys = blocks * KEY_BLOCK
        low = low_half((rows, PAIR))
        key_low = low_half((keys, PAIR))
        block_low = low_half((KEY_BLOCK, PAIR))
        place = lax.broadcasted_iota(jnp.int32, (KEY_BLOCK, PAIR), 1)
        three = jnp.where(place % HALF < 3, 1.0, 0.0).astype(bf16)
        lone = [
            jnp.where(place < 3, 1.0, 0.0).astype(bf16),
            jnp.where((place >= HALF) & (place < HALF + 3), 1.0, 0.0).astype(bf16),
        ]
        side = side_ref[0]
        hot = hot_ref[0, :keys, :]
        for n in range(PAIRS):
            cols = slice(n * PAIR, (n + 1) * PAIR)
            kv = slice(2 * n * PAIR, 2 * (n + 1) * PAIR)
            both = in_order(first, own_ref[0, :, kv], peer_ref[0, :, kv])[:keys]
            k, v = both[:, :PAIR], both[:, PAIR:]
            ks = dot_nn(hot, m_ref[:, cols]).astype(bf16)
            kt = k.T
            q = q_ref[0, :, cols]
            do = do_ref[:, cols]
            dd = dd_ref[:, cols]
            lse = lse_ref[0, :, cols]
            kc = (jnp.where(key_low, k, ks), jnp.where(key_low, ks, k))
            qc = (jnp.where(low, q, side), jnp.where(low, side, q))
            qe = tuple(jnp.concatenate([c, lse], axis=1) for c in qc)
            dc = (jnp.where(low, do, dd), jnp.where(low, dd, do))
            dq = [None, None]
            dks = []
            dvs = []
            gs = []
            for b in range(blocks):
                at = slice(b * KEY_BLOCK, (b + 1) * KEY_BLOCK)
                vb = v[at]
                vc = (jnp.where(block_low, vb, three), jnp.where(block_low, three, vb))
                part_v = []
                part_k = []
                for head in (0, 1):
                    kb = jnp.concatenate([kc[head][at], lone[head]], axis=1)
                    p = jnp.exp(dot_nt(kb, qe[head]))
                    dp = dot_nt(vc[head], dc[head])
                    ds = (p * dp).astype(bf16)
                    part_v.append(dot_nn(p.astype(bf16), do))
                    part_k.append(dot_nn(ds, qc[head]))
                    part = dot_nn(kt[head * HALF : (head + 1) * HALF, at], ds)
                    dq[head] = part if dq[head] is None else dq[head] + part
                dvs.append(jnp.where(block_low, part_v[0], part_v[1]).astype(bf16))
                dks.append(jnp.where(block_low, part_k[0], part_k[1]).astype(bf16))
                gs.append(jnp.where(block_low, part_k[1], part_k[0]).astype(bf16))
            dq_ref[:, cols] = (jnp.concatenate(dq, axis=0).T * score_scale).astype(bf16)
            cell_ref[0, :, cols] = dot_nn(turned_ref[0, :, :keys], jnp.concatenate(gs, axis=0))
            if keys < total:
                zero = [jnp.zeros((total - keys, PAIR), bf16)]
                dks = dks + zero
                dvs = dvs + zero
            grads = jnp.concatenate([jnp.concatenate(dks, axis=0), jnp.concatenate(dvs, axis=0)], axis=1)
            keep_ref[:, kv] = jnp.where(first, grads[:rows], grads[rows:])
            send_ref[:, kv] = jnp.where(first, grads[rows:], grads[:rows])

    for blocks in range(1, total // KEY_BLOCK + 1):
        pl.when(sp[1] == blocks)(functools.partial(variant, blocks))


def attend_back_call(
    sp, q_all, kv_all, peer_all, side_all, hot_all, matrix, lse_all, do, dd, turned_all, cell_all
):
    rows, width = q_all.shape[1], q_all.shape[2]
    cols = PAIRS * PAIR
    part = at_window(rows, cols)
    kv = at_window(rows, 2 * cols)
    flat = columns(rows, cols)
    flat_kv = columns(rows, 2 * cols)
    out_kv = jax.ShapeDtypeStruct((rows, 2 * width), bf16)
    return call(
        attend_back_body,
        sp,
        (width // cols,),
        [
            (q_all, part),
            (kv_all, kv),
            (peer_all, kv),
            (side_all, whole_window(rows, PAIR)),
            (hot_all, whole_window(2 * rows, PAIR)),
            (matrix, columns(PAIR, cols)),
            (lse_all, part),
            (do, flat),
            (dd, flat),
            (turned_all, whole_window(HALF, 2 * rows)),
        ],
        [(jax.ShapeDtypeStruct((rows, width), bf16), flat), (out_kv, flat_kv), (out_kv, flat_kv)],
        [(cell_all, at_window(HALF, cols))],
        us=20,
    )


def input_back_body(
    sp, dq_ref, own_ref, got_ref, db1_ref, w_ref, dj_ref, sj_ref, fresh_ref, total
):
    step = pl.program_id(0)
    dq = dq_ref[...]
    cols = dq.shape[1]
    both = own_ref[...].astype(f32) + got_ref[...].astype(f32)
    part = lambda at: jnp.concatenate(
        [both[:, p + at : p + at + PAIR] for p in range(0, 2 * cols, 2 * PAIR)], axis=1
    )
    dk = part(0).astype(bf16)
    dv32 = part(PAIR)
    dv = dv32.astype(bf16)
    dj_ref[0, :, :cols] = dq
    dj_ref[0, :, cols : 2 * cols] = dk
    dj_ref[0, :, 2 * cols :] = dv
    sj_ref[0] = jnp.concatenate(
        [column_sum(dq.astype(f32)), column_sum(dv32), jnp.zeros((6, cols), f32)], axis=0
    )
    width = w_ref.shape[0]
    dx = None
    for j, value in enumerate((dq, dk, dv)):
        at = pl.ds(pl.multiple_of(j * width + step * cols, cols), cols)
        term = dot_nt(value, w_ref[:, at])
        dx = term if dx is None else dx + term

    @pl.when(step == 0)
    def _():
        total[...] = dx + db1_ref[0].astype(f32)

    @pl.when(step > 0)
    def _():
        total[...] += dx

    @pl.when(step == pl.num_programs(0) - 1)
    def _():
        fresh_ref[...] = total[...].astype(bf16)


def input_back_call(sp, dq, own, got, db1_all, weight, dj_all, sj_all):
    rows, width = dq.shape
    cols = PAIRS * PAIR
    steps = width // cols
    return call(
        input_back_body,
        sp,
        (steps,),
        [
            (dq, columns(rows, cols)), (own, columns(rows, 2 * cols)), (got, columns(rows, 2 * cols)),
            (db1_all, whole_window(rows, width)), (weight, RESIDENT),
        ],
        [(jax.ShapeDtypeStruct((rows, width), bf16), pl.BlockSpec((rows, width), lambda i, sp: (0, 0)))],
        [
            (dj_all, at_window(rows, 3 * cols)), (sj_all, at_window(8, cols)),
        ],
        [pltpu.VMEM((rows, width), f32)],
        us=4,
    )


def weight_body(splits, sp, *refs):
    count = len(splits)
    lefts, rights = refs[:count], refs[count : 2 * count]
    give_ref, keep_ref = refs[2 * count : 2 * count + 2]
    turned = refs[2 * count + 2 :]
    step = pl.program_id(0)
    windows, rows, half = lefts[0].shape[0], lefts[0].shape[1], lefts[0].shape[2] // 2
    first = sp[2] == 0

    @pl.when(step == 0)
    def _():
        for left, scratch in zip(lefts, turned):
            for w in range(windows):
                at = slice(w * rows, (w + 1) * rows)
                low, high = left[w, :, :half], left[w, :, half:]
                scratch[:half, at] = jnp.where(first, high, low).T
                scratch[half:, at] = jnp.where(first, low, high).T

    for (begin, end), right, scratch in zip(splits, rights, turned):

        @pl.when((step >= begin) & (step < end))
        def _(right=right, scratch=scratch):
            out = dot_nn(scratch[...], right[...].reshape(windows * rows, right.shape[2])).astype(bf16)
            give_ref[...] = out[:half]
            keep_ref[...] = out[half:]


def weight_call(sp, windows, pairs):
    rows, width = pairs[0][0].shape[1:]
    splits = []
    begin = 0
    for _, right in pairs:
        splits.append((begin, begin + right.shape[2] // FF_BLOCK))
        begin = splits[-1][1]

    def left_spec():
        return pl.BlockSpec(
            (windows, rows, width), lambda i, sp: (0, 0, 0), pipeline_mode=pl.Buffered(1)
        )

    def right_spec(begin, end):
        return pl.BlockSpec(
            (windows, rows, FF_BLOCK), lambda i, sp: (0, 0, jnp.clip(i - begin, 0, end - begin - 1))
        )

    half = (
        jax.ShapeDtypeStruct((width // 2, begin * FF_BLOCK), bf16), columns(width // 2, FF_BLOCK)
    )
    return call(
        functools.partial(weight_body, tuple(splits)),
        sp,
        (begin,),
        [(left, left_spec()) for left, _ in pairs]
        + [(right, right_spec(*split)) for (_, right), split in zip(pairs, splits)],
        [half, half],
        [],
        [pltpu.VMEM((width, windows * rows), bf16)] * len(pairs),
        us=12,
    )


def spread_body(moves, sp, mine_ref, got_ref, *out_refs):
    half = pl.num_programs(0) // 2
    mine = (pl.program_id(0) // half) == sp[2]
    value = jnp.where(mine, mine_ref[...], got_ref[...]).astype(f32)
    for (out, to), begin, count in moves:
        out_refs[out][:, to : to + count] = value[:, begin : begin + count]


def spread_call(sp, mine, got, widths, moves):
    half, cols = mine.shape
    block = half // 4
    turn = lambda i, sp, core: jnp.where(i // 4 == core, i % 4, jnp.where(core == 0, 3, 0))
    return call(
        functools.partial(spread_body, moves),
        sp,
        (8,),
        [
            (mine, pl.BlockSpec((block, cols), lambda i, sp: (turn(i, sp, sp[2]), 0))),
            (got, pl.BlockSpec((block, cols), lambda i, sp: (turn(i, sp, 1 - sp[2]), 0))),
        ],
        [
            (jax.ShapeDtypeStruct((2 * half, w), f32), pl.BlockSpec((block, w), lambda i, sp: (i, 0)))
            for w in widths
        ],
        [],
        us=5,
    )


def bucket_maps(position_cells, counts):
    key = jnp.arange(HALF, dtype=jnp.int32)[:, None]
    query = jnp.arange(HALF, dtype=jnp.int32)[None, :]
    begins = (0, position_cells, position_cells + GRID, HALF)
    bucket = jnp.full((HALF, HALF), -1, jnp.int32)
    base = 0
    for j, offset in enumerate((counts[0] // 2, GRID - 1, GRID - 1)):
        inside = (key >= begins[j]) & (key < begins[j + 1]) & (query >= begins[j]) & (query < begins[j + 1])
        ids = jnp.clip(query - key, -offset, counts[j] - 1 - offset) + offset + base
        bucket = jnp.where(inside, ids, bucket)
        base += counts[j]
    return bucket[:, :, None] == jnp.arange(base, dtype=jnp.int32)


def cell_matrix(tables, maps, position_cells):
    whole = jnp.concatenate(tables, axis=0)
    heads = whole.shape[1]
    whole = whole.reshape(-1, heads // 2, 2)[:, :, ::-1].reshape(-1, heads)
    m = jnp.einsum("bh,xcb->xhc", whole, maps.astype(bf16), preferred_element_type=f32)
    m = m.reshape(HALF, heads * HALF).astype(bf16)
    lane = jnp.arange(heads * HALF, dtype=jnp.int32) % HALF
    dead = jnp.where(lane < position_cells, masked, 0.0).astype(bf16)[None]
    return jnp.concatenate([m, dead, jnp.zeros((HALF - 1, heads * HALF), bf16)], axis=0)


def table_grads(cells, maps, counts):
    heads = cells.shape[1] // HALF
    whole = jnp.einsum(
        "xcb,xhc->bh", maps.astype(f32), cells.reshape(HALF, heads, HALF), precision=lax.Precision.HIGHEST
    )
    whole = whole.reshape(-1, heads // 2, 2)[:, :, ::-1].reshape(-1, heads)
    a, b = counts[0], counts[0] + counts[1]
    return [whole[:a], whole[a:b], whole[b:]]


class Ring:
    def __init__(self, count):
        self.count = count
        self.index = lax.axis_index("dp")
        bits = list(range(1, count.bit_length() - 1))
        turned = bits[:2][::-1] + bits[2:]
        self.steps = list(zip(bits, turned))

    def bit(self, step):
        even, odd = step
        return jnp.where(self.index % 2 == 0, (self.index >> even) & 1, (self.index >> odd) & 1)

    def send(self, a, step):
        even, odd = step
        pairs = [(i, i ^ (1 << (even if i % 2 == 0 else odd))) for i in range(self.count)]
        return lax.ppermute(a, "dp", pairs)

    def swap(self, a):
        return lax.ppermute(a, "dp", [(i, i ^ 1) for i in range(self.count)])

    def reduce(self, part):
        for step in self.steps:
            half = part.shape[0] // 2
            bit = self.bit(step)
            keep = lax.dynamic_slice_in_dim(part, bit * half, half, 0)
            give = lax.dynamic_slice_in_dim(part, (1 - bit) * half, half, 0)
            part = keep + self.send(give, step)
        return part

    def gather(self, part):
        for step in self.steps[::-1]:
            first = self.bit(step) == 0
            got = self.send(part, step)
            part = jnp.concatenate(
                [jnp.where(first, part, got), jnp.where(first, got, part)], axis=0
            )
        return part

    def whole(self, part):
        got = self.swap(part).astype(f32)
        part = part.astype(f32)
        first = self.index % 2 == 0
        return jnp.concatenate([jnp.where(first, part, got), jnp.where(first, got, part)], axis=0)

    def total(self, part):
        for bit in range(self.count.bit_length() - 1):
            part = part + lax.ppermute(part, "dp", [(i, i ^ (1 << bit)) for i in range(self.count)])
        return part


SLOTS = (
    ("F", 0, None),
    ("F", 1, 0),
    ("B", None, 0),
    ("F", 2, 1),
    ("B", 0, 1),
    ("F", 3, 2),
    ("B", 1, 2),
    ("F", None, 3),
    ("B", 2, 3),
    ("B", 3, None),
)


def on_device(
    boundary, doc_lengths, horizontal, vertical, attention_in, attention_out, expand_weight,
    contract_weight, norm_gains, bias_rows, expand_bias, position_table, horizontal_table,
    vertical_table,
):
    section = lax.axis_index("section")
    dp_count = lax.axis_size("dp")
    core = lax.axis_index("dp") % 2
    swap = [(i, i ^ 1) for i in range(dp_count)]
    exchange = lambda a: lax.ppermute(a, "dp", swap)

    own = boundary[0]
    micro, slots, width = own.shape
    rows = slots // 2
    windows = 2 * micro
    hidden = expand_weight.shape[2]
    heads = position_table.shape[2]
    pairs = heads // 2
    w_in, w_out, w1, w2 = in_vmem([attention_in[0], attention_out[0], expand_weight[0], contract_weight[0]])
    gains = norm_gains[0].astype(f32)
    biases = bias_rows[0].astype(f32)
    eb = expand_bias.astype(f32)
    in_bias = jnp.concatenate([biases[0], jnp.zeros_like(biases[0]), biases[1]])[None]
    tables = (position_table[0], horizontal_table[0], vertical_table[0])
    counts = tuple(t.shape[0] for t in tables)
    position_cells = slots // SPAN
    maps = bucket_maps(position_cells, counts)
    ring = Ring(dp_count)

    def both(mine, theirs):
        return jnp.concatenate(
            [jnp.where(core == 0, mine, theirs), jnp.where(core == 0, theirs, mine)], axis=0
        )

    halves = own.reshape(micro, 2, rows, width)
    own_half = jnp.where(core == 0, halves[:, 0], halves[:, 1])
    other_half = jnp.where(core == 0, halves[:, 1], halves[:, 0])
    spare = lambda a: jnp.concatenate([a, a[:1]], axis=0)
    own_all = spare(both(own_half, exchange(other_half)))
    places = jnp.concatenate(
        [horizontal, vertical, jnp.broadcast_to(doc_lengths[:, None], (micro, PAIR))], axis=1
    )
    places = spare(both(places, exchange(places)))
    across_cell = places[:, :slots] // SPAN
    down_cell = places[:, slots : 2 * slots] // SPAN
    lengths = places[:, 2 * slots]
    ids = jnp.arange(slots, dtype=jnp.int32)
    position_cell = jnp.broadcast_to((ids // SPAN)[None], (windows + 1, slots))

    def hot_of(cells, lanes, axis):
        p, a, d = (jnp.expand_dims(c, axis) for c in cells)
        lanes = jnp.expand_dims(lanes, (0, 3 - axis))
        return (lanes == p) | (lanes == a + position_cells) | (lanes == d + position_cells + GRID)

    cells = (position_cell, across_cell, down_cell)
    cell_ids = jnp.arange(PAIR, dtype=jnp.int32)
    turned_all = hot_of(cells, cell_ids[:HALF], 1).astype(bf16)
    dead = (ids[None, :] >= lengths[:, None])[:, :, None] & (cell_ids == HALF)
    hot_all = (hot_of(cells, cell_ids, 2) | dead).astype(bf16)
    take = lambda c: jnp.where(core == 0, c[:, :rows], c[:, rows:])
    side_all = hot_of(tuple(take(c) for c in cells), cell_ids % HALF, 2).astype(bf16)
    matrix = cell_matrix(tables, maps, position_cells)

    sel = (cell_ids[:, None] // HALF != cell_ids[None, :] // HALF).astype(bf16)

    blocks_of = (lengths + KEY_BLOCK - 1) // KEY_BLOCK
    blocks_of = jnp.where(jnp.arange(windows + 1) < windows, blocks_of, 0)
    infos = []
    for _, zero, one in SLOTS:
        w = jnp.where(
            section == 0, windows if zero is None else zero, windows if one is None else one
        ).astype(jnp.int32)
        infos.append(jnp.stack([w, blocks_of[w], core.astype(jnp.int32), lengths[w], section.astype(jnp.int32)]))

    widths = dict(
        x=width, q=width, kv=2 * width, a=width, rest=width, lse=width, peer=2 * width, n1=width, h1=width,
        g=hidden, d=hidden, n2=width, db2=width, df=hidden, db1=width, dj=3 * width,
    )
    shapes = {n: jax.ShapeDtypeStruct((windows + 1, rows, c), bf16) for n, c in widths.items()}
    shapes["r"] = jax.ShapeDtypeStruct((windows + 1, rows, PAIR), f32)
    shapes["st"] = shapes["sj"] = jax.ShapeDtypeStruct((windows + 1, 8, width), f32)
    shapes["se"] = jax.ShapeDtypeStruct((windows + 1, 1, hidden), f32)
    shapes["cell"] = jax.ShapeDtypeStruct((windows + 1, HALF, width), f32)
    st = dict(zip(shapes, unwritten(list(shapes.values()))))

    def forward(sp, s, got):
        x, q, kv, fresh = qkv_call(sp, own_all, got, w_in, in_bias, s["x"], s["q"], s["kv"])
        s = dict(s, x=x, q=q, kv=kv)
        mixed = ("a", "rest", "lse", "peer")
        s.update(
            zip(mixed, attend_call(
                sp, q, fresh, exchange(fresh), side_all, hot_all, matrix, tuple(s[n] for n in mixed)
            ))
        )
        names = ("n1", "h1", "g", "d", "n2", "r")
        outs = dense_call(
            sp, s["a"], x, w_out, w1, w2, gains, biases, eb, tuple(s[n] for n in names)
        )
        s.update(zip(names, outs[:-1]))
        return s, outs[-1]

    def dense_back(sp, s, got):
        names = ("db2", "df", "db1", "st", "se")
        outs = dense_back_call(
            sp, own_all, got, s["n2"], s["r"], s["d"], s["n1"], s["a"], s["rest"], w_out, w1, w2, gains,
            sel, tuple(s[n] for n in names),
        )
        s = dict(s)
        s.update(zip(names, outs[:5]))
        return s, tuple(outs[5:])

    def attend_back(sp, s, grads):
        cell, dq, keep, send = attend_back_call(
            sp, s["q"], s["kv"], s["peer"], side_all, hot_all, matrix, s["lse"], *grads, turned_all,
            s["cell"],
        )
        s = dict(s, cell=cell)
        dj, sj, fresh = input_back_call(
            sp, dq, keep, exchange(send), s["db1"], w_in, s["dj"], s["sj"]
        )
        return dict(s, dj=dj, sj=sj), fresh

    got = {}
    finals = {}
    grads_in = {}
    nothing = jnp.zeros((rows, width), bf16)

    for number, (kind, zero, one) in enumerate(SLOTS[:-1]):
        sp = infos[number]
        if kind == "F":
            st, out = forward(sp, st, got.pop(("F", one), nothing))
            if one is not None:
                finals[one] = out
            if zero is not None:
                got["F", zero] = lax.ppermute(out, "section", [(0, 1)])
        else:
            st, grads = dense_back(sp, st, got.pop(("B", zero), nothing))
            st, out = attend_back(sp, st, grads)
            if zero is not None:
                grads_in[zero] = out
            if one is not None:
                got["B", one] = lax.ppermute(out, "section", [(1, 0)])

    sp = infos[-1]
    barrier = lax.optimization_barrier

    def start_sum(pairs):
        give, keep = weight_call(sp, windows, pairs)
        return keep + exchange(give)

    def spread(part, widths, moves):
        return spread_call(sp, part, exchange(part), widths, moves)

    st, grads = dense_back(sp, st, got.pop(("B", SLOTS[-1][1])))
    sums_contract = start_sum([(st["db2"], st["g"])])
    sums_expand = start_sum([(st["h1"], st["df"])])
    grads, sums_contract, sums_expand = barrier((grads, sums_contract, sums_expand))
    sums_contract = ring.reduce(sums_contract)
    sums_expand = ring.reduce(sums_expand)
    st, grads_in[SLOTS[-1][1]] = attend_back(sp, st, grads)
    sums_attend = ring.reduce(start_sum([(st["x"], st["dj"]), (st["a"], st["db1"])]))
    natural = [((0, 0), 0, hidden)]
    (g_contract,) = spread(ring.gather(sums_contract), [hidden], natural)
    (g_expand,) = spread(ring.gather(sums_expand), [hidden], natural)
    cols = PAIRS * PAIR
    moves = [
        ((0, j * width + i * cols), (3 * i + j) * cols, cols) for i in range(width // cols) for j in range(3)
    ] + [((1, 0), 3 * width, width)]
    g_in, g_out = spread(ring.gather(sums_attend), [3 * width, width], moves)

    sums = jnp.sum(st["st"][:windows], axis=0)
    joined_sums = jnp.sum(st["sj"][:windows], axis=0)
    wide = jnp.sum(st["se"][:windows], axis=0)
    small = [
        joined_sums[0:2], sums[0:6], wide,
    ] + table_grads(jnp.sum(st["cell"][:windows], axis=0), maps, counts)
    packed = jnp.concatenate([s.reshape(-1) for s in small])
    size = packed.shape[0]
    packed = jnp.pad(packed, (0, -size % 1024)).reshape(-1, PAIR)
    packed = ring.total(packed).reshape(-1)
    pieces = []
    begin = 0
    for s in small:
        count = math.prod(s.shape)
        pieces.append(packed[begin : begin + count].reshape(s.shape))
        begin += count
    joined_sums, sums, wide, table_p, table_h, table_v = pieces
    grad_bias = jnp.concatenate([joined_sums, sums[0:4]], axis=0)
    grad_gain = sums[4:6]

    result = [jnp.where(section == 0, grads_in[w], finals[w]) for w in range(windows)]
    mine_first, mine_second = jnp.stack(result[:micro]), jnp.stack(result[micro:])
    keep = jnp.where(core == 0, mine_first, mine_second)
    give = exchange(jnp.where(core == 0, mine_second, mine_first))
    out_halves = jnp.stack(
        [jnp.where(core == 0, keep, give), jnp.where(core == 0, give, keep)], axis=1
    )
    boundary_out = out_halves.reshape(1, micro, slots, width)
    return (
        boundary_out, g_in[None], g_out[None], g_expand[None], g_contract[None], grad_gain[None], grad_bias[None], wide,
        table_p[None], table_h[None], table_v[None],
    )


def solution(mesh):
    section = P("section", None, None)
    placed = (
        P("section", "dp", None, None), P("dp"), P("dp", None), P("dp", None), section, section,
        section, section, section, section, P("section", None), section, section, section,
    )
    return jax.shard_map(
        on_device,
        mesh=mesh,
        in_specs=placed,
        out_specs=(
            P("section", "dp", None, None), section, section, section, section, section, section,
            P("section", None), section, section, section,
        ),
        check_vma=False,
    )
```

```python
import functools
import math

import jax
import jax.numpy as jnp
from jax import lax
from jax.experimental import pallas as pl
from jax.experimental.pallas import tpu as pltpu
from jax.sharding import PartitionSpec as P

GRID = 16
SPAN = 32
KEY_BLOCK = 256
ROW_BLOCK = 256
FF_BLOCK = 768
PAIRS = 2
HALF = 64
PAIR = 128

epsilon = 1e-05
masked = -1e30
score_scale = 0.125
VMEM_LIMIT = 40 * 1024 * 1024

f32 = jnp.float32
bf16 = jnp.bfloat16

dot_nn = lambda a, b: lax.dot_general(a, b, (((1,), (0,)), ((), ())), preferred_element_type=f32)
dot_nt = lambda a, b: lax.dot_general(a, b, (((1,), (1,)), ((), ())), preferred_element_type=f32)
dot_tn = lambda a, b: lax.dot_general(a, b, (((0,), (0,)), ((), ())), preferred_element_type=f32)


def params_for(axes):
    return pltpu.CompilerParams(
        dimension_semantics=("arbitrary",) * axes, vmem_limit_bytes=VMEM_LIMIT
    )


ANY = pl.BlockSpec(memory_space=pl.ANY)


def like(a):
    return jax.ShapeDtypeStruct(a.shape, a.dtype)


RESIDENT = pl.BlockSpec(memory_space=pltpu.VMEM)


def fixed(shape):
    return pl.BlockSpec(shape, lambda i, sp: (0,) * len(shape), pipeline_mode=pl.Buffered(1))


def this_step(count):
    return pl.ds(pl.multiple_of(pl.program_id(0) * count, count), count)


def stacked(rows, cols):
    return pl.BlockSpec((1, rows, cols), lambda i, sp: (sp[0], i, 0))


def plain(rows, cols):
    return pl.BlockSpec((rows, cols), lambda i, sp: (i, 0))


class Row:
    def __init__(self, table, base):
        self.table = table
        self.base = base

    def __getitem__(self, at):
        return self.table[self.base + at]


def shifted(spec, base):
    if spec.index_map is None:
        return spec
    inner = spec.index_map
    return pl.BlockSpec(
        spec.block_shape, lambda i, sp: inner(i, Row(sp, base)), pipeline_mode=spec.pipeline_mode
    )


def call(body, sp, grid, ins, outs, aliased, scratch=(), us=10):
    held = lambda a, s: pltpu.with_memory_space_constraint(a, pltpu.HBM) if a.ndim == 3 else a
    operands = [held(a, s) for a, s in ins] + [held(a, s) for a, s in aliased]
    table, base = sp
    in_specs = [shifted(s, base) for _, s in ins] + [ANY] * len(aliased)
    out_shape = [pltpu.HBM(a.shape, a.dtype) for a, _ in aliased] + [s for s, _ in outs]
    out_specs = [shifted(s, base) for _, s in aliased] + [shifted(s, base) for _, s in outs]
    kept = len(aliased)
    first = len(ins)

    def run(sp_ref, *refs):
        body(Row(sp_ref, base), *refs[:first], *refs[first + kept :])

    return pl.pallas_call(
        run,
        grid_spec=pltpu.PrefetchScalarGridSpec(
            num_scalar_prefetch=1,
            grid=grid,
            in_specs=in_specs,
            out_specs=out_specs,
            scratch_shapes=list(scratch),
        ),
        out_shape=out_shape,
        input_output_aliases={1 + first + j: j for j in range(kept)},
        compiler_params=params_for(len(grid)),
        cost_estimate=pl.CostEstimate(
            flops=us * 1_000_000_000, bytes_accessed=us * 1_000_000, transcendentals=0
        ),
    )(table, *operands)


def unwritten(shapes):
    return pl.pallas_call(
        lambda *refs: None, out_shape=[pltpu.HBM(s.shape, s.dtype) for s in shapes], out_specs=[ANY] * len(shapes),
        compiler_params=pltpu.CompilerParams(vmem_limit_bytes=2 * 1024 * 1024),
    )()


def in_vmem(arrays):
    def body(*refs):
        count = len(arrays)
        copies = [
            pltpu.make_async_copy(refs[j], refs[count + j], refs[-1].at[j]) for j in range(count)
        ]
        for copy in copies:
            copy.start()
        for copy in copies:
            copy.wait()

    return pl.pallas_call(
        body,
        out_shape=[pltpu.VMEM(a.shape, a.dtype) for a in arrays],
        in_specs=[ANY] * len(arrays),
        out_specs=[RESIDENT] * len(arrays),
        scratch_shapes=[pltpu.SemaphoreType.DMA((len(arrays),))],
        compiler_params=pltpu.CompilerParams(vmem_limit_bytes=2 * 1024 * 1024),
    )(*[pltpu.with_memory_space_constraint(a, pltpu.HBM) for a in arrays])


def at_window(rows, cols):
    return pl.BlockSpec((1, rows, cols), lambda i, sp: (sp[0], 0, i))


def whole_window(rows, cols):
    return pl.BlockSpec((1, rows, cols), lambda i, sp: (sp[0], 0, 0))


def columns(rows, cols, begin=0):
    return pl.BlockSpec((rows, cols), lambda i, sp: (0, begin + i))


def qkv_body(sp, x_ref, got_ref, w_ref, b_ref, x_out, q_ref, kv_ref, fresh_ref):
    width = x_ref.shape[2]
    cols = q_ref.shape[2]
    x = jnp.where(sp[4] == 1, got_ref[...], x_ref[0])

    @pl.when(pl.program_id(0) == 0)
    def _():
        x_out[0] = x

    def part(j):
        at = pl.ds(pl.multiple_of(j * width + pl.program_id(0) * cols, cols), cols)
        return dot_nn(x, w_ref[:, at]) + b_ref[:, at]

    q_ref[0] = (part(0).astype(bf16) * score_scale).astype(bf16)
    k = part(1).astype(bf16)
    v = part(2).astype(bf16)
    for begin in range(0, cols, PAIR):
        for value, at in ((k, 0), (v, PAIR)):
            to = slice(2 * begin + at, 2 * begin + at + PAIR)
            kv_ref[0, :, to] = value[:, begin : begin + PAIR]
            fresh_ref[:, to] = value[:, begin : begin + PAIR]


def qkv_call(sp, own_all, got, weight, bias, x_all, q_all, kv_all):
    rows, width = x_all.shape[1], x_all.shape[2]
    cols = PAIRS * PAIR
    return call(
        qkv_body,
        sp,
        (width // cols,),
        [
            (own_all, whole_window(rows, width)), (got, fixed(got.shape)), (weight, RESIDENT),
            (bias, fixed(bias.shape)),
        ],
        [(jax.ShapeDtypeStruct((rows, 2 * width), bf16), columns(rows, 2 * cols))],
        [
            (x_all, whole_window(rows, width)), (q_all, at_window(rows, cols)),
            (kv_all, at_window(rows, 2 * cols)),
        ],
        us=4,
    )


def low_half(shape):
    return lax.broadcasted_iota(jnp.int32, shape, 1) < HALF


def split_three(value):
    place = lax.broadcasted_iota(jnp.int32, value.shape, 1) % HALF
    high = value.astype(bf16).astype(f32)
    rest = value - high
    mid = rest.astype(bf16).astype(f32)
    last = rest - mid
    out = jnp.where(place == 0, high, jnp.where(place == 1, mid, jnp.where(place == 2, last, 0.0)))
    return out.astype(bf16)


def in_order(first, own, peer):
    return jnp.concatenate([jnp.where(first, own, peer), jnp.where(first, peer, own)], axis=0)


def attend_body(
    sp, q_ref, own_ref, peer_ref, side_ref, hot_ref, m_ref, a_ref, rest_ref, lse_ref, kept_ref
):
    rows = q_ref.shape[1]
    first = sp[2] == 0
    kept_ref[0] = peer_ref[...]

    def variant(keys):
        low = low_half((rows, PAIR))
        key_low = low_half((keys, PAIR))
        one = jnp.ones((keys, PAIR), bf16)
        side = side_ref[0]
        hot = hot_ref[0, :keys, :]
        for n in range(PAIRS):
            cols = slice(n * PAIR, (n + 1) * PAIR)
            kv = slice(2 * n * PAIR, 2 * (n + 1) * PAIR)
            both = in_order(first, own_ref[:, kv], peer_ref[:, kv])[:keys]
            k, v = both[:, :PAIR], both[:, PAIR:]
            ks = dot_nn(hot, m_ref[:, cols]).astype(bf16)
            q = q_ref[0, :, cols]
            outs = []
            peaks = []
            for head in (0, 1):
                pick = (lambda m, x, y: jnp.where(m, x, y)) if head == 0 else (
                    lambda m, x, y: jnp.where(m, y, x)
                )
                s = dot_nt(pick(low, q, side), pick(key_low, k, ks))
                peak = jnp.max(s, axis=1, keepdims=True)
                e = jnp.exp(s - peak).astype(bf16)
                outs.append(dot_nn(e, pick(key_low, v, one)))
                peaks.append(peak)
            top = jnp.where(low, outs[0], outs[1])
            total = pltpu.roll(jnp.where(low, outs[1], outs[0]), HALF, 1)
            mixed = top / total
            mixed_low = mixed.astype(bf16)
            a_ref[0, :, cols] = mixed_low
            rest_ref[0, :, cols] = (mixed - mixed_low.astype(f32)).astype(bf16)
            lse = jnp.where(low, peaks[0], peaks[1]) + jnp.log(total)
            lse_ref[0, :, cols] = split_three(-lse)

    for blocks in range(1, 2 * rows // KEY_BLOCK + 1):
        pl.when(sp[1] == blocks)(functools.partial(variant, blocks * KEY_BLOCK))


def attend_call(sp, q_all, kv_own, kv_peer, side_all, hot_all, matrix, bufs):
    rows, width = q_all.shape[1], q_all.shape[2]
    cols = PAIRS * PAIR
    part = at_window(rows, cols)
    return call(
        attend_body,
        sp,
        (width // cols,),
        [
            (q_all, part),
            (kv_own, columns(rows, 2 * cols)),
            (kv_peer, columns(rows, 2 * cols)),
            (side_all, whole_window(rows, PAIR)),
            (hot_all, whole_window(2 * rows, PAIR)),
            (matrix, columns(PAIR, cols)),
        ],
        [],
        [(b, part) for b in bufs[:-1]] + [(bufs[-1], at_window(rows, 2 * cols))],
        us=14,
    )


def gelu_both(x):
    cdf = 0.5 + 0.5 * lax.erf(x * math.sqrt(0.5))
    bell = jnp.exp(x * x * -0.5)
    return x * cdf, cdf + x * bell * (1.0 / math.sqrt(2.0 * math.pi))


def centered(u):
    c = u - jnp.mean(u, axis=1, keepdims=True)
    r = lax.rsqrt(jnp.mean(c * c, axis=1, keepdims=True) + epsilon)
    return c * r, r


class Moves:
    def __init__(self, sems):
        self.sems = sems
        self.used = 0
        self.out = []

    def start(self, source, target):
        copy = pltpu.make_async_copy(source, target, self.sems.at[self.used])
        self.used += 1
        copy.start()
        return copy

    def write(self, source, target):
        self.out.append(self.start(source, target))

    def finish(self):
        for copy in self.out:
            copy.wait()


def chunks(width):
    return [slice(c, c + FF_BLOCK) for c in range(0, width, FF_BLOCK)]


def dense_body(
    sp, a_ref, x_ref, wo_ref, w1_ref, w2_ref, gain_ref, bias_ref, eb_ref,
    n1_hbm, h1_hbm, g_hbm, d_hbm, n2_hbm, r_hbm, fresh_ref,
    n1_ref, h1_ref, g_ref, d_ref, n2_ref, r_ref, sems,
):
    w = sp[0]
    moves = Moves(sems)
    parts = chunks(w1_ref.shape[1])
    u1 = dot_nn(a_ref[0], wo_ref[...]) + bias_ref[2:3, :] + x_ref[0].astype(f32)
    n1, r1 = centered(u1)
    h1 = n1 * gain_ref[0:1, :] + bias_ref[3:4, :]
    h1_low = h1.astype(bf16)
    n1_ref[...] = n1.astype(bf16)
    h1_ref[...] = h1_low
    moves.write(n1_ref, n1_hbm.at[w])
    moves.write(h1_ref, h1_hbm.at[w])
    u2 = h1 + bias_ref[4:5, :]
    for c in parts:
        g, d = gelu_both(dot_nn(h1_low, w1_ref[:, c]) + eb_ref[:, c])
        g = g.astype(bf16)
        g_ref[:, c] = g
        d_ref[:, c] = d.astype(bf16)
        moves.write(g_ref.at[:, c], g_hbm.at[w, :, c])
        moves.write(d_ref.at[:, c], d_hbm.at[w, :, c])
        u2 = u2 + dot_nt(g, w2_ref[:, c])
    n2, r2 = centered(u2)
    n2_ref[...] = n2.astype(bf16)
    moves.write(n2_ref, n2_hbm.at[w])
    r_ref[...] = jnp.where(low_half(r_ref.shape), r1, r2)
    moves.write(r_ref, r_hbm.at[w])
    fresh_ref[...] = (n2 * gain_ref[1:2, :] + bias_ref[5:6, :]).astype(bf16)
    moves.finish()


def dense_call(sp, a_all, x_all, wo, w1, w2, gains, biases, eb, bufs):
    rows, width = a_all.shape[1], a_all.shape[2]
    hidden = w1.shape[1]
    row = whole_window(rows, width)
    vmem = lambda *shape: pltpu.VMEM(shape, bf16)
    return call(
        dense_body,
        sp,
        (1,),
        [
            (a_all, row), (x_all, row), (wo, RESIDENT), (w1, RESIDENT), (w2, RESIDENT), (gains, fixed(gains.shape)),
            (biases, fixed(biases.shape)), (eb, fixed(eb.shape)),
        ],
        [(jax.ShapeDtypeStruct((rows, width), bf16), pl.BlockSpec((rows, width), lambda i, sp: (0, 0)))],
        [(b, ANY) for b in bufs],
        [
            vmem(rows, width), vmem(rows, width), vmem(rows, hidden), vmem(rows, hidden), vmem(rows, width),
            pltpu.VMEM((rows, PAIR), f32), pltpu.SemaphoreType.DMA((4 + 2 * (hidden // FF_BLOCK),)),
        ],
        us=10,
    )


def column_sum(v):
    return jnp.sum(v, axis=0, keepdims=True)


def norm_back(dy, n, r, gain):
    dn = dy * gain
    return r * (dn - jnp.mean(dn, axis=1, keepdims=True) - n * jnp.mean(dn * n, axis=1, keepdims=True))


def dense_back_body(
    sp, dy_ref, got_ref, n2_ref, r_ref, gain_ref, sel_ref, wo_ref, w1_ref, w2_ref, d_hbm, n1_hbm, a_hbm,
    rest_hbm, db2_hbm, df_hbm, db1_hbm, st_ref, se_ref, do_ref, dd_ref,
    d_ref, n1_ref, a_ref, rest_ref, db2_ref, df_ref, db1_ref, sems,
):
    w = sp[0]
    width = dy_ref.shape[2]
    moves = Moves(sems)
    parts = chunks(w1_ref.shape[1])
    loads = [moves.start(d_hbm.at[w, :, c], d_ref.at[:, c]) for c in parts]
    last = [
        moves.start(n1_hbm.at[w], n1_ref), moves.start(a_hbm.at[w], a_ref),
        moves.start(rest_hbm.at[w], rest_ref),
    ]
    r = r_ref[0]
    dy = jnp.where(sp[4] == 1, dy_ref[0], got_ref[...]).astype(f32)
    n2 = n2_ref[0].astype(f32)
    du2 = norm_back(dy, n2, r[:, HALF : HALF + 1], gain_ref[1:2, :])
    db2 = du2.astype(bf16)
    db2_ref[...] = db2
    moves.write(db2_ref, db2_hbm.at[w])
    st_ref[0, 2:3, :] = column_sum(du2)
    st_ref[0, 3:4, :] = column_sum(dy)
    st_ref[0, 5:6, :] = column_sum(dy * n2)
    st_ref[0, 6:8, :] = jnp.zeros((2, width), f32)
    dh1 = du2
    for c, load in zip(parts, loads):
        load.wait()
        df = dot_nn(db2, w2_ref[:, c]) * d_ref[:, c].astype(f32)
        se_ref[0, :, c] = column_sum(df)
        df = df.astype(bf16)
        df_ref[:, c] = df
        moves.write(df_ref.at[:, c], df_hbm.at[w, :, c])
        dh1 = dh1 + dot_nt(df, w1_ref[:, c])
    for load in last:
        load.wait()
    n1 = n1_ref[...].astype(f32)
    du1 = norm_back(dh1, n1, r[:, 0:1], gain_ref[0:1, :])
    db1 = du1.astype(bf16)
    db1_ref[...] = db1
    moves.write(db1_ref, db1_hbm.at[w])
    st_ref[0, 0:1, :] = column_sum(du1)
    st_ref[0, 1:2, :] = column_sum(dh1)
    st_ref[0, 4:5, :] = column_sum(dh1 * n1)
    do = dot_nt(db1, wo_ref[...]).astype(bf16)
    do_ref[...] = do
    mixed = do.astype(f32) * (a_ref[...].astype(f32) + rest_ref[...].astype(f32))
    high = mixed.astype(bf16)
    low = (mixed - high.astype(f32)).astype(bf16)
    for begin in range(0, width, PAIR):
        cols = slice(begin, begin + PAIR)
        inner = dot_nn(high[:, cols], sel_ref[...]) + dot_nn(low[:, cols], sel_ref[...])
        dd_ref[:, cols] = split_three(-inner)
    moves.finish()


def dense_back_call(
    sp, dy_all, got, n2_all, r_all, d_all, n1_all, a_all, rest_all, wo, w1, w2, gains, sel, bufs
):
    rows, width = got.shape
    hidden = w1.shape[1]
    row = whole_window(rows, width)
    db2_all, df_all, db1_all, st_all, se_all = bufs
    flat = (jax.ShapeDtypeStruct((rows, width), bf16), pl.BlockSpec((rows, width), lambda i, sp: (0, 0)))
    vmem = lambda *shape: pltpu.VMEM(shape, bf16)
    return call(
        dense_back_body,
        sp,
        (1,),
        [
            (dy_all, row), (got, fixed(got.shape)), (n2_all, row), (r_all, whole_window(rows, PAIR)),
            (gains, fixed(gains.shape)), (sel, fixed(sel.shape)), (wo, RESIDENT), (w1, RESIDENT),
            (w2, RESIDENT),
        ]
        + [(b, ANY) for b in (d_all, n1_all, a_all, rest_all)],
        [flat, flat],
        [
            (db2_all, ANY), (df_all, ANY), (db1_all, ANY), (st_all, whole_window(8, width)),
            (se_all, whole_window(1, hidden)),
        ],
        [
            vmem(rows, hidden), vmem(rows, width), vmem(rows, width), vmem(rows, width), vmem(rows, width),
            vmem(rows, hidden), vmem(rows, width), pltpu.SemaphoreType.DMA((5 + 2 * (hidden // FF_BLOCK),)),
        ],
        us=10,
    )


def attend_back_body(
    sp, q_ref, own_ref, peer_ref, side_ref, hot_ref, m_ref, lse_ref, do_ref, dd_ref, turned_ref,
    cell_ref, dq_ref, keep_ref, send_ref,
):
    rows = q_ref.shape[1]
    total = 2 * rows
    first = sp[2] == 0

    def variant(blocks):
        keys = blocks * KEY_BLOCK
        low = low_half((rows, PAIR))
        key_low = low_half((keys, PAIR))
        block_low = low_half((KEY_BLOCK, PAIR))
        place = lax.broadcasted_iota(jnp.int32, (KEY_BLOCK, PAIR), 1)
        three = jnp.where(place % HALF < 3, 1.0, 0.0).astype(bf16)
        lone = [
            jnp.where(place < 3, 1.0, 0.0).astype(bf16),
            jnp.where((place >= HALF) & (place < HALF + 3), 1.0, 0.0).astype(bf16),
        ]
        side = side_ref[0]
        hot = hot_ref[0, :keys, :]
        for n in range(PAIRS):
            cols = slice(n * PAIR, (n + 1) * PAIR)
            kv = slice(2 * n * PAIR, 2 * (n + 1) * PAIR)
            both = in_order(first, own_ref[0, :, kv], peer_ref[0, :, kv])[:keys]
            k, v = both[:, :PAIR], both[:, PAIR:]
            ks = dot_nn(hot, m_ref[:, cols]).astype(bf16)
            kt = k.T
            q = q_ref[0, :, cols]
            do = do_ref[:, cols]
            dd = dd_ref[:, cols]
            lse = lse_ref[0, :, cols]
            kc = (jnp.where(key_low, k, ks), jnp.where(key_low, ks, k))
            qc = (jnp.where(low, q, side), jnp.where(low, side, q))
            qe = tuple(jnp.concatenate([c, lse], axis=1) for c in qc)
            dc = (jnp.where(low, do, dd), jnp.where(low, dd, do))
            dq = [None, None]
            dks = []
            dvs = []
            gs = []
            for b in range(blocks):
                at = slice(b * KEY_BLOCK, (b + 1) * KEY_BLOCK)
                vb = v[at]
                vc = (jnp.where(block_low, vb, three), jnp.where(block_low, three, vb))
                part_v = []
                part_k = []
                for head in (0, 1):
                    kb = jnp.concatenate([kc[head][at], lone[head]], axis=1)
                    p = jnp.exp(dot_nt(kb, qe[head]))
                    dp = dot_nt(vc[head], dc[head])
                    ds = (p * dp).astype(bf16)
                    part_v.append(dot_nn(p.astype(bf16), do))
                    part_k.append(dot_nn(ds, qc[head]))
                    part = dot_nn(kt[head * HALF : (head + 1) * HALF, at], ds)
                    dq[head] = part if dq[head] is None else dq[head] + part
                dvs.append(jnp.where(block_low, part_v[0], part_v[1]).astype(bf16))
                dks.append(jnp.where(block_low, part_k[0], part_k[1]).astype(bf16))
                gs.append(jnp.where(block_low, part_k[1], part_k[0]).astype(bf16))
            dq_ref[:, cols] = (jnp.concatenate(dq, axis=0).T * score_scale).astype(bf16)
            cell_ref[0, :, cols] = dot_nn(turned_ref[0, :, :keys], jnp.concatenate(gs, axis=0))
            if keys < total:
                zero = [jnp.zeros((total - keys, PAIR), bf16)]
                dks = dks + zero
                dvs = dvs + zero
            grads = jnp.concatenate([jnp.concatenate(dks, axis=0), jnp.concatenate(dvs, axis=0)], axis=1)
            keep_ref[:, kv] = jnp.where(first, grads[:rows], grads[rows:])
            send_ref[:, kv] = jnp.where(first, grads[rows:], grads[:rows])

    for blocks in range(1, total // KEY_BLOCK + 1):
        pl.when(sp[1] == blocks)(functools.partial(variant, blocks))


def attend_back_call(
    sp, q_all, kv_all, peer_all, side_all, hot_all, matrix, lse_all, do, dd, turned_all, cell_all
):
    rows, width = q_all.shape[1], q_all.shape[2]
    cols = PAIRS * PAIR
    part = at_window(rows, cols)
    kv = at_window(rows, 2 * cols)
    flat = columns(rows, cols)
    flat_kv = columns(rows, 2 * cols)
    out_kv = jax.ShapeDtypeStruct((rows, 2 * width), bf16)
    return call(
        attend_back_body,
        sp,
        (width // cols,),
        [
            (q_all, part),
            (kv_all, kv),
            (peer_all, kv),
            (side_all, whole_window(rows, PAIR)),
            (hot_all, whole_window(2 * rows, PAIR)),
            (matrix, columns(PAIR, cols)),
            (lse_all, part),
            (do, flat),
            (dd, flat),
            (turned_all, whole_window(HALF, 2 * rows)),
        ],
        [(jax.ShapeDtypeStruct((rows, width), bf16), flat), (out_kv, flat_kv), (out_kv, flat_kv)],
        [(cell_all, at_window(HALF, cols))],
        us=20,
    )


def input_back_body(
    sp, dq_ref, own_ref, got_ref, db1_ref, w_ref, dj_ref, sj_ref, fresh_ref, total
):
    step = pl.program_id(0)
    dq = dq_ref[...]
    cols = dq.shape[1]
    both = own_ref[...].astype(f32) + got_ref[...].astype(f32)
    part = lambda at: jnp.concatenate(
        [both[:, p + at : p + at + PAIR] for p in range(0, 2 * cols, 2 * PAIR)], axis=1
    )
    dk = part(0).astype(bf16)
    dv32 = part(PAIR)
    dv = dv32.astype(bf16)
    dj_ref[0, :, :cols] = dq
    dj_ref[0, :, cols : 2 * cols] = dk
    dj_ref[0, :, 2 * cols :] = dv
    sj_ref[0] = jnp.concatenate(
        [column_sum(dq.astype(f32)), column_sum(dv32), jnp.zeros((6, cols), f32)], axis=0
    )
    width = w_ref.shape[0]
    dx = None
    for j, value in enumerate((dq, dk, dv)):
        at = pl.ds(pl.multiple_of(j * width + step * cols, cols), cols)
        term = dot_nt(value, w_ref[:, at])
        dx = term if dx is None else dx + term

    @pl.when(step == 0)
    def _():
        total[...] = dx + db1_ref[0].astype(f32)

    @pl.when(step > 0)
    def _():
        total[...] += dx

    @pl.when(step == pl.num_programs(0) - 1)
    def _():
        fresh_ref[...] = total[...].astype(bf16)


def input_back_call(sp, dq, own, got, db1_all, weight, dj_all, sj_all):
    rows, width = dq.shape
    cols = PAIRS * PAIR
    steps = width // cols
    return call(
        input_back_body,
        sp,
        (steps,),
        [
            (dq, columns(rows, cols)), (own, columns(rows, 2 * cols)), (got, columns(rows, 2 * cols)),
            (db1_all, whole_window(rows, width)), (weight, RESIDENT),
        ],
        [(jax.ShapeDtypeStruct((rows, width), bf16), pl.BlockSpec((rows, width), lambda i, sp: (0, 0)))],
        [
            (dj_all, at_window(rows, 3 * cols)), (sj_all, at_window(8, cols)),
        ],
        [pltpu.VMEM((rows, width), f32)],
        us=4,
    )


def weight_body(splits, sp, *refs):
    count = len(splits)
    lefts, rights = refs[:count], refs[count : 2 * count]
    give_ref, keep_ref = refs[2 * count : 2 * count + 2]
    turned = refs[2 * count + 2 :]
    step = pl.program_id(0)
    windows, rows, half = lefts[0].shape[0], lefts[0].shape[1], lefts[0].shape[2] // 2
    first = sp[2] == 0

    @pl.when(step == 0)
    def _():
        for left, scratch in zip(lefts, turned):
            for w in range(windows):
                at = slice(w * rows, (w + 1) * rows)
                low, high = left[w, :, :half], left[w, :, half:]
                scratch[:half, at] = jnp.where(first, high, low).T
                scratch[half:, at] = jnp.where(first, low, high).T

    for (begin, end), right, scratch in zip(splits, rights, turned):

        @pl.when((step >= begin) & (step < end))
        def _(right=right, scratch=scratch):
            out = dot_nn(scratch[...], right[...].reshape(windows * rows, right.shape[2])).astype(bf16)
            give_ref[...] = out[:half]
            keep_ref[...] = out[half:]


def weight_call(sp, windows, pairs):
    rows, width = pairs[0][0].shape[1:]
    splits = []
    begin = 0
    for _, right in pairs:
        splits.append((begin, begin + right.shape[2] // FF_BLOCK))
        begin = splits[-1][1]

    def left_spec():
        return pl.BlockSpec(
            (windows, rows, width), lambda i, sp: (0, 0, 0), pipeline_mode=pl.Buffered(1)
        )

    def right_spec(begin, end):
        return pl.BlockSpec(
            (windows, rows, FF_BLOCK), lambda i, sp: (0, 0, jnp.clip(i - begin, 0, end - begin - 1))
        )

    half = (
        jax.ShapeDtypeStruct((width // 2, begin * FF_BLOCK), bf16), columns(width // 2, FF_BLOCK)
    )
    return call(
        functools.partial(weight_body, tuple(splits)),
        sp,
        (begin,),
        [(left, left_spec()) for left, _ in pairs]
        + [(right, right_spec(*split)) for (_, right), split in zip(pairs, splits)],
        [half, half],
        [],
        [pltpu.VMEM((width, windows * rows), bf16)] * len(pairs),
        us=12,
    )


def spread_body(moves, sp, mine_ref, got_ref, *out_refs):
    half = pl.num_programs(0) // 2
    mine = (pl.program_id(0) // half) == sp[2]
    value = jnp.where(mine, mine_ref[...], got_ref[...]).astype(f32)
    for (out, to), begin, count in moves:
        out_refs[out][:, to : to + count] = value[:, begin : begin + count]


def spread_call(sp, mine, got, widths, moves):
    half, cols = mine.shape
    block = half // 4
    turn = lambda i, sp, core: jnp.where(i // 4 == core, i % 4, jnp.where(core == 0, 3, 0))
    return call(
        functools.partial(spread_body, moves),
        sp,
        (8,),
        [
            (mine, pl.BlockSpec((block, cols), lambda i, sp: (turn(i, sp, sp[2]), 0))),
            (got, pl.BlockSpec((block, cols), lambda i, sp: (turn(i, sp, 1 - sp[2]), 0))),
        ],
        [
            (jax.ShapeDtypeStruct((2 * half, w), f32), pl.BlockSpec((block, w), lambda i, sp: (i, 0)))
            for w in widths
        ],
        [],
        us=5,
    )


def bucket_maps(position_cells, counts):
    key = jnp.arange(HALF, dtype=jnp.int32)[:, None]
    query = jnp.arange(HALF, dtype=jnp.int32)[None, :]
    begins = (0, position_cells, position_cells + GRID, HALF)
    bucket = jnp.full((HALF, HALF), -1, jnp.int32)
    base = 0
    for j, offset in enumerate((counts[0] // 2, GRID - 1, GRID - 1)):
        inside = (key >= begins[j]) & (key < begins[j + 1]) & (query >= begins[j]) & (query < begins[j + 1])
        ids = jnp.clip(query - key, -offset, counts[j] - 1 - offset) + offset + base
        bucket = jnp.where(inside, ids, bucket)
        base += counts[j]
    return bucket[:, :, None] == jnp.arange(base, dtype=jnp.int32)


def cell_matrix(tables, maps, position_cells):
    whole = jnp.concatenate(tables, axis=0)
    heads = whole.shape[1]
    whole = whole.reshape(-1, heads // 2, 2)[:, :, ::-1].reshape(-1, heads)
    m = jnp.einsum("bh,xcb->xhc", whole, maps.astype(bf16), preferred_element_type=f32)
    m = m.reshape(HALF, heads * HALF).astype(bf16)
    lane = jnp.arange(heads * HALF, dtype=jnp.int32) % HALF
    dead = jnp.where(lane < position_cells, masked, 0.0).astype(bf16)[None]
    return jnp.concatenate([m, dead, jnp.zeros((HALF - 1, heads * HALF), bf16)], axis=0)


def table_grads(cells, maps, counts):
    heads = cells.shape[1] // HALF
    whole = jnp.einsum(
        "xcb,xhc->bh", maps.astype(f32), cells.reshape(HALF, heads, HALF), precision=lax.Precision.HIGHEST
    )
    whole = whole.reshape(-1, heads // 2, 2)[:, :, ::-1].reshape(-1, heads)
    a, b = counts[0], counts[0] + counts[1]
    return [whole[:a], whole[a:b], whole[b:]]


def after(value, earlier):
    return lax.optimization_barrier((value, earlier))[0]


class Ring:
    def __init__(self, count):
        self.count = count
        self.index = lax.axis_index("dp")
        bits = list(range(1, count.bit_length() - 1))
        turned = bits[:2][::-1] + bits[2:]
        self.steps = list(zip(bits, turned))

    def bit(self, step):
        even, odd = step
        return jnp.where(self.index % 2 == 0, (self.index >> even) & 1, (self.index >> odd) & 1)

    def send(self, a, step):
        even, odd = step
        pairs = [(i, i ^ (1 << (even if i % 2 == 0 else odd))) for i in range(self.count)]
        return lax.ppermute(a, "dp", pairs)

    def swap(self, a):
        return lax.ppermute(a, "dp", [(i, i ^ 1) for i in range(self.count)])

    def halve(self, part, step):
        half = part.shape[0] // 2
        bit = self.bit(step)
        keep = lax.dynamic_slice_in_dim(part, bit * half, half, 0)
        give = lax.dynamic_slice_in_dim(part, (1 - bit) * half, half, 0)
        return keep, self.send(give, step)

    def join(self, part, got, step):
        first = self.bit(step) == 0
        return jnp.concatenate([jnp.where(first, part, got), jnp.where(first, got, part)], axis=0)

    def stages(self, give, keep):
        got = self.swap(give)
        order = yield
        part = keep + order(got)
        for step in self.steps:
            keep, got = self.halve(part, step)
            order = yield part
            part = keep + order(got)
        for step in self.steps[::-1]:
            got = self.send(part, step)
            order = yield part
            part = self.join(part, order(got), step)
        got = self.swap(part)
        order = yield part
        self.result = (part, order(got))
        yield self.result[1]

    def totals(self, part):
        for bit in range(self.count.bit_length() - 1):
            got = lax.ppermute(part, "dp", [(i, i ^ (1 << bit)) for i in range(self.count)])
            order = yield part
            part = part + order(got)
        yield part


SLOTS = (
    ("F", 0, None),
    ("F", 1, 0),
    ("B", None, 0),
    ("F", 2, 1),
    ("B", 0, 1),
    ("F", 3, 2),
    ("B", 1, 2),
    ("F", None, 3),
    ("B", 2, 3),
    ("B", 3, None),
)


def on_device(
    boundary, doc_lengths, horizontal, vertical, attention_in, attention_out, expand_weight,
    contract_weight, norm_gains, bias_rows, expand_bias, position_table, horizontal_table,
    vertical_table,
):
    section = lax.axis_index("section")
    dp_count = lax.axis_size("dp")
    core = lax.axis_index("dp") % 2
    swap = [(i, i ^ 1) for i in range(dp_count)]
    exchange = lambda a: lax.ppermute(a, "dp", swap)

    own = boundary[0]
    micro, slots, width = own.shape
    rows = slots // 2
    windows = 2 * micro
    hidden = expand_weight.shape[2]
    heads = position_table.shape[2]
    pairs = heads // 2
    w_in, w_out, w1, w2 = in_vmem([attention_in[0], attention_out[0], expand_weight[0], contract_weight[0]])
    gains = norm_gains[0].astype(f32)
    biases = bias_rows[0].astype(f32)
    eb = expand_bias.astype(f32)
    in_bias = jnp.concatenate([biases[0], jnp.zeros_like(biases[0]), biases[1]])[None]
    tables = (position_table[0], horizontal_table[0], vertical_table[0])
    counts = tuple(t.shape[0] for t in tables)
    position_cells = slots // SPAN
    maps = bucket_maps(position_cells, counts)
    ring = Ring(dp_count)

    def both(mine, theirs):
        return jnp.concatenate(
            [jnp.where(core == 0, mine, theirs), jnp.where(core == 0, theirs, mine)], axis=0
        )

    halves = own.reshape(micro, 2, rows, width)
    own_half = jnp.where(core == 0, halves[:, 0], halves[:, 1])
    other_half = jnp.where(core == 0, halves[:, 1], halves[:, 0])
    spare = lambda a: jnp.concatenate([a, a[:1]], axis=0)
    own_all = spare(both(own_half, exchange(other_half)))
    places = jnp.concatenate(
        [horizontal, vertical, jnp.broadcast_to(doc_lengths[:, None], (micro, PAIR))], axis=1
    )
    places = spare(both(places, exchange(places)))
    across_cell = places[:, :slots] // SPAN
    down_cell = places[:, slots : 2 * slots] // SPAN
    lengths = places[:, 2 * slots]
    ids = jnp.arange(slots, dtype=jnp.int32)
    position_cell = jnp.broadcast_to((ids // SPAN)[None], (windows + 1, slots))

    def hot_of(cells, lanes, axis):
        p, a, d = (jnp.expand_dims(c, axis) for c in cells)
        lanes = jnp.expand_dims(lanes, (0, 3 - axis))
        return (lanes == p) | (lanes == a + position_cells) | (lanes == d + position_cells + GRID)

    cells = (position_cell, across_cell, down_cell)
    cell_ids = jnp.arange(PAIR, dtype=jnp.int32)
    turned_all = hot_of(cells, cell_ids[:HALF], 1).astype(bf16)
    dead = (ids[None, :] >= lengths[:, None])[:, :, None] & (cell_ids == HALF)
    hot_all = (hot_of(cells, cell_ids, 2) | dead).astype(bf16)
    take = lambda c: jnp.where(core == 0, c[:, :rows], c[:, rows:])
    side_all = hot_of(tuple(take(c) for c in cells), cell_ids % HALF, 2).astype(bf16)
    matrix = cell_matrix(tables, maps, position_cells)

    sel = (cell_ids[:, None] // HALF != cell_ids[None, :] // HALF).astype(bf16)

    blocks_of = (lengths + KEY_BLOCK - 1) // KEY_BLOCK
    blocks_of = jnp.where(jnp.arange(windows + 1) < windows, blocks_of, 0)
    infos = []
    for _, zero, one in SLOTS:
        w = jnp.where(
            section == 0, windows if zero is None else zero, windows if one is None else one
        ).astype(jnp.int32)
        infos.append(w)
    infos = jnp.stack(infos)
    infos = jnp.stack(
        [infos, blocks_of[infos], jnp.full_like(infos, core), lengths[infos], jnp.full_like(infos, section)],
        axis=1,
    )
    facts = infos.shape[1]
    infos = infos.reshape(-1)

    widths = dict(
        x=width, q=width, kv=2 * width, a=width, rest=width, lse=width, peer=2 * width, n1=width, h1=width,
        g=hidden, d=hidden, n2=width, db2=width, df=hidden, db1=width, dj=3 * width,
    )
    shapes = {n: jax.ShapeDtypeStruct((windows + 1, rows, c), bf16) for n, c in widths.items()}
    shapes["r"] = jax.ShapeDtypeStruct((windows + 1, rows, PAIR), f32)
    shapes["st"] = shapes["sj"] = jax.ShapeDtypeStruct((windows + 1, 8, width), f32)
    shapes["se"] = jax.ShapeDtypeStruct((windows + 1, 1, hidden), f32)
    shapes["cell"] = jax.ShapeDtypeStruct((windows + 1, HALF, width), f32)
    st = dict(zip(shapes, unwritten(list(shapes.values()))))

    def forward(sp, s, got):
        x, q, kv, fresh = qkv_call(sp, own_all, got, w_in, in_bias, s["x"], s["q"], s["kv"])
        s = dict(s, x=x, q=q, kv=kv)
        mixed = ("a", "rest", "lse", "peer")
        s.update(
            zip(mixed, attend_call(
                sp, q, fresh, exchange(fresh), side_all, hot_all, matrix, tuple(s[n] for n in mixed)
            ))
        )
        names = ("n1", "h1", "g", "d", "n2", "r")
        outs = dense_call(
            sp, s["a"], x, w_out, w1, w2, gains, biases, eb, tuple(s[n] for n in names)
        )
        s.update(zip(names, outs[:-1]))
        return s, outs[-1]

    def dense_back(sp, s, got):
        names = ("db2", "df", "db1", "st", "se")
        outs = dense_back_call(
            sp, own_all, got, s["n2"], s["r"], s["d"], s["n1"], s["a"], s["rest"], w_out, w1, w2, gains,
            sel, tuple(s[n] for n in names),
        )
        s = dict(s)
        s.update(zip(names, outs[:5]))
        return s, tuple(outs[5:])

    def attend_back_kernel(sp, s, grads):
        return attend_back_call(
            sp, s["q"], s["kv"], s["peer"], side_all, hot_all, matrix, s["lse"], *grads, turned_all,
            s["cell"],
        )

    def input_back(sp, s, dq, keep, got):
        dj, sj, fresh = input_back_call(sp, dq, keep, got, s["db1"], w_in, s["dj"], s["sj"])
        return dict(s, dj=dj, sj=sj), fresh

    def attend_back(sp, s, grads):
        cell, dq, keep, send = attend_back_kernel(sp, s, grads)
        return input_back(sp, dict(s, cell=cell), dq, keep, exchange(send))

    got = {}
    finals = {}
    grads_in = {}
    nothing = jnp.zeros((rows, width), bf16)

    for number, (kind, zero, one) in enumerate(SLOTS[:-1]):
        sp = (infos, number * facts)
        if kind == "F":
            st, out = forward(sp, st, got.pop(("F", one), nothing))
            if one is not None:
                finals[one] = out
            if zero is not None:
                got["F", zero] = lax.ppermute(out, "section", [(0, 1)])
        else:
            st, grads = dense_back(sp, st, got.pop(("B", zero), nothing))
            st, out = attend_back(sp, st, grads)
            if zero is not None:
                grads_in[zero] = out
            if one is not None:
                got["B", one] = lax.ppermute(out, "section", [(1, 0)])

    sp = (infos, (len(SLOTS) - 1) * facts)

    class Chain:
        def __init__(self, stages, count):
            self.stages = stages
            self.left = count
            next(stages)

        def advance(self, earlier):
            self.last = self.stages.send(lambda got: after(got, earlier))
            self.left -= 1
            return self.last

    def weight_sum(pairs):
        give, keep = weight_call(sp, windows, pairs)
        return give, Chain(ring.stages(give, keep), 2 * len(ring.steps) + 2)

    natural = [((0, 0), 0, hidden)]
    cols = PAIRS * PAIR
    moves = [
        ((0, j * width + i * cols), (3 * i + j) * cols, cols) for i in range(width // cols) for j in range(3)
    ] + [((1, 0), 3 * width, width)]

    st, grads = dense_back(sp, st, got.pop(("B", SLOTS[-1][1])))
    given, contract = weight_sum([(st["db2"], st["g"])])
    given, expand = weight_sum([(after(st["h1"], given), st["df"])])
    done = contract.advance(given)
    grads = tuple(after(g, done) for g in grads)
    cell, dq, keep, send = attend_back_kernel(sp, st, grads)
    got = exchange(send)
    done = expand.advance(dq)
    done = contract.advance(done)
    got = after(got, done)
    st, grads_in[SLOTS[-1][1]] = input_back(sp, dict(st, cell=cell), dq, keep, got)
    done = contract.advance(st["dj"])
    given, attend = weight_sum([(after(st["x"], done), st["dj"]), (st["a"], st["db1"])])

    later = lambda a: after(a, given)
    of_windows = lambda name: jnp.sum(later(st[name])[:windows], axis=0)
    small = [of_windows("sj")[0:2], of_windows("st")[0:6], of_windows("se")] + table_grads(
        of_windows("cell"), maps, counts
    )
    packed = jnp.concatenate([p.reshape(-1) for p in small])
    packed = jnp.pad(packed, (0, -packed.shape[0] % (8 * PAIR))).reshape(-1, PAIR)
    totals = Chain(ring.totals(packed), dp_count.bit_length() - 1)
    result = [later(jnp.where(section == 0, grads_in[w], finals[w])) for w in range(windows)]
    mine_first, mine_second = jnp.stack(result[:micro]), jnp.stack(result[micro:])
    keep_rows = jnp.where(core == 0, mine_first, mine_second)
    got_rows = exchange(jnp.where(core == 0, mine_second, mine_first))

    def assembled(got_rows):
        out_halves = jnp.stack(
            [jnp.where(core == 0, keep_rows, got_rows), jnp.where(core == 0, got_rows, keep_rows)], axis=1
        )
        return out_halves.reshape(1, micro, slots, width)

    done = expand.advance(packed)
    chains = {"contract": contract, "expand": expand, "attend": attend, "totals": totals}
    kinds = {"contract": ([hidden], natural), "expand": ([hidden], natural), "attend": ([3 * width, width], moves)}
    outputs = {}
    boundary_out = None
    while any(chain.left for chain in chains.values()):
        for name, chain in chains.items():
            if chain.left:
                done = chain.advance(done)
                if not chain.left and name in kinds:
                    outputs[name] = spread_call(sp, *ring.result, *kinds[name])
                    done = outputs[name][0]
        if boundary_out is None and not totals.left:
            boundary_out = assembled(after(got_rows, done))
            done = boundary_out
    (g_contract,), (g_expand,), (g_in, g_out) = (outputs[n] for n in ("contract", "expand", "attend"))
    packed = totals.last.reshape(-1)
    pieces = []
    begin = 0
    for p in small:
        count = math.prod(p.shape)
        pieces.append(packed[begin : begin + count].reshape(p.shape))
        begin += count
    joined_sums, sums, wide, table_p, table_h, table_v = pieces
    grad_bias = jnp.concatenate([joined_sums, sums[0:4]], axis=0)
    grad_gain = sums[4:6]
    return (
        boundary_out, g_in[None], g_out[None], g_expand[None], g_contract[None], grad_gain[None],
        grad_bias[None], wide, table_p[None], table_h[None], table_v[None],
    )


def solution(mesh):
    section = P("section", None, None)
    placed = (
        P("section", "dp", None, None), P("dp"), P("dp", None), P("dp", None), section, section,
        section, section, section, section, P("section", None), section, section, section,
    )
    return jax.shard_map(
        on_device,
        mesh=mesh,
        in_specs=placed,
        out_specs=(
            P("section", "dp", None, None), section, section, section, section, section, section,
            P("section", None), section, section, section,
        ),
        check_vma=False,
    )
```

```python
import functools
import math

import jax
import jax.numpy as jnp
from jax import lax
from jax.experimental import pallas as pl
from jax.experimental.pallas import tpu as pltpu
from jax.sharding import PartitionSpec as P

GRID = 16
SPAN = 32
KEY_BLOCK = 256
ROW_BLOCK = 256
FF_BLOCK = 768
PAIRS = 2
HALF = 64
PAIR = 128

epsilon = 1e-05
masked = -1e30
score_scale = 0.125
VMEM_LIMIT = 40 * 1024 * 1024

f32 = jnp.float32
bf16 = jnp.bfloat16

dot_nn = lambda a, b: lax.dot_general(a, b, (((1,), (0,)), ((), ())), preferred_element_type=f32)
dot_nt = lambda a, b: lax.dot_general(a, b, (((1,), (1,)), ((), ())), preferred_element_type=f32)
dot_tn = lambda a, b: lax.dot_general(a, b, (((0,), (0,)), ((), ())), preferred_element_type=f32)


def params_for(axes):
    return pltpu.CompilerParams(
        dimension_semantics=("arbitrary",) * axes, vmem_limit_bytes=VMEM_LIMIT
    )


ANY = pl.BlockSpec(memory_space=pl.ANY)


def like(a):
    return jax.ShapeDtypeStruct(a.shape, a.dtype)


RESIDENT = pl.BlockSpec(memory_space=pltpu.VMEM)


def fixed(shape):
    return pl.BlockSpec(shape, lambda i, sp: (0,) * len(shape), pipeline_mode=pl.Buffered(1))


def this_step(count):
    return pl.ds(pl.multiple_of(pl.program_id(0) * count, count), count)


def stacked(rows, cols):
    return pl.BlockSpec((1, rows, cols), lambda i, sp: (sp[0], i, 0))


def plain(rows, cols):
    return pl.BlockSpec((rows, cols), lambda i, sp: (i, 0))


class Row:
    def __init__(self, table, base):
        self.table = table
        self.base = base

    def __getitem__(self, at):
        return self.table[self.base + at]


def shifted(spec, base):
    if spec.index_map is None:
        return spec
    inner = spec.index_map
    return pl.BlockSpec(
        spec.block_shape, lambda i, sp: inner(i, Row(sp, base)), pipeline_mode=spec.pipeline_mode
    )


def call(body, sp, grid, ins, outs, aliased, scratch=(), us=10):
    held = lambda a, s: pltpu.with_memory_space_constraint(a, pltpu.HBM) if a.ndim == 3 else a
    operands = [held(a, s) for a, s in ins] + [held(a, s) for a, s in aliased]
    table, base = sp
    in_specs = [shifted(s, base) for _, s in ins] + [ANY] * len(aliased)
    out_shape = [pltpu.HBM(a.shape, a.dtype) for a, _ in aliased] + [s for s, _ in outs]
    out_specs = [shifted(s, base) for _, s in aliased] + [shifted(s, base) for _, s in outs]
    kept = len(aliased)
    first = len(ins)

    def run(sp_ref, *refs):
        body(Row(sp_ref, base), *refs[:first], *refs[first + kept :])

    return pl.pallas_call(
        run,
        grid_spec=pltpu.PrefetchScalarGridSpec(
            num_scalar_prefetch=1,
            grid=grid,
            in_specs=in_specs,
            out_specs=out_specs,
            scratch_shapes=list(scratch),
        ),
        out_shape=out_shape,
        input_output_aliases={1 + first + j: j for j in range(kept)},
        compiler_params=params_for(len(grid)),
        cost_estimate=pl.CostEstimate(
            flops=us * 1_000_000_000, bytes_accessed=us * 1_000_000, transcendentals=0
        ),
    )(table, *operands)


def unwritten(shapes):
    return pl.pallas_call(
        lambda *refs: None, out_shape=[pltpu.HBM(s.shape, s.dtype) for s in shapes], out_specs=[ANY] * len(shapes),
        compiler_params=pltpu.CompilerParams(vmem_limit_bytes=2 * 1024 * 1024),
    )()


def in_vmem(arrays):
    def body(*refs):
        count = len(arrays)
        copies = [
            pltpu.make_async_copy(refs[j], refs[count + j], refs[-1].at[j]) for j in range(count)
        ]
        for copy in copies:
            copy.start()
        for copy in copies:
            copy.wait()

    return pl.pallas_call(
        body,
        out_shape=[pltpu.VMEM(a.shape, a.dtype) for a in arrays],
        in_specs=[ANY] * len(arrays),
        out_specs=[RESIDENT] * len(arrays),
        scratch_shapes=[pltpu.SemaphoreType.DMA((len(arrays),))],
        compiler_params=pltpu.CompilerParams(vmem_limit_bytes=2 * 1024 * 1024),
    )(*[pltpu.with_memory_space_constraint(a, pltpu.HBM) for a in arrays])


def at_window(rows, cols):
    return pl.BlockSpec((1, rows, cols), lambda i, sp: (sp[0], 0, i))


def whole_window(rows, cols):
    return pl.BlockSpec((1, rows, cols), lambda i, sp: (sp[0], 0, 0))


def as_given(rows, cols):
    return pl.BlockSpec((1, rows, cols), lambda i, sp: (sp[5], 0, 0))


def columns(rows, cols, begin=0):
    return pl.BlockSpec((rows, cols), lambda i, sp: (0, begin + i))


def qkv_body(sp, x_ref, got_ref, w_ref, b_ref, x_out, q_ref, kv_ref, fresh_ref):
    width = x_ref.shape[2]
    cols = q_ref.shape[2]
    x = jnp.where(sp[4] == 1, got_ref[...], x_ref[0])

    @pl.when(pl.program_id(0) == 0)
    def _():
        x_out[0] = x

    def part(j):
        at = pl.ds(pl.multiple_of(j * width + pl.program_id(0) * cols, cols), cols)
        return dot_nn(x, w_ref[:, at]) + b_ref[:, at]

    q_ref[0] = (part(0).astype(bf16) * score_scale).astype(bf16)
    k = part(1).astype(bf16)
    v = part(2).astype(bf16)
    for begin in range(0, cols, PAIR):
        for value, at in ((k, 0), (v, PAIR)):
            to = slice(2 * begin + at, 2 * begin + at + PAIR)
            kv_ref[0, :, to] = value[:, begin : begin + PAIR]
            fresh_ref[:, to] = value[:, begin : begin + PAIR]


def qkv_call(sp, own_all, got, weight, bias, x_all, q_all, kv_all):
    rows, width = x_all.shape[1], x_all.shape[2]
    cols = PAIRS * PAIR
    return call(
        qkv_body,
        sp,
        (width // cols,),
        [
            (own_all, as_given(rows, width)), (got, fixed(got.shape)), (weight, RESIDENT),
            (bias, fixed(bias.shape)),
        ],
        [(jax.ShapeDtypeStruct((rows, 2 * width), bf16), columns(rows, 2 * cols))],
        [
            (x_all, whole_window(rows, width)), (q_all, at_window(rows, cols)),
            (kv_all, at_window(rows, 2 * cols)),
        ],
        us=4,
    )


def low_half(shape):
    return lax.broadcasted_iota(jnp.int32, shape, 1) < HALF


def split_three(value):
    place = lax.broadcasted_iota(jnp.int32, value.shape, 1) % HALF
    high = value.astype(bf16).astype(f32)
    rest = value - high
    mid = rest.astype(bf16).astype(f32)
    last = rest - mid
    out = jnp.where(place == 0, high, jnp.where(place == 1, mid, jnp.where(place == 2, last, 0.0)))
    return out.astype(bf16)


def in_order(first, own, peer):
    return jnp.concatenate([jnp.where(first, own, peer), jnp.where(first, peer, own)], axis=0)


def attend_body(
    sp, q_ref, own_ref, peer_ref, side_ref, hot_ref, m_ref, a_ref, rest_ref, lse_ref, kept_ref
):
    rows = q_ref.shape[1]
    first = sp[2] == 0
    kept_ref[0] = peer_ref[...]

    def variant(keys):
        low = low_half((rows, PAIR))
        key_low = low_half((keys, PAIR))
        one = jnp.ones((keys, PAIR), bf16)
        side = side_ref[0]
        hot = hot_ref[0, :keys, :]
        for n in range(PAIRS):
            cols = slice(n * PAIR, (n + 1) * PAIR)
            kv = slice(2 * n * PAIR, 2 * (n + 1) * PAIR)
            both = in_order(first, own_ref[:, kv], peer_ref[:, kv])[:keys]
            k, v = both[:, :PAIR], both[:, PAIR:]
            ks = dot_nn(hot, m_ref[:, cols]).astype(bf16)
            q = q_ref[0, :, cols]
            outs = []
            peaks = []
            for head in (0, 1):
                pick = (lambda m, x, y: jnp.where(m, x, y)) if head == 0 else (
                    lambda m, x, y: jnp.where(m, y, x)
                )
                s = dot_nt(pick(low, q, side), pick(key_low, k, ks))
                peak = jnp.max(s, axis=1, keepdims=True)
                e = jnp.exp(s - peak).astype(bf16)
                outs.append(dot_nn(e, pick(key_low, v, one)))
                peaks.append(peak)
            top = jnp.where(low, outs[0], outs[1])
            total = pltpu.roll(jnp.where(low, outs[1], outs[0]), HALF, 1)
            mixed = top / total
            mixed_low = mixed.astype(bf16)
            a_ref[0, :, cols] = mixed_low
            rest_ref[0, :, cols] = (mixed - mixed_low.astype(f32)).astype(bf16)
            lse = jnp.where(low, peaks[0], peaks[1]) + jnp.log(total)
            lse_ref[0, :, cols] = split_three(-lse)

    for blocks in range(1, 2 * rows // KEY_BLOCK + 1):
        pl.when(sp[1] == blocks)(functools.partial(variant, blocks * KEY_BLOCK))


def attend_call(sp, q_all, kv_own, kv_peer, side_all, hot_all, matrix, bufs):
    rows, width = q_all.shape[1], q_all.shape[2]
    cols = PAIRS * PAIR
    part = at_window(rows, cols)
    return call(
        attend_body,
        sp,
        (width // cols,),
        [
            (q_all, part),
            (kv_own, columns(rows, 2 * cols)),
            (kv_peer, columns(rows, 2 * cols)),
            (side_all, as_given(rows, PAIR)),
            (hot_all, as_given(2 * rows, PAIR)),
            (matrix, columns(PAIR, cols)),
        ],
        [],
        [(b, part) for b in bufs[:-1]] + [(bufs[-1], at_window(rows, 2 * cols))],
        us=14,
    )


def gelu_both(x):
    cdf = 0.5 + 0.5 * lax.erf(x * math.sqrt(0.5))
    bell = jnp.exp(x * x * -0.5)
    return x * cdf, cdf + x * bell * (1.0 / math.sqrt(2.0 * math.pi))


def centered(u):
    c = u - jnp.mean(u, axis=1, keepdims=True)
    r = lax.rsqrt(jnp.mean(c * c, axis=1, keepdims=True) + epsilon)
    return c * r, r


class Moves:
    def __init__(self, sems):
        self.sems = sems
        self.used = 0
        self.out = []

    def start(self, source, target):
        copy = pltpu.make_async_copy(source, target, self.sems.at[self.used])
        self.used += 1
        copy.start()
        return copy

    def write(self, source, target):
        self.out.append(self.start(source, target))

    def finish(self):
        for copy in self.out:
            copy.wait()


def chunks(width):
    return [slice(c, c + FF_BLOCK) for c in range(0, width, FF_BLOCK)]


def dense_body(
    sp, a_ref, x_ref, wo_ref, w1_ref, w2_ref, gain_ref, bias_ref, eb_ref,
    n1_hbm, h1_hbm, g_hbm, d_hbm, n2_hbm, r_hbm, fresh_ref,
    n1_ref, h1_ref, g_ref, d_ref, n2_ref, r_ref, sems,
):
    w = sp[0]
    moves = Moves(sems)
    parts = chunks(w1_ref.shape[1])
    u1 = dot_nn(a_ref[0], wo_ref[...]) + bias_ref[2:3, :] + x_ref[0].astype(f32)
    n1, r1 = centered(u1)
    h1 = n1 * gain_ref[0:1, :] + bias_ref[3:4, :]
    h1_low = h1.astype(bf16)
    n1_ref[...] = n1.astype(bf16)
    h1_ref[...] = h1_low
    moves.write(n1_ref, n1_hbm.at[w])
    moves.write(h1_ref, h1_hbm.at[w])
    u2 = h1 + bias_ref[4:5, :]
    for c in parts:
        g, d = gelu_both(dot_nn(h1_low, w1_ref[:, c]) + eb_ref[:, c])
        g = g.astype(bf16)
        g_ref[:, c] = g
        d_ref[:, c] = d.astype(bf16)
        moves.write(g_ref.at[:, c], g_hbm.at[w, :, c])
        moves.write(d_ref.at[:, c], d_hbm.at[w, :, c])
        u2 = u2 + dot_nt(g, w2_ref[:, c])
    n2, r2 = centered(u2)
    n2_ref[...] = n2.astype(bf16)
    moves.write(n2_ref, n2_hbm.at[w])
    r_ref[...] = jnp.where(low_half(r_ref.shape), r1, r2)
    moves.write(r_ref, r_hbm.at[w])
    fresh_ref[...] = (n2 * gain_ref[1:2, :] + bias_ref[5:6, :]).astype(bf16)
    moves.finish()


def dense_call(sp, a_all, x_all, wo, w1, w2, gains, biases, eb, bufs):
    rows, width = a_all.shape[1], a_all.shape[2]
    hidden = w1.shape[1]
    row = whole_window(rows, width)
    vmem = lambda *shape: pltpu.VMEM(shape, bf16)
    return call(
        dense_body,
        sp,
        (1,),
        [
            (a_all, row), (x_all, row), (wo, RESIDENT), (w1, RESIDENT), (w2, RESIDENT), (gains, fixed(gains.shape)),
            (biases, fixed(biases.shape)), (eb, fixed(eb.shape)),
        ],
        [(jax.ShapeDtypeStruct((rows, width), bf16), pl.BlockSpec((rows, width), lambda i, sp: (0, 0)))],
        [(b, ANY) for b in bufs],
        [
            vmem(rows, width), vmem(rows, width), vmem(rows, hidden), vmem(rows, hidden), vmem(rows, width),
            pltpu.VMEM((rows, PAIR), f32), pltpu.SemaphoreType.DMA((4 + 2 * (hidden // FF_BLOCK),)),
        ],
        us=10,
    )


def column_sum(v):
    return jnp.sum(v, axis=0, keepdims=True)


def norm_back(dy, n, r, gain):
    dn = dy * gain
    return r * (dn - jnp.mean(dn, axis=1, keepdims=True) - n * jnp.mean(dn * n, axis=1, keepdims=True))


def dense_back_body(
    sp, dy_ref, got_ref, n2_ref, r_ref, gain_ref, sel_ref, wo_ref, w1_ref, w2_ref, d_hbm, n1_hbm, a_hbm,
    rest_hbm, db2_hbm, df_hbm, db1_hbm, st_ref, se_ref, do_ref, dd_ref,
    d_ref, n1_ref, a_ref, rest_ref, db2_ref, df_ref, db1_ref, sems,
):
    w = sp[0]
    width = dy_ref.shape[2]
    moves = Moves(sems)
    parts = chunks(w1_ref.shape[1])
    loads = [moves.start(d_hbm.at[w, :, c], d_ref.at[:, c]) for c in parts]
    last = [
        moves.start(n1_hbm.at[w], n1_ref), moves.start(a_hbm.at[w], a_ref),
        moves.start(rest_hbm.at[w], rest_ref),
    ]
    r = r_ref[0]
    dy = jnp.where(sp[4] == 1, dy_ref[0], got_ref[...]).astype(f32)
    n2 = n2_ref[0].astype(f32)
    du2 = norm_back(dy, n2, r[:, HALF : HALF + 1], gain_ref[1:2, :])
    db2 = du2.astype(bf16)
    db2_ref[...] = db2
    moves.write(db2_ref, db2_hbm.at[w])
    st_ref[0, 2:3, :] = column_sum(du2)
    st_ref[0, 3:4, :] = column_sum(dy)
    st_ref[0, 5:6, :] = column_sum(dy * n2)
    st_ref[0, 6:8, :] = jnp.zeros((2, width), f32)
    dh1 = du2
    for c, load in zip(parts, loads):
        load.wait()
        df = dot_nn(db2, w2_ref[:, c]) * d_ref[:, c].astype(f32)
        se_ref[0, :, c] = column_sum(df)
        df = df.astype(bf16)
        df_ref[:, c] = df
        moves.write(df_ref.at[:, c], df_hbm.at[w, :, c])
        dh1 = dh1 + dot_nt(df, w1_ref[:, c])
    for load in last:
        load.wait()
    n1 = n1_ref[...].astype(f32)
    du1 = norm_back(dh1, n1, r[:, 0:1], gain_ref[0:1, :])
    db1 = du1.astype(bf16)
    db1_ref[...] = db1
    moves.write(db1_ref, db1_hbm.at[w])
    st_ref[0, 0:1, :] = column_sum(du1)
    st_ref[0, 1:2, :] = column_sum(dh1)
    st_ref[0, 4:5, :] = column_sum(dh1 * n1)
    do = dot_nt(db1, wo_ref[...]).astype(bf16)
    do_ref[...] = do
    mixed = do.astype(f32) * (a_ref[...].astype(f32) + rest_ref[...].astype(f32))
    high = mixed.astype(bf16)
    low = (mixed - high.astype(f32)).astype(bf16)
    for begin in range(0, width, PAIR):
        cols = slice(begin, begin + PAIR)
        inner = dot_nn(high[:, cols], sel_ref[...]) + dot_nn(low[:, cols], sel_ref[...])
        dd_ref[:, cols] = split_three(-inner)
    moves.finish()


def dense_back_call(
    sp, dy_all, got, n2_all, r_all, d_all, n1_all, a_all, rest_all, wo, w1, w2, gains, sel, bufs
):
    rows, width = got.shape
    hidden = w1.shape[1]
    row = whole_window(rows, width)
    db2_all, df_all, db1_all, st_all, se_all = bufs
    flat = (jax.ShapeDtypeStruct((rows, width), bf16), pl.BlockSpec((rows, width), lambda i, sp: (0, 0)))
    vmem = lambda *shape: pltpu.VMEM(shape, bf16)
    return call(
        dense_back_body,
        sp,
        (1,),
        [
            (dy_all, as_given(rows, width)), (got, fixed(got.shape)), (n2_all, row), (r_all, whole_window(rows, PAIR)),
            (gains, fixed(gains.shape)), (sel, fixed(sel.shape)), (wo, RESIDENT), (w1, RESIDENT),
            (w2, RESIDENT),
        ]
        + [(b, ANY) for b in (d_all, n1_all, a_all, rest_all)],
        [flat, flat],
        [
            (db2_all, ANY), (df_all, ANY), (db1_all, ANY), (st_all, whole_window(8, width)),
            (se_all, whole_window(1, hidden)),
        ],
        [
            vmem(rows, hidden), vmem(rows, width), vmem(rows, width), vmem(rows, width), vmem(rows, width),
            vmem(rows, hidden), vmem(rows, width), pltpu.SemaphoreType.DMA((5 + 2 * (hidden // FF_BLOCK),)),
        ],
        us=10,
    )


def attend_back_body(
    sp, q_ref, own_ref, peer_ref, side_ref, hot_ref, m_ref, lse_ref, do_ref, dd_ref, turned_ref,
    cell_ref, dq_ref, keep_ref, send_ref,
):
    rows = q_ref.shape[1]
    total = 2 * rows
    first = sp[2] == 0

    def variant(blocks):
        keys = blocks * KEY_BLOCK
        low = low_half((rows, PAIR))
        key_low = low_half((keys, PAIR))
        block_low = low_half((KEY_BLOCK, PAIR))
        place = lax.broadcasted_iota(jnp.int32, (KEY_BLOCK, PAIR), 1)
        three = jnp.where(place % HALF < 3, 1.0, 0.0).astype(bf16)
        lone = [
            jnp.where(place < 3, 1.0, 0.0).astype(bf16),
            jnp.where((place >= HALF) & (place < HALF + 3), 1.0, 0.0).astype(bf16),
        ]
        side = side_ref[0]
        hot = hot_ref[0, :keys, :]
        for n in range(PAIRS):
            cols = slice(n * PAIR, (n + 1) * PAIR)
            kv = slice(2 * n * PAIR, 2 * (n + 1) * PAIR)
            both = in_order(first, own_ref[0, :, kv], peer_ref[0, :, kv])[:keys]
            k, v = both[:, :PAIR], both[:, PAIR:]
            ks = dot_nn(hot, m_ref[:, cols]).astype(bf16)
            kt = k.T
            q = q_ref[0, :, cols]
            do = do_ref[:, cols]
            dd = dd_ref[:, cols]
            lse = lse_ref[0, :, cols]
            kc = (jnp.where(key_low, k, ks), jnp.where(key_low, ks, k))
            qc = (jnp.where(low, q, side), jnp.where(low, side, q))
            qe = tuple(jnp.concatenate([c, lse], axis=1) for c in qc)
            dc = (jnp.where(low, do, dd), jnp.where(low, dd, do))
            dq = [None, None]
            dks = []
            dvs = []
            gs = []
            for b in range(blocks):
                at = slice(b * KEY_BLOCK, (b + 1) * KEY_BLOCK)
                vb = v[at]
                vc = (jnp.where(block_low, vb, three), jnp.where(block_low, three, vb))
                part_v = []
                part_k = []
                for head in (0, 1):
                    kb = jnp.concatenate([kc[head][at], lone[head]], axis=1)
                    p = jnp.exp(dot_nt(kb, qe[head]))
                    dp = dot_nt(vc[head], dc[head])
                    ds = (p * dp).astype(bf16)
                    part_v.append(dot_nn(p.astype(bf16), do))
                    part_k.append(dot_nn(ds, qc[head]))
                    part = dot_nn(kt[head * HALF : (head + 1) * HALF, at], ds)
                    dq[head] = part if dq[head] is None else dq[head] + part
                dvs.append(jnp.where(block_low, part_v[0], part_v[1]).astype(bf16))
                dks.append(jnp.where(block_low, part_k[0], part_k[1]).astype(bf16))
                gs.append(jnp.where(block_low, part_k[1], part_k[0]).astype(bf16))
            dq_ref[:, cols] = (jnp.concatenate(dq, axis=0).T * score_scale).astype(bf16)
            cell_ref[0, :, cols] = dot_nn(turned_ref[0, :, :keys], jnp.concatenate(gs, axis=0))
            if keys < total:
                zero = [jnp.zeros((total - keys, PAIR), bf16)]
                dks = dks + zero
                dvs = dvs + zero
            grads = jnp.concatenate([jnp.concatenate(dks, axis=0), jnp.concatenate(dvs, axis=0)], axis=1)
            keep_ref[:, kv] = jnp.where(first, grads[:rows], grads[rows:])
            send_ref[:, kv] = jnp.where(first, grads[rows:], grads[:rows])

    for blocks in range(1, total // KEY_BLOCK + 1):
        pl.when(sp[1] == blocks)(functools.partial(variant, blocks))


def attend_back_call(
    sp, q_all, kv_all, peer_all, side_all, hot_all, matrix, lse_all, do, dd, turned_all, cell_all
):
    rows, width = q_all.shape[1], q_all.shape[2]
    cols = PAIRS * PAIR
    part = at_window(rows, cols)
    kv = at_window(rows, 2 * cols)
    flat = columns(rows, cols)
    flat_kv = columns(rows, 2 * cols)
    out_kv = jax.ShapeDtypeStruct((rows, 2 * width), bf16)
    return call(
        attend_back_body,
        sp,
        (width // cols,),
        [
            (q_all, part),
            (kv_all, kv),
            (peer_all, kv),
            (side_all, as_given(rows, PAIR)),
            (hot_all, as_given(2 * rows, PAIR)),
            (matrix, columns(PAIR, cols)),
            (lse_all, part),
            (do, flat),
            (dd, flat),
            (turned_all, as_given(HALF, 2 * rows)),
        ],
        [(jax.ShapeDtypeStruct((rows, width), bf16), flat), (out_kv, flat_kv), (out_kv, flat_kv)],
        [(cell_all, at_window(HALF, cols))],
        us=20,
    )


def input_back_body(
    sp, dq_ref, own_ref, got_ref, db1_ref, w_ref, dj_ref, sj_ref, fresh_ref, total
):
    step = pl.program_id(0)
    dq = dq_ref[...]
    cols = dq.shape[1]
    both = own_ref[...].astype(f32) + got_ref[...].astype(f32)
    part = lambda at: jnp.concatenate(
        [both[:, p + at : p + at + PAIR] for p in range(0, 2 * cols, 2 * PAIR)], axis=1
    )
    dk = part(0).astype(bf16)
    dv32 = part(PAIR)
    dv = dv32.astype(bf16)
    dj_ref[0, :, :cols] = dq
    dj_ref[0, :, cols : 2 * cols] = dk
    dj_ref[0, :, 2 * cols :] = dv
    sj_ref[0] = jnp.concatenate(
        [column_sum(dq.astype(f32)), column_sum(dv32), jnp.zeros((6, cols), f32)], axis=0
    )
    width = w_ref.shape[0]
    dx = None
    for j, value in enumerate((dq, dk, dv)):
        at = pl.ds(pl.multiple_of(j * width + step * cols, cols), cols)
        term = dot_nt(value, w_ref[:, at])
        dx = term if dx is None else dx + term

    @pl.when(step == 0)
    def _():
        total[...] = dx + db1_ref[0].astype(f32)

    @pl.when(step > 0)
    def _():
        total[...] += dx

    @pl.when(step == pl.num_programs(0) - 1)
    def _():
        fresh_ref[...] = total[...].astype(bf16)


def input_back_call(sp, dq, own, got, db1_all, weight, dj_all, sj_all):
    rows, width = dq.shape
    cols = PAIRS * PAIR
    steps = width // cols
    return call(
        input_back_body,
        sp,
        (steps,),
        [
            (dq, columns(rows, cols)), (own, columns(rows, 2 * cols)), (got, columns(rows, 2 * cols)),
            (db1_all, whole_window(rows, width)), (weight, RESIDENT),
        ],
        [(jax.ShapeDtypeStruct((rows, width), bf16), pl.BlockSpec((rows, width), lambda i, sp: (0, 0)))],
        [
            (dj_all, at_window(rows, 3 * cols)), (sj_all, at_window(8, cols)),
        ],
        [pltpu.VMEM((rows, width), f32)],
        us=4,
    )


def weight_body(splits, based, sp, *refs):
    count = len(splits)
    lefts, rights = refs[:count], refs[count : 2 * count]
    base_refs = refs[2 * count : 2 * count + 2] if based else ()
    give_ref, keep_ref = refs[-2:]
    step = pl.program_id(0)
    windows, rows, width = lefts[0].shape
    half = width // 2
    first = sp[2] == 0

    for (begin, end), left, right in zip(splits, lefts, rights):

        @pl.when((step >= begin) & (step < end))
        def _(left=left, right=right):
            flat = left[...].reshape(windows * rows, width)
            out = dot_tn(flat, right[...].reshape(windows * rows, right.shape[2]))
            give = jnp.where(first, out[half:], out[:half])
            keep = jnp.where(first, out[:half], out[half:])
            if based:
                give = give + base_refs[0][...].astype(f32)
                keep = keep + base_refs[1][...].astype(f32)
            give_ref[...] = give.astype(bf16)
            keep_ref[...] = keep.astype(bf16)


def weight_call(sp, at, windows, pairs, base=()):
    rows, width = pairs[0][0].shape[1:]
    splits = []
    begin = 0
    for _, right in pairs:
        splits.append((begin, begin + right.shape[2] // FF_BLOCK))
        begin = splits[-1][1]

    def left_spec():
        return pl.BlockSpec(
            (windows, rows, width), lambda i, sp: (at, 0, 0), pipeline_mode=pl.Buffered(1)
        )

    def right_spec(begin, end):
        return pl.BlockSpec(
            (windows, rows, FF_BLOCK), lambda i, sp: (at, 0, jnp.clip(i - begin, 0, end - begin - 1))
        )

    half = columns(width // 2, FF_BLOCK)
    shape = jax.ShapeDtypeStruct((width // 2, begin * FF_BLOCK), bf16)
    return call(
        functools.partial(weight_body, tuple(splits), bool(base)),
        sp,
        (begin,),
        [(left, left_spec()) for left, _ in pairs]
        + [(right, right_spec(*split)) for (_, right), split in zip(pairs, splits)]
        + [(b, half) for b in base],
        [(shape, half), (shape, half)],
        [],
        us=5 + 3 * windows,
    )


def spread_body(moves, sp, mine_ref, got_ref, *out_refs):
    half = pl.num_programs(0) // 2
    mine = (pl.program_id(0) // half) == sp[2]
    value = jnp.where(mine, mine_ref[...], got_ref[...]).astype(f32)
    for (out, to), begin, count in moves:
        out_refs[out][:, to : to + count] = value[:, begin : begin + count]


def spread_call(sp, mine, got, widths, moves):
    half, cols = mine.shape
    block = half // 4
    turn = lambda i, sp, core: jnp.where(i // 4 == core, i % 4, jnp.where(core == 0, 3, 0))
    return call(
        functools.partial(spread_body, moves),
        sp,
        (8,),
        [
            (mine, pl.BlockSpec((block, cols), lambda i, sp: (turn(i, sp, sp[2]), 0))),
            (got, pl.BlockSpec((block, cols), lambda i, sp: (turn(i, sp, 1 - sp[2]), 0))),
        ],
        [
            (jax.ShapeDtypeStruct((2 * half, w), f32), pl.BlockSpec((block, w), lambda i, sp: (i, 0)))
            for w in widths
        ],
        [],
        us=5,
    )


def bucket_maps(position_cells, counts):
    key = jnp.arange(HALF, dtype=jnp.int32)[:, None]
    query = jnp.arange(HALF, dtype=jnp.int32)[None, :]
    begins = (0, position_cells, position_cells + GRID, HALF)
    bucket = jnp.full((HALF, HALF), -1, jnp.int32)
    base = 0
    for j, offset in enumerate((counts[0] // 2, GRID - 1, GRID - 1)):
        inside = (key >= begins[j]) & (key < begins[j + 1]) & (query >= begins[j]) & (query < begins[j + 1])
        ids = jnp.clip(query - key, -offset, counts[j] - 1 - offset) + offset + base
        bucket = jnp.where(inside, ids, bucket)
        base += counts[j]
    return bucket[:, :, None] == jnp.arange(base, dtype=jnp.int32)


def cell_matrix(tables, maps, position_cells):
    whole = jnp.concatenate(tables, axis=0)
    heads = whole.shape[1]
    whole = whole.reshape(-1, heads // 2, 2)[:, :, ::-1].reshape(-1, heads)
    m = jnp.einsum("bh,xcb->xhc", whole, maps.astype(bf16), preferred_element_type=f32)
    m = m.reshape(HALF, heads * HALF).astype(bf16)
    lane = jnp.arange(heads * HALF, dtype=jnp.int32) % HALF
    dead = jnp.where(lane < position_cells, masked, 0.0).astype(bf16)[None]
    return jnp.concatenate([m, dead, jnp.zeros((HALF - 1, heads * HALF), bf16)], axis=0)


def table_grads(cells, maps, counts):
    heads = cells.shape[1] // HALF
    whole = jnp.einsum(
        "xcb,xhc->bh", maps.astype(f32), cells.reshape(HALF, heads, HALF), precision=lax.Precision.HIGHEST
    )
    whole = whole.reshape(-1, heads // 2, 2)[:, :, ::-1].reshape(-1, heads)
    a, b = counts[0], counts[0] + counts[1]
    return [whole[:a], whole[a:b], whole[b:]]


def after(value, earlier):
    return lax.optimization_barrier((value, earlier))[0]


class Ring:
    def __init__(self, count):
        self.count = count
        self.index = lax.axis_index("dp")
        bits = list(range(1, count.bit_length() - 1))
        turned = bits[:2][::-1] + bits[2:]
        self.mixed = list(zip(bits, turned))
        self.plain = list(zip(bits, bits))

    def bit(self, step):
        even, odd = step
        return jnp.where(self.index % 2 == 0, (self.index >> even) & 1, (self.index >> odd) & 1)

    def send(self, a, step):
        even, odd = step
        pairs = [(i, i ^ (1 << (even if i % 2 == 0 else odd))) for i in range(self.count)]
        return lax.ppermute(a, "dp", pairs)

    def swap(self, a):
        return lax.ppermute(a, "dp", [(i, i ^ 1) for i in range(self.count)])

    def halve(self, part, step):
        half = part.shape[0] // 2
        bit = self.bit(step)
        keep = lax.dynamic_slice_in_dim(part, bit * half, half, 0)
        give = lax.dynamic_slice_in_dim(part, (1 - bit) * half, half, 0)
        return keep, self.send(give, step)

    def join(self, part, got, step):
        first = self.bit(step) == 0
        return jnp.concatenate([jnp.where(first, part, got), jnp.where(first, got, part)], axis=0)

    def stages(self, give, keep, steps):
        got = self.swap(give)
        order = yield
        part = keep + order(got)
        for step in steps:
            keep, got = self.halve(part, step)
            order = yield part
            part = keep + order(got)
        for step in steps[::-1]:
            got = self.send(part, step)
            order = yield part
            part = self.join(part, order(got), step)
        got = self.swap(part)
        order = yield part
        self.result = (part, order(got))
        yield self.result[1]

    def totals(self, part):
        for bit in range(self.count.bit_length() - 1):
            got = lax.ppermute(part, "dp", [(i, i ^ (1 << bit)) for i in range(self.count)])
            order = yield part
            part = part + order(got)
        yield part


SLOTS = (
    ("F", 0, None),
    ("F", 1, 0),
    ("B", None, 0),
    ("F", 2, 1),
    ("B", 0, 1),
    ("F", 3, 2),
    ("B", 1, 2),
    ("F", None, 3),
    ("B", 2, 3),
    ("B", 3, None),
)


def on_device(
    boundary, doc_lengths, horizontal, vertical, attention_in, attention_out, expand_weight,
    contract_weight, norm_gains, bias_rows, expand_bias, position_table, horizontal_table,
    vertical_table,
):
    section = lax.axis_index("section")
    dp_count = lax.axis_size("dp")
    core = lax.axis_index("dp") % 2
    swap = [(i, i ^ 1) for i in range(dp_count)]
    exchange = lambda a: lax.ppermute(a, "dp", swap)

    own = boundary[0]
    micro, slots, width = own.shape
    rows = slots // 2
    windows = 2 * micro
    hidden = expand_weight.shape[2]
    heads = position_table.shape[2]
    pairs = heads // 2
    w_in, w_out, w1, w2 = in_vmem([attention_in[0], attention_out[0], expand_weight[0], contract_weight[0]])
    gains = norm_gains[0].astype(f32)
    biases = bias_rows[0].astype(f32)
    eb = expand_bias.astype(f32)
    in_bias = jnp.concatenate([biases[0], jnp.zeros_like(biases[0]), biases[1]])[None]
    tables = (position_table[0], horizontal_table[0], vertical_table[0])
    counts = tuple(t.shape[0] for t in tables)
    position_cells = slots // SPAN
    maps = bucket_maps(position_cells, counts)
    ring = Ring(dp_count)

    def both(mine, theirs):
        return jnp.concatenate(
            [jnp.where(core == 0, mine, theirs), jnp.where(core == 0, theirs, mine)], axis=0
        )

    halves = own.reshape(micro, 2, rows, width)
    own_half = jnp.where(core == 0, halves[:, 0], halves[:, 1])
    other_half = jnp.where(core == 0, halves[:, 1], halves[:, 0])
    own_all = both(own_half, exchange(other_half))
    places = jnp.concatenate(
        [horizontal, vertical, jnp.broadcast_to(doc_lengths[:, None], (micro, PAIR))], axis=1
    )
    places = both(places, exchange(places))
    across_cell = places[:, :slots] // SPAN
    down_cell = places[:, slots : 2 * slots] // SPAN
    lengths = places[:, 2 * slots]
    ids = jnp.arange(slots, dtype=jnp.int32)
    position_cell = jnp.broadcast_to((ids // SPAN)[None], (windows, slots))

    def hot_of(cells, lanes, axis):
        p, a, d = (jnp.expand_dims(c, axis) for c in cells)
        lanes = jnp.expand_dims(lanes, (0, 3 - axis))
        return (lanes == p) | (lanes == a + position_cells) | (lanes == d + position_cells + GRID)

    cells = (position_cell, across_cell, down_cell)
    cell_ids = jnp.arange(PAIR, dtype=jnp.int32)
    turned_all = hot_of(cells, cell_ids[:HALF], 1).astype(bf16)
    dead = (ids[None, :] >= lengths[:, None])[:, :, None] & (cell_ids == HALF)
    hot_all = (hot_of(cells, cell_ids, 2) | dead).astype(bf16)
    take = lambda c: jnp.where(core == 0, c[:, :rows], c[:, rows:])
    side_all = hot_of(tuple(take(c) for c in cells), cell_ids % HALF, 2).astype(bf16)
    matrix = cell_matrix(tables, maps, position_cells)

    sel = (cell_ids[:, None] // HALF != cell_ids[None, :] // HALF).astype(bf16)

    window_ids = jnp.arange(windows, dtype=jnp.int32)
    mine, theirs = lengths[:windows][:, None], lengths[:windows][None, :]
    ahead = (theirs > mine) | ((theirs == mine) & (window_ids[None, :] < window_ids[:, None]))
    rank = jnp.sum(ahead.astype(jnp.int32), axis=1)
    picks = jnp.stack(
        [jnp.array([windows if w is None else w for w in slots_of], jnp.int32) for slots_of in zip(*[s[1:] for s in SLOTS])]
    )
    infos = jnp.where(section == 0, picks[0], picks[1])
    hits = infos[:, None] == rank[None, :]
    given_ids = jnp.sum(jnp.where(hits, window_ids[None, :], 0), axis=1)
    given_lengths = jnp.sum(jnp.where(hits, lengths[None, :windows], 0), axis=1)
    infos = jnp.stack(
        [
            infos, (given_lengths + KEY_BLOCK - 1) // KEY_BLOCK, jnp.full_like(infos, core),
            given_lengths, jnp.full_like(infos, section), given_ids,
        ],
        axis=1,
    )
    facts = infos.shape[1]
    infos = infos.reshape(-1)

    widths = dict(
        x=width, q=width, kv=2 * width, a=width, rest=width, lse=width, peer=2 * width, n1=width, h1=width,
        g=hidden, d=hidden, n2=width, db2=width, df=hidden, db1=width, dj=3 * width,
    )
    shapes = {n: jax.ShapeDtypeStruct((windows + 1, rows, c), bf16) for n, c in widths.items()}
    shapes["r"] = jax.ShapeDtypeStruct((windows + 1, rows, PAIR), f32)
    shapes["st"] = shapes["sj"] = jax.ShapeDtypeStruct((windows + 1, 8, width), f32)
    shapes["se"] = jax.ShapeDtypeStruct((windows + 1, 1, hidden), f32)
    shapes["cell"] = jax.ShapeDtypeStruct((windows + 1, HALF, width), f32)
    st = dict(zip(shapes, unwritten(list(shapes.values()))))

    def forward(sp, s, got):
        x, q, kv, fresh = qkv_call(sp, own_all, got, w_in, in_bias, s["x"], s["q"], s["kv"])
        s = dict(s, x=x, q=q, kv=kv)
        mixed = ("a", "rest", "lse", "peer")
        s.update(
            zip(mixed, attend_call(
                sp, q, fresh, exchange(fresh), side_all, hot_all, matrix, tuple(s[n] for n in mixed)
            ))
        )
        names = ("n1", "h1", "g", "d", "n2", "r")
        outs = dense_call(
            sp, s["a"], x, w_out, w1, w2, gains, biases, eb, tuple(s[n] for n in names)
        )
        s.update(zip(names, outs[:-1]))
        return s, outs[-1]

    def dense_back(sp, s, got):
        names = ("db2", "df", "db1", "st", "se")
        outs = dense_back_call(
            sp, own_all, got, s["n2"], s["r"], s["d"], s["n1"], s["a"], s["rest"], w_out, w1, w2, gains,
            sel, tuple(s[n] for n in names),
        )
        s = dict(s)
        s.update(zip(names, outs[:5]))
        return s, tuple(outs[5:])

    def attend_back_kernel(sp, s, grads):
        return attend_back_call(
            sp, s["q"], s["kv"], s["peer"], side_all, hot_all, matrix, s["lse"], *grads, turned_all,
            s["cell"],
        )

    def input_back(sp, s, dq, keep, got):
        dj, sj, fresh = input_back_call(sp, dq, keep, got, s["db1"], w_in, s["dj"], s["sj"])
        return dict(s, dj=dj, sj=sj), fresh

    def attend_back(sp, s, grads):
        cell, dq, keep, send = attend_back_kernel(sp, s, grads)
        return input_back(sp, dict(s, cell=cell), dq, keep, exchange(send))

    got = {}
    finals = {}
    grads_in = {}
    nothing = jnp.zeros((rows, width), bf16)

    for number, (kind, zero, one) in enumerate(SLOTS[:-1]):
        sp = (infos, number * facts)
        if kind == "F":
            st, out = forward(sp, st, got.pop(("F", one), nothing))
            if one is not None:
                finals[one] = out
            if zero is not None:
                got["F", zero] = lax.ppermute(out, "section", [(0, 1)])
        else:
            st, grads = dense_back(sp, st, got.pop(("B", zero), nothing))
            st, out = attend_back(sp, st, grads)
            if zero is not None:
                grads_in[zero] = out
            if one is not None:
                got["B", one] = lax.ppermute(out, "section", [(1, 0)])

    sp = (infos, (len(SLOTS) - 1) * facts)

    class Chain:
        def __init__(self, stages, count):
            self.stages = stages
            self.left = count
            next(stages)

        def advance(self, earlier):
            self.last = self.stages.send(lambda got: after(got, earlier))
            self.left -= 1
            return self.last

    def weight_sum(steps, give, keep):
        return give, Chain(ring.stages(give, keep, steps), 2 * len(steps) + 2)

    natural = [((0, 0), 0, hidden)]
    cols = PAIRS * PAIR
    moves = [
        ((0, j * width + i * cols), (3 * i + j) * cols, cols) for i in range(width // cols) for j in range(3)
    ] + [((1, 0), 3 * width, width)]

    others = windows - 1
    part_contract = weight_call(sp, 0, others, [(after(st["db2"], out), st["g"])])
    part_expand = weight_call(sp, 0, others, [(after(st["h1"], part_contract[0]), st["df"])])
    rows_in = after(got.pop(("B", SLOTS[-1][1])), part_expand[0])
    st, grads = dense_back(sp, st, rows_in)
    halves = weight_call(sp, others, 1, [(st["db2"], st["g"])], part_contract)
    given, contract = weight_sum(ring.mixed, *halves)
    halves = weight_call(sp, others, 1, [(after(st["h1"], given), st["df"])], part_expand)
    given, expand = weight_sum(ring.plain, *halves)
    done = contract.advance(given)
    grads = tuple(after(g, done) for g in grads)
    cell, dq, keep, send = attend_back_kernel(sp, st, grads)
    got = exchange(send)
    done = expand.advance(dq)
    done = contract.advance(done)
    got = after(got, done)
    st, grads_in[SLOTS[-1][1]] = input_back(sp, dict(st, cell=cell), dq, keep, got)
    done = contract.advance(st["dj"])
    halves = weight_call(sp, 0, windows, [(after(st["x"], done), st["dj"]), (st["a"], st["db1"])])
    given, attend = weight_sum(ring.mixed, *halves)

    later = lambda a: after(a, given)
    of_windows = lambda name: jnp.sum(later(st[name])[:windows], axis=0)
    small = [of_windows("sj")[0:2], of_windows("st")[0:6], of_windows("se")] + table_grads(
        of_windows("cell"), maps, counts
    )
    packed = jnp.concatenate([p.reshape(-1) for p in small])
    packed = jnp.pad(packed, (0, -packed.shape[0] % (8 * PAIR))).reshape(-1, PAIR)
    totals = Chain(ring.totals(packed), dp_count.bit_length() - 1)
    result = [later(jnp.where(section == 0, grads_in[w], finals[w])) for w in range(windows)]
    result = jnp.stack(result)
    ordered = [lax.dynamic_index_in_dim(result, rank[w], 0, keepdims=False) for w in range(windows)]
    mine_first, mine_second = jnp.stack(ordered[:micro]), jnp.stack(ordered[micro:])
    keep_rows = jnp.where(core == 0, mine_first, mine_second)
    got_rows = exchange(jnp.where(core == 0, mine_second, mine_first))

    def assembled(got_rows):
        out_halves = jnp.stack(
            [jnp.where(core == 0, keep_rows, got_rows), jnp.where(core == 0, got_rows, keep_rows)], axis=1
        )
        return out_halves.reshape(1, micro, slots, width)

    done = expand.advance(packed)
    chains = {"contract": contract, "expand": expand, "attend": attend, "totals": totals}
    kinds = {"contract": ([hidden], natural), "expand": ([hidden], natural), "attend": ([3 * width, width], moves)}
    outputs = {}
    boundary_out = None
    while any(chain.left for chain in chains.values()):
        for name, chain in chains.items():
            if chain.left:
                done = chain.advance(done)
                if not chain.left and name in kinds:
                    outputs[name] = spread_call(sp, *ring.result, *kinds[name])
                    done = outputs[name][0]
        if boundary_out is None and not totals.left:
            boundary_out = assembled(after(got_rows, done))
            done = boundary_out
    (g_contract,), (g_expand,), (g_in, g_out) = (outputs[n] for n in ("contract", "expand", "attend"))
    packed = totals.last.reshape(-1)
    pieces = []
    begin = 0
    for p in small:
        count = math.prod(p.shape)
        pieces.append(packed[begin : begin + count].reshape(p.shape))
        begin += count
    joined_sums, sums, wide, table_p, table_h, table_v = pieces
    grad_bias = jnp.concatenate([joined_sums, sums[0:4]], axis=0)
    grad_gain = sums[4:6]
    return (
        boundary_out, g_in[None], g_out[None], g_expand[None], g_contract[None], grad_gain[None],
        grad_bias[None], wide, table_p[None], table_h[None], table_v[None],
    )


def solution(mesh):
    section = P("section", None, None)
    placed = (
        P("section", "dp", None, None), P("dp"), P("dp", None), P("dp", None), section, section,
        section, section, section, section, P("section", None), section, section, section,
    )
    return jax.shard_map(
        on_device,
        mesh=mesh,
        in_specs=placed,
        out_specs=(
            P("section", "dp", None, None), section, section, section, section, section, section,
            P("section", None), section, section, section,
        ),
        check_vma=False,
    )
```

```python
import functools
import math

import jax
import jax.numpy as jnp
from jax import lax
from jax.experimental import pallas as pl
from jax.experimental.pallas import tpu as pltpu
from jax.sharding import PartitionSpec as P

GRID = 16
SPAN = 32
KEY_BLOCK = 256
ROW_BLOCK = 256
FF_BLOCK = 768
PAIRS = 2
HALF = 64
PAIR = 128

epsilon = 1e-05
masked = -1e30
score_scale = 0.125
VMEM_LIMIT = 40 * 1024 * 1024

f32 = jnp.float32
bf16 = jnp.bfloat16

dot_nn = lambda a, b: lax.dot_general(a, b, (((1,), (0,)), ((), ())), preferred_element_type=f32)
dot_nt = lambda a, b: lax.dot_general(a, b, (((1,), (1,)), ((), ())), preferred_element_type=f32)
dot_tn = lambda a, b: lax.dot_general(a, b, (((0,), (0,)), ((), ())), preferred_element_type=f32)


def params_for(axes):
    return pltpu.CompilerParams(
        dimension_semantics=("arbitrary",) * axes, vmem_limit_bytes=VMEM_LIMIT
    )


ANY = pl.BlockSpec(memory_space=pl.ANY)


def like(a):
    return jax.ShapeDtypeStruct(a.shape, a.dtype)


RESIDENT = pl.BlockSpec(memory_space=pltpu.VMEM)


def fixed(shape):
    return pl.BlockSpec(shape, lambda i, sp: (0,) * len(shape), pipeline_mode=pl.Buffered(1))


def this_step(count):
    return pl.ds(pl.multiple_of(pl.program_id(0) * count, count), count)


def stacked(rows, cols):
    return pl.BlockSpec((1, rows, cols), lambda i, sp: (sp[0], i, 0))


def plain(rows, cols):
    return pl.BlockSpec((rows, cols), lambda i, sp: (i, 0))


class Row:
    def __init__(self, table, base):
        self.table = table
        self.base = base

    def __getitem__(self, at):
        return self.table[self.base + at]


def shifted(spec, base):
    if spec.index_map is None:
        return spec
    inner = spec.index_map
    return pl.BlockSpec(
        spec.block_shape, lambda i, sp: inner(i, Row(sp, base)), pipeline_mode=spec.pipeline_mode
    )


def call(body, sp, grid, ins, outs, aliased, scratch=(), us=10):
    held = lambda a, s: pltpu.with_memory_space_constraint(a, pltpu.HBM) if a.ndim == 3 else a
    operands = [held(a, s) for a, s in ins] + [held(a, s) for a, s in aliased]
    table, base = sp
    in_specs = [shifted(s, base) for _, s in ins] + [ANY] * len(aliased)
    out_shape = [pltpu.HBM(a.shape, a.dtype) for a, _ in aliased] + [s for s, _ in outs]
    out_specs = [shifted(s, base) for _, s in aliased] + [shifted(s, base) for _, s in outs]
    kept = len(aliased)
    first = len(ins)

    def run(sp_ref, *refs):
        body(Row(sp_ref, base), *refs[:first], *refs[first + kept :])

    return pl.pallas_call(
        run,
        grid_spec=pltpu.PrefetchScalarGridSpec(
            num_scalar_prefetch=1,
            grid=grid,
            in_specs=in_specs,
            out_specs=out_specs,
            scratch_shapes=list(scratch),
        ),
        out_shape=out_shape,
        input_output_aliases={1 + first + j: j for j in range(kept)},
        compiler_params=params_for(len(grid)),
        cost_estimate=pl.CostEstimate(
            flops=us * 1_000_000_000, bytes_accessed=us * 1_000_000, transcendentals=0
        ),
    )(table, *operands)


def unwritten(shapes):
    return pl.pallas_call(
        lambda *refs: None, out_shape=[pltpu.HBM(s.shape, s.dtype) for s in shapes], out_specs=[ANY] * len(shapes),
        compiler_params=pltpu.CompilerParams(vmem_limit_bytes=2 * 1024 * 1024),
    )()


def in_vmem(arrays):
    def body(*refs):
        count = len(arrays)
        copies = [
            pltpu.make_async_copy(refs[j], refs[count + j], refs[-1].at[j]) for j in range(count)
        ]
        for copy in copies:
            copy.start()
        for copy in copies:
            copy.wait()

    return pl.pallas_call(
        body,
        out_shape=[pltpu.VMEM(a.shape, a.dtype) for a in arrays],
        in_specs=[ANY] * len(arrays),
        out_specs=[RESIDENT] * len(arrays),
        scratch_shapes=[pltpu.SemaphoreType.DMA((len(arrays),))],
        compiler_params=pltpu.CompilerParams(vmem_limit_bytes=2 * 1024 * 1024),
    )(*[pltpu.with_memory_space_constraint(a, pltpu.HBM) for a in arrays])


def at_window(rows, cols):
    return pl.BlockSpec((1, rows, cols), lambda i, sp: (sp[0], 0, i))


def whole_window(rows, cols):
    return pl.BlockSpec((1, rows, cols), lambda i, sp: (sp[0], 0, 0))


def as_given(rows, cols):
    return pl.BlockSpec((1, rows, cols), lambda i, sp: (sp[5], 0, 0))


def columns(rows, cols, begin=0):
    return pl.BlockSpec((rows, cols), lambda i, sp: (0, begin + i))


def qkv_body(sp, x_ref, got_ref, w_ref, b_ref, x_out, q_ref, kv_ref, fresh_ref):
    width = x_ref.shape[2]
    cols = q_ref.shape[2]
    x = jnp.where(sp[4] == 1, got_ref[...], x_ref[0])

    @pl.when(pl.program_id(0) == 0)
    def _():
        x_out[0] = x

    def part(j):
        at = pl.ds(pl.multiple_of(j * width + pl.program_id(0) * cols, cols), cols)
        return dot_nn(x, w_ref[:, at]) + b_ref[:, at]

    q_ref[0] = (part(0).astype(bf16) * score_scale).astype(bf16)
    k = part(1).astype(bf16)
    v = part(2).astype(bf16)
    for begin in range(0, cols, PAIR):
        for value, at in ((k, 0), (v, PAIR)):
            to = slice(2 * begin + at, 2 * begin + at + PAIR)
            kv_ref[0, :, to] = value[:, begin : begin + PAIR]
            fresh_ref[:, to] = value[:, begin : begin + PAIR]


def qkv_call(sp, own_all, got, weight, bias, x_all, q_all, kv_all):
    rows, width = x_all.shape[1], x_all.shape[2]
    cols = PAIRS * PAIR
    return call(
        qkv_body,
        sp,
        (width // cols,),
        [
            (own_all, as_given(rows, width)), (got, fixed(got.shape)), (weight, RESIDENT),
            (bias, fixed(bias.shape)),
        ],
        [(jax.ShapeDtypeStruct((rows, 2 * width), bf16), columns(rows, 2 * cols))],
        [
            (x_all, whole_window(rows, width)), (q_all, at_window(rows, cols)),
            (kv_all, at_window(rows, 2 * cols)),
        ],
        us=4,
    )


def low_half(shape):
    return lax.broadcasted_iota(jnp.int32, shape, 1) < HALF


def split_three(value):
    place = lax.broadcasted_iota(jnp.int32, value.shape, 1) % HALF
    high = value.astype(bf16).astype(f32)
    rest = value - high
    mid = rest.astype(bf16).astype(f32)
    last = rest - mid
    out = jnp.where(place == 0, high, jnp.where(place == 1, mid, jnp.where(place == 2, last, 0.0)))
    return out.astype(bf16)


def in_order(first, own, peer):
    return jnp.concatenate([jnp.where(first, own, peer), jnp.where(first, peer, own)], axis=0)


def attend_body(
    sp, q_ref, own_ref, peer_ref, side_ref, hot_ref, m_ref, a_ref, rest_ref, lse_ref, kept_ref
):
    rows = q_ref.shape[1]
    first = sp[2] == 0
    kept_ref[0] = peer_ref[...]

    def variant(keys):
        low = low_half((rows, PAIR))
        key_low = low_half((keys, PAIR))
        one = jnp.ones((keys, PAIR), bf16)
        side = side_ref[0]
        hot = hot_ref[0, :keys, :]
        for n in range(PAIRS):
            cols = slice(n * PAIR, (n + 1) * PAIR)
            kv = slice(2 * n * PAIR, 2 * (n + 1) * PAIR)
            both = in_order(first, own_ref[:, kv], peer_ref[:, kv])[:keys]
            k, v = both[:, :PAIR], both[:, PAIR:]
            ks = dot_nn(hot, m_ref[:, cols]).astype(bf16)
            q = q_ref[0, :, cols]
            outs = []
            peaks = []
            for head in (0, 1):
                pick = (lambda m, x, y: jnp.where(m, x, y)) if head == 0 else (
                    lambda m, x, y: jnp.where(m, y, x)
                )
                s = dot_nt(pick(low, q, side), pick(key_low, k, ks))
                peak = jnp.max(s, axis=1, keepdims=True)
                e = jnp.exp(s - peak).astype(bf16)
                outs.append(dot_nn(e, pick(key_low, v, one)))
                peaks.append(peak)
            top = jnp.where(low, outs[0], outs[1])
            total = pltpu.roll(jnp.where(low, outs[1], outs[0]), HALF, 1)
            mixed = top / total
            mixed_low = mixed.astype(bf16)
            a_ref[0, :, cols] = mixed_low
            rest_ref[0, :, cols] = (mixed - mixed_low.astype(f32)).astype(bf16)
            lse = jnp.where(low, peaks[0], peaks[1]) + jnp.log(total)
            lse_ref[0, :, cols] = split_three(-lse)

    for blocks in range(1, 2 * rows // KEY_BLOCK + 1):
        pl.when(sp[1] == blocks)(functools.partial(variant, blocks * KEY_BLOCK))


def attend_call(sp, q_all, kv_own, kv_peer, side_all, hot_all, matrix, bufs):
    rows, width = q_all.shape[1], q_all.shape[2]
    cols = PAIRS * PAIR
    part = at_window(rows, cols)
    return call(
        attend_body,
        sp,
        (width // cols,),
        [
            (q_all, part),
            (kv_own, columns(rows, 2 * cols)),
            (kv_peer, columns(rows, 2 * cols)),
            (side_all, as_given(rows, PAIR)),
            (hot_all, as_given(2 * rows, PAIR)),
            (matrix, columns(PAIR, cols)),
        ],
        [],
        [(b, part) for b in bufs[:-1]] + [(bufs[-1], at_window(rows, 2 * cols))],
        us=14,
    )


def gelu_both(x):
    cdf = 0.5 + 0.5 * lax.erf(x * math.sqrt(0.5))
    bell = jnp.exp(x * x * -0.5)
    return x * cdf, cdf + x * bell * (1.0 / math.sqrt(2.0 * math.pi))


def centered(u):
    c = u - jnp.mean(u, axis=1, keepdims=True)
    r = lax.rsqrt(jnp.mean(c * c, axis=1, keepdims=True) + epsilon)
    return c * r, r


class Moves:
    def __init__(self, sems):
        self.sems = sems
        self.used = 0
        self.out = []

    def start(self, source, target):
        copy = pltpu.make_async_copy(source, target, self.sems.at[self.used])
        self.used += 1
        copy.start()
        return copy

    def write(self, source, target):
        self.out.append(self.start(source, target))

    def finish(self):
        for copy in self.out:
            copy.wait()


def chunks(width):
    return [slice(c, c + FF_BLOCK) for c in range(0, width, FF_BLOCK)]


def dense_body(
    sp, a_ref, x_ref, wo_ref, w1_ref, w2_ref, gain_ref, bias_ref, eb_ref,
    n1_hbm, h1_hbm, g_hbm, d_hbm, n2_hbm, r_hbm, fresh_ref,
    n1_ref, h1_ref, g_ref, d_ref, n2_ref, r_ref, sems,
):
    w = sp[0]
    moves = Moves(sems)
    parts = chunks(w1_ref.shape[1])
    u1 = dot_nn(a_ref[0], wo_ref[...]) + bias_ref[2:3, :] + x_ref[0].astype(f32)
    n1, r1 = centered(u1)
    h1 = n1 * gain_ref[0:1, :] + bias_ref[3:4, :]
    h1_low = h1.astype(bf16)
    n1_ref[...] = n1.astype(bf16)
    h1_ref[...] = h1_low
    moves.write(n1_ref, n1_hbm.at[w])
    moves.write(h1_ref, h1_hbm.at[w])
    u2 = h1 + bias_ref[4:5, :]
    for c in parts:
        g, d = gelu_both(dot_nn(h1_low, w1_ref[:, c]) + eb_ref[:, c])
        g = g.astype(bf16)
        g_ref[:, c] = g
        d_ref[:, c] = d.astype(bf16)
        moves.write(g_ref.at[:, c], g_hbm.at[w, :, c])
        moves.write(d_ref.at[:, c], d_hbm.at[w, :, c])
        u2 = u2 + dot_nt(g, w2_ref[:, c])
    n2, r2 = centered(u2)
    n2_ref[...] = n2.astype(bf16)
    moves.write(n2_ref, n2_hbm.at[w])
    r_ref[...] = jnp.where(low_half(r_ref.shape), r1, r2)
    moves.write(r_ref, r_hbm.at[w])
    fresh_ref[...] = (n2 * gain_ref[1:2, :] + bias_ref[5:6, :]).astype(bf16)
    moves.finish()


def dense_call(sp, a_all, x_all, wo, w1, w2, gains, biases, eb, bufs):
    rows, width = a_all.shape[1], a_all.shape[2]
    hidden = w1.shape[1]
    row = whole_window(rows, width)
    vmem = lambda *shape: pltpu.VMEM(shape, bf16)
    return call(
        dense_body,
        sp,
        (1,),
        [
            (a_all, row), (x_all, row), (wo, RESIDENT), (w1, RESIDENT), (w2, RESIDENT), (gains, fixed(gains.shape)),
            (biases, fixed(biases.shape)), (eb, fixed(eb.shape)),
        ],
        [(jax.ShapeDtypeStruct((rows, width), bf16), pl.BlockSpec((rows, width), lambda i, sp: (0, 0)))],
        [(b, ANY) for b in bufs],
        [
            vmem(rows, width), vmem(rows, width), vmem(rows, hidden), vmem(rows, hidden), vmem(rows, width),
            pltpu.VMEM((rows, PAIR), f32), pltpu.SemaphoreType.DMA((4 + 2 * (hidden // FF_BLOCK),)),
        ],
        us=10,
    )


def column_sum(v):
    return jnp.sum(v, axis=0, keepdims=True)


def norm_back(dy, n, r, gain):
    dn = dy * gain
    return r * (dn - jnp.mean(dn, axis=1, keepdims=True) - n * jnp.mean(dn * n, axis=1, keepdims=True))


def dense_back_body(
    sp, dy_ref, got_ref, n2_ref, r_ref, gain_ref, sel_ref, wo_ref, w1_ref, w2_ref, d_hbm, n1_hbm, a_hbm,
    rest_hbm, db2_hbm, df_hbm, db1_hbm, st_ref, se_ref, do_ref, dd_ref,
    d_ref, n1_ref, a_ref, rest_ref, db2_ref, df_ref, db1_ref, sems,
):
    w = sp[0]
    width = dy_ref.shape[2]
    moves = Moves(sems)
    parts = chunks(w1_ref.shape[1])
    loads = [moves.start(d_hbm.at[w, :, c], d_ref.at[:, c]) for c in parts]
    last = [
        moves.start(n1_hbm.at[w], n1_ref), moves.start(a_hbm.at[w], a_ref),
        moves.start(rest_hbm.at[w], rest_ref),
    ]
    r = r_ref[0]
    dy = jnp.where(sp[4] == 1, dy_ref[0], got_ref[...]).astype(f32)
    n2 = n2_ref[0].astype(f32)
    du2 = norm_back(dy, n2, r[:, HALF : HALF + 1], gain_ref[1:2, :])
    db2 = du2.astype(bf16)
    db2_ref[...] = db2
    moves.write(db2_ref, db2_hbm.at[w])
    st_ref[0, 2:3, :] = column_sum(du2)
    st_ref[0, 3:4, :] = column_sum(dy)
    st_ref[0, 5:6, :] = column_sum(dy * n2)
    st_ref[0, 6:8, :] = jnp.zeros((2, width), f32)
    dh1 = du2
    for c, load in zip(parts, loads):
        load.wait()
        df = dot_nn(db2, w2_ref[:, c]) * d_ref[:, c].astype(f32)
        se_ref[0, :, c] = column_sum(df)
        df = df.astype(bf16)
        df_ref[:, c] = df
        moves.write(df_ref.at[:, c], df_hbm.at[w, :, c])
        dh1 = dh1 + dot_nt(df, w1_ref[:, c])
    for load in last:
        load.wait()
    n1 = n1_ref[...].astype(f32)
    du1 = norm_back(dh1, n1, r[:, 0:1], gain_ref[0:1, :])
    db1 = du1.astype(bf16)
    db1_ref[...] = db1
    moves.write(db1_ref, db1_hbm.at[w])
    st_ref[0, 0:1, :] = column_sum(du1)
    st_ref[0, 1:2, :] = column_sum(dh1)
    st_ref[0, 4:5, :] = column_sum(dh1 * n1)
    do = dot_nt(db1, wo_ref[...]).astype(bf16)
    do_ref[...] = do
    mixed = do.astype(f32) * (a_ref[...].astype(f32) + rest_ref[...].astype(f32))
    high = mixed.astype(bf16)
    low = (mixed - high.astype(f32)).astype(bf16)
    for begin in range(0, width, PAIR):
        cols = slice(begin, begin + PAIR)
        inner = dot_nn(high[:, cols], sel_ref[...]) + dot_nn(low[:, cols], sel_ref[...])
        dd_ref[:, cols] = split_three(-inner)
    moves.finish()


def dense_back_call(
    sp, dy_all, got, n2_all, r_all, d_all, n1_all, a_all, rest_all, wo, w1, w2, gains, sel, bufs
):
    rows, width = got.shape
    hidden = w1.shape[1]
    row = whole_window(rows, width)
    db2_all, df_all, db1_all, st_all, se_all = bufs
    flat = (jax.ShapeDtypeStruct((rows, width), bf16), pl.BlockSpec((rows, width), lambda i, sp: (0, 0)))
    vmem = lambda *shape: pltpu.VMEM(shape, bf16)
    return call(
        dense_back_body,
        sp,
        (1,),
        [
            (dy_all, as_given(rows, width)), (got, fixed(got.shape)), (n2_all, row), (r_all, whole_window(rows, PAIR)),
            (gains, fixed(gains.shape)), (sel, fixed(sel.shape)), (wo, RESIDENT), (w1, RESIDENT),
            (w2, RESIDENT),
        ]
        + [(b, ANY) for b in (d_all, n1_all, a_all, rest_all)],
        [flat, flat],
        [
            (db2_all, ANY), (df_all, ANY), (db1_all, ANY), (st_all, whole_window(8, width)),
            (se_all, whole_window(1, hidden)),
        ],
        [
            vmem(rows, hidden), vmem(rows, width), vmem(rows, width), vmem(rows, width), vmem(rows, width),
            vmem(rows, hidden), vmem(rows, width), pltpu.SemaphoreType.DMA((5 + 2 * (hidden // FF_BLOCK),)),
        ],
        us=10,
    )


def attend_back_body(
    sp, q_ref, own_ref, peer_ref, side_ref, hot_ref, m_ref, lse_ref, do_ref, dd_ref, turned_ref,
    cell_ref, dq_ref, keep_ref, send_ref,
):
    rows = q_ref.shape[1]
    total = 2 * rows
    first = sp[2] == 0

    def variant(blocks):
        keys = blocks * KEY_BLOCK
        low = low_half((rows, PAIR))
        key_low = low_half((keys, PAIR))
        block_low = low_half((KEY_BLOCK, PAIR))
        place = lax.broadcasted_iota(jnp.int32, (KEY_BLOCK, PAIR), 1)
        three = jnp.where(place % HALF < 3, 1.0, 0.0).astype(bf16)
        lone = [
            jnp.where(place < 3, 1.0, 0.0).astype(bf16),
            jnp.where((place >= HALF) & (place < HALF + 3), 1.0, 0.0).astype(bf16),
        ]
        side = side_ref[0]
        hot = hot_ref[0, :keys, :]
        for n in range(PAIRS):
            cols = slice(n * PAIR, (n + 1) * PAIR)
            kv = slice(2 * n * PAIR, 2 * (n + 1) * PAIR)
            both = in_order(first, own_ref[0, :, kv], peer_ref[0, :, kv])[:keys]
            k, v = both[:, :PAIR], both[:, PAIR:]
            ks = dot_nn(hot, m_ref[:, cols]).astype(bf16)
            kt = k.T
            q = q_ref[0, :, cols]
            do = do_ref[:, cols]
            dd = dd_ref[:, cols]
            lse = lse_ref[0, :, cols]
            kc = (jnp.where(key_low, k, ks), jnp.where(key_low, ks, k))
            qc = (jnp.where(low, q, side), jnp.where(low, side, q))
            qe = tuple(jnp.concatenate([c, lse], axis=1) for c in qc)
            dc = (jnp.where(low, do, dd), jnp.where(low, dd, do))
            dq = [None, None]
            dks = []
            dvs = []
            gs = []
            for b in range(blocks):
                at = slice(b * KEY_BLOCK, (b + 1) * KEY_BLOCK)
                vb = v[at]
                vc = (jnp.where(block_low, vb, three), jnp.where(block_low, three, vb))
                part_v = []
                part_k = []
                for head in (0, 1):
                    kb = jnp.concatenate([kc[head][at], lone[head]], axis=1)
                    p = jnp.exp(dot_nt(kb, qe[head]))
                    dp = dot_nt(vc[head], dc[head])
                    ds = (p * dp).astype(bf16)
                    part_v.append(dot_nn(p.astype(bf16), do))
                    part_k.append(dot_nn(ds, qc[head]))
                    part = dot_nn(kt[head * HALF : (head + 1) * HALF, at], ds)
                    dq[head] = part if dq[head] is None else dq[head] + part
                dvs.append(jnp.where(block_low, part_v[0], part_v[1]).astype(bf16))
                dks.append(jnp.where(block_low, part_k[0], part_k[1]).astype(bf16))
                gs.append(jnp.where(block_low, part_k[1], part_k[0]).astype(bf16))
            dq_ref[:, cols] = (jnp.concatenate(dq, axis=0).T * score_scale).astype(bf16)
            cell_ref[0, :, cols] = dot_nn(turned_ref[0, :, :keys], jnp.concatenate(gs, axis=0))
            if keys < total:
                zero = [jnp.zeros((total - keys, PAIR), bf16)]
                dks = dks + zero
                dvs = dvs + zero
            grads = jnp.concatenate([jnp.concatenate(dks, axis=0), jnp.concatenate(dvs, axis=0)], axis=1)
            keep_ref[:, kv] = jnp.where(first, grads[:rows], grads[rows:])
            send_ref[:, kv] = jnp.where(first, grads[rows:], grads[:rows])

    for blocks in range(1, total // KEY_BLOCK + 1):
        pl.when(sp[1] == blocks)(functools.partial(variant, blocks))


def attend_back_call(
    sp, q_all, kv_all, peer_all, side_all, hot_all, matrix, lse_all, do, dd, turned_all, cell_all
):
    rows, width = q_all.shape[1], q_all.shape[2]
    cols = PAIRS * PAIR
    part = at_window(rows, cols)
    kv = at_window(rows, 2 * cols)
    flat = columns(rows, cols)
    flat_kv = columns(rows, 2 * cols)
    out_kv = jax.ShapeDtypeStruct((rows, 2 * width), bf16)
    return call(
        attend_back_body,
        sp,
        (width // cols,),
        [
            (q_all, part),
            (kv_all, kv),
            (peer_all, kv),
            (side_all, as_given(rows, PAIR)),
            (hot_all, as_given(2 * rows, PAIR)),
            (matrix, columns(PAIR, cols)),
            (lse_all, part),
            (do, flat),
            (dd, flat),
            (turned_all, as_given(HALF, 2 * rows)),
        ],
        [(jax.ShapeDtypeStruct((rows, width), bf16), flat), (out_kv, flat_kv), (out_kv, flat_kv)],
        [(cell_all, at_window(HALF, cols))],
        us=20,
    )


def input_back_body(
    sp, dq_ref, own_ref, got_ref, db1_ref, w_ref, dj_ref, sj_ref, fresh_ref, total
):
    step = pl.program_id(0)
    dq = dq_ref[...]
    cols = dq.shape[1]
    both = own_ref[...].astype(f32) + got_ref[...].astype(f32)
    part = lambda at: jnp.concatenate(
        [both[:, p + at : p + at + PAIR] for p in range(0, 2 * cols, 2 * PAIR)], axis=1
    )
    dk = part(0).astype(bf16)
    dv32 = part(PAIR)
    dv = dv32.astype(bf16)
    dj_ref[0, :, :cols] = dq
    dj_ref[0, :, cols : 2 * cols] = dk
    dj_ref[0, :, 2 * cols :] = dv
    sj_ref[0] = jnp.concatenate(
        [column_sum(dq.astype(f32)), column_sum(dv32), jnp.zeros((6, cols), f32)], axis=0
    )
    width = w_ref.shape[0]
    dx = None
    for j, value in enumerate((dq, dk, dv)):
        at = pl.ds(pl.multiple_of(j * width + step * cols, cols), cols)
        term = dot_nt(value, w_ref[:, at])
        dx = term if dx is None else dx + term

    @pl.when(step == 0)
    def _():
        total[...] = dx + db1_ref[0].astype(f32)

    @pl.when(step > 0)
    def _():
        total[...] += dx

    @pl.when(step == pl.num_programs(0) - 1)
    def _():
        fresh_ref[...] = total[...].astype(bf16)


def input_back_call(sp, dq, own, got, db1_all, weight, dj_all, sj_all):
    rows, width = dq.shape
    cols = PAIRS * PAIR
    steps = width // cols
    return call(
        input_back_body,
        sp,
        (steps,),
        [
            (dq, columns(rows, cols)), (own, columns(rows, 2 * cols)), (got, columns(rows, 2 * cols)),
            (db1_all, whole_window(rows, width)), (weight, RESIDENT),
        ],
        [(jax.ShapeDtypeStruct((rows, width), bf16), pl.BlockSpec((rows, width), lambda i, sp: (0, 0)))],
        [
            (dj_all, at_window(rows, 3 * cols)), (sj_all, at_window(8, cols)),
        ],
        [pltpu.VMEM((rows, width), f32)],
        us=4,
    )


def weight_body(splits, based, sp, *refs):
    count = len(splits)
    lefts, rights = refs[:count], refs[count : 2 * count]
    base_refs = refs[2 * count : 2 * count + 2] if based else ()
    give_ref, keep_ref = refs[-2:]
    step = pl.program_id(0)
    windows, rows, width = lefts[0].shape
    half = width // 2
    first = sp[2] == 0

    for (begin, end), left, right in zip(splits, lefts, rights):

        @pl.when((step >= begin) & (step < end))
        def _(left=left, right=right):
            flat = left[...].reshape(windows * rows, width)
            out = dot_tn(flat, right[...].reshape(windows * rows, right.shape[2]))
            give = jnp.where(first, out[half:], out[:half])
            keep = jnp.where(first, out[:half], out[half:])
            if based:
                give = give + base_refs[0][...].astype(f32)
                keep = keep + base_refs[1][...].astype(f32)
            give_ref[...] = give.astype(bf16)
            keep_ref[...] = keep.astype(bf16)


def weight_call(sp, at, windows, pairs, base=()):
    rows, width = pairs[0][0].shape[1:]
    splits = []
    begin = 0
    for _, right in pairs:
        splits.append((begin, begin + right.shape[2] // FF_BLOCK))
        begin = splits[-1][1]

    def left_spec():
        return pl.BlockSpec(
            (windows, rows, width), lambda i, sp: (at, 0, 0), pipeline_mode=pl.Buffered(1)
        )

    def right_spec(begin, end):
        return pl.BlockSpec(
            (windows, rows, FF_BLOCK), lambda i, sp: (at, 0, jnp.clip(i - begin, 0, end - begin - 1))
        )

    half = columns(width // 2, FF_BLOCK)
    shape = jax.ShapeDtypeStruct((width // 2, begin * FF_BLOCK), bf16)
    return call(
        functools.partial(weight_body, tuple(splits), bool(base)),
        sp,
        (begin,),
        [(left, left_spec()) for left, _ in pairs]
        + [(right, right_spec(*split)) for (_, right), split in zip(pairs, splits)]
        + [(b, half) for b in base],
        [(shape, half), (shape, half)],
        [],
        us=5 + 3 * windows,
    )


def spread_body(moves, sp, mine_ref, got_ref, *out_refs):
    half = pl.num_programs(0) // 2
    mine = (pl.program_id(0) // half) == sp[2]
    value = jnp.where(mine, mine_ref[...], got_ref[...]).astype(f32)
    for (out, to), begin, count in moves:
        out_refs[out][:, to : to + count] = value[:, begin : begin + count]


def spread_call(sp, mine, got, widths, moves):
    half, cols = mine.shape
    block = half // 4
    turn = lambda i, sp, core: jnp.where(i // 4 == core, i % 4, jnp.where(core == 0, 3, 0))
    return call(
        functools.partial(spread_body, moves),
        sp,
        (8,),
        [
            (mine, pl.BlockSpec((block, cols), lambda i, sp: (turn(i, sp, sp[2]), 0))),
            (got, pl.BlockSpec((block, cols), lambda i, sp: (turn(i, sp, 1 - sp[2]), 0))),
        ],
        [
            (jax.ShapeDtypeStruct((2 * half, w), f32), pl.BlockSpec((block, w), lambda i, sp: (i, 0)))
            for w in widths
        ],
        [],
        us=5,
    )


def bucket_maps(position_cells, counts):
    key = jnp.arange(HALF, dtype=jnp.int32)[:, None]
    query = jnp.arange(HALF, dtype=jnp.int32)[None, :]
    begins = (0, position_cells, position_cells + GRID, HALF)
    bucket = jnp.full((HALF, HALF), -1, jnp.int32)
    base = 0
    for j, offset in enumerate((counts[0] // 2, GRID - 1, GRID - 1)):
        inside = (key >= begins[j]) & (key < begins[j + 1]) & (query >= begins[j]) & (query < begins[j + 1])
        ids = jnp.clip(query - key, -offset, counts[j] - 1 - offset) + offset + base
        bucket = jnp.where(inside, ids, bucket)
        base += counts[j]
    return bucket[:, :, None] == jnp.arange(base, dtype=jnp.int32)


def cell_matrix(tables, maps, position_cells):
    whole = jnp.concatenate(tables, axis=0)
    heads = whole.shape[1]
    whole = whole.reshape(-1, heads // 2, 2)[:, :, ::-1].reshape(-1, heads)
    m = jnp.einsum("bh,xcb->xhc", whole, maps.astype(bf16), preferred_element_type=f32)
    m = m.reshape(HALF, heads * HALF).astype(bf16)
    lane = jnp.arange(heads * HALF, dtype=jnp.int32) % HALF
    dead = jnp.where(lane < position_cells, masked, 0.0).astype(bf16)[None]
    return jnp.concatenate([m, dead, jnp.zeros((HALF - 1, heads * HALF), bf16)], axis=0)


def table_grads(cells, maps, counts):
    heads = cells.shape[1] // HALF
    whole = jnp.einsum(
        "xcb,xhc->bh", maps.astype(f32), cells.reshape(HALF, heads, HALF), precision=lax.Precision.HIGHEST
    )
    whole = whole.reshape(-1, heads // 2, 2)[:, :, ::-1].reshape(-1, heads)
    a, b = counts[0], counts[0] + counts[1]
    return [whole[:a], whole[a:b], whole[b:]]


def after(value, earlier):
    return lax.optimization_barrier((value, earlier))[0]


class Ring:
    def __init__(self, count):
        self.count = count
        self.index = lax.axis_index("dp")
        bits = list(range(1, count.bit_length() - 1))
        turned = bits[:2][::-1] + bits[2:]
        self.mixed = list(zip(bits, turned))
        self.plain = list(zip(bits, bits))

    def bit(self, step):
        even, odd = step
        return jnp.where(self.index % 2 == 0, (self.index >> even) & 1, (self.index >> odd) & 1)

    def send(self, a, step):
        even, odd = step
        pairs = [(i, i ^ (1 << (even if i % 2 == 0 else odd))) for i in range(self.count)]
        return lax.ppermute(a, "dp", pairs)

    def swap(self, a):
        return lax.ppermute(a, "dp", [(i, i ^ 1) for i in range(self.count)])

    def halve(self, part, step):
        half = part.shape[0] // 2
        bit = self.bit(step)
        keep = lax.dynamic_slice_in_dim(part, bit * half, half, 0)
        give = lax.dynamic_slice_in_dim(part, (1 - bit) * half, half, 0)
        return keep, self.send(give, step)

    def join(self, part, got, step):
        first = self.bit(step) == 0
        return jnp.concatenate([jnp.where(first, part, got), jnp.where(first, got, part)], axis=0)

    def stages(self, give, keep, steps):
        got = self.swap(give)
        order = yield
        part = keep + order(got)
        for step in steps:
            keep, got = self.halve(part, step)
            order = yield part
            part = keep + order(got)
        for step in steps[::-1]:
            got = self.send(part, step)
            order = yield part
            part = self.join(part, order(got), step)
        got = self.swap(part)
        order = yield part
        self.result = (part, order(got))
        yield self.result[1]

    def totals(self, part):
        for bit in range(self.count.bit_length() - 1):
            got = lax.ppermute(part, "dp", [(i, i ^ (1 << bit)) for i in range(self.count)])
            order = yield part
            part = part + order(got)
        yield part


SLOTS = (
    ("F", 0, None),
    ("F", 1, 0),
    ("B", None, 0),
    ("F", 2, 1),
    ("B", 0, 1),
    ("F", 3, 2),
    ("B", 1, 2),
    ("F", None, 3),
    ("B", 2, 3),
    ("B", 3, None),
)


def on_device(
    boundary, doc_lengths, horizontal, vertical, attention_in, attention_out, expand_weight,
    contract_weight, norm_gains, bias_rows, expand_bias, position_table, horizontal_table,
    vertical_table,
):
    section = lax.axis_index("section")
    dp_count = lax.axis_size("dp")
    core = lax.axis_index("dp") % 2
    swap = [(i, i ^ 1) for i in range(dp_count)]
    exchange = lambda a: lax.ppermute(a, "dp", swap)

    own = boundary[0]
    micro, slots, width = own.shape
    rows = slots // 2
    windows = 2 * micro
    hidden = expand_weight.shape[2]
    heads = position_table.shape[2]
    pairs = heads // 2
    w_in, w_out, w1, w2 = in_vmem([attention_in[0], attention_out[0], expand_weight[0], contract_weight[0]])
    gains = norm_gains[0].astype(f32)
    biases = bias_rows[0].astype(f32)
    eb = expand_bias.astype(f32)
    in_bias = jnp.concatenate([biases[0], jnp.zeros_like(biases[0]), biases[1]])[None]
    tables = (position_table[0], horizontal_table[0], vertical_table[0])
    counts = tuple(t.shape[0] for t in tables)
    position_cells = slots // SPAN
    maps = bucket_maps(position_cells, counts)
    ring = Ring(dp_count)

    def both(mine, theirs):
        return jnp.concatenate(
            [jnp.where(core == 0, mine, theirs), jnp.where(core == 0, theirs, mine)], axis=0
        )

    halves = own.reshape(micro, 2, rows, width)
    own_half = jnp.where(core == 0, halves[:, 0], halves[:, 1])
    other_half = jnp.where(core == 0, halves[:, 1], halves[:, 0])
    own_all = both(own_half, exchange(other_half))
    places = jnp.concatenate(
        [horizontal, vertical, jnp.broadcast_to(doc_lengths[:, None], (micro, PAIR))], axis=1
    )
    places = both(places, exchange(places))
    across_cell = places[:, :slots] // SPAN
    down_cell = places[:, slots : 2 * slots] // SPAN
    lengths = places[:, 2 * slots]
    ids = jnp.arange(slots, dtype=jnp.int32)
    position_cell = jnp.broadcast_to((ids // SPAN)[None], (windows, slots))

    def hot_of(cells, lanes, axis):
        p, a, d = (jnp.expand_dims(c, axis) for c in cells)
        lanes = jnp.expand_dims(lanes, (0, 3 - axis))
        return (lanes == p) | (lanes == a + position_cells) | (lanes == d + position_cells + GRID)

    cells = (position_cell, across_cell, down_cell)
    cell_ids = jnp.arange(PAIR, dtype=jnp.int32)
    turned_all = hot_of(cells, cell_ids[:HALF], 1).astype(bf16)
    dead = (ids[None, :] >= lengths[:, None])[:, :, None] & (cell_ids == HALF)
    hot_all = (hot_of(cells, cell_ids, 2) | dead).astype(bf16)
    take = lambda c: jnp.where(core == 0, c[:, :rows], c[:, rows:])
    side_all = hot_of(tuple(take(c) for c in cells), cell_ids % HALF, 2).astype(bf16)
    matrix = cell_matrix(tables, maps, position_cells)

    sel = (cell_ids[:, None] // HALF != cell_ids[None, :] // HALF).astype(bf16)

    window_ids = jnp.arange(windows, dtype=jnp.int32)
    mine, theirs = lengths[:windows][:, None], lengths[:windows][None, :]
    ahead = (theirs > mine) | ((theirs == mine) & (window_ids[None, :] < window_ids[:, None]))
    rank = jnp.sum(ahead.astype(jnp.int32), axis=1)
    picks = jnp.stack(
        [jnp.array([windows if w is None else w for w in slots_of], jnp.int32) for slots_of in zip(*[s[1:] for s in SLOTS])]
    )
    infos = jnp.where(section == 0, picks[0], picks[1])
    hits = infos[:, None] == rank[None, :]
    given_ids = jnp.sum(jnp.where(hits, window_ids[None, :], 0), axis=1)
    given_lengths = jnp.sum(jnp.where(hits, lengths[None, :windows], 0), axis=1)
    infos = jnp.stack(
        [
            infos, (given_lengths + KEY_BLOCK - 1) // KEY_BLOCK, jnp.full_like(infos, core),
            given_lengths, jnp.full_like(infos, section), given_ids,
        ],
        axis=1,
    )
    facts = infos.shape[1]
    infos = infos.reshape(-1)

    widths = dict(
        x=width, q=width, kv=2 * width, a=width, rest=width, lse=width, peer=2 * width, n1=width, h1=width,
        g=hidden, d=hidden, n2=width, db2=width, df=hidden, db1=width, dj=3 * width,
    )
    shapes = {n: jax.ShapeDtypeStruct((windows + 1, rows, c), bf16) for n, c in widths.items()}
    shapes["r"] = jax.ShapeDtypeStruct((windows + 1, rows, PAIR), f32)
    shapes["st"] = shapes["sj"] = jax.ShapeDtypeStruct((windows + 1, 8, width), f32)
    shapes["se"] = jax.ShapeDtypeStruct((windows + 1, 1, hidden), f32)
    shapes["cell"] = jax.ShapeDtypeStruct((windows + 1, HALF, width), f32)
    st = dict(zip(shapes, unwritten(list(shapes.values()))))

    def forward(sp, s, got):
        x, q, kv, fresh = qkv_call(sp, own_all, got, w_in, in_bias, s["x"], s["q"], s["kv"])
        s = dict(s, x=x, q=q, kv=kv)
        mixed = ("a", "rest", "lse", "peer")
        s.update(
            zip(mixed, attend_call(
                sp, q, fresh, exchange(fresh), side_all, hot_all, matrix, tuple(s[n] for n in mixed)
            ))
        )
        names = ("n1", "h1", "g", "d", "n2", "r")
        outs = dense_call(
            sp, s["a"], x, w_out, w1, w2, gains, biases, eb, tuple(s[n] for n in names)
        )
        s.update(zip(names, outs[:-1]))
        return s, outs[-1]

    def dense_back(sp, s, got):
        names = ("db2", "df", "db1", "st", "se")
        outs = dense_back_call(
            sp, own_all, got, s["n2"], s["r"], s["d"], s["n1"], s["a"], s["rest"], w_out, w1, w2, gains,
            sel, tuple(s[n] for n in names),
        )
        s = dict(s)
        s.update(zip(names, outs[:5]))
        return s, tuple(outs[5:])

    def attend_back_kernel(sp, s, grads):
        return attend_back_call(
            sp, s["q"], s["kv"], s["peer"], side_all, hot_all, matrix, s["lse"], *grads, turned_all,
            s["cell"],
        )

    def input_back(sp, s, dq, keep, got):
        dj, sj, fresh = input_back_call(sp, dq, keep, got, s["db1"], w_in, s["dj"], s["sj"])
        return dict(s, dj=dj, sj=sj), fresh

    def attend_back(sp, s, grads):
        cell, dq, keep, send = attend_back_kernel(sp, s, grads)
        return input_back(sp, dict(s, cell=cell), dq, keep, exchange(send))

    got = {}
    finals = {}
    grads_in = {}
    nothing = jnp.zeros((rows, width), bf16)

    for number, (kind, zero, one) in enumerate(SLOTS[:-1]):
        sp = (infos, number * facts)
        if kind == "F":
            st, out = forward(sp, st, got.pop(("F", one), nothing))
            if one is not None:
                finals[one] = out
            if zero is not None:
                got["F", zero] = lax.ppermute(out, "section", [(0, 1)])
        else:
            st, grads = dense_back(sp, st, got.pop(("B", zero), nothing))
            st, out = attend_back(sp, st, grads)
            if zero is not None:
                grads_in[zero] = out
            if one is not None:
                got["B", one] = lax.ppermute(out, "section", [(1, 0)])

    sp = (infos, (len(SLOTS) - 1) * facts)

    class Chain:
        def __init__(self, stages, count):
            self.stages = stages
            self.left = count
            next(stages)

        def advance(self, earlier):
            self.last = self.stages.send(lambda got: after(got, earlier))
            self.left -= 1
            return self.last

    def weight_sum(steps, give, keep):
        return give, Chain(ring.stages(give, keep, steps), 2 * len(steps) + 2)

    natural = [((0, 0), 0, hidden)]
    cols = PAIRS * PAIR
    moves = [
        ((0, j * width + i * cols), (3 * i + j) * cols, cols) for i in range(width // cols) for j in range(3)
    ] + [((1, 0), 3 * width, width)]

    others = windows - 1
    part_contract = weight_call(sp, 0, others, [(after(st["db2"], out), st["g"])])
    part_expand = weight_call(sp, 0, others, [(after(st["h1"], part_contract[0]), st["df"])])
    rows_in = after(got.pop(("B", SLOTS[-1][1])), part_expand[0])
    st, grads = dense_back(sp, st, rows_in)
    halves = weight_call(sp, others, 1, [(st["db2"], st["g"])], part_contract)
    given, contract = weight_sum(ring.mixed, *halves)
    halves = weight_call(sp, others, 1, [(after(st["h1"], given), st["df"])], part_expand)
    given, expand = weight_sum(ring.plain, *halves)
    done = contract.advance(given)
    grads = tuple(after(g, done) for g in grads)
    cell, dq, keep, send = attend_back_kernel(sp, st, grads)
    got = exchange(send)
    done = expand.advance(dq)
    done = contract.advance(done)
    got = after(got, done)
    st, grads_in[SLOTS[-1][1]] = input_back(sp, dict(st, cell=cell), dq, keep, got)
    halves = weight_call(sp, 0, windows, [(st["x"], st["dj"]), (st["a"], st["db1"])])
    given, attend = weight_sum(ring.mixed, *halves)
    done = contract.advance(given)

    later = lambda a: after(a, given)
    of_windows = lambda name: jnp.sum(later(st[name])[:windows], axis=0)
    small = [of_windows("sj")[0:2], of_windows("st")[0:6], of_windows("se")] + table_grads(
        of_windows("cell"), maps, counts
    )
    packed = jnp.concatenate([p.reshape(-1) for p in small])
    packed = jnp.pad(packed, (0, -packed.shape[0] % (8 * PAIR))).reshape(-1, PAIR)
    totals = Chain(ring.totals(packed), dp_count.bit_length() - 1)
    result = [jnp.where(section == 0, later(grads_in[w]), later(finals[w])) for w in range(windows)]
    result = jnp.stack(result)
    ranks = later(rank)
    ordered = [lax.dynamic_index_in_dim(result, ranks[w], 0, keepdims=False) for w in range(windows)]
    mine_first, mine_second = jnp.stack(ordered[:micro]), jnp.stack(ordered[micro:])
    keep_rows = jnp.where(core == 0, mine_first, mine_second)
    got_rows = exchange(jnp.where(core == 0, mine_second, mine_first))

    def assembled(got_rows):
        out_halves = jnp.stack(
            [jnp.where(core == 0, keep_rows, got_rows), jnp.where(core == 0, got_rows, keep_rows)], axis=1
        )
        return out_halves.reshape(1, micro, slots, width)

    done = expand.advance(done)
    chains = {"attend": attend, "contract": contract, "expand": expand, "totals": totals}
    kinds = {"contract": ([hidden], natural), "expand": ([hidden], natural), "attend": ([3 * width, width], moves)}
    outputs = {}
    waiting = []
    boundary_out = None
    while any(chain.left for chain in chains.values()):
        for name, chain in chains.items():
            if not chain.left:
                continue
            done = chain.advance(done)
            for other, (mine, theirs) in waiting:
                outputs[other] = spread_call(sp, after(mine, done), theirs, *kinds[other])
                done = outputs[other][0]
            waiting = [(name, ring.result)] if not chain.left and name in kinds else []
        if boundary_out is None and not totals.left:
            boundary_out = assembled(after(got_rows, done))
            done = boundary_out
    for other, halves in waiting:
        outputs[other] = spread_call(sp, *halves, *kinds[other])
    (g_contract,), (g_expand,), (g_in, g_out) = (outputs[n] for n in ("contract", "expand", "attend"))
    packed = totals.last.reshape(-1)
    pieces = []
    begin = 0
    for p in small:
        count = math.prod(p.shape)
        pieces.append(packed[begin : begin + count].reshape(p.shape))
        begin += count
    joined_sums, sums, wide, table_p, table_h, table_v = pieces
    grad_bias = jnp.concatenate([joined_sums, sums[0:4]], axis=0)
    grad_gain = sums[4:6]
    return (
        boundary_out, g_in[None], g_out[None], g_expand[None], g_contract[None], grad_gain[None],
        grad_bias[None], wide, table_p[None], table_h[None], table_v[None],
    )


def solution(mesh):
    section = P("section", None, None)
    placed = (
        P("section", "dp", None, None), P("dp"), P("dp", None), P("dp", None), section, section,
        section, section, section, section, P("section", None), section, section, section,
    )
    return jax.shard_map(
        on_device,
        mesh=mesh,
        in_specs=placed,
        out_specs=(
            P("section", "dp", None, None), section, section, section, section, section, section,
            P("section", None), section, section, section,
        ),
        check_vma=False,
    )
```

```python
import functools
import math

import jax
import jax.numpy as jnp
from jax import lax
from jax.experimental import pallas as pl
from jax.experimental.pallas import tpu as pltpu
from jax.sharding import PartitionSpec as P

GRID = 16
SPAN = 32
KEY_BLOCK = 256
ROW_BLOCK = 256
FF_BLOCK = 768
PAIRS = 2
HALF = 64
PAIR = 128

epsilon = 1e-05
masked = -1e30
score_scale = 0.125
VMEM_LIMIT = 40 * 1024 * 1024

f32 = jnp.float32
bf16 = jnp.bfloat16

dot_nn = lambda a, b: lax.dot_general(a, b, (((1,), (0,)), ((), ())), preferred_element_type=f32)
dot_nt = lambda a, b: lax.dot_general(a, b, (((1,), (1,)), ((), ())), preferred_element_type=f32)
dot_tn = lambda a, b: lax.dot_general(a, b, (((0,), (0,)), ((), ())), preferred_element_type=f32)


def params_for(axes):
    return pltpu.CompilerParams(
        dimension_semantics=("arbitrary",) * axes, vmem_limit_bytes=VMEM_LIMIT
    )


ANY = pl.BlockSpec(memory_space=pl.ANY)


def like(a):
    return jax.ShapeDtypeStruct(a.shape, a.dtype)


RESIDENT = pl.BlockSpec(memory_space=pltpu.VMEM)


def fixed(shape):
    return pl.BlockSpec(shape, lambda i, sp: (0,) * len(shape), pipeline_mode=pl.Buffered(1))


def this_step(count):
    return pl.ds(pl.multiple_of(pl.program_id(0) * count, count), count)


def stacked(rows, cols):
    return pl.BlockSpec((1, rows, cols), lambda i, sp: (sp[0], i, 0))


def plain(rows, cols):
    return pl.BlockSpec((rows, cols), lambda i, sp: (i, 0))


class Row:
    def __init__(self, table, base):
        self.table = table
        self.base = base

    def __getitem__(self, at):
        return self.table[self.base + at]


def shifted(spec, base):
    if spec.index_map is None:
        return spec
    inner = spec.index_map
    return pl.BlockSpec(
        spec.block_shape, lambda i, sp: inner(i, Row(sp, base)), pipeline_mode=spec.pipeline_mode
    )


def call(body, sp, grid, ins, outs, aliased, scratch=(), us=10):
    held = lambda a, s: pltpu.with_memory_space_constraint(a, pltpu.HBM) if a.ndim == 3 else a
    operands = [held(a, s) for a, s in ins] + [held(a, s) for a, s in aliased]
    table, base = sp
    in_specs = [shifted(s, base) for _, s in ins] + [ANY] * len(aliased)
    out_shape = [pltpu.HBM(a.shape, a.dtype) for a, _ in aliased] + [s for s, _ in outs]
    out_specs = [shifted(s, base) for _, s in aliased] + [shifted(s, base) for _, s in outs]
    kept = len(aliased)
    first = len(ins)

    def run(sp_ref, *refs):
        body(Row(sp_ref, base), *refs[:first], *refs[first + kept :])

    return pl.pallas_call(
        run,
        grid_spec=pltpu.PrefetchScalarGridSpec(
            num_scalar_prefetch=1,
            grid=grid,
            in_specs=in_specs,
            out_specs=out_specs,
            scratch_shapes=list(scratch),
        ),
        out_shape=out_shape,
        input_output_aliases={1 + first + j: j for j in range(kept)},
        compiler_params=params_for(len(grid)),
        cost_estimate=pl.CostEstimate(
            flops=us * 1_000_000_000, bytes_accessed=us * 1_000_000, transcendentals=0
        ),
    )(table, *operands)


def unwritten(shapes):
    return pl.pallas_call(
        lambda *refs: None, out_shape=[pltpu.HBM(s.shape, s.dtype) for s in shapes], out_specs=[ANY] * len(shapes),
        compiler_params=pltpu.CompilerParams(vmem_limit_bytes=2 * 1024 * 1024),
    )()


def in_vmem(arrays):
    def body(*refs):
        count = len(arrays)
        copies = [
            pltpu.make_async_copy(refs[j], refs[count + j], refs[-1].at[j]) for j in range(count)
        ]
        for copy in copies:
            copy.start()
        for copy in copies:
            copy.wait()

    return pl.pallas_call(
        body,
        out_shape=[pltpu.VMEM(a.shape, a.dtype) for a in arrays],
        in_specs=[ANY] * len(arrays),
        out_specs=[RESIDENT] * len(arrays),
        scratch_shapes=[pltpu.SemaphoreType.DMA((len(arrays),))],
        compiler_params=pltpu.CompilerParams(vmem_limit_bytes=2 * 1024 * 1024),
    )(*[pltpu.with_memory_space_constraint(a, pltpu.HBM) for a in arrays])


def at_window(rows, cols):
    return pl.BlockSpec((1, rows, cols), lambda i, sp: (sp[0], 0, i))


def whole_window(rows, cols):
    return pl.BlockSpec((1, rows, cols), lambda i, sp: (sp[0], 0, 0))


def as_given(rows, cols):
    return pl.BlockSpec((1, rows, cols), lambda i, sp: (sp[5], 0, 0))


def columns(rows, cols, begin=0):
    return pl.BlockSpec((rows, cols), lambda i, sp: (0, begin + i))


def qkv_body(sp, x_ref, got_ref, w_ref, b_ref, x_out, q_ref, kv_ref, fresh_ref):
    width = x_ref.shape[2]
    cols = q_ref.shape[2]
    x = jnp.where(sp[4] == 1, got_ref[...], x_ref[0])

    @pl.when(pl.program_id(0) == 0)
    def _():
        x_out[0] = x

    def part(j):
        at = pl.ds(pl.multiple_of(j * width + pl.program_id(0) * cols, cols), cols)
        return dot_nn(x, w_ref[:, at]) + b_ref[:, at]

    q_ref[0] = (part(0).astype(bf16) * score_scale).astype(bf16)
    k = part(1).astype(bf16)
    v = part(2).astype(bf16)
    for begin in range(0, cols, PAIR):
        for value, at in ((k, 0), (v, PAIR)):
            to = slice(2 * begin + at, 2 * begin + at + PAIR)
            kv_ref[0, :, to] = value[:, begin : begin + PAIR]
            fresh_ref[:, to] = value[:, begin : begin + PAIR]


def qkv_call(sp, own_all, got, weight, bias, x_all, q_all, kv_all):
    rows, width = x_all.shape[1], x_all.shape[2]
    cols = PAIRS * PAIR
    return call(
        qkv_body,
        sp,
        (width // cols,),
        [
            (own_all, as_given(rows, width)), (got, fixed(got.shape)), (weight, RESIDENT),
            (bias, fixed(bias.shape)),
        ],
        [(jax.ShapeDtypeStruct((rows, 2 * width), bf16), columns(rows, 2 * cols))],
        [
            (x_all, whole_window(rows, width)), (q_all, at_window(rows, cols)),
            (kv_all, at_window(rows, 2 * cols)),
        ],
        us=4,
    )


def low_half(shape):
    return lax.broadcasted_iota(jnp.int32, shape, 1) < HALF


def split_three(value):
    place = lax.broadcasted_iota(jnp.int32, value.shape, 1) % HALF
    high = value.astype(bf16).astype(f32)
    rest = value - high
    mid = rest.astype(bf16).astype(f32)
    last = rest - mid
    out = jnp.where(place == 0, high, jnp.where(place == 1, mid, jnp.where(place == 2, last, 0.0)))
    return out.astype(bf16)


def in_order(first, own, peer):
    return jnp.concatenate([jnp.where(first, own, peer), jnp.where(first, peer, own)], axis=0)


def attend_body(
    sp, q_ref, own_ref, peer_ref, side_ref, hot_ref, m_ref, a_ref, rest_ref, lse_ref, kept_ref
):
    rows = q_ref.shape[1]
    first = sp[2] == 0
    kept_ref[0] = peer_ref[...]

    def variant(keys):
        low = low_half((rows, PAIR))
        key_low = low_half((keys, PAIR))
        one = jnp.ones((keys, PAIR), bf16)
        side = side_ref[0]
        hot = hot_ref[0, :keys, :]
        for n in range(PAIRS):
            cols = slice(n * PAIR, (n + 1) * PAIR)
            kv = slice(2 * n * PAIR, 2 * (n + 1) * PAIR)
            both = in_order(first, own_ref[:, kv], peer_ref[:, kv])[:keys]
            k, v = both[:, :PAIR], both[:, PAIR:]
            ks = dot_nn(hot, m_ref[:, cols]).astype(bf16)
            q = q_ref[0, :, cols]
            outs = []
            peaks = []
            for head in (0, 1):
                pick = (lambda m, x, y: jnp.where(m, x, y)) if head == 0 else (
                    lambda m, x, y: jnp.where(m, y, x)
                )
                s = dot_nt(pick(low, q, side), pick(key_low, k, ks))
                peak = jnp.max(s, axis=1, keepdims=True)
                e = jnp.exp(s - peak).astype(bf16)
                outs.append(dot_nn(e, pick(key_low, v, one)))
                peaks.append(peak)
            top = jnp.where(low, outs[0], outs[1])
            total = pltpu.roll(jnp.where(low, outs[1], outs[0]), HALF, 1)
            mixed = top / total
            mixed_low = mixed.astype(bf16)
            a_ref[0, :, cols] = mixed_low
            rest_ref[0, :, cols] = (mixed - mixed_low.astype(f32)).astype(bf16)
            lse = jnp.where(low, peaks[0], peaks[1]) + jnp.log(total)
            lse_ref[0, :, cols] = split_three(-lse)

    for blocks in range(1, 2 * rows // KEY_BLOCK + 1):
        pl.when(sp[1] == blocks)(functools.partial(variant, blocks * KEY_BLOCK))


def attend_call(sp, q_all, kv_own, kv_peer, side_all, hot_all, matrix, bufs):
    rows, width = q_all.shape[1], q_all.shape[2]
    cols = PAIRS * PAIR
    part = at_window(rows, cols)
    return call(
        attend_body,
        sp,
        (width // cols,),
        [
            (q_all, part),
            (kv_own, columns(rows, 2 * cols)),
            (kv_peer, columns(rows, 2 * cols)),
            (side_all, as_given(rows, PAIR)),
            (hot_all, as_given(2 * rows, PAIR)),
            (matrix, columns(PAIR, cols)),
        ],
        [],
        [(b, part) for b in bufs[:-1]] + [(bufs[-1], at_window(rows, 2 * cols))],
        us=14,
    )


def gelu_both(x):
    cdf = 0.5 + 0.5 * lax.erf(x * math.sqrt(0.5))
    bell = jnp.exp(x * x * -0.5)
    return x * cdf, cdf + x * bell * (1.0 / math.sqrt(2.0 * math.pi))


def centered(u):
    c = u - jnp.mean(u, axis=1, keepdims=True)
    r = lax.rsqrt(jnp.mean(c * c, axis=1, keepdims=True) + epsilon)
    return c * r, r


class Moves:
    def __init__(self, sems):
        self.sems = sems
        self.used = 0
        self.out = []

    def start(self, source, target):
        copy = pltpu.make_async_copy(source, target, self.sems.at[self.used])
        self.used += 1
        copy.start()
        return copy

    def write(self, source, target):
        self.out.append(self.start(source, target))

    def finish(self):
        for copy in self.out:
            copy.wait()


def chunks(width):
    return [slice(c, c + FF_BLOCK) for c in range(0, width, FF_BLOCK)]


def dense_body(
    sp, a_ref, x_ref, wo_ref, w1_ref, w2_ref, gain_ref, bias_ref, eb_ref,
    n1_hbm, h1_hbm, g_hbm, d_hbm, n2_hbm, r_hbm, fresh_ref,
    n1_ref, h1_ref, g_ref, d_ref, n2_ref, r_ref, sems,
):
    w = sp[0]
    moves = Moves(sems)
    parts = chunks(w1_ref.shape[1])
    u1 = dot_nn(a_ref[0], wo_ref[...]) + bias_ref[2:3, :] + x_ref[0].astype(f32)
    n1, r1 = centered(u1)
    h1 = n1 * gain_ref[0:1, :] + bias_ref[3:4, :]
    h1_low = h1.astype(bf16)
    n1_ref[...] = n1.astype(bf16)
    h1_ref[...] = h1_low
    moves.write(n1_ref, n1_hbm.at[w])
    moves.write(h1_ref, h1_hbm.at[w])
    u2 = h1 + bias_ref[4:5, :]
    for c in parts:
        g, d = gelu_both(dot_nn(h1_low, w1_ref[:, c]) + eb_ref[:, c])
        g = g.astype(bf16)
        g_ref[:, c] = g
        d_ref[:, c] = d.astype(bf16)
        moves.write(g_ref.at[:, c], g_hbm.at[w, :, c])
        moves.write(d_ref.at[:, c], d_hbm.at[w, :, c])
        u2 = u2 + dot_nt(g, w2_ref[:, c])
    n2, r2 = centered(u2)
    n2_ref[...] = n2.astype(bf16)
    moves.write(n2_ref, n2_hbm.at[w])
    r_ref[...] = jnp.where(low_half(r_ref.shape), r1, r2)
    moves.write(r_ref, r_hbm.at[w])
    fresh_ref[...] = (n2 * gain_ref[1:2, :] + bias_ref[5:6, :]).astype(bf16)
    moves.finish()


def dense_call(sp, a_all, x_all, wo, w1, w2, gains, biases, eb, bufs):
    rows, width = a_all.shape[1], a_all.shape[2]
    hidden = w1.shape[1]
    row = whole_window(rows, width)
    vmem = lambda *shape: pltpu.VMEM(shape, bf16)
    return call(
        dense_body,
        sp,
        (1,),
        [
            (a_all, row), (x_all, row), (wo, RESIDENT), (w1, RESIDENT), (w2, RESIDENT), (gains, fixed(gains.shape)),
            (biases, fixed(biases.shape)), (eb, fixed(eb.shape)),
        ],
        [(jax.ShapeDtypeStruct((rows, width), bf16), pl.BlockSpec((rows, width), lambda i, sp: (0, 0)))],
        [(b, ANY) for b in bufs],
        [
            vmem(rows, width), vmem(rows, width), vmem(rows, hidden), vmem(rows, hidden), vmem(rows, width),
            pltpu.VMEM((rows, PAIR), f32), pltpu.SemaphoreType.DMA((4 + 2 * (hidden // FF_BLOCK),)),
        ],
        us=10,
    )


def column_sum(v):
    return jnp.sum(v, axis=0, keepdims=True)


def norm_back(dy, n, r, gain):
    dn = dy * gain
    return r * (dn - jnp.mean(dn, axis=1, keepdims=True) - n * jnp.mean(dn * n, axis=1, keepdims=True))


def dense_back_body(
    sp, dy_ref, got_ref, n2_ref, r_ref, gain_ref, sel_ref, wo_ref, w1_ref, w2_ref, d_hbm, n1_hbm, a_hbm,
    rest_hbm, db2_hbm, df_hbm, db1_hbm, st_ref, se_ref, do_ref, dd_ref,
    d_ref, n1_ref, a_ref, rest_ref, db2_ref, df_ref, db1_ref, sems,
):
    w = sp[0]
    width = dy_ref.shape[2]
    moves = Moves(sems)
    parts = chunks(w1_ref.shape[1])
    loads = [moves.start(d_hbm.at[w, :, c], d_ref.at[:, c]) for c in parts]
    last = [
        moves.start(n1_hbm.at[w], n1_ref), moves.start(a_hbm.at[w], a_ref),
        moves.start(rest_hbm.at[w], rest_ref),
    ]
    r = r_ref[0]
    dy = jnp.where(sp[4] == 1, dy_ref[0], got_ref[...]).astype(f32)
    n2 = n2_ref[0].astype(f32)
    du2 = norm_back(dy, n2, r[:, HALF : HALF + 1], gain_ref[1:2, :])
    db2 = du2.astype(bf16)
    db2_ref[...] = db2
    moves.write(db2_ref, db2_hbm.at[w])
    st_ref[0, 2:3, :] = column_sum(du2)
    st_ref[0, 3:4, :] = column_sum(dy)
    st_ref[0, 5:6, :] = column_sum(dy * n2)
    st_ref[0, 6:8, :] = jnp.zeros((2, width), f32)
    dh1 = du2
    for c, load in zip(parts, loads):
        load.wait()
        df = dot_nn(db2, w2_ref[:, c]) * d_ref[:, c].astype(f32)
        se_ref[0, :, c] = column_sum(df)
        df = df.astype(bf16)
        df_ref[:, c] = df
        moves.write(df_ref.at[:, c], df_hbm.at[w, :, c])
        dh1 = dh1 + dot_nt(df, w1_ref[:, c])
    for load in last:
        load.wait()
    n1 = n1_ref[...].astype(f32)
    du1 = norm_back(dh1, n1, r[:, 0:1], gain_ref[0:1, :])
    db1 = du1.astype(bf16)
    db1_ref[...] = db1
    moves.write(db1_ref, db1_hbm.at[w])
    st_ref[0, 0:1, :] = column_sum(du1)
    st_ref[0, 1:2, :] = column_sum(dh1)
    st_ref[0, 4:5, :] = column_sum(dh1 * n1)
    do = dot_nt(db1, wo_ref[...]).astype(bf16)
    do_ref[...] = do
    mixed = do.astype(f32) * (a_ref[...].astype(f32) + rest_ref[...].astype(f32))
    high = mixed.astype(bf16)
    low = (mixed - high.astype(f32)).astype(bf16)
    for begin in range(0, width, PAIR):
        cols = slice(begin, begin + PAIR)
        inner = dot_nn(high[:, cols], sel_ref[...]) + dot_nn(low[:, cols], sel_ref[...])
        dd_ref[:, cols] = split_three(-inner)
    moves.finish()


def dense_back_call(
    sp, dy_all, got, n2_all, r_all, d_all, n1_all, a_all, rest_all, wo, w1, w2, gains, sel, bufs
):
    rows, width = got.shape
    hidden = w1.shape[1]
    row = whole_window(rows, width)
    db2_all, df_all, db1_all, st_all, se_all = bufs
    flat = (jax.ShapeDtypeStruct((rows, width), bf16), pl.BlockSpec((rows, width), lambda i, sp: (0, 0)))
    vmem = lambda *shape: pltpu.VMEM(shape, bf16)
    return call(
        dense_back_body,
        sp,
        (1,),
        [
            (dy_all, as_given(rows, width)), (got, fixed(got.shape)), (n2_all, row), (r_all, whole_window(rows, PAIR)),
            (gains, fixed(gains.shape)), (sel, fixed(sel.shape)), (wo, RESIDENT), (w1, RESIDENT),
            (w2, RESIDENT),
        ]
        + [(b, ANY) for b in (d_all, n1_all, a_all, rest_all)],
        [flat, flat],
        [
            (db2_all, ANY), (df_all, ANY), (db1_all, ANY), (st_all, whole_window(8, width)),
            (se_all, whole_window(1, hidden)),
        ],
        [
            vmem(rows, hidden), vmem(rows, width), vmem(rows, width), vmem(rows, width), vmem(rows, width),
            vmem(rows, hidden), vmem(rows, width), pltpu.SemaphoreType.DMA((5 + 2 * (hidden // FF_BLOCK),)),
        ],
        us=10,
    )


def attend_back_body(
    sp, q_ref, own_ref, peer_ref, side_ref, hot_ref, m_ref, lse_ref, do_ref, dd_ref, turned_ref,
    cell_ref, dq_ref, keep_ref, send_ref,
):
    rows = q_ref.shape[1]
    total = 2 * rows
    first = sp[2] == 0

    def variant(blocks):
        keys = blocks * KEY_BLOCK
        low = low_half((rows, PAIR))
        key_low = low_half((keys, PAIR))
        block_low = low_half((KEY_BLOCK, PAIR))
        place = lax.broadcasted_iota(jnp.int32, (KEY_BLOCK, PAIR), 1)
        three = jnp.where(place % HALF < 3, 1.0, 0.0).astype(bf16)
        lone = [
            jnp.where(place < 3, 1.0, 0.0).astype(bf16),
            jnp.where((place >= HALF) & (place < HALF + 3), 1.0, 0.0).astype(bf16),
        ]
        side = side_ref[0]
        hot = hot_ref[0, :keys, :]
        for n in range(PAIRS):
            cols = slice(n * PAIR, (n + 1) * PAIR)
            kv = slice(2 * n * PAIR, 2 * (n + 1) * PAIR)
            both = in_order(first, own_ref[0, :, kv], peer_ref[0, :, kv])[:keys]
            k, v = both[:, :PAIR], both[:, PAIR:]
            ks = dot_nn(hot, m_ref[:, cols]).astype(bf16)
            kt = k.T
            q = q_ref[0, :, cols]
            do = do_ref[:, cols]
            dd = dd_ref[:, cols]
            lse = lse_ref[0, :, cols]
            kc = (jnp.where(key_low, k, ks), jnp.where(key_low, ks, k))
            qc = (jnp.where(low, q, side), jnp.where(low, side, q))
            qe = tuple(jnp.concatenate([c, lse], axis=1) for c in qc)
            dc = (jnp.where(low, do, dd), jnp.where(low, dd, do))
            dq = [None, None]
            dks = []
            dvs = []
            gs = []
            for b in range(blocks):
                at = slice(b * KEY_BLOCK, (b + 1) * KEY_BLOCK)
                vb = v[at]
                vc = (jnp.where(block_low, vb, three), jnp.where(block_low, three, vb))
                part_v = []
                part_k = []
                for head in (0, 1):
                    kb = jnp.concatenate([kc[head][at], lone[head]], axis=1)
                    p = jnp.exp(dot_nt(kb, qe[head]))
                    dp = dot_nt(vc[head], dc[head])
                    ds = (p * dp).astype(bf16)
                    part_v.append(dot_nn(p.astype(bf16), do))
                    part_k.append(dot_nn(ds, qc[head]))
                    part = dot_nn(kt[head * HALF : (head + 1) * HALF, at], ds)
                    dq[head] = part if dq[head] is None else dq[head] + part
                dvs.append(jnp.where(block_low, part_v[0], part_v[1]).astype(bf16))
                dks.append(jnp.where(block_low, part_k[0], part_k[1]).astype(bf16))
                gs.append(jnp.where(block_low, part_k[1], part_k[0]).astype(bf16))
            dq_ref[:, cols] = (jnp.concatenate(dq, axis=0).T * score_scale).astype(bf16)
            cell_ref[0, :, cols] = dot_nn(turned_ref[0, :, :keys], jnp.concatenate(gs, axis=0))
            if keys < total:
                zero = [jnp.zeros((total - keys, PAIR), bf16)]
                dks = dks + zero
                dvs = dvs + zero
            grads = jnp.concatenate([jnp.concatenate(dks, axis=0), jnp.concatenate(dvs, axis=0)], axis=1)
            keep_ref[:, kv] = jnp.where(first, grads[:rows], grads[rows:])
            send_ref[:, kv] = jnp.where(first, grads[rows:], grads[:rows])

    for blocks in range(1, total // KEY_BLOCK + 1):
        pl.when(sp[1] == blocks)(functools.partial(variant, blocks))


def attend_back_call(
    sp, q_all, kv_all, peer_all, side_all, hot_all, matrix, lse_all, do, dd, turned_all, cell_all
):
    rows, width = q_all.shape[1], q_all.shape[2]
    cols = PAIRS * PAIR
    part = at_window(rows, cols)
    kv = at_window(rows, 2 * cols)
    flat = columns(rows, cols)
    flat_kv = columns(rows, 2 * cols)
    out_kv = jax.ShapeDtypeStruct((rows, 2 * width), bf16)
    return call(
        attend_back_body,
        sp,
        (width // cols,),
        [
            (q_all, part),
            (kv_all, kv),
            (peer_all, kv),
            (side_all, as_given(rows, PAIR)),
            (hot_all, as_given(2 * rows, PAIR)),
            (matrix, columns(PAIR, cols)),
            (lse_all, part),
            (do, flat),
            (dd, flat),
            (turned_all, as_given(HALF, 2 * rows)),
        ],
        [(jax.ShapeDtypeStruct((rows, width), bf16), flat), (out_kv, flat_kv), (out_kv, flat_kv)],
        [(cell_all, at_window(HALF, cols))],
        us=20,
    )


def input_back_body(
    sp, dq_ref, own_ref, got_ref, db1_ref, w_ref, dj_ref, sj_ref, fresh_ref, total
):
    step = pl.program_id(0)
    dq = dq_ref[...]
    cols = dq.shape[1]
    both = own_ref[...].astype(f32) + got_ref[...].astype(f32)
    part = lambda at: jnp.concatenate(
        [both[:, p + at : p + at + PAIR] for p in range(0, 2 * cols, 2 * PAIR)], axis=1
    )
    dk = part(0).astype(bf16)
    dv32 = part(PAIR)
    dv = dv32.astype(bf16)
    dj_ref[0, :, :cols] = dq
    dj_ref[0, :, cols : 2 * cols] = dk
    dj_ref[0, :, 2 * cols :] = dv
    sj_ref[0] = jnp.concatenate(
        [column_sum(dq.astype(f32)), column_sum(dv32), jnp.zeros((6, cols), f32)], axis=0
    )
    width = w_ref.shape[0]
    dx = None
    for j, value in enumerate((dq, dk, dv)):
        at = pl.ds(pl.multiple_of(j * width + step * cols, cols), cols)
        term = dot_nt(value, w_ref[:, at])
        dx = term if dx is None else dx + term

    @pl.when(step == 0)
    def _():
        total[...] = dx + db1_ref[0].astype(f32)

    @pl.when(step > 0)
    def _():
        total[...] += dx

    @pl.when(step == pl.num_programs(0) - 1)
    def _():
        fresh_ref[...] = total[...].astype(bf16)


def input_back_call(sp, dq, own, got, db1_all, weight, dj_all, sj_all):
    rows, width = dq.shape
    cols = PAIRS * PAIR
    steps = width // cols
    return call(
        input_back_body,
        sp,
        (steps,),
        [
            (dq, columns(rows, cols)), (own, columns(rows, 2 * cols)), (got, columns(rows, 2 * cols)),
            (db1_all, whole_window(rows, width)), (weight, RESIDENT),
        ],
        [(jax.ShapeDtypeStruct((rows, width), bf16), pl.BlockSpec((rows, width), lambda i, sp: (0, 0)))],
        [
            (dj_all, at_window(rows, 3 * cols)), (sj_all, at_window(8, cols)),
        ],
        [pltpu.VMEM((rows, width), f32)],
        us=4,
    )


def weight_body(splits, based, sp, *refs):
    count = len(splits)
    lefts, rights = refs[:count], refs[count : 2 * count]
    base_refs = refs[2 * count : 2 * count + 2] if based else ()
    give_ref, keep_ref = refs[-2:]
    step = pl.program_id(0)
    windows, rows, width = lefts[0].shape
    half = width // 2
    first = sp[2] == 0

    for (begin, end), left, right in zip(splits, lefts, rights):

        @pl.when((step >= begin) & (step < end))
        def _(left=left, right=right):
            flat = left[...].reshape(windows * rows, width)
            out = dot_tn(flat, right[...].reshape(windows * rows, right.shape[2]))
            give = jnp.where(first, out[half:], out[:half])
            keep = jnp.where(first, out[:half], out[half:])
            if based:
                give = give + base_refs[0][...].astype(f32)
                keep = keep + base_refs[1][...].astype(f32)
            give_ref[...] = give.astype(bf16)
            keep_ref[...] = keep.astype(bf16)


def weight_call(sp, at, windows, pairs, base=()):
    rows, width = pairs[0][0].shape[1:]
    splits = []
    begin = 0
    for _, right in pairs:
        splits.append((begin, begin + right.shape[2] // FF_BLOCK))
        begin = splits[-1][1]

    def left_spec():
        return pl.BlockSpec(
            (windows, rows, width), lambda i, sp: (at, 0, 0), pipeline_mode=pl.Buffered(1)
        )

    def right_spec(begin, end):
        return pl.BlockSpec(
            (windows, rows, FF_BLOCK), lambda i, sp: (at, 0, jnp.clip(i - begin, 0, end - begin - 1))
        )

    half = columns(width // 2, FF_BLOCK)
    shape = jax.ShapeDtypeStruct((width // 2, begin * FF_BLOCK), bf16)
    return call(
        functools.partial(weight_body, tuple(splits), bool(base)),
        sp,
        (begin,),
        [(left, left_spec()) for left, _ in pairs]
        + [(right, right_spec(*split)) for (_, right), split in zip(pairs, splits)]
        + [(b, half) for b in base],
        [(shape, half), (shape, half)],
        [],
        us=5 + 3 * windows,
    )


def spread_body(moves, sp, mine_ref, got_ref, *out_refs):
    half = pl.num_programs(0) // 2
    mine = (pl.program_id(0) // half) == sp[2]
    value = jnp.where(mine, mine_ref[...], got_ref[...]).astype(f32)
    for (out, to), begin, count in moves:
        out_refs[out][:, to : to + count] = value[:, begin : begin + count]


def spread_call(sp, mine, got, widths, moves):
    half, cols = mine.shape
    block = half // 4
    turn = lambda i, sp, core: jnp.where(i // 4 == core, i % 4, jnp.where(core == 0, 3, 0))
    return call(
        functools.partial(spread_body, moves),
        sp,
        (8,),
        [
            (mine, pl.BlockSpec((block, cols), lambda i, sp: (turn(i, sp, sp[2]), 0))),
            (got, pl.BlockSpec((block, cols), lambda i, sp: (turn(i, sp, 1 - sp[2]), 0))),
        ],
        [
            (jax.ShapeDtypeStruct((2 * half, w), f32), pl.BlockSpec((block, w), lambda i, sp: (i, 0)))
            for w in widths
        ],
        [],
        us=5,
    )


def bucket_maps(position_cells, counts):
    key = jnp.arange(HALF, dtype=jnp.int32)[:, None]
    query = jnp.arange(HALF, dtype=jnp.int32)[None, :]
    begins = (0, position_cells, position_cells + GRID, HALF)
    bucket = jnp.full((HALF, HALF), -1, jnp.int32)
    base = 0
    for j, offset in enumerate((counts[0] // 2, GRID - 1, GRID - 1)):
        inside = (key >= begins[j]) & (key < begins[j + 1]) & (query >= begins[j]) & (query < begins[j + 1])
        ids = jnp.clip(query - key, -offset, counts[j] - 1 - offset) + offset + base
        bucket = jnp.where(inside, ids, bucket)
        base += counts[j]
    return bucket[:, :, None] == jnp.arange(base, dtype=jnp.int32)


def cell_matrix(tables, maps, position_cells):
    whole = jnp.concatenate(tables, axis=0)
    heads = whole.shape[1]
    whole = whole.reshape(-1, heads // 2, 2)[:, :, ::-1].reshape(-1, heads)
    m = jnp.einsum("bh,xcb->xhc", whole, maps.astype(bf16), preferred_element_type=f32)
    m = m.reshape(HALF, heads * HALF).astype(bf16)
    lane = jnp.arange(heads * HALF, dtype=jnp.int32) % HALF
    dead = jnp.where(lane < position_cells, masked, 0.0).astype(bf16)[None]
    return jnp.concatenate([m, dead, jnp.zeros((HALF - 1, heads * HALF), bf16)], axis=0)


def table_grads(cells, maps, counts):
    heads = cells.shape[1] // HALF
    whole = jnp.einsum(
        "xcb,xhc->bh", maps.astype(f32), cells.reshape(HALF, heads, HALF), precision=lax.Precision.HIGHEST
    )
    whole = whole.reshape(-1, heads // 2, 2)[:, :, ::-1].reshape(-1, heads)
    a, b = counts[0], counts[0] + counts[1]
    return [whole[:a], whole[a:b], whole[b:]]


def after(value, earlier):
    return lax.optimization_barrier((value, earlier))[0]


class Ring:
    def __init__(self, count):
        self.count = count
        self.index = lax.axis_index("dp")
        bits = list(range(1, count.bit_length() - 1))
        turned = bits[:2][::-1] + bits[2:]
        self.mixed = list(zip(bits, turned))
        self.plain = list(zip(bits, bits))

    def bit(self, step):
        even, odd = step
        return jnp.where(self.index % 2 == 0, (self.index >> even) & 1, (self.index >> odd) & 1)

    def send(self, a, step):
        even, odd = step
        pairs = [(i, i ^ (1 << (even if i % 2 == 0 else odd))) for i in range(self.count)]
        return lax.ppermute(a, "dp", pairs)

    def swap(self, a):
        return lax.ppermute(a, "dp", [(i, i ^ 1) for i in range(self.count)])

    def halve(self, part, step):
        half = part.shape[0] // 2
        bit = self.bit(step)
        keep = lax.dynamic_slice_in_dim(part, bit * half, half, 0)
        give = lax.dynamic_slice_in_dim(part, (1 - bit) * half, half, 0)
        return keep, self.send(give, step)

    def join(self, part, got, step):
        first = self.bit(step) == 0
        return jnp.concatenate([jnp.where(first, part, got), jnp.where(first, got, part)], axis=0)

    def stages(self, give, keep, steps):
        got = self.swap(give)
        order = yield
        part = keep + order(got)
        for step in steps:
            keep, got = self.halve(part, step)
            order = yield part
            part = keep + order(got)
        for step in steps[::-1]:
            got = self.send(part, step)
            order = yield part
            part = self.join(part, order(got), step)
        got = self.swap(part)
        order = yield part
        self.result = (part, order(got))
        yield self.result[1]

    def totals(self, part):
        for bit in range(self.count.bit_length() - 1):
            got = lax.ppermute(part, "dp", [(i, i ^ (1 << bit)) for i in range(self.count)])
            order = yield part
            part = part + order(got)
        yield part


SLOTS = (
    ("F", 0, None),
    ("F", 1, 0),
    ("B", None, 0),
    ("F", 2, 1),
    ("B", 0, 1),
    ("F", 3, 2),
    ("B", 1, 2),
    ("F", None, 3),
    ("B", 2, 3),
    ("B", 3, None),
)


def on_device(
    boundary, doc_lengths, horizontal, vertical, attention_in, attention_out, expand_weight,
    contract_weight, norm_gains, bias_rows, expand_bias, position_table, horizontal_table,
    vertical_table,
):
    section = lax.axis_index("section")
    dp_count = lax.axis_size("dp")
    core = lax.axis_index("dp") % 2
    swap = [(i, i ^ 1) for i in range(dp_count)]
    exchange = lambda a: lax.ppermute(a, "dp", swap)

    own = boundary[0]
    micro, slots, width = own.shape
    rows = slots // 2
    windows = 2 * micro
    hidden = expand_weight.shape[2]
    heads = position_table.shape[2]
    pairs = heads // 2
    w_in, w_out, w1, w2 = in_vmem([attention_in[0], attention_out[0], expand_weight[0], contract_weight[0]])
    gains = norm_gains[0].astype(f32)
    biases = bias_rows[0].astype(f32)
    eb = expand_bias.astype(f32)
    in_bias = jnp.concatenate([biases[0], jnp.zeros_like(biases[0]), biases[1]])[None]
    tables = (position_table[0], horizontal_table[0], vertical_table[0])
    counts = tuple(t.shape[0] for t in tables)
    position_cells = slots // SPAN
    maps = bucket_maps(position_cells, counts)
    ring = Ring(dp_count)

    def both(mine, theirs):
        return jnp.concatenate(
            [jnp.where(core == 0, mine, theirs), jnp.where(core == 0, theirs, mine)], axis=0
        )

    halves = own.reshape(micro, 2, rows, width)
    own_half = jnp.where(core == 0, halves[:, 0], halves[:, 1])
    other_half = jnp.where(core == 0, halves[:, 1], halves[:, 0])
    own_all = both(own_half, exchange(other_half))
    places = jnp.concatenate(
        [horizontal, vertical, jnp.broadcast_to(doc_lengths[:, None], (micro, PAIR))], axis=1
    )
    places = both(places, exchange(places))
    across_cell = places[:, :slots] // SPAN
    down_cell = places[:, slots : 2 * slots] // SPAN
    lengths = places[:, 2 * slots]
    ids = jnp.arange(slots, dtype=jnp.int32)
    position_cell = jnp.broadcast_to((ids // SPAN)[None], (windows, slots))

    def hot_of(cells, lanes, axis):
        p, a, d = (jnp.expand_dims(c, axis) for c in cells)
        lanes = jnp.expand_dims(lanes, (0, 3 - axis))
        return (lanes == p) | (lanes == a + position_cells) | (lanes == d + position_cells + GRID)

    cells = (position_cell, across_cell, down_cell)
    cell_ids = jnp.arange(PAIR, dtype=jnp.int32)
    turned_all = hot_of(cells, cell_ids[:HALF], 1).astype(bf16)
    dead = (ids[None, :] >= lengths[:, None])[:, :, None] & (cell_ids == HALF)
    hot_all = (hot_of(cells, cell_ids, 2) | dead).astype(bf16)
    take = lambda c: jnp.where(core == 0, c[:, :rows], c[:, rows:])
    side_all = hot_of(tuple(take(c) for c in cells), cell_ids % HALF, 2).astype(bf16)
    matrix = cell_matrix(tables, maps, position_cells)

    sel = (cell_ids[:, None] // HALF != cell_ids[None, :] // HALF).astype(bf16)

    window_ids = jnp.arange(windows, dtype=jnp.int32)
    mine, theirs = lengths[:windows][:, None], lengths[:windows][None, :]
    ahead = (theirs > mine) | ((theirs == mine) & (window_ids[None, :] < window_ids[:, None]))
    rank = jnp.sum(ahead.astype(jnp.int32), axis=1)
    picks = jnp.stack(
        [jnp.array([windows if w is None else w for w in slots_of], jnp.int32) for slots_of in zip(*[s[1:] for s in SLOTS])]
    )
    infos = jnp.where(section == 0, picks[0], picks[1])
    hits = infos[:, None] == rank[None, :]
    given_ids = jnp.sum(jnp.where(hits, window_ids[None, :], 0), axis=1)
    given_lengths = jnp.sum(jnp.where(hits, lengths[None, :windows], 0), axis=1)
    infos = jnp.stack(
        [
            infos, (given_lengths + KEY_BLOCK - 1) // KEY_BLOCK, jnp.full_like(infos, core),
            given_lengths, jnp.full_like(infos, section), given_ids,
        ],
        axis=1,
    )
    facts = infos.shape[1]
    infos = infos.reshape(-1)

    widths = dict(
        x=width, q=width, kv=2 * width, a=width, rest=width, lse=width, peer=2 * width, n1=width, h1=width,
        g=hidden, d=hidden, n2=width, db2=width, df=hidden, db1=width, dj=3 * width,
    )
    shapes = {n: jax.ShapeDtypeStruct((windows + 1, rows, c), bf16) for n, c in widths.items()}
    shapes["r"] = jax.ShapeDtypeStruct((windows + 1, rows, PAIR), f32)
    shapes["st"] = shapes["sj"] = jax.ShapeDtypeStruct((windows + 1, 8, width), f32)
    shapes["se"] = jax.ShapeDtypeStruct((windows + 1, 1, hidden), f32)
    shapes["cell"] = jax.ShapeDtypeStruct((windows + 1, HALF, width), f32)
    st = dict(zip(shapes, unwritten(list(shapes.values()))))

    def forward(sp, s, got):
        x, q, kv, fresh = qkv_call(sp, own_all, got, w_in, in_bias, s["x"], s["q"], s["kv"])
        s = dict(s, x=x, q=q, kv=kv)
        mixed = ("a", "rest", "lse", "peer")
        s.update(
            zip(mixed, attend_call(
                sp, q, fresh, exchange(fresh), side_all, hot_all, matrix, tuple(s[n] for n in mixed)
            ))
        )
        names = ("n1", "h1", "g", "d", "n2", "r")
        outs = dense_call(
            sp, s["a"], x, w_out, w1, w2, gains, biases, eb, tuple(s[n] for n in names)
        )
        s.update(zip(names, outs[:-1]))
        return s, outs[-1]

    def dense_back(sp, s, got):
        names = ("db2", "df", "db1", "st", "se")
        outs = dense_back_call(
            sp, own_all, got, s["n2"], s["r"], s["d"], s["n1"], s["a"], s["rest"], w_out, w1, w2, gains,
            sel, tuple(s[n] for n in names),
        )
        s = dict(s)
        s.update(zip(names, outs[:5]))
        return s, tuple(outs[5:])

    def attend_back_kernel(sp, s, grads):
        return attend_back_call(
            sp, s["q"], s["kv"], s["peer"], side_all, hot_all, matrix, s["lse"], *grads, turned_all,
            s["cell"],
        )

    def input_back(sp, s, dq, keep, got):
        dj, sj, fresh = input_back_call(sp, dq, keep, got, s["db1"], w_in, s["dj"], s["sj"])
        return dict(s, dj=dj, sj=sj), fresh

    def attend_back(sp, s, grads):
        cell, dq, keep, send = attend_back_kernel(sp, s, grads)
        return input_back(sp, dict(s, cell=cell), dq, keep, exchange(send))

    got = {}
    finals = {}
    grads_in = {}
    nothing = jnp.zeros((rows, width), bf16)

    for number, (kind, zero, one) in enumerate(SLOTS[:-1]):
        sp = (infos, number * facts)
        if kind == "F":
            st, out = forward(sp, st, got.pop(("F", one), nothing))
            if one is not None:
                finals[one] = out
            if zero is not None:
                got["F", zero] = lax.ppermute(out, "section", [(0, 1)])
        else:
            st, grads = dense_back(sp, st, got.pop(("B", zero), nothing))
            st, out = attend_back(sp, st, grads)
            if zero is not None:
                grads_in[zero] = out
            if one is not None:
                got["B", one] = lax.ppermute(out, "section", [(1, 0)])

    sp = (infos, (len(SLOTS) - 1) * facts)

    class Chain:
        def __init__(self, stages, count):
            self.stages = stages
            self.left = count
            next(stages)

        def advance(self, earlier):
            self.last = self.stages.send(lambda got: after(got, earlier))
            self.left -= 1
            return self.last

    def weight_sum(steps, give, keep):
        return give, Chain(ring.stages(give, keep, steps), 2 * len(steps) + 2)

    natural = [((0, 0), 0, hidden)]
    cols = PAIRS * PAIR
    moves = [
        ((0, j * width + i * cols), (3 * i + j) * cols, cols) for i in range(width // cols) for j in range(3)
    ] + [((1, 0), 3 * width, width)]

    others = windows - 1
    part_contract = weight_call(sp, 0, others, [(after(st["db2"], out), st["g"])])
    part_expand = weight_call(sp, 0, others, [(after(st["h1"], part_contract[0]), st["df"])])
    rows_in = after(got.pop(("B", SLOTS[-1][1])), part_expand[0])
    st, grads = dense_back(sp, st, rows_in)
    halves = weight_call(sp, others, 1, [(st["db2"], st["g"])], part_contract)
    given, contract = weight_sum(ring.plain, *halves)
    halves = weight_call(sp, others, 1, [(after(st["h1"], given), st["df"])], part_expand)
    given, expand = weight_sum(ring.plain, *halves)
    done = contract.advance(given)
    grads = tuple(after(g, done) for g in grads)
    cell, dq, keep, send = attend_back_kernel(sp, st, grads)
    got = exchange(send)
    done = expand.advance(dq)
    done = contract.advance(done)
    got = after(got, done)
    st, grads_in[SLOTS[-1][1]] = input_back(sp, dict(st, cell=cell), dq, keep, got)
    halves = weight_call(sp, 0, windows, [(st["x"], st["dj"]), (st["a"], st["db1"])])
    given, attend = weight_sum(ring.mixed, *halves)
    done = contract.advance(given)
    done = expand.advance(done)
    done = attend.advance(done)

    result = [jnp.where(section == 0, after(grads_in[w], done), after(finals[w], done)) for w in range(windows)]
    result = jnp.stack(result)
    ranks = after(rank, done)
    ordered = [lax.dynamic_index_in_dim(result, ranks[w], 0, keepdims=False) for w in range(windows)]
    mine_first, mine_second = jnp.stack(ordered[:micro]), jnp.stack(ordered[micro:])
    keep_rows = jnp.where(core == 0, mine_first, mine_second)
    give_rows = jnp.where(core == 0, mine_second, mine_first)
    got_rows = exchange(give_rows)

    def assembled(got_rows):
        out_halves = jnp.stack(
            [jnp.where(core == 0, keep_rows, got_rows), jnp.where(core == 0, got_rows, keep_rows)], axis=1
        )
        return out_halves.reshape(1, micro, slots, width)

    done = attend.advance(give_rows)
    done = contract.advance(done)
    done = expand.advance(done)

    of_windows = lambda name: jnp.sum(after(st[name], done)[:windows], axis=0)
    small = [of_windows("sj")[0:2], of_windows("st")[0:6], of_windows("se")] + table_grads(
        of_windows("cell"), maps, counts
    )
    packed = jnp.concatenate([p.reshape(-1) for p in small])
    packed = jnp.pad(packed, (0, -packed.shape[0] % (8 * PAIR))).reshape(-1, PAIR)
    totals = Chain(ring.totals(packed), dp_count.bit_length() - 1)
    done = packed
    chains = {"attend": attend, "contract": contract, "expand": expand, "totals": totals}
    kinds = {"contract": ([hidden], natural), "expand": ([hidden], natural), "attend": ([3 * width, width], moves)}
    outputs = {}
    waiting = []
    boundary_out = None
    while any(chain.left for chain in chains.values()):
        for name, chain in chains.items():
            if not chain.left:
                continue
            done = chain.advance(done)
            for other, (mine, theirs) in waiting:
                outputs[other] = spread_call(sp, after(mine, done), theirs, *kinds[other])
                done = outputs[other][0]
            waiting = [(name, ring.result)] if not chain.left and name in kinds else []
        if boundary_out is None and not totals.left:
            boundary_out = assembled(after(got_rows, done))
            done = boundary_out
    for other, halves in waiting:
        outputs[other] = spread_call(sp, *halves, *kinds[other])
    (g_contract,), (g_expand,), (g_in, g_out) = (outputs[n] for n in ("contract", "expand", "attend"))
    packed = totals.last.reshape(-1)
    pieces = []
    begin = 0
    for p in small:
        count = math.prod(p.shape)
        pieces.append(packed[begin : begin + count].reshape(p.shape))
        begin += count
    joined_sums, sums, wide, table_p, table_h, table_v = pieces
    grad_bias = jnp.concatenate([joined_sums, sums[0:4]], axis=0)
    grad_gain = sums[4:6]
    return (
        boundary_out, g_in[None], g_out[None], g_expand[None], g_contract[None], grad_gain[None],
        grad_bias[None], wide, table_p[None], table_h[None], table_v[None],
    )


def solution(mesh):
    section = P("section", None, None)
    placed = (
        P("section", "dp", None, None), P("dp"), P("dp", None), P("dp", None), section, section,
        section, section, section, section, P("section", None), section, section, section,
    )
    return jax.shard_map(
        on_device,
        mesh=mesh,
        in_specs=placed,
        out_specs=(
            P("section", "dp", None, None), section, section, section, section, section, section,
            P("section", None), section, section, section,
        ),
        check_vma=False,
    )
```

```python
import functools
import math

import jax
import jax.numpy as jnp
from jax import lax
from jax.experimental import pallas as pl
from jax.experimental.pallas import tpu as pltpu
from jax.sharding import PartitionSpec as P

GRID = 16
SPAN = 32
KEY_BLOCK = 256
ROW_BLOCK = 256
FF_BLOCK = 768
PAIRS = 2
HALF = 64
PAIR = 128

epsilon = 1e-05
masked = -1e30
score_scale = 0.125
VMEM_LIMIT = 40 * 1024 * 1024

f32 = jnp.float32
bf16 = jnp.bfloat16

dot_nn = lambda a, b: lax.dot_general(a, b, (((1,), (0,)), ((), ())), preferred_element_type=f32)
dot_nt = lambda a, b: lax.dot_general(a, b, (((1,), (1,)), ((), ())), preferred_element_type=f32)
dot_tn = lambda a, b: lax.dot_general(a, b, (((0,), (0,)), ((), ())), preferred_element_type=f32)


def params_for(axes):
    return pltpu.CompilerParams(
        dimension_semantics=("arbitrary",) * axes, vmem_limit_bytes=VMEM_LIMIT
    )


ANY = pl.BlockSpec(memory_space=pl.ANY)


def like(a):
    return jax.ShapeDtypeStruct(a.shape, a.dtype)


RESIDENT = pl.BlockSpec(memory_space=pltpu.VMEM)


def fixed(shape):
    return pl.BlockSpec(shape, lambda i, sp: (0,) * len(shape), pipeline_mode=pl.Buffered(1))


def this_step(count):
    return pl.ds(pl.multiple_of(pl.program_id(0) * count, count), count)


def stacked(rows, cols):
    return pl.BlockSpec((1, rows, cols), lambda i, sp: (sp[0], i, 0))


def plain(rows, cols):
    return pl.BlockSpec((rows, cols), lambda i, sp: (i, 0))


class Row:
    def __init__(self, table, base):
        self.table = table
        self.base = base

    def __getitem__(self, at):
        return self.table[self.base + at]


def shifted(spec, base):
    if spec.index_map is None:
        return spec
    inner = spec.index_map
    return pl.BlockSpec(
        spec.block_shape, lambda i, sp: inner(i, Row(sp, base)), pipeline_mode=spec.pipeline_mode
    )


def call(body, sp, grid, ins, outs, aliased, scratch=(), us=10):
    held = lambda a, s: pltpu.with_memory_space_constraint(a, pltpu.HBM) if a.ndim == 3 else a
    operands = [held(a, s) for a, s in ins] + [held(a, s) for a, s in aliased]
    table, base = sp
    in_specs = [shifted(s, base) for _, s in ins] + [ANY] * len(aliased)
    out_shape = [pltpu.HBM(a.shape, a.dtype) for a, _ in aliased] + [s for s, _ in outs]
    out_specs = [shifted(s, base) for _, s in aliased] + [shifted(s, base) for _, s in outs]
    kept = len(aliased)
    first = len(ins)

    def run(sp_ref, *refs):
        body(Row(sp_ref, base), *refs[:first], *refs[first + kept :])

    return pl.pallas_call(
        run,
        grid_spec=pltpu.PrefetchScalarGridSpec(
            num_scalar_prefetch=1,
            grid=grid,
            in_specs=in_specs,
            out_specs=out_specs,
            scratch_shapes=list(scratch),
        ),
        out_shape=out_shape,
        input_output_aliases={1 + first + j: j for j in range(kept)},
        compiler_params=params_for(len(grid)),
        cost_estimate=pl.CostEstimate(
            flops=us * 1_000_000_000, bytes_accessed=us * 1_000_000, transcendentals=0
        ),
    )(table, *operands)


def unwritten(shapes):
    return pl.pallas_call(
        lambda *refs: None, out_shape=[pltpu.HBM(s.shape, s.dtype) for s in shapes], out_specs=[ANY] * len(shapes),
        compiler_params=pltpu.CompilerParams(vmem_limit_bytes=2 * 1024 * 1024),
    )()


def in_vmem(arrays):
    def body(*refs):
        count = len(arrays)
        copies = [
            pltpu.make_async_copy(refs[j], refs[count + j], refs[-1].at[j]) for j in range(count)
        ]
        for copy in copies:
            copy.start()
        for copy in copies:
            copy.wait()

    return pl.pallas_call(
        body,
        out_shape=[pltpu.VMEM(a.shape, a.dtype) for a in arrays],
        in_specs=[ANY] * len(arrays),
        out_specs=[RESIDENT] * len(arrays),
        scratch_shapes=[pltpu.SemaphoreType.DMA((len(arrays),))],
        compiler_params=pltpu.CompilerParams(vmem_limit_bytes=2 * 1024 * 1024),
    )(*[pltpu.with_memory_space_constraint(a, pltpu.HBM) for a in arrays])


def at_window(rows, cols):
    return pl.BlockSpec((1, rows, cols), lambda i, sp: (sp[0], 0, i))


def whole_window(rows, cols):
    return pl.BlockSpec((1, rows, cols), lambda i, sp: (sp[0], 0, 0))


def as_given(rows, cols):
    return pl.BlockSpec((1, rows, cols), lambda i, sp: (sp[5], 0, 0))


def columns(rows, cols, begin=0):
    return pl.BlockSpec((rows, cols), lambda i, sp: (0, begin + i))


def qkv_body(sp, x_ref, got_ref, w_ref, b_ref, x_out, q_ref, kv_ref, fresh_ref):
    width = x_ref.shape[2]
    cols = q_ref.shape[2]
    x = jnp.where(sp[4] == 1, got_ref[...], x_ref[0])

    @pl.when(pl.program_id(0) == 0)
    def _():
        x_out[0] = x

    def part(j):
        at = pl.ds(pl.multiple_of(j * width + pl.program_id(0) * cols, cols), cols)
        return dot_nn(x, w_ref[:, at]) + b_ref[:, at]

    q_ref[0] = (part(0).astype(bf16) * score_scale).astype(bf16)
    k = part(1).astype(bf16)
    v = part(2).astype(bf16)
    for begin in range(0, cols, PAIR):
        for value, at in ((k, 0), (v, PAIR)):
            to = slice(2 * begin + at, 2 * begin + at + PAIR)
            kv_ref[0, :, to] = value[:, begin : begin + PAIR]
            fresh_ref[:, to] = value[:, begin : begin + PAIR]


def qkv_call(sp, own_all, got, weight, bias, x_all, q_all, kv_all):
    rows, width = x_all.shape[1], x_all.shape[2]
    cols = PAIRS * PAIR
    return call(
        qkv_body,
        sp,
        (width // cols,),
        [
            (own_all, as_given(rows, width)), (got, fixed(got.shape)), (weight, RESIDENT),
            (bias, fixed(bias.shape)),
        ],
        [(jax.ShapeDtypeStruct((rows, 2 * width), bf16), columns(rows, 2 * cols))],
        [
            (x_all, whole_window(rows, width)), (q_all, at_window(rows, cols)),
            (kv_all, at_window(rows, 2 * cols)),
        ],
        us=4,
    )


def low_half(shape):
    return lax.broadcasted_iota(jnp.int32, shape, 1) < HALF


def split_three(value):
    place = lax.broadcasted_iota(jnp.int32, value.shape, 1) % HALF
    high = value.astype(bf16).astype(f32)
    rest = value - high
    mid = rest.astype(bf16).astype(f32)
    last = rest - mid
    out = jnp.where(place == 0, high, jnp.where(place == 1, mid, jnp.where(place == 2, last, 0.0)))
    return out.astype(bf16)


def in_order(first, own, peer):
    return jnp.concatenate([jnp.where(first, own, peer), jnp.where(first, peer, own)], axis=0)


def attend_body(
    sp, q_ref, own_ref, peer_ref, side_ref, hot_ref, m_ref, a_ref, rest_ref, lse_ref, kept_ref
):
    rows = q_ref.shape[1]
    first = sp[2] == 0
    kept_ref[0] = peer_ref[...]

    def variant(keys):
        low = low_half((rows, PAIR))
        key_low = low_half((keys, PAIR))
        one = jnp.ones((keys, PAIR), bf16)
        side = side_ref[0]
        hot = hot_ref[0, :keys, :]
        for n in range(PAIRS):
            cols = slice(n * PAIR, (n + 1) * PAIR)
            kv = slice(2 * n * PAIR, 2 * (n + 1) * PAIR)
            both = in_order(first, own_ref[:, kv], peer_ref[:, kv])[:keys]
            k, v = both[:, :PAIR], both[:, PAIR:]
            ks = dot_nn(hot, m_ref[:, cols]).astype(bf16)
            q = q_ref[0, :, cols]
            outs = []
            peaks = []
            for head in (0, 1):
                pick = (lambda m, x, y: jnp.where(m, x, y)) if head == 0 else (
                    lambda m, x, y: jnp.where(m, y, x)
                )
                s = dot_nt(pick(low, q, side), pick(key_low, k, ks))
                peak = jnp.max(s, axis=1, keepdims=True)
                e = jnp.exp(s - peak).astype(bf16)
                outs.append(dot_nn(e, pick(key_low, v, one)))
                peaks.append(peak)
            top = jnp.where(low, outs[0], outs[1])
            total = pltpu.roll(jnp.where(low, outs[1], outs[0]), HALF, 1)
            mixed = top / total
            mixed_low = mixed.astype(bf16)
            a_ref[0, :, cols] = mixed_low
            rest_ref[0, :, cols] = (mixed - mixed_low.astype(f32)).astype(bf16)
            lse = jnp.where(low, peaks[0], peaks[1]) + jnp.log(total)
            lse_ref[0, :, cols] = split_three(-lse)

    for blocks in range(1, 2 * rows // KEY_BLOCK + 1):
        pl.when(sp[1] == blocks)(functools.partial(variant, blocks * KEY_BLOCK))


def attend_call(sp, q_all, kv_own, kv_peer, side_all, hot_all, matrix, bufs):
    rows, width = q_all.shape[1], q_all.shape[2]
    cols = PAIRS * PAIR
    part = at_window(rows, cols)
    return call(
        attend_body,
        sp,
        (width // cols,),
        [
            (q_all, part),
            (kv_own, columns(rows, 2 * cols)),
            (kv_peer, columns(rows, 2 * cols)),
            (side_all, as_given(rows, PAIR)),
            (hot_all, as_given(2 * rows, PAIR)),
            (matrix, columns(PAIR, cols)),
        ],
        [],
        [(b, part) for b in bufs[:-1]] + [(bufs[-1], at_window(rows, 2 * cols))],
        us=14,
    )


def gelu_both(x):
    cdf = 0.5 + 0.5 * lax.erf(x * math.sqrt(0.5))
    bell = jnp.exp(x * x * -0.5)
    return x * cdf, cdf + x * bell * (1.0 / math.sqrt(2.0 * math.pi))


def centered(u):
    c = u - jnp.mean(u, axis=1, keepdims=True)
    r = lax.rsqrt(jnp.mean(c * c, axis=1, keepdims=True) + epsilon)
    return c * r, r


class Moves:
    def __init__(self, sems):
        self.sems = sems
        self.used = 0
        self.out = []

    def start(self, source, target):
        copy = pltpu.make_async_copy(source, target, self.sems.at[self.used])
        self.used += 1
        copy.start()
        return copy

    def write(self, source, target):
        self.out.append(self.start(source, target))

    def finish(self):
        for copy in self.out:
            copy.wait()


def chunks(width):
    return [slice(c, c + FF_BLOCK) for c in range(0, width, FF_BLOCK)]


def dense_body(
    sp, a_ref, x_ref, wo_ref, w1_ref, w2_ref, gain_ref, bias_ref, eb_ref,
    n1_hbm, h1_hbm, g_hbm, d_hbm, n2_hbm, r_hbm, fresh_ref,
    n1_ref, h1_ref, g_ref, d_ref, n2_ref, r_ref, sems,
):
    w = sp[0]
    moves = Moves(sems)
    parts = chunks(w1_ref.shape[1])
    u1 = dot_nn(a_ref[0], wo_ref[...]) + bias_ref[2:3, :] + x_ref[0].astype(f32)
    n1, r1 = centered(u1)
    h1 = n1 * gain_ref[0:1, :] + bias_ref[3:4, :]
    h1_low = h1.astype(bf16)
    n1_ref[...] = n1.astype(bf16)
    h1_ref[...] = h1_low
    moves.write(n1_ref, n1_hbm.at[w])
    moves.write(h1_ref, h1_hbm.at[w])
    u2 = h1 + bias_ref[4:5, :]
    for c in parts:
        g, d = gelu_both(dot_nn(h1_low, w1_ref[:, c]) + eb_ref[:, c])
        g = g.astype(bf16)
        g_ref[:, c] = g
        d_ref[:, c] = d.astype(bf16)
        moves.write(g_ref.at[:, c], g_hbm.at[w, :, c])
        moves.write(d_ref.at[:, c], d_hbm.at[w, :, c])
        u2 = u2 + dot_nt(g, w2_ref[:, c])
    n2, r2 = centered(u2)
    n2_ref[...] = n2.astype(bf16)
    moves.write(n2_ref, n2_hbm.at[w])
    r_ref[...] = jnp.where(low_half(r_ref.shape), r1, r2)
    moves.write(r_ref, r_hbm.at[w])
    fresh_ref[...] = (n2 * gain_ref[1:2, :] + bias_ref[5:6, :]).astype(bf16)
    moves.finish()


def dense_call(sp, a_all, x_all, wo, w1, w2, gains, biases, eb, bufs):
    rows, width = a_all.shape[1], a_all.shape[2]
    hidden = w1.shape[1]
    row = whole_window(rows, width)
    vmem = lambda *shape: pltpu.VMEM(shape, bf16)
    return call(
        dense_body,
        sp,
        (1,),
        [
            (a_all, row), (x_all, row), (wo, RESIDENT), (w1, RESIDENT), (w2, RESIDENT), (gains, fixed(gains.shape)),
            (biases, fixed(biases.shape)), (eb, fixed(eb.shape)),
        ],
        [(jax.ShapeDtypeStruct((rows, width), bf16), pl.BlockSpec((rows, width), lambda i, sp: (0, 0)))],
        [(b, ANY) for b in bufs],
        [
            vmem(rows, width), vmem(rows, width), vmem(rows, hidden), vmem(rows, hidden), vmem(rows, width),
            pltpu.VMEM((rows, PAIR), f32), pltpu.SemaphoreType.DMA((4 + 2 * (hidden // FF_BLOCK),)),
        ],
        us=10,
    )


def column_sum(v):
    return jnp.sum(v, axis=0, keepdims=True)


def norm_back(dy, n, r, gain):
    dn = dy * gain
    return r * (dn - jnp.mean(dn, axis=1, keepdims=True) - n * jnp.mean(dn * n, axis=1, keepdims=True))


def dense_back_body(
    sp, dy_ref, got_ref, n2_ref, r_ref, gain_ref, sel_ref, wo_ref, w1_ref, w2_ref, d_hbm, n1_hbm, a_hbm,
    rest_hbm, db2_hbm, df_hbm, db1_hbm, st_ref, se_ref, do_ref, dd_ref,
    d_ref, n1_ref, a_ref, rest_ref, db2_ref, df_ref, db1_ref, sems,
):
    w = sp[0]
    width = dy_ref.shape[2]
    moves = Moves(sems)
    parts = chunks(w1_ref.shape[1])
    loads = [moves.start(d_hbm.at[w, :, c], d_ref.at[:, c]) for c in parts]
    last = [
        moves.start(n1_hbm.at[w], n1_ref), moves.start(a_hbm.at[w], a_ref),
        moves.start(rest_hbm.at[w], rest_ref),
    ]
    r = r_ref[0]
    dy = jnp.where(sp[4] == 1, dy_ref[0], got_ref[...]).astype(f32)
    n2 = n2_ref[0].astype(f32)
    du2 = norm_back(dy, n2, r[:, HALF : HALF + 1], gain_ref[1:2, :])
    db2 = du2.astype(bf16)
    db2_ref[...] = db2
    moves.write(db2_ref, db2_hbm.at[w])
    st_ref[0, 2:3, :] = column_sum(du2)
    st_ref[0, 3:4, :] = column_sum(dy)
    st_ref[0, 5:6, :] = column_sum(dy * n2)
    st_ref[0, 6:8, :] = jnp.zeros((2, width), f32)
    dh1 = du2
    for c, load in zip(parts, loads):
        load.wait()
        df = dot_nn(db2, w2_ref[:, c]) * d_ref[:, c].astype(f32)
        se_ref[0, :, c] = column_sum(df)
        df = df.astype(bf16)
        df_ref[:, c] = df
        moves.write(df_ref.at[:, c], df_hbm.at[w, :, c])
        dh1 = dh1 + dot_nt(df, w1_ref[:, c])
    for load in last:
        load.wait()
    n1 = n1_ref[...].astype(f32)
    du1 = norm_back(dh1, n1, r[:, 0:1], gain_ref[0:1, :])
    db1 = du1.astype(bf16)
    db1_ref[...] = db1
    moves.write(db1_ref, db1_hbm.at[w])
    st_ref[0, 0:1, :] = column_sum(du1)
    st_ref[0, 1:2, :] = column_sum(dh1)
    st_ref[0, 4:5, :] = column_sum(dh1 * n1)
    do = dot_nt(db1, wo_ref[...]).astype(bf16)
    do_ref[...] = do
    mixed = do.astype(f32) * (a_ref[...].astype(f32) + rest_ref[...].astype(f32))
    high = mixed.astype(bf16)
    low = (mixed - high.astype(f32)).astype(bf16)
    for begin in range(0, width, PAIR):
        cols = slice(begin, begin + PAIR)
        inner = dot_nn(high[:, cols], sel_ref[...]) + dot_nn(low[:, cols], sel_ref[...])
        dd_ref[:, cols] = split_three(-inner)
    moves.finish()


def dense_back_call(
    sp, dy_all, got, n2_all, r_all, d_all, n1_all, a_all, rest_all, wo, w1, w2, gains, sel, bufs
):
    rows, width = got.shape
    hidden = w1.shape[1]
    row = whole_window(rows, width)
    db2_all, df_all, db1_all, st_all, se_all = bufs
    flat = (jax.ShapeDtypeStruct((rows, width), bf16), pl.BlockSpec((rows, width), lambda i, sp: (0, 0)))
    vmem = lambda *shape: pltpu.VMEM(shape, bf16)
    return call(
        dense_back_body,
        sp,
        (1,),
        [
            (dy_all, as_given(rows, width)), (got, fixed(got.shape)), (n2_all, row), (r_all, whole_window(rows, PAIR)),
            (gains, fixed(gains.shape)), (sel, fixed(sel.shape)), (wo, RESIDENT), (w1, RESIDENT),
            (w2, RESIDENT),
        ]
        + [(b, ANY) for b in (d_all, n1_all, a_all, rest_all)],
        [flat, flat],
        [
            (db2_all, ANY), (df_all, ANY), (db1_all, ANY), (st_all, whole_window(8, width)),
            (se_all, whole_window(1, hidden)),
        ],
        [
            vmem(rows, hidden), vmem(rows, width), vmem(rows, width), vmem(rows, width), vmem(rows, width),
            vmem(rows, hidden), vmem(rows, width), pltpu.SemaphoreType.DMA((5 + 2 * (hidden // FF_BLOCK),)),
        ],
        us=10,
    )


def attend_back_body(
    sp, q_ref, own_ref, peer_ref, side_ref, hot_ref, m_ref, lse_ref, do_ref, dd_ref, turned_ref,
    cell_ref, dq_ref, keep_ref, send_ref,
):
    rows = q_ref.shape[1]
    total = 2 * rows
    first = sp[2] == 0

    def variant(blocks):
        keys = blocks * KEY_BLOCK
        low = low_half((rows, PAIR))
        key_low = low_half((keys, PAIR))
        block_low = low_half((KEY_BLOCK, PAIR))
        place = lax.broadcasted_iota(jnp.int32, (KEY_BLOCK, PAIR), 1)
        three = jnp.where(place % HALF < 3, 1.0, 0.0).astype(bf16)
        lone = [
            jnp.where(place < 3, 1.0, 0.0).astype(bf16),
            jnp.where((place >= HALF) & (place < HALF + 3), 1.0, 0.0).astype(bf16),
        ]
        side = side_ref[0]
        hot = hot_ref[0, :keys, :]
        for n in range(PAIRS):
            cols = slice(n * PAIR, (n + 1) * PAIR)
            kv = slice(2 * n * PAIR, 2 * (n + 1) * PAIR)
            both = in_order(first, own_ref[0, :, kv], peer_ref[0, :, kv])[:keys]
            k, v = both[:, :PAIR], both[:, PAIR:]
            ks = dot_nn(hot, m_ref[:, cols]).astype(bf16)
            kt = k.T
            q = q_ref[0, :, cols]
            do = do_ref[:, cols]
            dd = dd_ref[:, cols]
            lse = lse_ref[0, :, cols]
            kc = (jnp.where(key_low, k, ks), jnp.where(key_low, ks, k))
            qc = (jnp.where(low, q, side), jnp.where(low, side, q))
            qe = tuple(jnp.concatenate([c, lse], axis=1) for c in qc)
            dc = (jnp.where(low, do, dd), jnp.where(low, dd, do))
            dq = [None, None]
            dks = []
            dvs = []
            gs = []
            for b in range(blocks):
                at = slice(b * KEY_BLOCK, (b + 1) * KEY_BLOCK)
                vb = v[at]
                vc = (jnp.where(block_low, vb, three), jnp.where(block_low, three, vb))
                part_v = []
                part_k = []
                for head in (0, 1):
                    kb = jnp.concatenate([kc[head][at], lone[head]], axis=1)
                    p = jnp.exp(dot_nt(kb, qe[head]))
                    dp = dot_nt(vc[head], dc[head])
                    ds = (p * dp).astype(bf16)
                    part_v.append(dot_nn(p.astype(bf16), do))
                    part_k.append(dot_nn(ds, qc[head]))
                    part = dot_nn(kt[head * HALF : (head + 1) * HALF, at], ds)
                    dq[head] = part if dq[head] is None else dq[head] + part
                dvs.append(jnp.where(block_low, part_v[0], part_v[1]).astype(bf16))
                dks.append(jnp.where(block_low, part_k[0], part_k[1]).astype(bf16))
                gs.append(jnp.where(block_low, part_k[1], part_k[0]).astype(bf16))
            dq_ref[:, cols] = (jnp.concatenate(dq, axis=0).T * score_scale).astype(bf16)
            cell_ref[0, :, cols] = dot_nn(turned_ref[0, :, :keys], jnp.concatenate(gs, axis=0))
            if keys < total:
                zero = [jnp.zeros((total - keys, PAIR), bf16)]
                dks = dks + zero
                dvs = dvs + zero
            grads = jnp.concatenate([jnp.concatenate(dks, axis=0), jnp.concatenate(dvs, axis=0)], axis=1)
            keep_ref[:, kv] = jnp.where(first, grads[:rows], grads[rows:])
            send_ref[:, kv] = jnp.where(first, grads[rows:], grads[:rows])

    for blocks in range(1, total // KEY_BLOCK + 1):
        pl.when(sp[1] == blocks)(functools.partial(variant, blocks))


def attend_back_call(
    sp, q_all, kv_all, peer_all, side_all, hot_all, matrix, lse_all, do, dd, turned_all, cell_all
):
    rows, width = q_all.shape[1], q_all.shape[2]
    cols = PAIRS * PAIR
    part = at_window(rows, cols)
    kv = at_window(rows, 2 * cols)
    flat = columns(rows, cols)
    flat_kv = columns(rows, 2 * cols)
    out_kv = jax.ShapeDtypeStruct((rows, 2 * width), bf16)
    return call(
        attend_back_body,
        sp,
        (width // cols,),
        [
            (q_all, part),
            (kv_all, kv),
            (peer_all, kv),
            (side_all, as_given(rows, PAIR)),
            (hot_all, as_given(2 * rows, PAIR)),
            (matrix, columns(PAIR, cols)),
            (lse_all, part),
            (do, flat),
            (dd, flat),
            (turned_all, as_given(HALF, 2 * rows)),
        ],
        [(jax.ShapeDtypeStruct((rows, width), bf16), flat), (out_kv, flat_kv), (out_kv, flat_kv)],
        [(cell_all, at_window(HALF, cols))],
        us=20,
    )


def input_back_body(
    sp, dq_ref, own_ref, got_ref, db1_ref, w_ref, dj_ref, sj_ref, fresh_ref, total
):
    step = pl.program_id(0)
    dq = dq_ref[...]
    cols = dq.shape[1]
    both = own_ref[...].astype(f32) + got_ref[...].astype(f32)
    part = lambda at: jnp.concatenate(
        [both[:, p + at : p + at + PAIR] for p in range(0, 2 * cols, 2 * PAIR)], axis=1
    )
    dk = part(0).astype(bf16)
    dv32 = part(PAIR)
    dv = dv32.astype(bf16)
    dj_ref[0, :, :cols] = dq
    dj_ref[0, :, cols : 2 * cols] = dk
    dj_ref[0, :, 2 * cols :] = dv
    sj_ref[0] = jnp.concatenate(
        [column_sum(dq.astype(f32)), column_sum(dv32), jnp.zeros((6, cols), f32)], axis=0
    )
    width = w_ref.shape[0]
    dx = None
    for j, value in enumerate((dq, dk, dv)):
        at = pl.ds(pl.multiple_of(j * width + step * cols, cols), cols)
        term = dot_nt(value, w_ref[:, at])
        dx = term if dx is None else dx + term

    @pl.when(step == 0)
    def _():
        total[...] = dx + db1_ref[0].astype(f32)

    @pl.when(step > 0)
    def _():
        total[...] += dx

    @pl.when(step == pl.num_programs(0) - 1)
    def _():
        fresh_ref[...] = total[...].astype(bf16)


def input_back_call(sp, dq, own, got, db1_all, weight, dj_all, sj_all):
    rows, width = dq.shape
    cols = PAIRS * PAIR
    steps = width // cols
    return call(
        input_back_body,
        sp,
        (steps,),
        [
            (dq, columns(rows, cols)), (own, columns(rows, 2 * cols)), (got, columns(rows, 2 * cols)),
            (db1_all, whole_window(rows, width)), (weight, RESIDENT),
        ],
        [(jax.ShapeDtypeStruct((rows, width), bf16), pl.BlockSpec((rows, width), lambda i, sp: (0, 0)))],
        [
            (dj_all, at_window(rows, 3 * cols)), (sj_all, at_window(8, cols)),
        ],
        [pltpu.VMEM((rows, width), f32)],
        us=4,
    )


def weight_body(splits, based, sp, *refs):
    count = len(splits)
    lefts, rights = refs[:count], refs[count : 2 * count]
    base_refs = refs[2 * count : 2 * count + 2] if based else ()
    give_ref, keep_ref = refs[-2:]
    step = pl.program_id(0)
    windows, rows, width = lefts[0].shape
    half = width // 2
    first = sp[2] == 0

    for (begin, end), left, right in zip(splits, lefts, rights):

        @pl.when((step >= begin) & (step < end))
        def _(left=left, right=right):
            flat = left[...].reshape(windows * rows, width)
            out = dot_tn(flat, right[...].reshape(windows * rows, right.shape[2]))
            give = jnp.where(first, out[half:], out[:half])
            keep = jnp.where(first, out[:half], out[half:])
            if based:
                give = give + base_refs[0][...].astype(f32)
                keep = keep + base_refs[1][...].astype(f32)
            give_ref[...] = give.astype(bf16)
            keep_ref[...] = keep.astype(bf16)


def weight_call(sp, at, windows, pairs, base=()):
    rows, width = pairs[0][0].shape[1:]
    splits = []
    begin = 0
    for _, right in pairs:
        splits.append((begin, begin + right.shape[2] // FF_BLOCK))
        begin = splits[-1][1]

    def left_spec():
        return pl.BlockSpec(
            (windows, rows, width), lambda i, sp: (at, 0, 0), pipeline_mode=pl.Buffered(1)
        )

    def right_spec(begin, end):
        return pl.BlockSpec(
            (windows, rows, FF_BLOCK), lambda i, sp: (at, 0, jnp.clip(i - begin, 0, end - begin - 1))
        )

    half = columns(width // 2, FF_BLOCK)
    shape = jax.ShapeDtypeStruct((width // 2, begin * FF_BLOCK), bf16)
    return call(
        functools.partial(weight_body, tuple(splits), bool(base)),
        sp,
        (begin,),
        [(left, left_spec()) for left, _ in pairs]
        + [(right, right_spec(*split)) for (_, right), split in zip(pairs, splits)]
        + [(b, half) for b in base],
        [(shape, half), (shape, half)],
        [],
        us=5 + 3 * windows,
    )


def spread_body(moves, sp, mine_ref, got_ref, *out_refs):
    half = pl.num_programs(0) // 2
    mine = (pl.program_id(0) // half) == sp[2]
    value = jnp.where(mine, mine_ref[...], got_ref[...]).astype(f32)
    for (out, to), begin, count in moves:
        out_refs[out][:, to : to + count] = value[:, begin : begin + count]


def spread_call(sp, mine, got, widths, moves):
    half, cols = mine.shape
    block = half // 4
    turn = lambda i, sp, core: jnp.where(i // 4 == core, i % 4, jnp.where(core == 0, 3, 0))
    return call(
        functools.partial(spread_body, moves),
        sp,
        (8,),
        [
            (mine, pl.BlockSpec((block, cols), lambda i, sp: (turn(i, sp, sp[2]), 0))),
            (got, pl.BlockSpec((block, cols), lambda i, sp: (turn(i, sp, 1 - sp[2]), 0))),
        ],
        [
            (jax.ShapeDtypeStruct((2 * half, w), f32), pl.BlockSpec((block, w), lambda i, sp: (i, 0)))
            for w in widths
        ],
        [],
        us=5,
    )


def bucket_maps(position_cells, counts):
    key = jnp.arange(HALF, dtype=jnp.int32)[:, None]
    query = jnp.arange(HALF, dtype=jnp.int32)[None, :]
    begins = (0, position_cells, position_cells + GRID, HALF)
    bucket = jnp.full((HALF, HALF), -1, jnp.int32)
    base = 0
    for j, offset in enumerate((counts[0] // 2, GRID - 1, GRID - 1)):
        inside = (key >= begins[j]) & (key < begins[j + 1]) & (query >= begins[j]) & (query < begins[j + 1])
        ids = jnp.clip(query - key, -offset, counts[j] - 1 - offset) + offset + base
        bucket = jnp.where(inside, ids, bucket)
        base += counts[j]
    return bucket[:, :, None] == jnp.arange(base, dtype=jnp.int32)


def cell_matrix(tables, maps, position_cells):
    whole = jnp.concatenate(tables, axis=0)
    heads = whole.shape[1]
    whole = whole.reshape(-1, heads // 2, 2)[:, :, ::-1].reshape(-1, heads)
    m = jnp.einsum("bh,xcb->xhc", whole, maps.astype(bf16), preferred_element_type=f32)
    m = m.reshape(HALF, heads * HALF).astype(bf16)
    lane = jnp.arange(heads * HALF, dtype=jnp.int32) % HALF
    dead = jnp.where(lane < position_cells, masked, 0.0).astype(bf16)[None]
    return jnp.concatenate([m, dead, jnp.zeros((HALF - 1, heads * HALF), bf16)], axis=0)


def table_grads(cells, maps, counts):
    heads = cells.shape[1] // HALF
    whole = jnp.einsum(
        "xcb,xhc->bh", maps.astype(f32), cells.reshape(HALF, heads, HALF), precision=lax.Precision.HIGHEST
    )
    whole = whole.reshape(-1, heads // 2, 2)[:, :, ::-1].reshape(-1, heads)
    a, b = counts[0], counts[0] + counts[1]
    return [whole[:a], whole[a:b], whole[b:]]


def after(value, earlier):
    return lax.optimization_barrier((value, earlier))[0]


class Ring:
    def __init__(self, count):
        self.count = count
        self.index = lax.axis_index("dp")
        bits = list(range(1, count.bit_length() - 1))
        turned = bits[:2][::-1] + bits[2:]
        self.mixed = list(zip(bits, turned))
        self.plain = list(zip(bits, bits))

    def bit(self, step):
        even, odd = step
        return jnp.where(self.index % 2 == 0, (self.index >> even) & 1, (self.index >> odd) & 1)

    def send(self, a, step):
        even, odd = step
        pairs = [(i, i ^ (1 << (even if i % 2 == 0 else odd))) for i in range(self.count)]
        return lax.ppermute(a, "dp", pairs)

    def swap(self, a):
        return lax.ppermute(a, "dp", [(i, i ^ 1) for i in range(self.count)])

    def halve(self, part, step):
        half = part.shape[0] // 2
        bit = self.bit(step)
        keep = lax.dynamic_slice_in_dim(part, bit * half, half, 0)
        give = lax.dynamic_slice_in_dim(part, (1 - bit) * half, half, 0)
        return keep, self.send(give, step)

    def join(self, part, got, step):
        first = self.bit(step) == 0
        return jnp.concatenate([jnp.where(first, part, got), jnp.where(first, got, part)], axis=0)

    def stages(self, give, keep, steps):
        got = self.swap(give)
        order = yield
        part = keep + order(got)
        for step in steps[:-1]:
            keep, got = self.halve(part, step)
            order = yield part
            part = keep + order(got)
        for step in steps[-1:]:
            got = self.send(part, step)
            order = yield part
            part = part + order(got)
        for step in steps[:-1][::-1]:
            got = self.send(part, step)
            order = yield part
            part = self.join(part, order(got), step)
        got = self.swap(part)
        order = yield part
        self.result = (part, order(got))
        yield self.result[1]

    def totals(self, part):
        for bit in range(self.count.bit_length() - 1):
            got = lax.ppermute(part, "dp", [(i, i ^ (1 << bit)) for i in range(self.count)])
            order = yield part
            part = part + order(got)
        yield part


SLOTS = (
    ("F", 0, None),
    ("F", 1, 0),
    ("B", None, 0),
    ("F", 2, 1),
    ("B", 0, 1),
    ("F", 3, 2),
    ("B", 1, 2),
    ("F", None, 3),
    ("B", 2, 3),
    ("B", 3, None),
)


def on_device(
    boundary, doc_lengths, horizontal, vertical, attention_in, attention_out, expand_weight,
    contract_weight, norm_gains, bias_rows, expand_bias, position_table, horizontal_table,
    vertical_table,
):
    section = lax.axis_index("section")
    dp_count = lax.axis_size("dp")
    core = lax.axis_index("dp") % 2
    swap = [(i, i ^ 1) for i in range(dp_count)]
    exchange = lambda a: lax.ppermute(a, "dp", swap)

    own = boundary[0]
    micro, slots, width = own.shape
    rows = slots // 2
    windows = 2 * micro
    hidden = expand_weight.shape[2]
    heads = position_table.shape[2]
    pairs = heads // 2
    w_in, w_out, w1, w2 = in_vmem([attention_in[0], attention_out[0], expand_weight[0], contract_weight[0]])
    gains = norm_gains[0].astype(f32)
    biases = bias_rows[0].astype(f32)
    eb = expand_bias.astype(f32)
    in_bias = jnp.concatenate([biases[0], jnp.zeros_like(biases[0]), biases[1]])[None]
    tables = (position_table[0], horizontal_table[0], vertical_table[0])
    counts = tuple(t.shape[0] for t in tables)
    position_cells = slots // SPAN
    maps = bucket_maps(position_cells, counts)
    ring = Ring(dp_count)

    def both(mine, theirs):
        return jnp.concatenate(
            [jnp.where(core == 0, mine, theirs), jnp.where(core == 0, theirs, mine)], axis=0
        )

    halves = own.reshape(micro, 2, rows, width)
    own_half = jnp.where(core == 0, halves[:, 0], halves[:, 1])
    other_half = jnp.where(core == 0, halves[:, 1], halves[:, 0])
    own_all = both(own_half, exchange(other_half))
    places = jnp.concatenate(
        [horizontal, vertical, jnp.broadcast_to(doc_lengths[:, None], (micro, PAIR))], axis=1
    )
    places = both(places, exchange(places))
    across_cell = places[:, :slots] // SPAN
    down_cell = places[:, slots : 2 * slots] // SPAN
    lengths = places[:, 2 * slots]
    ids = jnp.arange(slots, dtype=jnp.int32)
    position_cell = jnp.broadcast_to((ids // SPAN)[None], (windows, slots))

    def hot_of(cells, lanes, axis):
        p, a, d = (jnp.expand_dims(c, axis) for c in cells)
        lanes = jnp.expand_dims(lanes, (0, 3 - axis))
        return (lanes == p) | (lanes == a + position_cells) | (lanes == d + position_cells + GRID)

    cells = (position_cell, across_cell, down_cell)
    cell_ids = jnp.arange(PAIR, dtype=jnp.int32)
    turned_all = hot_of(cells, cell_ids[:HALF], 1).astype(bf16)
    dead = (ids[None, :] >= lengths[:, None])[:, :, None] & (cell_ids == HALF)
    hot_all = (hot_of(cells, cell_ids, 2) | dead).astype(bf16)
    take = lambda c: jnp.where(core == 0, c[:, :rows], c[:, rows:])
    side_all = hot_of(tuple(take(c) for c in cells), cell_ids % HALF, 2).astype(bf16)
    matrix = cell_matrix(tables, maps, position_cells)

    sel = (cell_ids[:, None] // HALF != cell_ids[None, :] // HALF).astype(bf16)

    window_ids = jnp.arange(windows, dtype=jnp.int32)
    mine, theirs = lengths[:windows][:, None], lengths[:windows][None, :]
    ahead = (theirs > mine) | ((theirs == mine) & (window_ids[None, :] < window_ids[:, None]))
    rank = jnp.sum(ahead.astype(jnp.int32), axis=1)
    picks = jnp.stack(
        [jnp.array([windows if w is None else w for w in slots_of], jnp.int32) for slots_of in zip(*[s[1:] for s in SLOTS])]
    )
    infos = jnp.where(section == 0, picks[0], picks[1])
    hits = infos[:, None] == rank[None, :]
    given_ids = jnp.sum(jnp.where(hits, window_ids[None, :], 0), axis=1)
    given_lengths = jnp.sum(jnp.where(hits, lengths[None, :windows], 0), axis=1)
    infos = jnp.stack(
        [
            infos, (given_lengths + KEY_BLOCK - 1) // KEY_BLOCK, jnp.full_like(infos, core),
            given_lengths, jnp.full_like(infos, section), given_ids,
        ],
        axis=1,
    )
    facts = infos.shape[1]
    infos = infos.reshape(-1)

    widths = dict(
        x=width, q=width, kv=2 * width, a=width, rest=width, lse=width, peer=2 * width, n1=width, h1=width,
        g=hidden, d=hidden, n2=width, db2=width, df=hidden, db1=width, dj=3 * width,
    )
    shapes = {n: jax.ShapeDtypeStruct((windows + 1, rows, c), bf16) for n, c in widths.items()}
    shapes["r"] = jax.ShapeDtypeStruct((windows + 1, rows, PAIR), f32)
    shapes["st"] = shapes["sj"] = jax.ShapeDtypeStruct((windows + 1, 8, width), f32)
    shapes["se"] = jax.ShapeDtypeStruct((windows + 1, 1, hidden), f32)
    shapes["cell"] = jax.ShapeDtypeStruct((windows + 1, HALF, width), f32)
    st = dict(zip(shapes, unwritten(list(shapes.values()))))

    def forward(sp, s, got):
        x, q, kv, fresh = qkv_call(sp, own_all, got, w_in, in_bias, s["x"], s["q"], s["kv"])
        s = dict(s, x=x, q=q, kv=kv)
        mixed = ("a", "rest", "lse", "peer")
        s.update(
            zip(mixed, attend_call(
                sp, q, fresh, exchange(fresh), side_all, hot_all, matrix, tuple(s[n] for n in mixed)
            ))
        )
        names = ("n1", "h1", "g", "d", "n2", "r")
        outs = dense_call(
            sp, s["a"], x, w_out, w1, w2, gains, biases, eb, tuple(s[n] for n in names)
        )
        s.update(zip(names, outs[:-1]))
        return s, outs[-1]

    def dense_back(sp, s, got):
        names = ("db2", "df", "db1", "st", "se")
        outs = dense_back_call(
            sp, own_all, got, s["n2"], s["r"], s["d"], s["n1"], s["a"], s["rest"], w_out, w1, w2, gains,
            sel, tuple(s[n] for n in names),
        )
        s = dict(s)
        s.update(zip(names, outs[:5]))
        return s, tuple(outs[5:])

    def attend_back_kernel(sp, s, grads):
        return attend_back_call(
            sp, s["q"], s["kv"], s["peer"], side_all, hot_all, matrix, s["lse"], *grads, turned_all,
            s["cell"],
        )

    def input_back(sp, s, dq, keep, got):
        dj, sj, fresh = input_back_call(sp, dq, keep, got, s["db1"], w_in, s["dj"], s["sj"])
        return dict(s, dj=dj, sj=sj), fresh

    def attend_back(sp, s, grads):
        cell, dq, keep, send = attend_back_kernel(sp, s, grads)
        return input_back(sp, dict(s, cell=cell), dq, keep, exchange(send))

    got = {}
    finals = {}
    grads_in = {}
    nothing = jnp.zeros((rows, width), bf16)

    for number, (kind, zero, one) in enumerate(SLOTS[:-1]):
        sp = (infos, number * facts)
        if kind == "F":
            st, out = forward(sp, st, got.pop(("F", one), nothing))
            if one is not None:
                finals[one] = out
            if zero is not None:
                got["F", zero] = lax.ppermute(out, "section", [(0, 1)])
        else:
            st, grads = dense_back(sp, st, got.pop(("B", zero), nothing))
            st, out = attend_back(sp, st, grads)
            if zero is not None:
                grads_in[zero] = out
            if one is not None:
                got["B", one] = lax.ppermute(out, "section", [(1, 0)])

    sp = (infos, (len(SLOTS) - 1) * facts)

    class Chain:
        def __init__(self, stages, count):
            self.stages = stages
            self.left = count
            next(stages)

        def advance(self, earlier):
            self.last = self.stages.send(lambda got: after(got, earlier))
            self.left -= 1
            return self.last

    def weight_sum(steps, give, keep):
        return give, Chain(ring.stages(give, keep, steps), 2 * len(steps) + 1)

    natural = [((0, 0), 0, hidden)]
    cols = PAIRS * PAIR
    moves = [
        ((0, j * width + i * cols), (3 * i + j) * cols, cols) for i in range(width // cols) for j in range(3)
    ] + [((1, 0), 3 * width, width)]

    others = windows - 1
    part_contract = weight_call(sp, 0, others, [(after(st["db2"], out), st["g"])])
    part_expand = weight_call(sp, 0, others, [(after(st["h1"], part_contract[0]), st["df"])])
    rows_in = after(got.pop(("B", SLOTS[-1][1])), part_expand[0])
    st, grads = dense_back(sp, st, rows_in)
    halves = weight_call(sp, others, 1, [(st["db2"], st["g"])], part_contract)
    given, contract = weight_sum(ring.plain, *halves)
    halves = weight_call(sp, others, 1, [(after(st["h1"], given), st["df"])], part_expand)
    given, expand = weight_sum(ring.plain, *halves)
    done = contract.advance(given)
    grads = tuple(after(g, done) for g in grads)
    cell, dq, keep, send = attend_back_kernel(sp, st, grads)
    got = exchange(send)
    done = expand.advance(dq)
    done = contract.advance(done)
    got = after(got, done)
    st, grads_in[SLOTS[-1][1]] = input_back(sp, dict(st, cell=cell), dq, keep, got)
    halves = weight_call(sp, 0, windows, [(st["x"], st["dj"]), (st["a"], st["db1"])])
    given, attend = weight_sum(ring.mixed, *halves)
    done = contract.advance(given)
    done = expand.advance(done)
    done = attend.advance(done)

    result = [jnp.where(section == 0, after(grads_in[w], done), after(finals[w], done)) for w in range(windows)]
    result = jnp.stack(result)
    ranks = after(rank, done)
    ordered = [lax.dynamic_index_in_dim(result, ranks[w], 0, keepdims=False) for w in range(windows)]
    mine_first, mine_second = jnp.stack(ordered[:micro]), jnp.stack(ordered[micro:])
    keep_rows = jnp.where(core == 0, mine_first, mine_second)
    give_rows = jnp.where(core == 0, mine_second, mine_first)
    got_rows = exchange(give_rows)

    def assembled(got_rows):
        out_halves = jnp.stack(
            [jnp.where(core == 0, keep_rows, got_rows), jnp.where(core == 0, got_rows, keep_rows)], axis=1
        )
        return out_halves.reshape(1, micro, slots, width)

    done = attend.advance(give_rows)
    done = contract.advance(done)
    done = expand.advance(done)

    of_windows = lambda name: jnp.sum(after(st[name], done)[:windows], axis=0)
    small = [of_windows("sj")[0:2], of_windows("st")[0:6], of_windows("se")] + table_grads(
        of_windows("cell"), maps, counts
    )
    packed = jnp.concatenate([p.reshape(-1) for p in small])
    packed = jnp.pad(packed, (0, -packed.shape[0] % (8 * PAIR))).reshape(-1, PAIR)
    totals = Chain(ring.totals(packed), dp_count.bit_length() - 1)
    done = packed
    chains = {"attend": attend, "contract": contract, "expand": expand, "totals": totals}
    kinds = {"contract": ([hidden], natural), "expand": ([hidden], natural), "attend": ([3 * width, width], moves)}
    outputs = {}
    waiting = []
    boundary_out = None
    while any(chain.left for chain in chains.values()):
        for name, chain in chains.items():
            if not chain.left:
                continue
            done = chain.advance(done)
            for other, (mine, theirs) in waiting:
                outputs[other] = spread_call(sp, after(mine, done), theirs, *kinds[other])
                done = outputs[other][0]
            waiting = [(name, ring.result)] if not chain.left and name in kinds else []
        if boundary_out is None and not totals.left:
            boundary_out = assembled(after(got_rows, done))
            done = boundary_out
    for other, halves in waiting:
        outputs[other] = spread_call(sp, *halves, *kinds[other])
    (g_contract,), (g_expand,), (g_in, g_out) = (outputs[n] for n in ("contract", "expand", "attend"))
    packed = totals.last.reshape(-1)
    pieces = []
    begin = 0
    for p in small:
        count = math.prod(p.shape)
        pieces.append(packed[begin : begin + count].reshape(p.shape))
        begin += count
    joined_sums, sums, wide, table_p, table_h, table_v = pieces
    grad_bias = jnp.concatenate([joined_sums, sums[0:4]], axis=0)
    grad_gain = sums[4:6]
    return (
        boundary_out, g_in[None], g_out[None], g_expand[None], g_contract[None], grad_gain[None],
        grad_bias[None], wide, table_p[None], table_h[None], table_v[None],
    )


def solution(mesh):
    section = P("section", None, None)
    placed = (
        P("section", "dp", None, None), P("dp"), P("dp", None), P("dp", None), section, section,
        section, section, section, section, P("section", None), section, section, section,
    )
    return jax.shard_map(
        on_device,
        mesh=mesh,
        in_specs=placed,
        out_specs=(
            P("section", "dp", None, None), section, section, section, section, section, section,
            P("section", None), section, section, section,
        ),
        check_vma=False,
    )
```

```python
import functools
import math

import jax
import jax.numpy as jnp
from jax import lax
from jax.experimental import pallas as pl
from jax.experimental.pallas import tpu as pltpu
from jax.sharding import PartitionSpec as P

GRID = 16
SPAN = 32
KEY_BLOCK = 256
KEY_STEP = 128
LEAST_KEYS = 256
ROW_BLOCK = 256
FF_BLOCK = 768
PAIRS = 2
HALF = 64
PAIR = 128

epsilon = 1e-05
masked = -1e30
score_scale = 0.125
VMEM_LIMIT = 40 * 1024 * 1024

f32 = jnp.float32
bf16 = jnp.bfloat16

dot_nn = lambda a, b: lax.dot_general(a, b, (((1,), (0,)), ((), ())), preferred_element_type=f32)
dot_nt = lambda a, b: lax.dot_general(a, b, (((1,), (1,)), ((), ())), preferred_element_type=f32)
dot_tn = lambda a, b: lax.dot_general(a, b, (((0,), (0,)), ((), ())), preferred_element_type=f32)


def params_for(axes):
    return pltpu.CompilerParams(
        dimension_semantics=("arbitrary",) * axes, vmem_limit_bytes=VMEM_LIMIT
    )


ANY = pl.BlockSpec(memory_space=pl.ANY)


def like(a):
    return jax.ShapeDtypeStruct(a.shape, a.dtype)


RESIDENT = pl.BlockSpec(memory_space=pltpu.VMEM)


def fixed(shape):
    return pl.BlockSpec(shape, lambda i, sp: (0,) * len(shape), pipeline_mode=pl.Buffered(1))


def this_step(count):
    return pl.ds(pl.multiple_of(pl.program_id(0) * count, count), count)


def stacked(rows, cols):
    return pl.BlockSpec((1, rows, cols), lambda i, sp: (sp[0], i, 0))


def plain(rows, cols):
    return pl.BlockSpec((rows, cols), lambda i, sp: (i, 0))


class Row:
    def __init__(self, table, base):
        self.table = table
        self.base = base

    def __getitem__(self, at):
        return self.table[self.base + at]


def shifted(spec, base):
    if spec.index_map is None:
        return spec
    inner = spec.index_map
    return pl.BlockSpec(
        spec.block_shape, lambda i, sp: inner(i, Row(sp, base)), pipeline_mode=spec.pipeline_mode
    )


def call(body, sp, grid, ins, outs, aliased, scratch=(), us=10):
    held = lambda a, s: pltpu.with_memory_space_constraint(a, pltpu.HBM) if a.ndim == 3 else a
    operands = [held(a, s) for a, s in ins] + [held(a, s) for a, s in aliased]
    table, base = sp
    in_specs = [shifted(s, base) for _, s in ins] + [ANY] * len(aliased)
    out_shape = [pltpu.HBM(a.shape, a.dtype) for a, _ in aliased] + [s for s, _ in outs]
    out_specs = [shifted(s, base) for _, s in aliased] + [shifted(s, base) for _, s in outs]
    kept = len(aliased)
    first = len(ins)

    def run(sp_ref, *refs):
        body(Row(sp_ref, base), *refs[:first], *refs[first + kept :])

    return pl.pallas_call(
        run,
        grid_spec=pltpu.PrefetchScalarGridSpec(
            num_scalar_prefetch=1,
            grid=grid,
            in_specs=in_specs,
            out_specs=out_specs,
            scratch_shapes=list(scratch),
        ),
        out_shape=out_shape,
        input_output_aliases={1 + first + j: j for j in range(kept)},
        compiler_params=params_for(len(grid)),
        cost_estimate=pl.CostEstimate(
            flops=us * 1_000_000_000, bytes_accessed=us * 1_000_000, transcendentals=0
        ),
    )(table, *operands)


def unwritten(shapes):
    return pl.pallas_call(
        lambda *refs: None, out_shape=[pltpu.HBM(s.shape, s.dtype) for s in shapes], out_specs=[ANY] * len(shapes),
        compiler_params=pltpu.CompilerParams(vmem_limit_bytes=2 * 1024 * 1024),
    )()


def in_vmem(arrays):
    def body(*refs):
        count = len(arrays)
        copies = [
            pltpu.make_async_copy(refs[j], refs[count + j], refs[-1].at[j]) for j in range(count)
        ]
        for copy in copies:
            copy.start()
        for copy in copies:
            copy.wait()

    return pl.pallas_call(
        body,
        out_shape=[pltpu.VMEM(a.shape, a.dtype) for a in arrays],
        in_specs=[ANY] * len(arrays),
        out_specs=[RESIDENT] * len(arrays),
        scratch_shapes=[pltpu.SemaphoreType.DMA((len(arrays),))],
        compiler_params=pltpu.CompilerParams(vmem_limit_bytes=2 * 1024 * 1024),
    )(*[pltpu.with_memory_space_constraint(a, pltpu.HBM) for a in arrays])


def at_window(rows, cols):
    return pl.BlockSpec((1, rows, cols), lambda i, sp: (sp[0], 0, i))


def whole_window(rows, cols):
    return pl.BlockSpec((1, rows, cols), lambda i, sp: (sp[0], 0, 0))


def as_given(rows, cols):
    return pl.BlockSpec((1, rows, cols), lambda i, sp: (sp[5], 0, 0))


def columns(rows, cols, begin=0):
    return pl.BlockSpec((rows, cols), lambda i, sp: (0, begin + i))


def qkv_body(sp, x_ref, got_ref, w_ref, b_ref, x_out, q_ref, kv_ref, fresh_ref):
    width = x_ref.shape[2]
    cols = q_ref.shape[2]
    x = jnp.where(sp[4] == 1, got_ref[...], x_ref[0])

    @pl.when(pl.program_id(0) == 0)
    def _():
        x_out[0] = x

    def part(j):
        at = pl.ds(pl.multiple_of(j * width + pl.program_id(0) * cols, cols), cols)
        return dot_nn(x, w_ref[:, at]) + b_ref[:, at]

    q_ref[0] = (part(0).astype(bf16) * score_scale).astype(bf16)
    k = part(1).astype(bf16)
    v = part(2).astype(bf16)
    for begin in range(0, cols, PAIR):
        for value, at in ((k, 0), (v, PAIR)):
            to = slice(2 * begin + at, 2 * begin + at + PAIR)
            kv_ref[0, :, to] = value[:, begin : begin + PAIR]
            fresh_ref[:, to] = value[:, begin : begin + PAIR]


def qkv_call(sp, own_all, got, weight, bias, x_all, q_all, kv_all):
    rows, width = x_all.shape[1], x_all.shape[2]
    cols = PAIRS * PAIR
    return call(
        qkv_body,
        sp,
        (width // cols,),
        [
            (own_all, as_given(rows, width)), (got, fixed(got.shape)), (weight, RESIDENT),
            (bias, fixed(bias.shape)),
        ],
        [(jax.ShapeDtypeStruct((rows, 2 * width), bf16), columns(rows, 2 * cols))],
        [
            (x_all, whole_window(rows, width)), (q_all, at_window(rows, cols)),
            (kv_all, at_window(rows, 2 * cols)),
        ],
        us=4,
    )


def low_half(shape):
    return lax.broadcasted_iota(jnp.int32, shape, 1) < HALF


def split_three(value):
    place = lax.broadcasted_iota(jnp.int32, value.shape, 1) % HALF
    high = value.astype(bf16).astype(f32)
    rest = value - high
    mid = rest.astype(bf16).astype(f32)
    last = rest - mid
    out = jnp.where(place == 0, high, jnp.where(place == 1, mid, jnp.where(place == 2, last, 0.0)))
    return out.astype(bf16)


def in_order(first, own, peer):
    return jnp.concatenate([jnp.where(first, own, peer), jnp.where(first, peer, own)], axis=0)


def attend_body(
    sp, q_ref, own_ref, peer_ref, side_ref, hot_ref, m_ref, a_ref, rest_ref, lse_ref, kept_ref
):
    rows = q_ref.shape[1]
    first = sp[2] == 0
    kept_ref[0] = peer_ref[...]

    def variant(keys):
        low = low_half((rows, PAIR))
        key_low = low_half((keys, PAIR))
        one = jnp.ones((keys, PAIR), bf16)
        side = side_ref[0]
        hot = hot_ref[0, :keys, :]
        for n in range(PAIRS):
            cols = slice(n * PAIR, (n + 1) * PAIR)
            kv = slice(2 * n * PAIR, 2 * (n + 1) * PAIR)
            both = in_order(first, own_ref[:, kv], peer_ref[:, kv])[:keys]
            k, v = both[:, :PAIR], both[:, PAIR:]
            ks = dot_nn(hot, m_ref[:, cols]).astype(bf16)
            q = q_ref[0, :, cols]
            outs = []
            peaks = []
            for head in (0, 1):
                pick = (lambda m, x, y: jnp.where(m, x, y)) if head == 0 else (
                    lambda m, x, y: jnp.where(m, y, x)
                )
                s = dot_nt(pick(low, q, side), pick(key_low, k, ks))
                peak = jnp.max(s, axis=1, keepdims=True)
                e = jnp.exp(s - peak).astype(bf16)
                outs.append(dot_nn(e, pick(key_low, v, one)))
                peaks.append(peak)
            top = jnp.where(low, outs[0], outs[1])
            total = pltpu.roll(jnp.where(low, outs[1], outs[0]), HALF, 1)
            mixed = top / total
            mixed_low = mixed.astype(bf16)
            a_ref[0, :, cols] = mixed_low
            rest_ref[0, :, cols] = (mixed - mixed_low.astype(f32)).astype(bf16)
            lse = jnp.where(low, peaks[0], peaks[1]) + jnp.log(total)
            lse_ref[0, :, cols] = split_three(-lse)

    for keys in range(KEY_STEP, 2 * rows + 1, KEY_STEP):
        if keys >= LEAST_KEYS:
            pl.when(sp[1] == keys)(functools.partial(variant, keys))


def attend_call(sp, q_all, kv_own, kv_peer, side_all, hot_all, matrix, bufs):
    rows, width = q_all.shape[1], q_all.shape[2]
    cols = PAIRS * PAIR
    part = at_window(rows, cols)
    return call(
        attend_body,
        sp,
        (width // cols,),
        [
            (q_all, part),
            (kv_own, columns(rows, 2 * cols)),
            (kv_peer, columns(rows, 2 * cols)),
            (side_all, as_given(rows, PAIR)),
            (hot_all, as_given(2 * rows, PAIR)),
            (matrix, columns(PAIR, cols)),
        ],
        [],
        [(b, part) for b in bufs[:-1]] + [(bufs[-1], at_window(rows, 2 * cols))],
        us=14,
    )


def gelu_both(x):
    cdf = 0.5 + 0.5 * lax.erf(x * math.sqrt(0.5))
    bell = jnp.exp(x * x * -0.5)
    return x * cdf, cdf + x * bell * (1.0 / math.sqrt(2.0 * math.pi))


def centered(u):
    c = u - jnp.mean(u, axis=1, keepdims=True)
    r = lax.rsqrt(jnp.mean(c * c, axis=1, keepdims=True) + epsilon)
    return c * r, r


class Moves:
    def __init__(self, sems):
        self.sems = sems
        self.used = 0
        self.out = []

    def start(self, source, target):
        copy = pltpu.make_async_copy(source, target, self.sems.at[self.used])
        self.used += 1
        copy.start()
        return copy

    def write(self, source, target):
        self.out.append(self.start(source, target))

    def finish(self):
        for copy in self.out:
            copy.wait()


def chunks(width):
    return [slice(c, c + FF_BLOCK) for c in range(0, width, FF_BLOCK)]


def dense_body(
    sp, a_ref, x_ref, wo_ref, w1_ref, w2_ref, gain_ref, bias_ref, eb_ref,
    n1_hbm, h1_hbm, g_hbm, d_hbm, n2_hbm, r_hbm, fresh_ref,
    n1_ref, h1_ref, g_ref, d_ref, n2_ref, r_ref, sems,
):
    w = sp[0]
    moves = Moves(sems)
    parts = chunks(w1_ref.shape[1])
    u1 = dot_nn(a_ref[0], wo_ref[...]) + bias_ref[2:3, :] + x_ref[0].astype(f32)
    n1, r1 = centered(u1)
    h1 = n1 * gain_ref[0:1, :] + bias_ref[3:4, :]
    h1_low = h1.astype(bf16)
    n1_ref[...] = n1.astype(bf16)
    h1_ref[...] = h1_low
    moves.write(n1_ref, n1_hbm.at[w])
    moves.write(h1_ref, h1_hbm.at[w])
    u2 = h1 + bias_ref[4:5, :]
    for c in parts:
        g, d = gelu_both(dot_nn(h1_low, w1_ref[:, c]) + eb_ref[:, c])
        g = g.astype(bf16)
        g_ref[:, c] = g
        d_ref[:, c] = d.astype(bf16)
        moves.write(g_ref.at[:, c], g_hbm.at[w, :, c])
        moves.write(d_ref.at[:, c], d_hbm.at[w, :, c])
        u2 = u2 + dot_nt(g, w2_ref[:, c])
    n2, r2 = centered(u2)
    n2_ref[...] = n2.astype(bf16)
    moves.write(n2_ref, n2_hbm.at[w])
    r_ref[...] = jnp.where(low_half(r_ref.shape), r1, r2)
    moves.write(r_ref, r_hbm.at[w])
    fresh_ref[...] = (n2 * gain_ref[1:2, :] + bias_ref[5:6, :]).astype(bf16)
    moves.finish()


def dense_call(sp, a_all, x_all, wo, w1, w2, gains, biases, eb, bufs):
    rows, width = a_all.shape[1], a_all.shape[2]
    hidden = w1.shape[1]
    row = whole_window(rows, width)
    vmem = lambda *shape: pltpu.VMEM(shape, bf16)
    return call(
        dense_body,
        sp,
        (1,),
        [
            (a_all, row), (x_all, row), (wo, RESIDENT), (w1, RESIDENT), (w2, RESIDENT), (gains, fixed(gains.shape)),
            (biases, fixed(biases.shape)), (eb, fixed(eb.shape)),
        ],
        [(jax.ShapeDtypeStruct((rows, width), bf16), pl.BlockSpec((rows, width), lambda i, sp: (0, 0)))],
        [(b, ANY) for b in bufs],
        [
            vmem(rows, width), vmem(rows, width), vmem(rows, hidden), vmem(rows, hidden), vmem(rows, width),
            pltpu.VMEM((rows, PAIR), f32), pltpu.SemaphoreType.DMA((4 + 2 * (hidden // FF_BLOCK),)),
        ],
        us=10,
    )


def column_sum(v):
    return jnp.sum(v, axis=0, keepdims=True)


def norm_back(dy, n, r, gain):
    dn = dy * gain
    return r * (dn - jnp.mean(dn, axis=1, keepdims=True) - n * jnp.mean(dn * n, axis=1, keepdims=True))


def dense_back_body(
    sp, dy_ref, got_ref, n2_ref, r_ref, gain_ref, sel_ref, wo_ref, w1_ref, w2_ref, d_hbm, n1_hbm, a_hbm,
    rest_hbm, db2_hbm, df_hbm, db1_hbm, st_ref, se_ref, do_ref, dd_ref,
    d_ref, n1_ref, a_ref, rest_ref, db2_ref, df_ref, db1_ref, sems,
):
    w = sp[0]
    width = dy_ref.shape[2]
    moves = Moves(sems)
    parts = chunks(w1_ref.shape[1])
    loads = [moves.start(d_hbm.at[w, :, c], d_ref.at[:, c]) for c in parts]
    last = [
        moves.start(n1_hbm.at[w], n1_ref), moves.start(a_hbm.at[w], a_ref),
        moves.start(rest_hbm.at[w], rest_ref),
    ]
    r = r_ref[0]
    dy = jnp.where(sp[4] == 1, dy_ref[0], got_ref[...]).astype(f32)
    n2 = n2_ref[0].astype(f32)
    du2 = norm_back(dy, n2, r[:, HALF : HALF + 1], gain_ref[1:2, :])
    db2 = du2.astype(bf16)
    db2_ref[...] = db2
    moves.write(db2_ref, db2_hbm.at[w])
    st_ref[0, 2:3, :] = column_sum(du2)
    st_ref[0, 3:4, :] = column_sum(dy)
    st_ref[0, 5:6, :] = column_sum(dy * n2)
    st_ref[0, 6:8, :] = jnp.zeros((2, width), f32)
    dh1 = du2
    for c, load in zip(parts, loads):
        load.wait()
        df = dot_nn(db2, w2_ref[:, c]) * d_ref[:, c].astype(f32)
        se_ref[0, :, c] = column_sum(df)
        df = df.astype(bf16)
        df_ref[:, c] = df
        moves.write(df_ref.at[:, c], df_hbm.at[w, :, c])
        dh1 = dh1 + dot_nt(df, w1_ref[:, c])
    for load in last:
        load.wait()
    n1 = n1_ref[...].astype(f32)
    du1 = norm_back(dh1, n1, r[:, 0:1], gain_ref[0:1, :])
    db1 = du1.astype(bf16)
    db1_ref[...] = db1
    moves.write(db1_ref, db1_hbm.at[w])
    st_ref[0, 0:1, :] = column_sum(du1)
    st_ref[0, 1:2, :] = column_sum(dh1)
    st_ref[0, 4:5, :] = column_sum(dh1 * n1)
    do = dot_nt(db1, wo_ref[...]).astype(bf16)
    do_ref[...] = do
    mixed = do.astype(f32) * (a_ref[...].astype(f32) + rest_ref[...].astype(f32))
    high = mixed.astype(bf16)
    low = (mixed - high.astype(f32)).astype(bf16)
    for begin in range(0, width, PAIR):
        cols = slice(begin, begin + PAIR)
        inner = dot_nn(high[:, cols], sel_ref[...]) + dot_nn(low[:, cols], sel_ref[...])
        dd_ref[:, cols] = split_three(-inner)
    moves.finish()


def dense_back_call(
    sp, dy_all, got, n2_all, r_all, d_all, n1_all, a_all, rest_all, wo, w1, w2, gains, sel, bufs
):
    rows, width = got.shape
    hidden = w1.shape[1]
    row = whole_window(rows, width)
    db2_all, df_all, db1_all, st_all, se_all = bufs
    flat = (jax.ShapeDtypeStruct((rows, width), bf16), pl.BlockSpec((rows, width), lambda i, sp: (0, 0)))
    vmem = lambda *shape: pltpu.VMEM(shape, bf16)
    return call(
        dense_back_body,
        sp,
        (1,),
        [
            (dy_all, as_given(rows, width)), (got, fixed(got.shape)), (n2_all, row), (r_all, whole_window(rows, PAIR)),
            (gains, fixed(gains.shape)), (sel, fixed(sel.shape)), (wo, RESIDENT), (w1, RESIDENT),
            (w2, RESIDENT),
        ]
        + [(b, ANY) for b in (d_all, n1_all, a_all, rest_all)],
        [flat, flat],
        [
            (db2_all, ANY), (df_all, ANY), (db1_all, ANY), (st_all, whole_window(8, width)),
            (se_all, whole_window(1, hidden)),
        ],
        [
            vmem(rows, hidden), vmem(rows, width), vmem(rows, width), vmem(rows, width), vmem(rows, width),
            vmem(rows, hidden), vmem(rows, width), pltpu.SemaphoreType.DMA((5 + 2 * (hidden // FF_BLOCK),)),
        ],
        us=10,
    )


def attend_back_body(
    sp, q_ref, own_ref, peer_ref, side_ref, hot_ref, m_ref, lse_ref, do_ref, dd_ref, turned_ref,
    cell_ref, dq_ref, keep_ref, send_ref,
):
    rows = q_ref.shape[1]
    total = 2 * rows
    first = sp[2] == 0

    def variant(keys):
        low = low_half((rows, PAIR))
        key_low = low_half((keys, PAIR))
        place = lax.broadcasted_iota(jnp.int32, (KEY_BLOCK, PAIR), 1)
        three = jnp.where(place % HALF < 3, 1.0, 0.0).astype(bf16)
        lone = [
            jnp.where(place < 3, 1.0, 0.0).astype(bf16),
            jnp.where((place >= HALF) & (place < HALF + 3), 1.0, 0.0).astype(bf16),
        ]
        side = side_ref[0]
        hot = hot_ref[0, :keys, :]
        for n in range(PAIRS):
            cols = slice(n * PAIR, (n + 1) * PAIR)
            kv = slice(2 * n * PAIR, 2 * (n + 1) * PAIR)
            both = in_order(first, own_ref[0, :, kv], peer_ref[0, :, kv])[:keys]
            k, v = both[:, :PAIR], both[:, PAIR:]
            ks = dot_nn(hot, m_ref[:, cols]).astype(bf16)
            kt = k.T
            q = q_ref[0, :, cols]
            do = do_ref[:, cols]
            dd = dd_ref[:, cols]
            lse = lse_ref[0, :, cols]
            kc = (jnp.where(key_low, k, ks), jnp.where(key_low, ks, k))
            qc = (jnp.where(low, q, side), jnp.where(low, side, q))
            qe = tuple(jnp.concatenate([c, lse], axis=1) for c in qc)
            dc = (jnp.where(low, do, dd), jnp.where(low, dd, do))
            dq = [None, None]
            dks = []
            dvs = []
            gs = []
            for begin in range(0, keys, KEY_BLOCK):
                size = min(KEY_BLOCK, keys - begin)
                at = slice(begin, begin + size)
                block_low = low_half((size, PAIR))
                vb = v[at]
                vc = (jnp.where(block_low, vb, three[:size]), jnp.where(block_low, three[:size], vb))
                part_v = []
                part_k = []
                for head in (0, 1):
                    kb = jnp.concatenate([kc[head][at], lone[head][:size]], axis=1)
                    p = jnp.exp(dot_nt(kb, qe[head]))
                    dp = dot_nt(vc[head], dc[head])
                    ds = (p * dp).astype(bf16)
                    part_v.append(dot_nn(p.astype(bf16), do))
                    part_k.append(dot_nn(ds, qc[head]))
                    part = dot_nn(kt[head * HALF : (head + 1) * HALF, at], ds)
                    dq[head] = part if dq[head] is None else dq[head] + part
                dvs.append(jnp.where(block_low, part_v[0], part_v[1]).astype(bf16))
                dks.append(jnp.where(block_low, part_k[0], part_k[1]).astype(bf16))
                gs.append(jnp.where(block_low, part_k[1], part_k[0]).astype(bf16))
            dq_ref[:, cols] = (jnp.concatenate(dq, axis=0).T * score_scale).astype(bf16)
            cell_ref[0, :, cols] = dot_nn(turned_ref[0, :, :keys], jnp.concatenate(gs, axis=0))
            if keys < total:
                zero = [jnp.zeros((total - keys, PAIR), bf16)]
                dks = dks + zero
                dvs = dvs + zero
            grads = jnp.concatenate([jnp.concatenate(dks, axis=0), jnp.concatenate(dvs, axis=0)], axis=1)
            keep_ref[:, kv] = jnp.where(first, grads[:rows], grads[rows:])
            send_ref[:, kv] = jnp.where(first, grads[rows:], grads[:rows])

    for keys in range(KEY_STEP, total + 1, KEY_STEP):
        if keys >= LEAST_KEYS:
            pl.when(sp[1] == keys)(functools.partial(variant, keys))


def attend_back_call(
    sp, q_all, kv_all, peer_all, side_all, hot_all, matrix, lse_all, do, dd, turned_all, cell_all
):
    rows, width = q_all.shape[1], q_all.shape[2]
    cols = PAIRS * PAIR
    part = at_window(rows, cols)
    kv = at_window(rows, 2 * cols)
    flat = columns(rows, cols)
    flat_kv = columns(rows, 2 * cols)
    out_kv = jax.ShapeDtypeStruct((rows, 2 * width), bf16)
    return call(
        attend_back_body,
        sp,
        (width // cols,),
        [
            (q_all, part),
            (kv_all, kv),
            (peer_all, kv),
            (side_all, as_given(rows, PAIR)),
            (hot_all, as_given(2 * rows, PAIR)),
            (matrix, columns(PAIR, cols)),
            (lse_all, part),
            (do, flat),
            (dd, flat),
            (turned_all, as_given(HALF, 2 * rows)),
        ],
        [(jax.ShapeDtypeStruct((rows, width), bf16), flat), (out_kv, flat_kv), (out_kv, flat_kv)],
        [(cell_all, at_window(HALF, cols))],
        us=20,
    )


def input_back_body(
    sp, dq_ref, own_ref, got_ref, db1_ref, w_ref, dj_ref, sj_ref, fresh_ref, total
):
    step = pl.program_id(0)
    dq = dq_ref[...]
    cols = dq.shape[1]
    both = own_ref[...].astype(f32) + got_ref[...].astype(f32)
    part = lambda at: jnp.concatenate(
        [both[:, p + at : p + at + PAIR] for p in range(0, 2 * cols, 2 * PAIR)], axis=1
    )
    dk = part(0).astype(bf16)
    dv32 = part(PAIR)
    dv = dv32.astype(bf16)
    dj_ref[0, :, :cols] = dq
    dj_ref[0, :, cols : 2 * cols] = dk
    dj_ref[0, :, 2 * cols :] = dv
    sj_ref[0] = jnp.concatenate(
        [column_sum(dq.astype(f32)), column_sum(dv32), jnp.zeros((6, cols), f32)], axis=0
    )
    width = w_ref.shape[0]
    dx = None
    for j, value in enumerate((dq, dk, dv)):
        at = pl.ds(pl.multiple_of(j * width + step * cols, cols), cols)
        term = dot_nt(value, w_ref[:, at])
        dx = term if dx is None else dx + term

    @pl.when(step == 0)
    def _():
        total[...] = dx + db1_ref[0].astype(f32)

    @pl.when(step > 0)
    def _():
        total[...] += dx

    @pl.when(step == pl.num_programs(0) - 1)
    def _():
        fresh_ref[...] = total[...].astype(bf16)


def input_back_call(sp, dq, own, got, db1_all, weight, dj_all, sj_all):
    rows, width = dq.shape
    cols = PAIRS * PAIR
    steps = width // cols
    return call(
        input_back_body,
        sp,
        (steps,),
        [
            (dq, columns(rows, cols)), (own, columns(rows, 2 * cols)), (got, columns(rows, 2 * cols)),
            (db1_all, whole_window(rows, width)), (weight, RESIDENT),
        ],
        [(jax.ShapeDtypeStruct((rows, width), bf16), pl.BlockSpec((rows, width), lambda i, sp: (0, 0)))],
        [
            (dj_all, at_window(rows, 3 * cols)), (sj_all, at_window(8, cols)),
        ],
        [pltpu.VMEM((rows, width), f32)],
        us=4,
    )


def weight_body(splits, based, sp, *refs):
    count = len(splits)
    lefts, rights = refs[:count], refs[count : 2 * count]
    base_refs = refs[2 * count : 2 * count + 2] if based else ()
    give_ref, keep_ref = refs[-2:]
    step = pl.program_id(0)
    windows, rows, width = lefts[0].shape
    half = width // 2
    first = sp[2] == 0

    for (begin, end), left, right in zip(splits, lefts, rights):

        @pl.when((step >= begin) & (step < end))
        def _(left=left, right=right):
            flat = left[...].reshape(windows * rows, width)
            out = dot_tn(flat, right[...].reshape(windows * rows, right.shape[2]))
            give = jnp.where(first, out[half:], out[:half])
            keep = jnp.where(first, out[:half], out[half:])
            if based:
                give = give + base_refs[0][...].astype(f32)
                keep = keep + base_refs[1][...].astype(f32)
            give_ref[...] = give.astype(bf16)
            keep_ref[...] = keep.astype(bf16)


def weight_call(sp, at, windows, pairs, base=()):
    rows, width = pairs[0][0].shape[1:]
    splits = []
    begin = 0
    for _, right in pairs:
        splits.append((begin, begin + right.shape[2] // FF_BLOCK))
        begin = splits[-1][1]

    def left_spec():
        return pl.BlockSpec(
            (windows, rows, width), lambda i, sp: (at, 0, 0), pipeline_mode=pl.Buffered(1)
        )

    def right_spec(begin, end):
        return pl.BlockSpec(
            (windows, rows, FF_BLOCK), lambda i, sp: (at, 0, jnp.clip(i - begin, 0, end - begin - 1))
        )

    half = columns(width // 2, FF_BLOCK)
    shape = jax.ShapeDtypeStruct((width // 2, begin * FF_BLOCK), bf16)
    return call(
        functools.partial(weight_body, tuple(splits), bool(base)),
        sp,
        (begin,),
        [(left, left_spec()) for left, _ in pairs]
        + [(right, right_spec(*split)) for (_, right), split in zip(pairs, splits)]
        + [(b, half) for b in base],
        [(shape, half), (shape, half)],
        [],
        us=5 + 3 * windows,
    )


def spread_body(moves, sp, mine_ref, got_ref, *out_refs):
    half = pl.num_programs(0) // 2
    mine = (pl.program_id(0) // half) == sp[2]
    value = jnp.where(mine, mine_ref[...], got_ref[...]).astype(f32)
    for (out, to), begin, count in moves:
        out_refs[out][:, to : to + count] = value[:, begin : begin + count]


def spread_call(sp, mine, got, widths, moves):
    half, cols = mine.shape
    block = half // 4
    turn = lambda i, sp, core: jnp.where(i // 4 == core, i % 4, jnp.where(core == 0, 3, 0))
    return call(
        functools.partial(spread_body, moves),
        sp,
        (8,),
        [
            (mine, pl.BlockSpec((block, cols), lambda i, sp: (turn(i, sp, sp[2]), 0))),
            (got, pl.BlockSpec((block, cols), lambda i, sp: (turn(i, sp, 1 - sp[2]), 0))),
        ],
        [
            (jax.ShapeDtypeStruct((2 * half, w), f32), pl.BlockSpec((block, w), lambda i, sp: (i, 0)))
            for w in widths
        ],
        [],
        us=5,
    )


def bucket_maps(position_cells, counts):
    key = jnp.arange(HALF, dtype=jnp.int32)[:, None]
    query = jnp.arange(HALF, dtype=jnp.int32)[None, :]
    begins = (0, position_cells, position_cells + GRID, HALF)
    bucket = jnp.full((HALF, HALF), -1, jnp.int32)
    base = 0
    for j, offset in enumerate((counts[0] // 2, GRID - 1, GRID - 1)):
        inside = (key >= begins[j]) & (key < begins[j + 1]) & (query >= begins[j]) & (query < begins[j + 1])
        ids = jnp.clip(query - key, -offset, counts[j] - 1 - offset) + offset + base
        bucket = jnp.where(inside, ids, bucket)
        base += counts[j]
    return bucket[:, :, None] == jnp.arange(base, dtype=jnp.int32)


def cell_matrix(tables, maps, position_cells):
    whole = jnp.concatenate(tables, axis=0)
    heads = whole.shape[1]
    whole = whole.reshape(-1, heads // 2, 2)[:, :, ::-1].reshape(-1, heads)
    m = jnp.einsum("bh,xcb->xhc", whole, maps.astype(bf16), preferred_element_type=f32)
    m = m.reshape(HALF, heads * HALF).astype(bf16)
    lane = jnp.arange(heads * HALF, dtype=jnp.int32) % HALF
    dead = jnp.where(lane < position_cells, masked, 0.0).astype(bf16)[None]
    return jnp.concatenate([m, dead, jnp.zeros((HALF - 1, heads * HALF), bf16)], axis=0)


def table_grads(cells, maps, counts):
    heads = cells.shape[1] // HALF
    whole = jnp.einsum(
        "xcb,xhc->bh", maps.astype(f32), cells.reshape(HALF, heads, HALF), precision=lax.Precision.HIGHEST
    )
    whole = whole.reshape(-1, heads // 2, 2)[:, :, ::-1].reshape(-1, heads)
    a, b = counts[0], counts[0] + counts[1]
    return [whole[:a], whole[a:b], whole[b:]]


def after(value, earlier):
    return lax.optimization_barrier((value, earlier))[0]


class Ring:
    def __init__(self, count):
        self.count = count
        self.index = lax.axis_index("dp")
        bits = list(range(1, count.bit_length() - 1))
        turned = bits[:2][::-1] + bits[2:]
        self.mixed = list(zip(bits, turned))
        self.plain = list(zip(bits, bits))

    def bit(self, step):
        even, odd = step
        return jnp.where(self.index % 2 == 0, (self.index >> even) & 1, (self.index >> odd) & 1)

    def send(self, a, step):
        even, odd = step
        pairs = [(i, i ^ (1 << (even if i % 2 == 0 else odd))) for i in range(self.count)]
        return lax.ppermute(a, "dp", pairs)

    def swap(self, a):
        return lax.ppermute(a, "dp", [(i, i ^ 1) for i in range(self.count)])

    def halve(self, part, step):
        half = part.shape[0] // 2
        bit = self.bit(step)
        keep = lax.dynamic_slice_in_dim(part, bit * half, half, 0)
        give = lax.dynamic_slice_in_dim(part, (1 - bit) * half, half, 0)
        return keep, self.send(give, step)

    def join(self, part, got, step):
        first = self.bit(step) == 0
        return jnp.concatenate([jnp.where(first, part, got), jnp.where(first, got, part)], axis=0)

    def stages(self, give, keep, steps):
        got = self.swap(give)
        order = yield
        part = keep + order(got)
        for step in steps:
            keep, got = self.halve(part, step)
            order = yield part
            part = keep + order(got)
        for step in steps[::-1]:
            got = self.send(part, step)
            order = yield part
            part = self.join(part, order(got), step)
        got = self.swap(part)
        order = yield part
        self.result = (part, order(got))
        yield self.result[1]

    def totals(self, part):
        for bit in range(self.count.bit_length() - 1):
            got = lax.ppermute(part, "dp", [(i, i ^ (1 << bit)) for i in range(self.count)])
            order = yield part
            part = part + order(got)
        yield part


SLOTS = (
    ("F", 0, None),
    ("F", 1, 0),
    ("B", None, 0),
    ("F", 2, 1),
    ("B", 0, 1),
    ("F", 3, 2),
    ("B", 1, 2),
    ("F", None, 3),
    ("B", 2, 3),
    ("B", 3, None),
)


def on_device(
    boundary, doc_lengths, horizontal, vertical, attention_in, attention_out, expand_weight,
    contract_weight, norm_gains, bias_rows, expand_bias, position_table, horizontal_table,
    vertical_table,
):
    section = lax.axis_index("section")
    dp_count = lax.axis_size("dp")
    core = lax.axis_index("dp") % 2
    swap = [(i, i ^ 1) for i in range(dp_count)]
    exchange = lambda a: lax.ppermute(a, "dp", swap)

    own = boundary[0]
    micro, slots, width = own.shape
    rows = slots // 2
    windows = 2 * micro
    hidden = expand_weight.shape[2]
    heads = position_table.shape[2]
    pairs = heads // 2
    w_in, w_out, w1, w2 = in_vmem([attention_in[0], attention_out[0], expand_weight[0], contract_weight[0]])
    gains = norm_gains[0].astype(f32)
    biases = bias_rows[0].astype(f32)
    eb = expand_bias.astype(f32)
    in_bias = jnp.concatenate([biases[0], jnp.zeros_like(biases[0]), biases[1]])[None]
    tables = (position_table[0], horizontal_table[0], vertical_table[0])
    counts = tuple(t.shape[0] for t in tables)
    position_cells = slots // SPAN
    maps = bucket_maps(position_cells, counts)
    ring = Ring(dp_count)

    def both(mine, theirs):
        return jnp.concatenate(
            [jnp.where(core == 0, mine, theirs), jnp.where(core == 0, theirs, mine)], axis=0
        )

    halves = own.reshape(micro, 2, rows, width)
    own_half = jnp.where(core == 0, halves[:, 0], halves[:, 1])
    other_half = jnp.where(core == 0, halves[:, 1], halves[:, 0])
    own_all = both(own_half, exchange(other_half))
    places = jnp.concatenate(
        [horizontal, vertical, jnp.broadcast_to(doc_lengths[:, None], (micro, PAIR))], axis=1
    )
    places = both(places, exchange(places))
    across_cell = places[:, :slots] // SPAN
    down_cell = places[:, slots : 2 * slots] // SPAN
    lengths = places[:, 2 * slots]
    ids = jnp.arange(slots, dtype=jnp.int32)
    position_cell = jnp.broadcast_to((ids // SPAN)[None], (windows, slots))

    def hot_of(cells, lanes, axis):
        p, a, d = (jnp.expand_dims(c, axis) for c in cells)
        lanes = jnp.expand_dims(lanes, (0, 3 - axis))
        return (lanes == p) | (lanes == a + position_cells) | (lanes == d + position_cells + GRID)

    cells = (position_cell, across_cell, down_cell)
    cell_ids = jnp.arange(PAIR, dtype=jnp.int32)
    turned_all = hot_of(cells, cell_ids[:HALF], 1).astype(bf16)
    dead = (ids[None, :] >= lengths[:, None])[:, :, None] & (cell_ids == HALF)
    hot_all = (hot_of(cells, cell_ids, 2) | dead).astype(bf16)
    take = lambda c: jnp.where(core == 0, c[:, :rows], c[:, rows:])
    side_all = hot_of(tuple(take(c) for c in cells), cell_ids % HALF, 2).astype(bf16)
    matrix = cell_matrix(tables, maps, position_cells)

    sel = (cell_ids[:, None] // HALF != cell_ids[None, :] // HALF).astype(bf16)

    window_ids = jnp.arange(windows, dtype=jnp.int32)
    mine, theirs = lengths[:windows][:, None], lengths[:windows][None, :]
    ahead = (theirs > mine) | ((theirs == mine) & (window_ids[None, :] < window_ids[:, None]))
    rank = jnp.sum(ahead.astype(jnp.int32), axis=1)
    picks = jnp.stack(
        [jnp.array([windows if w is None else w for w in slots_of], jnp.int32) for slots_of in zip(*[s[1:] for s in SLOTS])]
    )
    infos = jnp.where(section == 0, picks[0], picks[1])
    hits = infos[:, None] == rank[None, :]
    given_ids = jnp.sum(jnp.where(hits, window_ids[None, :], 0), axis=1)
    given_lengths = jnp.sum(jnp.where(hits, lengths[None, :windows], 0), axis=1)
    infos = jnp.stack(
        [
            infos, (given_lengths + KEY_STEP - 1) // KEY_STEP * KEY_STEP, jnp.full_like(infos, core),
            given_lengths, jnp.full_like(infos, section), given_ids,
        ],
        axis=1,
    )
    facts = infos.shape[1]
    infos = infos.reshape(-1)

    widths = dict(
        x=width, q=width, kv=2 * width, a=width, rest=width, lse=width, peer=2 * width, n1=width, h1=width,
        g=hidden, d=hidden, n2=width, db2=width, df=hidden, db1=width, dj=3 * width,
    )
    shapes = {n: jax.ShapeDtypeStruct((windows + 1, rows, c), bf16) for n, c in widths.items()}
    shapes["r"] = jax.ShapeDtypeStruct((windows + 1, rows, PAIR), f32)
    shapes["st"] = shapes["sj"] = jax.ShapeDtypeStruct((windows + 1, 8, width), f32)
    shapes["se"] = jax.ShapeDtypeStruct((windows + 1, 1, hidden), f32)
    shapes["cell"] = jax.ShapeDtypeStruct((windows + 1, HALF, width), f32)
    st = dict(zip(shapes, unwritten(list(shapes.values()))))

    def forward(sp, s, got):
        x, q, kv, fresh = qkv_call(sp, own_all, got, w_in, in_bias, s["x"], s["q"], s["kv"])
        s = dict(s, x=x, q=q, kv=kv)
        mixed = ("a", "rest", "lse", "peer")
        s.update(
            zip(mixed, attend_call(
                sp, q, fresh, exchange(fresh), side_all, hot_all, matrix, tuple(s[n] for n in mixed)
            ))
        )
        names = ("n1", "h1", "g", "d", "n2", "r")
        outs = dense_call(
            sp, s["a"], x, w_out, w1, w2, gains, biases, eb, tuple(s[n] for n in names)
        )
        s.update(zip(names, outs[:-1]))
        return s, outs[-1]

    def dense_back(sp, s, got):
        names = ("db2", "df", "db1", "st", "se")
        outs = dense_back_call(
            sp, own_all, got, s["n2"], s["r"], s["d"], s["n1"], s["a"], s["rest"], w_out, w1, w2, gains,
            sel, tuple(s[n] for n in names),
        )
        s = dict(s)
        s.update(zip(names, outs[:5]))
        return s, tuple(outs[5:])

    def attend_back_kernel(sp, s, grads):
        return attend_back_call(
            sp, s["q"], s["kv"], s["peer"], side_all, hot_all, matrix, s["lse"], *grads, turned_all,
            s["cell"],
        )

    def input_back(sp, s, dq, keep, got):
        dj, sj, fresh = input_back_call(sp, dq, keep, got, s["db1"], w_in, s["dj"], s["sj"])
        return dict(s, dj=dj, sj=sj), fresh

    def attend_back(sp, s, grads):
        cell, dq, keep, send = attend_back_kernel(sp, s, grads)
        return input_back(sp, dict(s, cell=cell), dq, keep, exchange(send))

    got = {}
    finals = {}
    grads_in = {}
    nothing = jnp.zeros((rows, width), bf16)

    for number, (kind, zero, one) in enumerate(SLOTS[:-1]):
        sp = (infos, number * facts)
        if kind == "F":
            st, out = forward(sp, st, got.pop(("F", one), nothing))
            if one is not None:
                finals[one] = out
            if zero is not None:
                got["F", zero] = lax.ppermute(out, "section", [(0, 1)])
        else:
            st, grads = dense_back(sp, st, got.pop(("B", zero), nothing))
            st, out = attend_back(sp, st, grads)
            if zero is not None:
                grads_in[zero] = out
            if one is not None:
                got["B", one] = lax.ppermute(out, "section", [(1, 0)])

    sp = (infos, (len(SLOTS) - 1) * facts)

    class Chain:
        def __init__(self, stages, count):
            self.stages = stages
            self.left = count
            next(stages)

        def advance(self, earlier):
            self.last = self.stages.send(lambda got: after(got, earlier))
            self.left -= 1
            return self.last

    def weight_sum(steps, give, keep):
        return give, Chain(ring.stages(give, keep, steps), 2 * len(steps) + 2)

    natural = [((0, 0), 0, hidden)]
    cols = PAIRS * PAIR
    moves = [
        ((0, j * width + i * cols), (3 * i + j) * cols, cols) for i in range(width // cols) for j in range(3)
    ] + [((1, 0), 3 * width, width)]

    others = windows - 1
    part_contract = weight_call(sp, 0, others, [(after(st["db2"], out), st["g"])])
    part_expand = weight_call(sp, 0, others, [(after(st["h1"], part_contract[0]), st["df"])])
    rows_in = after(got.pop(("B", SLOTS[-1][1])), part_expand[0])
    st, grads = dense_back(sp, st, rows_in)
    halves = weight_call(sp, others, 1, [(st["db2"], st["g"])], part_contract)
    given, contract = weight_sum(ring.plain, *halves)
    halves = weight_call(sp, others, 1, [(after(st["h1"], given), st["df"])], part_expand)
    given, expand = weight_sum(ring.plain, *halves)
    done = contract.advance(given)
    grads = tuple(after(g, done) for g in grads)
    cell, dq, keep, send = attend_back_kernel(sp, st, grads)
    got = exchange(send)
    done = expand.advance(dq)
    done = contract.advance(done)
    got = after(got, done)
    st, grads_in[SLOTS[-1][1]] = input_back(sp, dict(st, cell=cell), dq, keep, got)
    halves = weight_call(sp, 0, windows, [(st["x"], st["dj"]), (st["a"], st["db1"])])
    given, attend = weight_sum(ring.mixed, *halves)
    done = contract.advance(given)
    done = expand.advance(done)
    done = attend.advance(done)

    result = [jnp.where(section == 0, after(grads_in[w], done), after(finals[w], done)) for w in range(windows)]
    result = jnp.stack(result)
    ranks = after(rank, done)
    ordered = [lax.dynamic_index_in_dim(result, ranks[w], 0, keepdims=False) for w in range(windows)]
    mine_first, mine_second = jnp.stack(ordered[:micro]), jnp.stack(ordered[micro:])
    keep_rows = jnp.where(core == 0, mine_first, mine_second)
    give_rows = jnp.where(core == 0, mine_second, mine_first)
    got_rows = exchange(give_rows)

    def assembled(got_rows):
        out_halves = jnp.stack(
            [jnp.where(core == 0, keep_rows, got_rows), jnp.where(core == 0, got_rows, keep_rows)], axis=1
        )
        return out_halves.reshape(1, micro, slots, width)

    done = attend.advance(give_rows)
    done = contract.advance(done)
    done = expand.advance(done)

    of_windows = lambda name: jnp.sum(after(st[name], done)[:windows], axis=0)
    small = [of_windows("sj")[0:2], of_windows("st")[0:6], of_windows("se")] + table_grads(
        of_windows("cell"), maps, counts
    )
    packed = jnp.concatenate([p.reshape(-1) for p in small])
    packed = jnp.pad(packed, (0, -packed.shape[0] % (8 * PAIR))).reshape(-1, PAIR)
    totals = Chain(ring.totals(packed), dp_count.bit_length() - 1)
    done = packed
    chains = {"attend": attend, "contract": contract, "expand": expand, "totals": totals}
    kinds = {"contract": ([hidden], natural), "expand": ([hidden], natural), "attend": ([3 * width, width], moves)}
    outputs = {}
    waiting = []
    boundary_out = None
    while any(chain.left for chain in chains.values()):
        for name, chain in chains.items():
            if not chain.left:
                continue
            done = chain.advance(done)
            for other, (mine, theirs) in waiting:
                outputs[other] = spread_call(sp, after(mine, done), theirs, *kinds[other])
                done = outputs[other][0]
            waiting = [(name, ring.result)] if not chain.left and name in kinds else []
        if boundary_out is None and not totals.left:
            boundary_out = assembled(after(got_rows, done))
            done = boundary_out
    for other, halves in waiting:
        outputs[other] = spread_call(sp, *halves, *kinds[other])
    (g_contract,), (g_expand,), (g_in, g_out) = (outputs[n] for n in ("contract", "expand", "attend"))
    packed = totals.last.reshape(-1)
    pieces = []
    begin = 0
    for p in small:
        count = math.prod(p.shape)
        pieces.append(packed[begin : begin + count].reshape(p.shape))
        begin += count
    joined_sums, sums, wide, table_p, table_h, table_v = pieces
    grad_bias = jnp.concatenate([joined_sums, sums[0:4]], axis=0)
    grad_gain = sums[4:6]
    return (
        boundary_out, g_in[None], g_out[None], g_expand[None], g_contract[None], grad_gain[None],
        grad_bias[None], wide, table_p[None], table_h[None], table_v[None],
    )


def solution(mesh):
    section = P("section", None, None)
    placed = (
        P("section", "dp", None, None), P("dp"), P("dp", None), P("dp", None), section, section,
        section, section, section, section, P("section", None), section, section, section,
    )
    return jax.shard_map(
        on_device,
        mesh=mesh,
        in_specs=placed,
        out_specs=(
            P("section", "dp", None, None), section, section, section, section, section, section,
            P("section", None), section, section, section,
        ),
        check_vma=False,
    )
```

```python
import functools
import math

import jax
import jax.numpy as jnp
from jax import lax
from jax.experimental import pallas as pl
from jax.experimental.pallas import tpu as pltpu
from jax.sharding import PartitionSpec as P

GRID = 16
SPAN = 32
KEY_BLOCK = 256
ROW_BLOCK = 256
FF_BLOCK = 768
PAIRS = 2
HALF = 64
PAIR = 128

epsilon = 1e-05
masked = -1e30
score_scale = 0.125
VMEM_LIMIT = 40 * 1024 * 1024

f32 = jnp.float32
bf16 = jnp.bfloat16

dot_nn = lambda a, b: lax.dot_general(a, b, (((1,), (0,)), ((), ())), preferred_element_type=f32)
dot_nt = lambda a, b: lax.dot_general(a, b, (((1,), (1,)), ((), ())), preferred_element_type=f32)
dot_tn = lambda a, b: lax.dot_general(a, b, (((0,), (0,)), ((), ())), preferred_element_type=f32)


def params_for(axes):
    return pltpu.CompilerParams(
        dimension_semantics=("arbitrary",) * axes, vmem_limit_bytes=VMEM_LIMIT
    )


ANY = pl.BlockSpec(memory_space=pl.ANY)


def like(a):
    return jax.ShapeDtypeStruct(a.shape, a.dtype)


RESIDENT = pl.BlockSpec(memory_space=pltpu.VMEM)


def fixed(shape):
    return pl.BlockSpec(shape, lambda i, sp: (0,) * len(shape), pipeline_mode=pl.Buffered(1))


def this_step(count):
    return pl.ds(pl.multiple_of(pl.program_id(0) * count, count), count)


def stacked(rows, cols):
    return pl.BlockSpec((1, rows, cols), lambda i, sp: (sp[0], i, 0))


def plain(rows, cols):
    return pl.BlockSpec((rows, cols), lambda i, sp: (i, 0))


class Row:
    def __init__(self, table, base):
        self.table = table
        self.base = base

    def __getitem__(self, at):
        return self.table[self.base + at]


def shifted(spec, base):
    if spec.index_map is None:
        return spec
    inner = spec.index_map
    return pl.BlockSpec(
        spec.block_shape, lambda i, sp: inner(i, Row(sp, base)), pipeline_mode=spec.pipeline_mode
    )


def call(body, sp, grid, ins, outs, aliased, scratch=(), us=10):
    held = lambda a, s: pltpu.with_memory_space_constraint(a, pltpu.HBM) if a.ndim == 3 else a
    operands = [held(a, s) for a, s in ins] + [held(a, s) for a, s in aliased]
    table, base = sp
    in_specs = [shifted(s, base) for _, s in ins] + [ANY] * len(aliased)
    out_shape = [pltpu.HBM(a.shape, a.dtype) for a, _ in aliased] + [s for s, _ in outs]
    out_specs = [shifted(s, base) for _, s in aliased] + [shifted(s, base) for _, s in outs]
    kept = len(aliased)
    first = len(ins)

    def run(sp_ref, *refs):
        body(Row(sp_ref, base), *refs[:first], *refs[first + kept :])

    return pl.pallas_call(
        run,
        grid_spec=pltpu.PrefetchScalarGridSpec(
            num_scalar_prefetch=1,
            grid=grid,
            in_specs=in_specs,
            out_specs=out_specs,
            scratch_shapes=list(scratch),
        ),
        out_shape=out_shape,
        input_output_aliases={1 + first + j: j for j in range(kept)},
        compiler_params=params_for(len(grid)),
        cost_estimate=pl.CostEstimate(
            flops=us * 1_000_000_000, bytes_accessed=us * 1_000_000, transcendentals=0
        ),
    )(table, *operands)


def unwritten(shapes):
    return pl.pallas_call(
        lambda *refs: None, out_shape=[pltpu.HBM(s.shape, s.dtype) for s in shapes], out_specs=[ANY] * len(shapes),
        compiler_params=pltpu.CompilerParams(vmem_limit_bytes=2 * 1024 * 1024),
    )()


def in_vmem(arrays):
    def body(*refs):
        count = len(arrays)
        copies = [
            pltpu.make_async_copy(refs[j], refs[count + j], refs[-1].at[j]) for j in range(count)
        ]
        for copy in copies:
            copy.start()
        for copy in copies:
            copy.wait()

    return pl.pallas_call(
        body,
        out_shape=[pltpu.VMEM(a.shape, a.dtype) for a in arrays],
        in_specs=[ANY] * len(arrays),
        out_specs=[RESIDENT] * len(arrays),
        scratch_shapes=[pltpu.SemaphoreType.DMA((len(arrays),))],
        compiler_params=pltpu.CompilerParams(vmem_limit_bytes=2 * 1024 * 1024),
    )(*[pltpu.with_memory_space_constraint(a, pltpu.HBM) for a in arrays])


def at_window(rows, cols):
    return pl.BlockSpec((1, rows, cols), lambda i, sp: (sp[0], 0, i))


def whole_window(rows, cols):
    return pl.BlockSpec((1, rows, cols), lambda i, sp: (sp[0], 0, 0))


def as_given(rows, cols):
    return pl.BlockSpec((1, rows, cols), lambda i, sp: (sp[5], 0, 0))


def columns(rows, cols, begin=0):
    return pl.BlockSpec((rows, cols), lambda i, sp: (0, begin + i))


def qkv_body(sp, x_ref, got_ref, w_ref, b_ref, x_out, q_ref, kv_ref, fresh_ref):
    width = x_ref.shape[2]
    cols = q_ref.shape[2]
    x = jnp.where(sp[4] == 1, got_ref[...], x_ref[0])

    @pl.when(pl.program_id(0) == 0)
    def _():
        x_out[0] = x

    def part(j):
        at = pl.ds(pl.multiple_of(j * width + pl.program_id(0) * cols, cols), cols)
        return dot_nn(x, w_ref[:, at]) + b_ref[:, at]

    q_ref[0] = (part(0).astype(bf16) * score_scale).astype(bf16)
    k = part(1).astype(bf16)
    v = part(2).astype(bf16)
    for begin in range(0, cols, PAIR):
        for value, at in ((k, 0), (v, PAIR)):
            to = slice(2 * begin + at, 2 * begin + at + PAIR)
            kv_ref[0, :, to] = value[:, begin : begin + PAIR]
            fresh_ref[:, to] = value[:, begin : begin + PAIR]


def qkv_call(sp, own_all, got, weight, bias, x_all, q_all, kv_all):
    rows, width = x_all.shape[1], x_all.shape[2]
    cols = PAIRS * PAIR
    return call(
        qkv_body,
        sp,
        (width // cols,),
        [
            (own_all, as_given(rows, width)), (got, fixed(got.shape)), (weight, RESIDENT),
            (bias, fixed(bias.shape)),
        ],
        [(jax.ShapeDtypeStruct((rows, 2 * width), bf16), columns(rows, 2 * cols))],
        [
            (x_all, whole_window(rows, width)), (q_all, at_window(rows, cols)),
            (kv_all, at_window(rows, 2 * cols)),
        ],
        us=4,
    )


def low_half(shape):
    return lax.broadcasted_iota(jnp.int32, shape, 1) < HALF


def split_three(value):
    place = lax.broadcasted_iota(jnp.int32, value.shape, 1) % HALF
    high = value.astype(bf16).astype(f32)
    rest = value - high
    mid = rest.astype(bf16).astype(f32)
    last = rest - mid
    out = jnp.where(place == 0, high, jnp.where(place == 1, mid, jnp.where(place == 2, last, 0.0)))
    return out.astype(bf16)


def in_order(first, own, peer):
    return jnp.concatenate([jnp.where(first, own, peer), jnp.where(first, peer, own)], axis=0)


def attend_body(
    sp, q_ref, own_ref, peer_ref, side_ref, hot_ref, m_ref, a_ref, rest_ref, lse_ref, kept_ref
):
    rows = q_ref.shape[1]
    first = sp[2] == 0
    kept_ref[0] = peer_ref[...]

    def variant(keys):
        low = low_half((rows, PAIR))
        key_low = low_half((keys, PAIR))
        one = jnp.ones((keys, PAIR), bf16)
        side = side_ref[0]
        hot = hot_ref[0, :keys, :]
        for n in range(PAIRS):
            cols = slice(n * PAIR, (n + 1) * PAIR)
            kv = slice(2 * n * PAIR, 2 * (n + 1) * PAIR)
            both = in_order(first, own_ref[:, kv], peer_ref[:, kv])[:keys]
            k, v = both[:, :PAIR], both[:, PAIR:]
            ks = dot_nn(hot, m_ref[:, cols]).astype(bf16)
            q = q_ref[0, :, cols]
            outs = []
            peaks = []
            for head in (0, 1):
                pick = (lambda m, x, y: jnp.where(m, x, y)) if head == 0 else (
                    lambda m, x, y: jnp.where(m, y, x)
                )
                s = dot_nt(pick(low, q, side), pick(key_low, k, ks))
                peak = jnp.max(s, axis=1, keepdims=True)
                e = jnp.exp(s - peak).astype(bf16)
                outs.append(dot_nn(e, pick(key_low, v, one)))
                peaks.append(peak)
            top = jnp.where(low, outs[0], outs[1])
            total = pltpu.roll(jnp.where(low, outs[1], outs[0]), HALF, 1)
            mixed = top / total
            mixed_low = mixed.astype(bf16)
            a_ref[0, :, cols] = mixed_low
            rest_ref[0, :, cols] = (mixed - mixed_low.astype(f32)).astype(bf16)
            lse = jnp.where(low, peaks[0], peaks[1]) + jnp.log(total)
            lse_ref[0, :, cols] = split_three(-lse)

    for blocks in range(1, 2 * rows // KEY_BLOCK + 1):
        pl.when(sp[1] == blocks)(functools.partial(variant, blocks * KEY_BLOCK))


def attend_call(sp, q_all, kv_own, kv_peer, side_all, hot_all, matrix, bufs):
    rows, width = q_all.shape[1], q_all.shape[2]
    cols = PAIRS * PAIR
    part = at_window(rows, cols)
    return call(
        attend_body,
        sp,
        (width // cols,),
        [
            (q_all, part),
            (kv_own, columns(rows, 2 * cols)),
            (kv_peer, columns(rows, 2 * cols)),
            (side_all, as_given(rows, PAIR)),
            (hot_all, as_given(2 * rows, PAIR)),
            (matrix, columns(PAIR, cols)),
        ],
        [],
        [(b, part) for b in bufs[:-1]] + [(bufs[-1], at_window(rows, 2 * cols))],
        us=14,
    )


def gelu_both(x):
    cdf = 0.5 + 0.5 * lax.erf(x * math.sqrt(0.5))
    bell = jnp.exp(x * x * -0.5)
    return x * cdf, cdf + x * bell * (1.0 / math.sqrt(2.0 * math.pi))


def centered(u):
    c = u - jnp.mean(u, axis=1, keepdims=True)
    r = lax.rsqrt(jnp.mean(c * c, axis=1, keepdims=True) + epsilon)
    return c * r, r


class Moves:
    def __init__(self, sems):
        self.sems = sems
        self.used = 0
        self.out = []

    def start(self, source, target):
        copy = pltpu.make_async_copy(source, target, self.sems.at[self.used])
        self.used += 1
        copy.start()
        return copy

    def write(self, source, target):
        self.out.append(self.start(source, target))

    def finish(self):
        for copy in self.out:
            copy.wait()


def chunks(width):
    return [slice(c, c + FF_BLOCK) for c in range(0, width, FF_BLOCK)]


def dense_body(
    sp, a_ref, x_ref, wo_ref, w1_ref, w2_ref, gain_ref, bias_ref, eb_ref,
    n1_hbm, h1_hbm, g_hbm, d_hbm, n2_hbm, r_hbm, fresh_ref,
    n1_ref, h1_ref, g_ref, d_ref, n2_ref, r_ref, sems,
):
    w = sp[0]
    moves = Moves(sems)
    parts = chunks(w1_ref.shape[1])
    u1 = dot_nn(a_ref[0], wo_ref[...]) + bias_ref[2:3, :] + x_ref[0].astype(f32)
    n1, r1 = centered(u1)
    h1 = n1 * gain_ref[0:1, :] + bias_ref[3:4, :]
    h1_low = h1.astype(bf16)
    n1_ref[...] = n1.astype(bf16)
    h1_ref[...] = h1_low
    moves.write(n1_ref, n1_hbm.at[w])
    moves.write(h1_ref, h1_hbm.at[w])
    u2 = h1 + bias_ref[4:5, :]
    for c in parts:
        g, d = gelu_both(dot_nn(h1_low, w1_ref[:, c]) + eb_ref[:, c])
        g = g.astype(bf16)
        g_ref[:, c] = g
        d_ref[:, c] = d.astype(bf16)
        moves.write(g_ref.at[:, c], g_hbm.at[w, :, c])
        moves.write(d_ref.at[:, c], d_hbm.at[w, :, c])
        u2 = u2 + dot_nt(g, w2_ref[:, c])
    n2, r2 = centered(u2)
    n2_ref[...] = n2.astype(bf16)
    moves.write(n2_ref, n2_hbm.at[w])
    r_ref[...] = jnp.where(low_half(r_ref.shape), r1, r2)
    moves.write(r_ref, r_hbm.at[w])
    fresh_ref[...] = (n2 * gain_ref[1:2, :] + bias_ref[5:6, :]).astype(bf16)
    moves.finish()


def dense_call(sp, a_all, x_all, wo, w1, w2, gains, biases, eb, bufs):
    rows, width = a_all.shape[1], a_all.shape[2]
    hidden = w1.shape[1]
    row = whole_window(rows, width)
    vmem = lambda *shape: pltpu.VMEM(shape, bf16)
    return call(
        dense_body,
        sp,
        (1,),
        [
            (a_all, row), (x_all, row), (wo, RESIDENT), (w1, RESIDENT), (w2, RESIDENT), (gains, fixed(gains.shape)),
            (biases, fixed(biases.shape)), (eb, fixed(eb.shape)),
        ],
        [(jax.ShapeDtypeStruct((rows, width), bf16), pl.BlockSpec((rows, width), lambda i, sp: (0, 0)))],
        [(b, ANY) for b in bufs],
        [
            vmem(rows, width), vmem(rows, width), vmem(rows, hidden), vmem(rows, hidden), vmem(rows, width),
            pltpu.VMEM((rows, PAIR), f32), pltpu.SemaphoreType.DMA((4 + 2 * (hidden // FF_BLOCK),)),
        ],
        us=10,
    )


def column_sum(v):
    return jnp.sum(v, axis=0, keepdims=True)


def norm_back(dy, n, r, gain):
    dn = dy * gain
    return r * (dn - jnp.mean(dn, axis=1, keepdims=True) - n * jnp.mean(dn * n, axis=1, keepdims=True))


def dense_back_body(
    sp, dy_ref, got_ref, n2_ref, r_ref, gain_ref, sel_ref, wo_ref, w1_ref, w2_ref, d_hbm, n1_hbm, a_hbm,
    rest_hbm, db2_hbm, df_hbm, db1_hbm, st_ref, se_ref, do_ref, dd_ref,
    d_ref, n1_ref, a_ref, rest_ref, db2_ref, df_ref, db1_ref, sems,
):
    w = sp[0]
    width = dy_ref.shape[2]
    moves = Moves(sems)
    parts = chunks(w1_ref.shape[1])
    loads = [moves.start(d_hbm.at[w, :, c], d_ref.at[:, c]) for c in parts]
    last = [
        moves.start(n1_hbm.at[w], n1_ref), moves.start(a_hbm.at[w], a_ref),
        moves.start(rest_hbm.at[w], rest_ref),
    ]
    r = r_ref[0]
    dy = jnp.where(sp[4] == 1, dy_ref[0], got_ref[...]).astype(f32)
    n2 = n2_ref[0].astype(f32)
    du2 = norm_back(dy, n2, r[:, HALF : HALF + 1], gain_ref[1:2, :])
    db2 = du2.astype(bf16)
    db2_ref[...] = db2
    moves.write(db2_ref, db2_hbm.at[w])
    st_ref[0, 2:3, :] = column_sum(du2)
    st_ref[0, 3:4, :] = column_sum(dy)
    st_ref[0, 5:6, :] = column_sum(dy * n2)
    st_ref[0, 6:8, :] = jnp.zeros((2, width), f32)
    dh1 = du2
    for c, load in zip(parts, loads):
        load.wait()
        df = dot_nn(db2, w2_ref[:, c]) * d_ref[:, c].astype(f32)
        se_ref[0, :, c] = column_sum(df)
        df = df.astype(bf16)
        df_ref[:, c] = df
        moves.write(df_ref.at[:, c], df_hbm.at[w, :, c])
        dh1 = dh1 + dot_nt(df, w1_ref[:, c])
    for load in last:
        load.wait()
    n1 = n1_ref[...].astype(f32)
    du1 = norm_back(dh1, n1, r[:, 0:1], gain_ref[0:1, :])
    db1 = du1.astype(bf16)
    db1_ref[...] = db1
    moves.write(db1_ref, db1_hbm.at[w])
    st_ref[0, 0:1, :] = column_sum(du1)
    st_ref[0, 1:2, :] = column_sum(dh1)
    st_ref[0, 4:5, :] = column_sum(dh1 * n1)
    do = dot_nt(db1, wo_ref[...]).astype(bf16)
    do_ref[...] = do
    mixed = do.astype(f32) * (a_ref[...].astype(f32) + rest_ref[...].astype(f32))
    high = mixed.astype(bf16)
    low = (mixed - high.astype(f32)).astype(bf16)
    for begin in range(0, width, PAIR):
        cols = slice(begin, begin + PAIR)
        inner = dot_nn(high[:, cols], sel_ref[...]) + dot_nn(low[:, cols], sel_ref[...])
        dd_ref[:, cols] = split_three(-inner)
    moves.finish()


def dense_back_call(
    sp, dy_all, got, n2_all, r_all, d_all, n1_all, a_all, rest_all, wo, w1, w2, gains, sel, bufs
):
    rows, width = got.shape
    hidden = w1.shape[1]
    row = whole_window(rows, width)
    db2_all, df_all, db1_all, st_all, se_all = bufs
    flat = (jax.ShapeDtypeStruct((rows, width), bf16), pl.BlockSpec((rows, width), lambda i, sp: (0, 0)))
    vmem = lambda *shape: pltpu.VMEM(shape, bf16)
    return call(
        dense_back_body,
        sp,
        (1,),
        [
            (dy_all, as_given(rows, width)), (got, fixed(got.shape)), (n2_all, row), (r_all, whole_window(rows, PAIR)),
            (gains, fixed(gains.shape)), (sel, fixed(sel.shape)), (wo, RESIDENT), (w1, RESIDENT),
            (w2, RESIDENT),
        ]
        + [(b, ANY) for b in (d_all, n1_all, a_all, rest_all)],
        [flat, flat],
        [
            (db2_all, ANY), (df_all, ANY), (db1_all, ANY), (st_all, whole_window(8, width)),
            (se_all, whole_window(1, hidden)),
        ],
        [
            vmem(rows, hidden), vmem(rows, width), vmem(rows, width), vmem(rows, width), vmem(rows, width),
            vmem(rows, hidden), vmem(rows, width), pltpu.SemaphoreType.DMA((5 + 2 * (hidden // FF_BLOCK),)),
        ],
        us=10,
    )


def attend_back_body(
    sp, q_ref, own_ref, peer_ref, side_ref, hot_ref, m_ref, lse_ref, do_ref, dd_ref, turned_ref,
    cell_ref, dq_ref, keep_ref, send_ref,
):
    rows = q_ref.shape[1]
    total = 2 * rows
    first = sp[2] == 0

    def variant(blocks):
        keys = blocks * KEY_BLOCK
        low = low_half((rows, PAIR))
        key_low = low_half((keys, PAIR))
        block_low = low_half((KEY_BLOCK, PAIR))
        place = lax.broadcasted_iota(jnp.int32, (KEY_BLOCK, PAIR), 1)
        three = jnp.where(place % HALF < 3, 1.0, 0.0).astype(bf16)
        lone = [
            jnp.where(place < 3, 1.0, 0.0).astype(bf16),
            jnp.where((place >= HALF) & (place < HALF + 3), 1.0, 0.0).astype(bf16),
        ]
        side = side_ref[0]
        hot = hot_ref[0, :keys, :]
        for n in range(PAIRS):
            cols = slice(n * PAIR, (n + 1) * PAIR)
            kv = slice(2 * n * PAIR, 2 * (n + 1) * PAIR)
            both = in_order(first, own_ref[0, :, kv], peer_ref[0, :, kv])[:keys]
            k, v = both[:, :PAIR], both[:, PAIR:]
            ks = dot_nn(hot, m_ref[:, cols]).astype(bf16)
            kt = k.T
            q = q_ref[0, :, cols]
            do = do_ref[:, cols]
            dd = dd_ref[:, cols]
            lse = lse_ref[0, :, cols]
            kc = (jnp.where(key_low, k, ks), jnp.where(key_low, ks, k))
            qc = (jnp.where(low, q, side), jnp.where(low, side, q))
            qe = tuple(jnp.concatenate([c, lse], axis=1) for c in qc)
            dc = (jnp.where(low, do, dd), jnp.where(low, dd, do))
            dq = [None, None]
            dks = []
            dvs = []
            gs = []
            for b in range(blocks):
                at = slice(b * KEY_BLOCK, (b + 1) * KEY_BLOCK)
                vb = v[at]
                vc = (jnp.where(block_low, vb, three), jnp.where(block_low, three, vb))
                part_v = []
                part_k = []
                for head in (0, 1):
                    kb = jnp.concatenate([kc[head][at], lone[head]], axis=1)
                    p = jnp.exp(dot_nt(kb, qe[head]))
                    dp = dot_nt(vc[head], dc[head])
                    ds = (p * dp).astype(bf16)
                    part_v.append(dot_nn(p.astype(bf16), do))
                    part_k.append(dot_nn(ds, qc[head]))
                    part = dot_nn(kt[head * HALF : (head + 1) * HALF, at], ds)
                    dq[head] = part if dq[head] is None else dq[head] + part
                dvs.append(jnp.where(block_low, part_v[0], part_v[1]).astype(bf16))
                dks.append(jnp.where(block_low, part_k[0], part_k[1]).astype(bf16))
                gs.append(jnp.where(block_low, part_k[1], part_k[0]).astype(bf16))
            dq_ref[:, cols] = (jnp.concatenate(dq, axis=0).T * score_scale).astype(bf16)
            cell_ref[0, :, cols] = dot_nn(turned_ref[0, :, :keys], jnp.concatenate(gs, axis=0))
            if keys < total:
                zero = [jnp.zeros((total - keys, PAIR), bf16)]
                dks = dks + zero
                dvs = dvs + zero
            grads = jnp.concatenate([jnp.concatenate(dks, axis=0), jnp.concatenate(dvs, axis=0)], axis=1)
            keep_ref[:, kv] = jnp.where(first, grads[:rows], grads[rows:])
            send_ref[:, kv] = jnp.where(first, grads[rows:], grads[:rows])

    for blocks in range(1, total // KEY_BLOCK + 1):
        pl.when(sp[1] == blocks)(functools.partial(variant, blocks))


def attend_back_call(
    sp, q_all, kv_all, peer_all, side_all, hot_all, matrix, lse_all, do, dd, turned_all, cell_all
):
    rows, width = q_all.shape[1], q_all.shape[2]
    cols = PAIRS * PAIR
    part = at_window(rows, cols)
    kv = at_window(rows, 2 * cols)
    flat = columns(rows, cols)
    flat_kv = columns(rows, 2 * cols)
    out_kv = jax.ShapeDtypeStruct((rows, 2 * width), bf16)
    return call(
        attend_back_body,
        sp,
        (width // cols,),
        [
            (q_all, part),
            (kv_all, kv),
            (peer_all, kv),
            (side_all, as_given(rows, PAIR)),
            (hot_all, as_given(2 * rows, PAIR)),
            (matrix, columns(PAIR, cols)),
            (lse_all, part),
            (do, flat),
            (dd, flat),
            (turned_all, as_given(HALF, 2 * rows)),
        ],
        [(jax.ShapeDtypeStruct((rows, width), bf16), flat), (out_kv, flat_kv), (out_kv, flat_kv)],
        [(cell_all, at_window(HALF, cols))],
        us=20,
    )


def input_back_body(
    sp, dq_ref, own_ref, got_ref, db1_ref, w_ref, dj_ref, sj_ref, fresh_ref, total
):
    step = pl.program_id(0)
    dq = dq_ref[...]
    cols = dq.shape[1]
    both = own_ref[...].astype(f32) + got_ref[...].astype(f32)
    part = lambda at: jnp.concatenate(
        [both[:, p + at : p + at + PAIR] for p in range(0, 2 * cols, 2 * PAIR)], axis=1
    )
    dk = part(0).astype(bf16)
    dv32 = part(PAIR)
    dv = dv32.astype(bf16)
    dj_ref[0, :, :cols] = dq
    dj_ref[0, :, cols : 2 * cols] = dk
    dj_ref[0, :, 2 * cols :] = dv
    sj_ref[0] = jnp.concatenate(
        [column_sum(dq.astype(f32)), column_sum(dv32), jnp.zeros((6, cols), f32)], axis=0
    )
    width = w_ref.shape[0]
    dx = None
    for j, value in enumerate((dq, dk, dv)):
        at = pl.ds(pl.multiple_of(j * width + step * cols, cols), cols)
        term = dot_nt(value, w_ref[:, at])
        dx = term if dx is None else dx + term

    @pl.when(step == 0)
    def _():
        total[...] = dx + db1_ref[0].astype(f32)

    @pl.when(step > 0)
    def _():
        total[...] += dx

    @pl.when(step == pl.num_programs(0) - 1)
    def _():
        fresh_ref[...] = total[...].astype(bf16)


def input_back_call(sp, dq, own, got, db1_all, weight, dj_all, sj_all):
    rows, width = dq.shape
    cols = PAIRS * PAIR
    steps = width // cols
    return call(
        input_back_body,
        sp,
        (steps,),
        [
            (dq, columns(rows, cols)), (own, columns(rows, 2 * cols)), (got, columns(rows, 2 * cols)),
            (db1_all, whole_window(rows, width)), (weight, RESIDENT),
        ],
        [(jax.ShapeDtypeStruct((rows, width), bf16), pl.BlockSpec((rows, width), lambda i, sp: (0, 0)))],
        [
            (dj_all, at_window(rows, 3 * cols)), (sj_all, at_window(8, cols)),
        ],
        [pltpu.VMEM((rows, width), f32)],
        us=4,
    )


def weight_body(splits, based, sp, *refs):
    count = len(splits)
    lefts, rights = refs[:count], refs[count : 2 * count]
    base_refs = refs[2 * count : 2 * count + 2] if based else ()
    give_ref, keep_ref = refs[-2:]
    step = pl.program_id(0)
    windows, rows, width = lefts[0].shape
    half = width // 2
    first = sp[2] == 0

    for (begin, end), left, right in zip(splits, lefts, rights):

        @pl.when((step >= begin) & (step < end))
        def _(left=left, right=right):
            flat = left[...].reshape(windows * rows, width)
            out = dot_tn(flat, right[...].reshape(windows * rows, right.shape[2]))
            give = jnp.where(first, out[half:], out[:half])
            keep = jnp.where(first, out[:half], out[half:])
            if based:
                give = give + base_refs[0][...].astype(f32)
                keep = keep + base_refs[1][...].astype(f32)
            give_ref[...] = give.astype(bf16)
            keep_ref[...] = keep.astype(bf16)


def weight_call(sp, at, windows, pairs, base=()):
    rows, width = pairs[0][0].shape[1:]
    splits = []
    begin = 0
    for _, right in pairs:
        splits.append((begin, begin + right.shape[2] // FF_BLOCK))
        begin = splits[-1][1]

    def left_spec():
        return pl.BlockSpec(
            (windows, rows, width), lambda i, sp: (at, 0, 0), pipeline_mode=pl.Buffered(1)
        )

    def right_spec(begin, end):
        return pl.BlockSpec(
            (windows, rows, FF_BLOCK), lambda i, sp: (at, 0, jnp.clip(i - begin, 0, end - begin - 1))
        )

    half = columns(width // 2, FF_BLOCK)
    shape = jax.ShapeDtypeStruct((width // 2, begin * FF_BLOCK), bf16)
    return call(
        functools.partial(weight_body, tuple(splits), bool(base)),
        sp,
        (begin,),
        [(left, left_spec()) for left, _ in pairs]
        + [(right, right_spec(*split)) for (_, right), split in zip(pairs, splits)]
        + [(b, half) for b in base],
        [(shape, half), (shape, half)],
        [],
        us=5 + 3 * windows,
    )


def spread_body(moves, sp, mine_ref, got_ref, *out_refs):
    half = pl.num_programs(0) // 2
    mine = (pl.program_id(0) // half) == sp[2]
    value = jnp.where(mine, mine_ref[...], got_ref[...]).astype(f32)
    for (out, to), begin, count in moves:
        out_refs[out][:, to : to + count] = value[:, begin : begin + count]


def spread_call(sp, mine, got, widths, moves):
    half, cols = mine.shape
    block = half // 4
    turn = lambda i, sp, core: jnp.where(i // 4 == core, i % 4, jnp.where(core == 0, 3, 0))
    return call(
        functools.partial(spread_body, moves),
        sp,
        (8,),
        [
            (mine, pl.BlockSpec((block, cols), lambda i, sp: (turn(i, sp, sp[2]), 0))),
            (got, pl.BlockSpec((block, cols), lambda i, sp: (turn(i, sp, 1 - sp[2]), 0))),
        ],
        [
            (jax.ShapeDtypeStruct((2 * half, w), f32), pl.BlockSpec((block, w), lambda i, sp: (i, 0)))
            for w in widths
        ],
        [],
        us=5,
    )


def bucket_maps(position_cells, counts):
    key = jnp.arange(HALF, dtype=jnp.int32)[:, None]
    query = jnp.arange(HALF, dtype=jnp.int32)[None, :]
    begins = (0, position_cells, position_cells + GRID, HALF)
    bucket = jnp.full((HALF, HALF), -1, jnp.int32)
    base = 0
    for j, offset in enumerate((counts[0] // 2, GRID - 1, GRID - 1)):
        inside = (key >= begins[j]) & (key < begins[j + 1]) & (query >= begins[j]) & (query < begins[j + 1])
        ids = jnp.clip(query - key, -offset, counts[j] - 1 - offset) + offset + base
        bucket = jnp.where(inside, ids, bucket)
        base += counts[j]
    return bucket[:, :, None] == jnp.arange(base, dtype=jnp.int32)


def cell_matrix(tables, maps, position_cells):
    whole = jnp.concatenate(tables, axis=0)
    heads = whole.shape[1]
    whole = whole.reshape(-1, heads // 2, 2)[:, :, ::-1].reshape(-1, heads)
    m = jnp.einsum("bh,xcb->xhc", whole, maps.astype(bf16), preferred_element_type=f32)
    m = m.reshape(HALF, heads * HALF).astype(bf16)
    lane = jnp.arange(heads * HALF, dtype=jnp.int32) % HALF
    dead = jnp.where(lane < position_cells, masked, 0.0).astype(bf16)[None]
    return jnp.concatenate([m, dead, jnp.zeros((HALF - 1, heads * HALF), bf16)], axis=0)


def table_grads(cells, maps, counts):
    heads = cells.shape[1] // HALF
    whole = jnp.einsum(
        "xcb,xhc->bh", maps.astype(f32), cells.reshape(HALF, heads, HALF), precision=lax.Precision.HIGHEST
    )
    whole = whole.reshape(-1, heads // 2, 2)[:, :, ::-1].reshape(-1, heads)
    a, b = counts[0], counts[0] + counts[1]
    return [whole[:a], whole[a:b], whole[b:]]


def after(value, earlier):
    return lax.optimization_barrier((value, earlier))[0]


class Ring:
    def __init__(self, count):
        self.count = count
        self.index = lax.axis_index("dp")
        bits = list(range(1, count.bit_length() - 1))
        turned = bits[:2][::-1] + bits[2:]
        self.mixed = list(zip(bits, turned))
        self.plain = list(zip(bits, bits))

    def bit(self, step):
        even, odd = step
        return jnp.where(self.index % 2 == 0, (self.index >> even) & 1, (self.index >> odd) & 1)

    def send(self, a, step):
        even, odd = step
        pairs = [(i, i ^ (1 << (even if i % 2 == 0 else odd))) for i in range(self.count)]
        return lax.ppermute(a, "dp", pairs)

    def swap(self, a):
        return lax.ppermute(a, "dp", [(i, i ^ 1) for i in range(self.count)])

    def halve(self, part, step):
        half = part.shape[0] // 2
        bit = self.bit(step)
        keep = lax.dynamic_slice_in_dim(part, bit * half, half, 0)
        give = lax.dynamic_slice_in_dim(part, (1 - bit) * half, half, 0)
        return keep, self.send(give, step)

    def join(self, part, got, step):
        first = self.bit(step) == 0
        return jnp.concatenate([jnp.where(first, part, got), jnp.where(first, got, part)], axis=0)

    def stages(self, give, keep, steps):
        got = self.swap(give)
        order = yield
        part = keep + order(got)
        for step in steps:
            keep, got = self.halve(part, step)
            order = yield part
            part = keep + order(got)
        for step in steps[::-1]:
            got = self.send(part, step)
            order = yield part
            part = self.join(part, order(got), step)
        got = self.swap(part)
        order = yield part
        self.result = (part, order(got))
        yield self.result[1]

    def totals(self, part):
        for bit in range(self.count.bit_length() - 1):
            got = lax.ppermute(part, "dp", [(i, i ^ (1 << bit)) for i in range(self.count)])
            order = yield part
            part = part + order(got)
        yield part


SLOTS = (
    ("F", 0, None),
    ("F", 1, 0),
    ("B", None, 0),
    ("F", 2, 1),
    ("B", 0, 1),
    ("F", 3, 2),
    ("B", 1, 2),
    ("F", None, 3),
    ("B", 2, 3),
    ("B", 3, None),
)


def on_device(
    boundary, doc_lengths, horizontal, vertical, attention_in, attention_out, expand_weight,
    contract_weight, norm_gains, bias_rows, expand_bias, position_table, horizontal_table,
    vertical_table,
):
    section = lax.axis_index("section")
    dp_count = lax.axis_size("dp")
    core = lax.axis_index("dp") % 2
    swap = [(i, i ^ 1) for i in range(dp_count)]
    exchange = lambda a: lax.ppermute(a, "dp", swap)

    own = boundary[0]
    micro, slots, width = own.shape
    rows = slots // 2
    windows = 2 * micro
    hidden = expand_weight.shape[2]
    heads = position_table.shape[2]
    pairs = heads // 2
    w_in, w_out, w1, w2 = in_vmem([attention_in[0], attention_out[0], expand_weight[0], contract_weight[0]])
    gains = norm_gains[0].astype(f32)
    biases = bias_rows[0].astype(f32)
    eb = expand_bias.astype(f32)
    in_bias = jnp.concatenate([biases[0], jnp.zeros_like(biases[0]), biases[1]])[None]
    tables = (position_table[0], horizontal_table[0], vertical_table[0])
    counts = tuple(t.shape[0] for t in tables)
    position_cells = slots // SPAN
    maps = bucket_maps(position_cells, counts)
    ring = Ring(dp_count)

    def both(mine, theirs):
        return jnp.concatenate(
            [jnp.where(core == 0, mine, theirs), jnp.where(core == 0, theirs, mine)], axis=0
        )

    halves = own.reshape(micro, 2, rows, width)
    own_half = jnp.where(core == 0, halves[:, 0], halves[:, 1])
    other_half = jnp.where(core == 0, halves[:, 1], halves[:, 0])
    own_all = both(own_half, exchange(other_half))
    places = jnp.concatenate(
        [horizontal, vertical, jnp.broadcast_to(doc_lengths[:, None], (micro, PAIR))], axis=1
    )
    places = both(places, exchange(places))
    across_cell = places[:, :slots] // SPAN
    down_cell = places[:, slots : 2 * slots] // SPAN
    lengths = places[:, 2 * slots]
    ids = jnp.arange(slots, dtype=jnp.int32)
    position_cell = jnp.broadcast_to((ids // SPAN)[None], (windows, slots))

    def hot_of(cells, lanes, axis):
        p, a, d = (jnp.expand_dims(c, axis) for c in cells)
        lanes = jnp.expand_dims(lanes, (0, 3 - axis))
        return (lanes == p) | (lanes == a + position_cells) | (lanes == d + position_cells + GRID)

    cells = (position_cell, across_cell, down_cell)
    cell_ids = jnp.arange(PAIR, dtype=jnp.int32)
    turned_all = hot_of(cells, cell_ids[:HALF], 1).astype(bf16)
    dead = (ids[None, :] >= lengths[:, None])[:, :, None] & (cell_ids == HALF)
    hot_all = (hot_of(cells, cell_ids, 2) | dead).astype(bf16)
    take = lambda c: jnp.where(core == 0, c[:, :rows], c[:, rows:])
    side_all = hot_of(tuple(take(c) for c in cells), cell_ids % HALF, 2).astype(bf16)
    matrix = cell_matrix(tables, maps, position_cells)

    sel = (cell_ids[:, None] // HALF != cell_ids[None, :] // HALF).astype(bf16)

    window_ids = jnp.arange(windows, dtype=jnp.int32)
    mine, theirs = lengths[:windows][:, None], lengths[:windows][None, :]
    ahead = (theirs > mine) | ((theirs == mine) & (window_ids[None, :] < window_ids[:, None]))
    rank = jnp.sum(ahead.astype(jnp.int32), axis=1)
    picks = jnp.stack(
        [jnp.array([windows if w is None else w for w in slots_of], jnp.int32) for slots_of in zip(*[s[1:] for s in SLOTS])]
    )
    infos = jnp.where(section == 0, picks[0], picks[1])
    hits = infos[:, None] == rank[None, :]
    given_ids = jnp.sum(jnp.where(hits, window_ids[None, :], 0), axis=1)
    given_lengths = jnp.sum(jnp.where(hits, lengths[None, :windows], 0), axis=1)
    infos = jnp.stack(
        [
            infos, (given_lengths + KEY_BLOCK - 1) // KEY_BLOCK, jnp.full_like(infos, core),
            given_lengths, jnp.full_like(infos, section), given_ids,
        ],
        axis=1,
    )
    facts = infos.shape[1]
    infos = infos.reshape(-1)

    widths = dict(
        x=width, q=width, kv=2 * width, a=width, rest=width, lse=width, peer=2 * width, n1=width, h1=width,
        g=hidden, d=hidden, n2=width, db2=width, df=hidden, db1=width, dj=3 * width,
    )
    shapes = {n: jax.ShapeDtypeStruct((windows + 1, rows, c), bf16) for n, c in widths.items()}
    shapes["r"] = jax.ShapeDtypeStruct((windows + 1, rows, PAIR), f32)
    shapes["st"] = shapes["sj"] = jax.ShapeDtypeStruct((windows + 1, 8, width), f32)
    shapes["se"] = jax.ShapeDtypeStruct((windows + 1, 1, hidden), f32)
    shapes["cell"] = jax.ShapeDtypeStruct((windows + 1, HALF, width), f32)
    st = dict(zip(shapes, unwritten(list(shapes.values()))))

    def forward(sp, s, got):
        x, q, kv, fresh = qkv_call(sp, own_all, got, w_in, in_bias, s["x"], s["q"], s["kv"])
        s = dict(s, x=x, q=q, kv=kv)
        mixed = ("a", "rest", "lse", "peer")
        s.update(
            zip(mixed, attend_call(
                sp, q, fresh, exchange(fresh), side_all, hot_all, matrix, tuple(s[n] for n in mixed)
            ))
        )
        names = ("n1", "h1", "g", "d", "n2", "r")
        outs = dense_call(
            sp, s["a"], x, w_out, w1, w2, gains, biases, eb, tuple(s[n] for n in names)
        )
        s.update(zip(names, outs[:-1]))
        return s, outs[-1]

    def dense_back(sp, s, got):
        names = ("db2", "df", "db1", "st", "se")
        outs = dense_back_call(
            sp, own_all, got, s["n2"], s["r"], s["d"], s["n1"], s["a"], s["rest"], w_out, w1, w2, gains,
            sel, tuple(s[n] for n in names),
        )
        s = dict(s)
        s.update(zip(names, outs[:5]))
        return s, tuple(outs[5:])

    def attend_back_kernel(sp, s, grads):
        return attend_back_call(
            sp, s["q"], s["kv"], s["peer"], side_all, hot_all, matrix, s["lse"], *grads, turned_all,
            s["cell"],
        )

    def input_back(sp, s, dq, keep, got):
        dj, sj, fresh = input_back_call(sp, dq, keep, got, s["db1"], w_in, s["dj"], s["sj"])
        return dict(s, dj=dj, sj=sj), fresh

    def attend_back(sp, s, grads):
        cell, dq, keep, send = attend_back_kernel(sp, s, grads)
        return input_back(sp, dict(s, cell=cell), dq, keep, exchange(send))

    got = {}
    finals = {}
    grads_in = {}
    nothing = jnp.zeros((rows, width), bf16)

    for number, (kind, zero, one) in enumerate(SLOTS[:-1]):
        sp = (infos, number * facts)
        if kind == "F":
            st, out = forward(sp, st, got.pop(("F", one), nothing))
            if one is not None:
                finals[one] = out
            if zero is not None:
                got["F", zero] = lax.ppermute(out, "section", [(0, 1)])
        else:
            st, grads = dense_back(sp, st, got.pop(("B", zero), nothing))
            st, out = attend_back(sp, st, grads)
            if zero is not None:
                grads_in[zero] = out
            if one is not None:
                got["B", one] = lax.ppermute(out, "section", [(1, 0)])

    sp = (infos, (len(SLOTS) - 1) * facts)

    class Chain:
        def __init__(self, stages, count):
            self.stages = stages
            self.left = count
            next(stages)

        def advance(self, earlier):
            self.last = self.stages.send(lambda got: after(got, earlier))
            self.left -= 1
            return self.last

    def weight_sum(steps, give, keep):
        return give, Chain(ring.stages(give, keep, steps), 2 * len(steps) + 2)

    natural = [((0, 0), 0, hidden)]
    cols = PAIRS * PAIR
    moves = [
        ((0, j * width + i * cols), (3 * i + j) * cols, cols) for i in range(width // cols) for j in range(3)
    ] + [((1, 0), 3 * width, width)]

    others = windows - 1
    part_contract = weight_call(sp, 0, others, [(after(st["db2"], out), st["g"])])
    part_expand = weight_call(sp, 0, others, [(after(st["h1"], part_contract[0]), st["df"])])
    rows_in = after(got.pop(("B", SLOTS[-1][1])), part_expand[0])
    st, grads = dense_back(sp, st, rows_in)
    halves = weight_call(sp, others, 1, [(st["db2"], st["g"])], part_contract)
    given, contract = weight_sum(ring.plain, *halves)
    halves = weight_call(sp, others, 1, [(after(st["h1"], given), st["df"])], part_expand)
    given, expand = weight_sum(ring.plain, *halves)
    done = contract.advance(given)
    grads = tuple(after(g, done) for g in grads)
    cell, dq, keep, send = attend_back_kernel(sp, st, grads)
    got = exchange(send)
    done = expand.advance(dq)
    got = after(got, done)
    st, grads_in[SLOTS[-1][1]] = input_back(sp, dict(st, cell=cell), dq, keep, got)
    done = contract.advance(st["dj"])
    halves = weight_call(sp, 0, windows, [(after(st["x"], done), st["dj"]), (st["a"], st["db1"])])
    given, attend = weight_sum(ring.mixed, *halves)
    done = contract.advance(given)
    done = expand.advance(done)
    done = attend.advance(done)

    result = [jnp.where(section == 0, after(grads_in[w], done), after(finals[w], done)) for w in range(windows)]
    result = jnp.stack(result)
    ranks = after(rank, done)
    ordered = [lax.dynamic_index_in_dim(result, ranks[w], 0, keepdims=False) for w in range(windows)]
    mine_first, mine_second = jnp.stack(ordered[:micro]), jnp.stack(ordered[micro:])
    keep_rows = jnp.where(core == 0, mine_first, mine_second)
    give_rows = jnp.where(core == 0, mine_second, mine_first)
    got_rows = exchange(give_rows)

    def assembled(got_rows):
        out_halves = jnp.stack(
            [jnp.where(core == 0, keep_rows, got_rows), jnp.where(core == 0, got_rows, keep_rows)], axis=1
        )
        return out_halves.reshape(1, micro, slots, width)

    done = attend.advance(give_rows)
    done = contract.advance(done)
    done = expand.advance(done)

    of_windows = lambda name: jnp.sum(after(st[name], done)[:windows], axis=0)
    small = [of_windows("sj")[0:2], of_windows("st")[0:6], of_windows("se")] + table_grads(
        of_windows("cell"), maps, counts
    )
    packed = jnp.concatenate([p.reshape(-1) for p in small])
    packed = jnp.pad(packed, (0, -packed.shape[0] % (8 * PAIR))).reshape(-1, PAIR)
    totals = Chain(ring.totals(packed), dp_count.bit_length() - 1)
    done = packed
    chains = {"attend": attend, "contract": contract, "expand": expand, "totals": totals}
    kinds = {"contract": ([hidden], natural), "expand": ([hidden], natural), "attend": ([3 * width, width], moves)}
    outputs = {}
    waiting = []
    boundary_out = None
    while any(chain.left for chain in chains.values()):
        for name, chain in chains.items():
            if not chain.left:
                continue
            done = chain.advance(done)
            for other, (mine, theirs) in waiting:
                outputs[other] = spread_call(sp, after(mine, done), theirs, *kinds[other])
                done = outputs[other][0]
            waiting = [(name, ring.result)] if not chain.left and name in kinds else []
        if boundary_out is None and not totals.left:
            boundary_out = assembled(after(got_rows, done))
            done = boundary_out
    for other, halves in waiting:
        outputs[other] = spread_call(sp, *halves, *kinds[other])
    (g_contract,), (g_expand,), (g_in, g_out) = (outputs[n] for n in ("contract", "expand", "attend"))
    packed = totals.last.reshape(-1)
    pieces = []
    begin = 0
    for p in small:
        count = math.prod(p.shape)
        pieces.append(packed[begin : begin + count].reshape(p.shape))
        begin += count
    joined_sums, sums, wide, table_p, table_h, table_v = pieces
    grad_bias = jnp.concatenate([joined_sums, sums[0:4]], axis=0)
    grad_gain = sums[4:6]
    return (
        boundary_out, g_in[None], g_out[None], g_expand[None], g_contract[None], grad_gain[None],
        grad_bias[None], wide, table_p[None], table_h[None], table_v[None],
    )


def solution(mesh):
    section = P("section", None, None)
    placed = (
        P("section", "dp", None, None), P("dp"), P("dp", None), P("dp", None), section, section,
        section, section, section, section, P("section", None), section, section, section,
    )
    return jax.shard_map(
        on_device,
        mesh=mesh,
        in_specs=placed,
        out_specs=(
            P("section", "dp", None, None), section, section, section, section, section, section,
            P("section", None), section, section, section,
        ),
        check_vma=False,
    )
```
